32 devices in a mesh: groups: 2 (over y), dp: 4 (over x, core), tensor: 4 (over z).
Axes of the slice: x: 2, y: 2, z: 4, core: 2. Of those that a mesh axis runs over, the one named last changes fastest.
Arguments:
- tokens: bfloat16 [4096, 4096], P(('groups', 'dp'), 'tensor'), parts along dimension 0, may hold values from -96 to 96
- query_key_value_weight: bfloat16 [4096, 6, 512], P(None, None, 'tensor'), may hold values from -0.09375 to 0.09375
- output_weight: bfloat16 [512, 4, 4096], P('tensor'), may hold values from -0.125 to 0.125
- adapter_down_maps: bfloat16 [8, 192, 4096], P(('groups', 'dp'), None, 'tensor'), parts along dimension 0, may hold values from -0.09375 to 0.09375
- adapter_up_maps: bfloat16 [8, 64, 6, 512], P(('groups', 'dp'), None, None, 'tensor'), parts along dimension 0, may hold values from -0.75 to 0.75
- output_down_maps: bfloat16 [8, 64, 4, 512], P(('groups', 'dp'), None, None, 'tensor'), parts along dimension 0, may hold values from -0.125 to 0.125
- output_up_maps: bfloat16 [8, 64, 4096], P(('groups', 'dp'), None, 'tensor'), parts along dimension 0, may hold values from -0.75 to 0.75
- request_adapter: int32 [8, 4], P(('groups', 'dp')), parts along dimension 0, may hold values from 0 to 3
- lengths: int32 [8, 4], P(('groups', 'dp')), parts along dimension 0, may hold values from 1 to 256, 512 in all within a row
Outputs:
- layer_out: bfloat16 [4096, 4096], P(('groups', 'dp'), 'tensor'), parts along dimension 0
The draws below stay inside these ranges and needn't reach their ends.
There are 2 independent parts, one for each index of `groups`. The reference program is written for one: setup_inputs(seed, part) draws one part's arguments, and reference() takes and returns one part's arrays. A program takes and returns all parts, laid end to end along the dimension named above; an argument that names none is the same for every part. Nothing has to cross between parts.
Inputs may be any that keep to these rules, and one draw needn't show every extreme that they name: `lengths`: each row sums to 512; its largest entry is 256.
All inputs are finite; a program needn't handle non-finite values.
Results may differ from the reference program's by a relative error of at most 0.01225.
The reference program's roundings to bfloat16 on the way count: a program that leaves them out, or rounds other values in their place, can miss the bound.
Values may be sent and summed in bfloat16 or wider, within the bound.
No kernel may reach another device: no remote copies, remote signals or barrier semaphores. Data moves between devices by JAX's collectives and lax.ppermute only.
A program may use at most 128 MiB of HBM per device.

```python
import math
import jax
import jax.numpy as jnp
import numpy as np
from jax import lax

MODEL_WIDTH = 4096
HD = 128
GROUP_QUERIES = 4
ADAPTER_RANK = 64
TOK_DEV = 512
REQ_DEV = 4
KEY_WIDTH = 512
TOKENS = 2048
ADAPTER_COUNT = 4
N_DP = 4
N_TENSOR = 4


def draw_tokens(key, part):
    key = jax.random.fold_in(key, 11)
    values = jnp.clip(jax.random.normal(key, (TOKENS, MODEL_WIDTH), jnp.float32), -6.0, 6.0)
    return values.astype(jnp.bfloat16)


def place_ends(values, stream_key, low, top_value):
    longest = values.shape.index(max(values.shape))
    spots = []
    for shift in (0, 1):
        where = [jax.random.randint(jax.random.fold_in(stream_key, axis), (), 0, length) for axis, length in enumerate(values.shape)]
        where[longest] = (where[longest] + shift) % values.shape[longest]
        spots.append(tuple(where))
    return values.at[spots[0]].set(low).at[spots[1]].set(top_value)


def levels(rng, dims, split, low, top_value):
    def one(axis_at, parts):
        heights = jax.random.uniform(jax.random.fold_in(jax.random.fold_in(rng, 6), axis_at), (parts,), jnp.float32, low / len(split), top_value / len(split))
        return jnp.repeat(jnp.exp(heights), dims[axis_at] // parts).reshape((-1,) + (1,) * (len(dims) - axis_at - 1))

    loudness = one(*split[0])
    for cut in split[1:]:
        loudness = loudness * one(*cut)
    return loudness


def profile(count, total, reach, skew):
    portions = [(1 << 20) // math.isqrt(standing ** skew) + 1 for standing in range(2, count + 1)]
    spare, holding = total - reach - (count - 1), [1] * (count - 1)
    while spare > 0:
        free = [i for i in range(count - 1) if holding[i] < reach]
        whole, remaining = sum([portions[i] for i in free]), spare
        for i in free:
            more = min(reach - holding[i], max(1, remaining * portions[i] // whole), spare)
            holding[i] = holding[i] + more
            spare = spare - more
    return np.array([reach] + holding)


def ragged(own_key, amount, total, most, skew):
    if amount == 2:
        one = jax.random.randint(own_key, (), max(1, total - most), min(most, total - 1) + 1)
        return jnp.stack([one, total - one])
    sizes = jnp.asarray(profile(amount, total, most, skew), jnp.int32)
    couples = (amount - 1) // 2
    source_of, taker = sizes[1:1 + 2 * couples:2], sizes[2:2 + 2 * couples:2]
    room = jnp.minimum(source_of - 1, most - taker)
    moved = jax.random.randint(jax.random.fold_in(own_key, 1), (couples,), 0, 1 << 20) % (room + 1)
    sizes = sizes.at[1:1 + 2 * couples:2].set(source_of - moved).at[2:2 + 2 * couples:2].set(taker + moved)
    return sizes[jax.random.permutation(jax.random.fold_in(own_key, 2), amount)]


def noise(own_key, extent, deviation, most, split=(), held_as=jnp.bfloat16):
    array = jax.random.normal(own_key, extent, jnp.float32) * deviation
    if len(split) > 0:
        array = levels(own_key, extent, split, -0.22, 0.18) * array
    return jnp.clip(array, min=-most, max=most).astype(held_as)


def setup_inputs(seed: int = 0, part: int = 0) -> dict:
    key_of = jax.random.split(jax.random.key(seed), 10)
    part_keys = jax.random.split(jax.random.fold_in(key_of[9], part), 10)
    tokens = draw_tokens(jax.random.fold_in(jax.random.fold_in(key_of[9], part), 71), part)
    query_key_value_weight = noise(key_of[1], (MODEL_WIDTH, GROUP_QUERIES + 2, KEY_WIDTH), MODEL_WIDTH ** -0.5, 0.09375, ((2, 4),))
    output_weight = noise(key_of[2], (KEY_WIDTH, GROUP_QUERIES, MODEL_WIDTH), (GROUP_QUERIES * KEY_WIDTH) ** -0.5, 0.125, ((0, 4),))
    adapter_down_maps = noise(part_keys[3], (ADAPTER_COUNT, 3 * ADAPTER_RANK, MODEL_WIDTH), MODEL_WIDTH ** -0.5, 0.09375, ((0, 4), (2, 4)))
    adapter_up_maps = noise(part_keys[4], (ADAPTER_COUNT, ADAPTER_RANK, GROUP_QUERIES + 2, KEY_WIDTH), ADAPTER_RANK ** -0.5, 0.75, ((0, 4), (3, 4)))
    output_down_maps = noise(part_keys[5], (ADAPTER_COUNT, ADAPTER_RANK, GROUP_QUERIES, KEY_WIDTH), (GROUP_QUERIES * KEY_WIDTH) ** -0.5, 0.125, ((0, 4), (3, 4)))
    output_up_maps = noise(part_keys[6], (ADAPTER_COUNT, ADAPTER_RANK, MODEL_WIDTH), ADAPTER_RANK ** -0.5, 0.75, ((0, 4), (2, 4)))
    request_adapter = place_ends(jax.random.randint(part_keys[7], (N_DP, REQ_DEV), 0, ADAPTER_COUNT), jax.random.fold_in(part_keys[7], 1), 0, ADAPTER_COUNT - 1).astype(jnp.int32)
    lengths = jax.vmap(lambda own: ragged(own, REQ_DEV, TOK_DEV, TOK_DEV // 2, 2))(jax.random.split(part_keys[8], N_DP)).reshape((N_DP, REQ_DEV)).astype(jnp.int32)
    return dict(tokens=tokens, query_key_value_weight=query_key_value_weight, output_weight=output_weight, adapter_down_maps=adapter_down_maps, adapter_up_maps=adapter_up_maps, output_down_maps=output_down_maps, output_up_maps=output_up_maps, request_adapter=request_adapter, lengths=lengths)


def layout(lengths_row, tok_count):
    req_ends = jnp.cumsum(lengths_row)
    starts = req_ends - lengths_row
    tok_index = jnp.arange(tok_count, dtype=jnp.int32)
    member = (tok_index[None, :] >= starts[:, None]) & (tok_index[None, :] < req_ends[:, None])
    weight_matrix = member.astype(jnp.float32)
    position = tok_index - lax.optimization_barrier(jnp.sum(jnp.where(member, starts[:, None], 0), axis=0)).astype(jnp.int32)
    order = jnp.arange(lengths_row.shape[0], dtype=jnp.int32)
    segment = lax.optimization_barrier(jnp.sum(jnp.where(member, order[:, None], 0), axis=0)).astype(jnp.int32)
    return (weight_matrix, position, segment)

def rotate(vectors, position):
    half_size = vectors.shape[-1] // 2
    inv_freq = 10000.0 ** (-2.0 * jnp.arange(half_size, dtype=jnp.float32) / vectors.shape[-1])
    angles = position.astype(jnp.float32)[:, None] * inv_freq[None, :]
    angles = angles.reshape((angles.shape[0],) + (1,) * (vectors.ndim - 2) + (half_size,))
    cosine = jnp.cos(angles)
    sine = jnp.sin(angles)
    first = vectors[..., :half_size]
    second = vectors[..., half_size:]
    return jnp.concatenate([first * cosine - second * sine, second * cosine + first * sine], axis=-1)

def attend(queries, keys_rot, values, position, segment):
    scores = jnp.einsum('tpgc,ugc->gptu', queries.astype(jnp.float32), keys_rot.astype(jnp.float32)) / math.sqrt(HD)
    allowed = (segment[:, None] == segment[None, :]) & (position[None, :] <= position[:, None])
    scores = jnp.where(allowed[None, None], scores, -1e+30)
    row_max = lax.optimization_barrier(jnp.max(scores, axis=-1, keepdims=True))
    weights_exp = jnp.exp(scores - row_max)
    probabilities = (weights_exp / lax.optimization_barrier(jnp.sum(weights_exp, axis=-1, keepdims=True))).astype(jnp.bfloat16)
    attended = jnp.einsum('gptu,ugc->tpgc', probabilities.astype(jnp.float32), values.astype(jnp.float32))
    return attended.astype(jnp.bfloat16)

def reference(tokens, query_key_value_weight, output_weight, adapter_down_maps, adapter_up_maps, output_down_maps, output_up_maps, request_adapter, lengths):
    flat_qkv = query_key_value_weight.reshape(MODEL_WIDTH, (GROUP_QUERIES + 2) * KEY_WIDTH)
    head_out = output_weight.reshape(N_TENSOR, HD, GROUP_QUERIES, MODEL_WIDTH).astype(jnp.float32)

    def one_block(block_args):
        block_rows, adapter_index_row, lengths_row = block_args
        weight_matrix, position, segment = layout(lengths_row, TOK_DEV)
        base_proj = jnp.dot(block_rows, flat_qkv, preferred_element_type=jnp.float32).reshape(TOK_DEV, GROUP_QUERIES + 2, N_TENSOR, HD)
        chosen_down = adapter_down_maps[adapter_index_row].astype(jnp.float32)
        partial_shrink = jnp.einsum('td,qkd->qtk', block_rows.astype(jnp.float32), chosen_down)
        reduced_rows = jnp.einsum('qt,qtk->tk', weight_matrix, partial_shrink).astype(jnp.bfloat16)
        masked = weight_matrix[:, :, None, None] * reduced_rows.reshape(TOK_DEV, 3, ADAPTER_RANK).astype(jnp.float32)[None]
        chosen_up = adapter_up_maps[adapter_index_row].astype(jnp.float32)
        query_extra = jnp.einsum('qtr,qrsc->tsc', masked[:, :, 0], chosen_up[:, :, :GROUP_QUERIES])
        key_extra = jnp.einsum('qtr,qrc->tc', masked[:, :, 1], chosen_up[:, :, GROUP_QUERIES])
        value_extra = jnp.einsum('qtr,qrc->tc', masked[:, :, 2], chosen_up[:, :, GROUP_QUERIES + 1])
        expanded = jnp.concatenate([query_extra, key_extra[:, None], value_extra[:, None]], axis=1)
        projected = base_proj + expanded.reshape(TOK_DEV, GROUP_QUERIES + 2, N_TENSOR, HD)
        queries = rotate(projected[:, :GROUP_QUERIES], position).astype(jnp.bfloat16)
        keys_rot = rotate(projected[:, GROUP_QUERIES], position).astype(jnp.bfloat16)
        values = projected[:, GROUP_QUERIES + 1].astype(jnp.bfloat16)
        attended = attend(queries, keys_rot, values, position, segment)
        partial_value = jnp.einsum('tpgc,gcpd->tgd', attended.astype(jnp.float32), head_out).astype(jnp.bfloat16)
        partial_value = lax.optimization_barrier(partial_value)
        plain_output = lax.optimization_barrier(jnp.sum(partial_value.astype(jnp.float32), axis=1))
        odown_sel = output_down_maps[adapter_index_row].astype(jnp.float32).reshape(REQ_DEV, ADAPTER_RANK, GROUP_QUERIES, N_TENSOR, HD)
        out_partial = jnp.einsum('tpgc,qrpgc->qtr', attended.astype(jnp.float32), odown_sel)
        out_shrink = jnp.einsum('qt,qtr->tr', weight_matrix, out_partial).astype(jnp.bfloat16)
        output_masked_rows = weight_matrix[:, :, None] * out_shrink.astype(jnp.float32)[None]
        adapter_output = jnp.einsum('aei,aiu->eu', output_masked_rows, output_up_maps[adapter_index_row].astype(jnp.float32))
        return (plain_output + adapter_output).astype(jnp.bfloat16)
    blocks = lax.map(one_block, (tokens.reshape(N_DP, TOK_DEV, MODEL_WIDTH), request_adapter, lengths))
    return blocks.reshape(TOKENS, MODEL_WIDTH)
```

```python
import functools
import math

import jax
import jax.numpy as jnp
from jax import lax
from jax.experimental import pallas as pl
from jax.experimental.pallas import tpu as pltpu
from jax.sharding import PartitionSpec as P

CHUNKS = 2
VMEM_BYTES = 48 * 1024 * 1024
PLANE = ("groups", "dp")


def attend_kernel(
    shards, first_row, outer, head_size, slots, ids_ref, start_ref, cos_ref, sin_ref, low_ref,
    up_ref, *refs
):
    token_refs, w_ref = refs[:shards], refs[shards]
    rest = refs[shards + 1 :]
    prior = rest[:2] if first_row else ()
    attended_ref, keys_ref, values_ref, acc_ref = rest[len(prior) :]
    step = pl.program_id(0)
    rows = acc_ref.shape[0]
    queries = slots - 2

    def wide(left, right):
        return jnp.concatenate([left, right], axis=1)

    def accumulate(token_ref, first):
        for pair in range(slots // 2):
            columns = slice(2 * pair * head_size, (2 * pair + 2) * head_size)
            if outer:
                depth = w_ref.shape[2]
                total = None
                for piece in range(w_ref.shape[0]):
                    part = jnp.dot(
                        token_ref[:, piece * depth : (piece + 1) * depth],
                        wide(w_ref[piece, 2 * pair], w_ref[piece, 2 * pair + 1]),
                        preferred_element_type=jnp.float32,
                    )
                    total = part if total is None else total + part
            else:
                total = jnp.dot(
                    token_ref[...],
                    wide(w_ref[2 * pair], w_ref[2 * pair + 1]),
                    preferred_element_type=jnp.float32,
                )
            if first:
                acc_ref[:, columns] = total
            else:
                acc_ref[:, columns] += total

    for number in range(shards):
        pl.when(step == number)(
            functools.partial(accumulate, token_refs[number], number == 0)
        )

    @pl.when(step == shards - 1)
    def _():
        cos, sin = cos_ref[...], sin_ref[...]

        def slot(index):
            which = 0 if index < queries else index - queries + 1
            extra = jnp.dot(low_ref[which], up_ref[index], preferred_element_type=jnp.float32)
            return acc_ref[:, index * head_size : (index + 1) * head_size] + extra

        def rotated(index):
            value = slot(index)
            turned = pltpu.roll(value, head_size // 2, 1)
            return (value * cos + turned * sin).astype(jnp.bfloat16)

        keys = rotated(queries)
        values = slot(queries + 1).astype(jnp.bfloat16)
        keys_ref[...] = keys
        values_ref[...] = values
        if first_row:
            keys = jnp.concatenate([prior[0][...], keys], axis=0)
            values = jnp.concatenate([prior[1][...], values], axis=0)
        key_rows = keys.shape[0]
        key_at = lax.broadcasted_iota(jnp.int32, (rows, key_rows), 1)
        row_at = lax.broadcasted_iota(jnp.int32, (rows, key_rows), 0) + first_row
        allowed = (key_at >= start_ref[...]) & (key_at <= row_at)
        for index in range(queries):
            scores = lax.dot_general(
                rotated(index), keys, (((1,), (1,)), ((), ())), preferred_element_type=jnp.float32
            )
            scores = jnp.where(allowed, scores * (1.0 / math.sqrt(head_size)), -1e30)
            weights = jnp.exp(scores - jnp.max(scores, axis=1, keepdims=True))
            scale = 1.0 / jnp.sum(weights, axis=1, keepdims=True)
            attended = jnp.dot(
                (weights * scale).astype(jnp.bfloat16), values, preferred_element_type=jnp.float32
            )
            attended_ref[:, index * head_size : (index + 1) * head_size] = attended.astype(
                jnp.bfloat16
            )


def attend_chunk(ids, start, cos, sin, low, up, tokens, weight, outer, prior):
    shards = len(tokens)
    rows, depth = tokens[0].shape
    slots, _, head_size = up.shape
    first_row = prior[0].shape[0] if prior else 0
    whole = pl.BlockSpec(memory_space=pltpu.VMEM)
    if outer:
        pieces = weight.shape[0] // shards
        w_spec = pl.BlockSpec(
            (pieces,) + weight.shape[1:], lambda step, ids_ref: (ids_ref[step], 0, 0, 0)
        )
    else:
        w_spec = pl.BlockSpec(
            (slots, depth, head_size), lambda step, ids_ref: (0, ids_ref[step], 0)
        )
    width = slots * head_size
    out = (
        jax.ShapeDtypeStruct((rows, width - 2 * head_size), jnp.bfloat16),
        jax.ShapeDtypeStruct((rows, head_size), jnp.bfloat16),
        jax.ShapeDtypeStruct((rows, head_size), jnp.bfloat16),
    )
    flops = 2 * rows * depth * shards * width
    return pl.pallas_call(
        functools.partial(attend_kernel, shards, first_row, outer, head_size, slots),
        out_shape=out,
        grid_spec=pltpu.PrefetchScalarGridSpec(
            num_scalar_prefetch=1,
            grid=(shards,),
            in_specs=[whole] * (5 + shards) + [w_spec] + [whole] * len(prior),
            out_specs=[whole] * 3,
            scratch_shapes=[pltpu.VMEM((rows, width), jnp.float32)],
        ),
        compiler_params=pltpu.CompilerParams(vmem_limit_bytes=VMEM_BYTES),
        cost_estimate=pl.CostEstimate(
            flops=2 * flops, bytes_accessed=2 * shards * depth * (width + rows), transcendentals=0
        ),
        name="attend",
    )(ids, start, cos, sin, low, up, *tokens, weight, *prior)


def output_kernel(groups, ids_ref, mask_ref, up_ref, *refs):
    attended_refs = refs[:groups]
    w_ref, down_ref, out_ref, acc_ref, low_ref = refs[groups:]
    step = pl.program_id(0)

    def accumulate(attended_ref, first):
        attended = attended_ref[...]
        part = jnp.dot(attended, w_ref[0], preferred_element_type=jnp.float32)
        low = lax.dot_general(
            attended, down_ref[0], (((1,), (1,)), ((), ())), preferred_element_type=jnp.float32
        )
        if first:
            acc_ref[...] = part
            low_ref[...] = low
        else:
            acc_ref[...] += part
            low_ref[...] += low

    for number in range(groups):
        pl.when(step == number)(
            functools.partial(accumulate, attended_refs[number], number == 0)
        )

    @pl.when(step == groups - 1)
    def _():
        low = low_ref[...].astype(jnp.bfloat16) * mask_ref[...]
        extra = jnp.dot(low, up_ref[...], preferred_element_type=jnp.float32)
        out_ref[...] = (acc_ref[...] + extra).astype(jnp.bfloat16)


def output_chunk(ids, mask, up, attended, weight, down):
    groups = len(attended)
    rows = attended[0].shape[0]
    features, columns = weight.shape[1:]
    ranks = down.shape[1]
    whole = pl.BlockSpec(memory_space=pltpu.VMEM)
    return pl.pallas_call(
        functools.partial(output_kernel, groups),
        out_shape=jax.ShapeDtypeStruct((rows, columns), jnp.bfloat16),
        grid_spec=pltpu.PrefetchScalarGridSpec(
            num_scalar_prefetch=1,
            grid=(groups,),
            in_specs=[whole] * (2 + groups)
            + [
                pl.BlockSpec((1, features, columns), lambda step, ids_ref: (ids_ref[step], 0, 0)),
                pl.BlockSpec((1, ranks, features), lambda step, ids_ref: (ids_ref[step], 0, 0)),
            ],
            out_specs=whole,
            scratch_shapes=[
                pltpu.VMEM((rows, columns), jnp.float32),
                pltpu.VMEM((rows, ranks), jnp.float32),
            ],
        ),
        compiler_params=pltpu.CompilerParams(vmem_limit_bytes=VMEM_BYTES),
        cost_estimate=pl.CostEstimate(
            flops=2 * rows * groups * features * (columns + ranks),
            bytes_accessed=2 * groups * features * (columns + ranks + rows),
            transcendentals=0,
        ),
        name="project_out",
    )(ids, mask, up, *attended, weight, down)


def local(
    plane_size,
    planes,
    tokens,
    query_key_value_weight,
    output_weight,
    adapter_down_maps,
    adapter_up_maps,
    output_down_maps,
    output_up_maps,
    request_adapter,
    lengths,
):
    token_rows, depth = tokens.shape
    _, slots, head_size = query_key_value_weight.shape
    queries = slots - 2
    rank = adapter_up_maps.shape[1]
    features = queries * head_size
    model_width = output_weight.shape[2]
    columns = model_width // planes
    pairs = planes // 2

    def worker(pair):
        return 2 * pair + 1 - pair % 2

    def outer(pair):
        return 2 * pair + pair % 2

    to_worker = [(outer(p), worker(p)) for p in range(pairs)]
    from_worker = [(worker(p), outer(p)) for p in range(pairs)]
    ring = [(worker(p), worker((p + 1) % pairs)) for p in range(pairs)]
    here = lax.axis_index("tensor")
    pair = here // 2
    is_worker = here == worker(pair)
    ids = []
    for step in range(pairs):
        source = (pair - step + pairs) % pairs
        ids += [worker(source), outer(source)]
    ids = jnp.stack(ids).astype(jnp.int32)
    place = lax.axis_index(PLANE)

    chunk_rows = token_rows // CHUNKS
    token_bundles = []
    for chunk in range(CHUNKS):
        own = tokens[chunk * chunk_rows : (chunk + 1) * chunk_rows]
        other = lax.ppermute(own, "tensor", to_worker)
        bundle = [own, other]
        for _ in range(pairs - 1):
            own = lax.ppermute(own, "tensor", ring)
            other = lax.ppermute(other, "tensor", ring)
            bundle += [own, other]
        token_bundles.append(bundle)

    weight = jnp.transpose(query_key_value_weight, (1, 0, 2))
    share = weight.shape[1] // plane_size
    piece = lax.dynamic_slice_in_dim(weight, place * share, share, axis=1)
    piece = lax.ppermute(piece, "tensor", to_worker)
    outer_weight = lax.all_gather(piece, PLANE, axis=0)

    request_ends = jnp.cumsum(lengths[0])
    request_starts = request_ends - lengths[0]
    at = jnp.arange(token_rows, dtype=jnp.int32)
    member = (at[:, None] >= request_starts[None, :]) & (at[:, None] < request_ends[None, :])
    start = jnp.sum(jnp.where(member, request_starts[None, :], 0), axis=1).astype(jnp.int32)
    position = at - start
    half = head_size // 2
    inv_freq = 10000.0 ** (-2.0 * jnp.arange(half, dtype=jnp.float32) / head_size)
    angles = position.astype(jnp.float32)[:, None] * inv_freq[None, :]
    cosine, sine = jnp.cos(angles), jnp.sin(angles)
    cos = jnp.concatenate([cosine, cosine], axis=1)
    sin = jnp.concatenate([-sine, sine], axis=1)

    down_all = lax.all_gather(adapter_down_maps, "dp", axis=0, tiled=True)
    up_own = jnp.transpose(adapter_up_maps[0], (1, 0, 2))
    up_pair = jnp.stack([up_own, lax.ppermute(up_own, "tensor", to_worker)])
    up_all = lax.all_gather(up_pair, "dp", axis=0)
    out_down_all = lax.all_gather(
        output_down_maps.reshape(rank, features), ("dp", "tensor"), axis=0
    ).reshape(-1, planes, rank, features)
    out_up_all = lax.all_gather(output_up_maps, "dp", axis=0, tiled=True)
    pool = up_all.shape[0]
    requests = request_adapter.shape[1]
    if pool <= requests:
        chosen = member @ jax.nn.one_hot(request_adapter[0], pool, dtype=jnp.float32) > 0.5
    else:
        chosen = member
        down_all, up_all, out_down_all, out_up_all = (
            jnp.take(maps, request_adapter[0], axis=0)
            for maps in (down_all, up_all, out_down_all, out_up_all)
        )
    count = chosen.shape[1]
    partial = jnp.einsum("td,akd->tak", tokens, down_all, preferred_element_type=jnp.float32)
    shrink = jnp.sum(jnp.where(chosen[:, :, None], partial, 0.0), axis=1)
    shrink = shrink + lax.ppermute(shrink, "tensor", to_worker)
    moving = shrink
    for _ in range(pairs - 1):
        moving = lax.ppermute(moving, "tensor", ring)
        shrink = shrink + moving
    shrink = shrink.astype(jnp.bfloat16).reshape(token_rows, 3, 1, rank)
    low = jnp.where(chosen[:, None, :, None], shrink, jnp.zeros((), jnp.bfloat16))
    low = jnp.transpose(low.reshape(token_rows, 3, count * rank), (1, 0, 2))
    ups = jnp.transpose(up_all, (1, 2, 0, 3, 4)).reshape(2, slots, count * rank, head_size)
    out_downs = jnp.transpose(out_down_all, (1, 0, 2, 3)).reshape(planes, count * rank, features)
    out_ups = out_up_all.reshape(count * rank, columns)
    out_mask = jnp.repeat(chosen.astype(jnp.bfloat16), rank, axis=1)

    lines = head_size // plane_size
    piece = lax.dynamic_slice_in_dim(output_weight, place * lines, lines, axis=0)
    piece = jnp.transpose(piece.reshape(lines, queries, planes, columns), (2, 1, 0, 3))
    piece = lax.all_to_all(piece, "tensor", 0, 0)
    gathered = lax.all_gather(piece, PLANE, axis=0)
    out_weight = jnp.transpose(gathered, (1, 2, 0, 3, 4)).reshape(planes, features, columns)

    outs = []
    prior = ((), ())
    for chunk in range(CHUNKS):
        rows = slice(chunk * chunk_rows, (chunk + 1) * chunk_rows)
        results = [
            attend_chunk(
                ids, start[rows, None], cos[rows], sin[rows], low[:, rows], ups[which],
                token_bundles[chunk], (weight, outer_weight)[which], which == 1, prior[which],
            )
            for which in range(2)
        ]
        prior = tuple(
            tuple(
                jnp.concatenate([old, new], axis=0) for old, new in zip(prior[which], result[1:])
            ) if prior[which] else result[1:]
            for which, result in enumerate(results)
        )
        bundle = [result[0] for result in results]
        attended = list(bundle)
        for _ in range(pairs - 1):
            bundle = [lax.ppermute(part, "tensor", ring) for part in bundle]
            attended += bundle
        attended = [
            jnp.where(is_worker, part, lax.ppermute(part, "tensor", from_worker))
            for part in attended
        ]
        outs.append(
            output_chunk(ids, out_mask[rows], out_ups, attended, out_weight, out_downs)
        )
    return jnp.concatenate(outs, axis=0)


def solution(mesh):
    in_specs = (
        P(PLANE, "tensor"),
        P(None, None, "tensor"),
        P("tensor", None, None),
        P(PLANE, None, "tensor"),
        P(PLANE, None, None, "tensor"),
        P(PLANE, None, None, "tensor"),
        P(PLANE, None, "tensor"),
        P(PLANE, None),
        P(PLANE, None),
    )
    function = functools.partial(
        local, mesh.shape["groups"] * mesh.shape["dp"], mesh.shape["tensor"]
    )
    return jax.shard_map(
        function, mesh=mesh, in_specs=in_specs, out_specs=P(PLANE, "tensor"), check_vma=False
    )
```

```python
import functools
import math

import jax
import jax.numpy as jnp
from jax import lax
from jax.experimental import pallas as pl
from jax.experimental.pallas import tpu as pltpu
from jax.sharding import PartitionSpec as P

CHUNKS = 2
VMEM_BYTES = 48 * 1024 * 1024
PLANE = ("groups", "dp")
WHOLE = pl.BlockSpec(memory_space=pltpu.VMEM)


def after(value, *earlier):
    return lax.optimization_barrier((value,) + earlier)[0]


def wide_slots(w_refs, pair):
    if len(w_refs[0].shape) == 3:
        parts = [w_ref[...] for w_ref in w_refs]
    else:
        parts = [
            w_ref[piece] for piece in range(w_refs[0].shape[0]) for w_ref in w_refs
        ]
    wide = [jnp.concatenate([part[2 * pair], part[2 * pair + 1]], axis=1) for part in parts]
    return wide[0] if len(wide) == 1 else jnp.concatenate(wide, axis=0)


def accumulate(acc_ref, token_refs, w_refs, first):
    slots, _, head_size = w_refs[0].shape[-3:]
    for pair in range(slots // 2):
        columns = slice(2 * pair * head_size, (2 * pair + 2) * head_size)
        weight = wide_slots(w_refs, pair)
        row = 0
        for token_ref in token_refs:
            rows = slice(row, row + token_ref.shape[0])
            row = rows.stop
            total = jnp.dot(token_ref[...], weight, preferred_element_type=jnp.float32)
            if first is None:
                acc_ref[rows, columns] = total
            else:
                acc_ref[rows, columns] = first[rows, columns] + total


def split_refs(refs, layout):
    groups, at = [], 0
    for count in layout:
        groups.append(refs[at : at + count])
        at += count
    return groups, refs[at:]


def project_kernel(layout, weights, ids_ref, *refs):
    tokens, rest = split_refs(refs, layout)
    w_refs, acc_ref = rest[:weights], rest[weights]
    step = pl.program_id(0)
    for number, token_refs in enumerate(tokens):
        pl.when(step == number)(
            functools.partial(
                accumulate, acc_ref, token_refs, w_refs, acc_ref if number else None
            )
        )


def attend_kernel(layout, weights, started, first_row, ids_ref, *refs):
    start_ref, cos_ref, sin_ref, low_ref, up_ref = refs[:5]
    tokens, rest = split_refs(refs[5:], layout)
    w_refs, rest = rest[:weights], rest[weights:]
    begun, rest = rest[:started], rest[started:]
    prior = rest[:2] if first_row else ()
    attended_ref, keys_ref, values_ref, acc_ref = rest[len(prior) :]
    slots, _, head_size = w_refs[0].shape[-3:]
    step = pl.program_id(0)
    rows = acc_ref.shape[0]
    block = min(rows, 256)
    queries = slots - 2

    for number, token_refs in enumerate(tokens):
        first = acc_ref if number else (begun[0] if begun else None)
        pl.when(step == number)(
            functools.partial(accumulate, acc_ref, token_refs, w_refs, first)
        )

    @pl.when(step == len(layout) - 1)
    def _():
        def slot(index, at):
            which = 0 if index < queries else index - queries + 1
            extra = jnp.dot(
                low_ref[which, at], up_ref[index], preferred_element_type=jnp.float32
            )
            return acc_ref[at, index * head_size : (index + 1) * head_size] + extra

        def rotated(index, at):
            value = slot(index, at)
            turned = pltpu.roll(value, head_size // 2, 1)
            return (value * cos_ref[at, :] + turned * sin_ref[at, :]).astype(jnp.bfloat16)

        for row in range(0, rows, block):
            at = slice(row, row + block)
            keys_ref[at, :] = rotated(queries, at)
            values_ref[at, :] = slot(queries + 1, at).astype(jnp.bfloat16)
            keys, values = keys_ref[: row + block], values_ref[: row + block]
            if first_row:
                keys = jnp.concatenate([prior[0][...], keys], axis=0)
                values = jnp.concatenate([prior[1][...], values], axis=0)
            key_rows = keys.shape[0]
            key_at = lax.broadcasted_iota(jnp.int32, (block, key_rows), 1)
            row_at = lax.broadcasted_iota(jnp.int32, (block, key_rows), 0) + (first_row + row)
            allowed = (key_at >= start_ref[at, :]) & (key_at <= row_at)
            for index in range(queries):
                scores = lax.dot_general(
                    rotated(index, at), keys, (((1,), (1,)), ((), ())),
                    preferred_element_type=jnp.float32,
                )
                scores = jnp.where(allowed, scores * (1.0 / math.sqrt(head_size)), -1e30)
                weights_exp = jnp.exp(scores - jnp.max(scores, axis=1, keepdims=True))
                scale = 1.0 / jnp.sum(weights_exp, axis=1, keepdims=True)
                attended = jnp.dot(
                    (weights_exp * scale).astype(jnp.bfloat16), values,
                    preferred_element_type=jnp.float32,
                )
                attended_ref[at, index * head_size : (index + 1) * head_size] = (
                    attended.astype(jnp.bfloat16)
                )


def weight_spec(weight, depth):
    if len(weight.shape) == 3:
        slots, _, head_size = weight.shape
        return pl.BlockSpec((slots, depth, head_size), lambda step, ids: (0, ids[step], 0))
    pieces = depth // (weight.shape[2] * weight.shape[0] // weight.shape[0])
    return pl.BlockSpec((pieces,) + weight.shape[1:], lambda step, ids: (ids[step], 0, 0, 0))


def weight_specs(weights, depth):
    if len(weights) == 1 and len(weights[0].shape) == 3:
        return [weight_spec(weights[0], depth)]
    pieces = depth // sum(weight.shape[2] for weight in weights)
    return [
        pl.BlockSpec((pieces,) + weight.shape[1:], lambda step, ids: (ids[step], 0, 0, 0))
        for weight in weights
    ]


PARAMS = pltpu.CompilerParams(vmem_limit_bytes=VMEM_BYTES)
COST = pl.CostEstimate(flops=1000, bytes_accessed=1000, transcendentals=0)


def project(ids, tokens, weights):
    depth = tokens[0][0].shape[1]
    rows = sum(part.shape[0] for part in tokens[0])
    slots, _, head_size = weights[0].shape[-3:]
    return pl.pallas_call(
        functools.partial(project_kernel, [len(parts) for parts in tokens], len(weights)),
        out_shape=jax.ShapeDtypeStruct((rows, slots * head_size), jnp.float32),
        grid_spec=pltpu.PrefetchScalarGridSpec(
            num_scalar_prefetch=1,
            grid=(len(tokens),),
            in_specs=[WHOLE] * sum(len(parts) for parts in tokens)
            + weight_specs(weights, depth),
            out_specs=WHOLE,
        ),
        compiler_params=PARAMS,
        cost_estimate=COST,
        name="project",
    )(ids, *[part for parts in tokens for part in parts], *weights)


def attend(ids, tables, up, tokens, weights, begun, prior):
    depth = tokens[0][0].shape[1]
    rows = sum(part.shape[0] for part in tokens[0])
    slots, _, head_size = weights[0].shape[-3:]
    first_row = prior[0].shape[0] if prior else 0
    out = (
        jax.ShapeDtypeStruct((rows, (slots - 2) * head_size), jnp.bfloat16),
        jax.ShapeDtypeStruct((rows, head_size), jnp.bfloat16),
        jax.ShapeDtypeStruct((rows, head_size), jnp.bfloat16),
    )
    parts = [part for parts in tokens for part in parts]
    return pl.pallas_call(
        functools.partial(
            attend_kernel, [len(item) for item in tokens], len(weights), len(begun), first_row
        ),
        out_shape=out,
        grid_spec=pltpu.PrefetchScalarGridSpec(
            num_scalar_prefetch=1,
            grid=(len(tokens),),
            in_specs=[WHOLE] * (5 + len(parts))
            + weight_specs(weights, depth)
            + [WHOLE] * (len(begun) + len(prior)),
            out_specs=[WHOLE] * 3,
            scratch_shapes=[pltpu.VMEM((rows, slots * head_size), jnp.float32)],
        ),
        compiler_params=PARAMS,
        cost_estimate=COST,
        name="attend",
    )(ids, *tables, up, *parts, *weights, *begun, *prior)


def output_kernel(groups, parts, begun, last, ids_ref, *refs):
    attended_refs, rest = refs[: groups * parts * 2], refs[groups * parts * 2 :]
    w_ref, down_ref = rest[:2]
    rest = rest[2:]
    begun_refs, rest = rest[: 2 * begun], rest[2 * begun :]
    if last:
        mask_ref, up_ref, out_ref, acc_ref, low_ref = rest
    else:
        acc_ref, low_ref = rest
    step = pl.program_id(0)

    def accumulate_group(number, side):
        row = 0
        for part in range(parts):
            attended = attended_refs[(number * parts + part) * 2 + side][...]
            at = slice(row, row + attended.shape[0])
            row = at.stop
            total = jnp.dot(attended, w_ref[0], preferred_element_type=jnp.float32)
            low = lax.dot_general(
                attended, down_ref[0], (((1,), (1,)), ((), ())),
                preferred_element_type=jnp.float32,
            )
            if number:
                total, low = acc_ref[at, :] + total, low_ref[at, :] + low
            elif begun:
                total, low = begun_refs[0][at, :] + total, begun_refs[1][at, :] + low
            acc_ref[at, :] = total
            low_ref[at, :] = low

    for number in range(groups):
        for side in range(2):
            pl.when((step == number) & (ids_ref[groups] == side))(
                functools.partial(accumulate_group, number, side)
            )

    if last:
        @pl.when(step == groups - 1)
        def _():
            low = low_ref[...].astype(jnp.bfloat16) * mask_ref[...]
            extra = jnp.dot(low, up_ref[...], preferred_element_type=jnp.float32)
            out_ref[...] = (acc_ref[...] + extra).astype(jnp.bfloat16)


def project_out(ids, is_worker, attended, weight, down, begun, final):
    groups, parts = len(attended), len(attended[0])
    rows = sum(part[0].shape[0] for part in attended[0])
    features, columns = weight.shape[1:]
    ranks = down.shape[1]
    ids = jnp.concatenate([ids, is_worker.astype(jnp.int32)[None]])
    flat = [array for group in attended for part in group for array in part]
    sums = [
        jax.ShapeDtypeStruct((rows, columns), jnp.float32),
        jax.ShapeDtypeStruct((rows, ranks), jnp.float32),
    ]
    return pl.pallas_call(
        functools.partial(output_kernel, groups, parts, len(begun) // 2, bool(final)),
        out_shape=jax.ShapeDtypeStruct((rows, columns), jnp.bfloat16) if final else sums,
        grid_spec=pltpu.PrefetchScalarGridSpec(
            num_scalar_prefetch=1,
            grid=(groups,),
            in_specs=[WHOLE] * len(flat)
            + [
                pl.BlockSpec((1, features, columns), lambda step, ids: (ids[step], 0, 0)),
                pl.BlockSpec((1, ranks, features), lambda step, ids: (ids[step], 0, 0)),
            ]
            + [WHOLE] * (len(begun) + len(final)),
            out_specs=WHOLE if final else [WHOLE] * 2,
            scratch_shapes=[pltpu.VMEM(item.shape, jnp.float32) for item in sums]
            if final else [],
        ),
        compiler_params=PARAMS,
        cost_estimate=COST,
        name="project_out",
    )(ids, *flat, weight, down, *begun, *final)


def gather_over(value, axis, size):
    here = lax.axis_index(axis)
    value = value[None]
    distance = size // 2
    while distance:
        moved = lax.ppermute(value, axis, [(i, i ^ distance) for i in range(size)])
        upper = (here // distance) % 2 == 1
        value = jnp.concatenate(
            [jnp.where(upper, moved, value), jnp.where(upper, value, moved)], axis=0
        )
        distance //= 2
    return value


def bit_order(size):
    order = [0]
    distance = size // 2
    while distance:
        order = order + [place + distance for place in order]
        distance //= 2
    return order


def local(
    dp_size,
    plane_size,
    planes,
    tokens,
    query_key_value_weight,
    output_weight,
    adapter_down_maps,
    adapter_up_maps,
    output_down_maps,
    output_up_maps,
    request_adapter,
    lengths,
):
    token_rows, depth = tokens.shape
    _, slots, head_size = query_key_value_weight.shape
    queries = slots - 2
    rank = adapter_up_maps.shape[1]
    features = queries * head_size
    columns = output_weight.shape[2] // planes
    pairs = planes // 2

    def worker(pair):
        return 2 * pair + 1 - pair % 2

    def outer(pair):
        return 2 * pair + pair % 2

    to_worker = [(outer(p), worker(p)) for p in range(pairs)]
    from_worker = [(worker(p), outer(p)) for p in range(pairs)]
    ring = [(worker(p), worker((p + 1) % pairs)) for p in range(pairs)]
    here = lax.axis_index("tensor")
    pair = here // 2
    is_worker = here == worker(pair)
    sources = [(pair - step + pairs) % pairs for step in range(pairs)]
    worker_ids = jnp.stack([worker(source) for source in sources]).astype(jnp.int32)
    outer_ids = jnp.stack([outer(source) for source in sources]).astype(jnp.int32)
    place = lax.axis_index(PLANE)

    own_tokens = [tokens]
    for _ in range(pairs - 1):
        own_tokens.append(lax.ppermute(own_tokens[-1], "tensor", ring))

    weight = jnp.transpose(query_key_value_weight, (1, 0, 2))
    share = weight.shape[1] // plane_size
    up_own = jnp.transpose(adapter_up_maps[0], (1, 0, 2))
    up_outer = lax.ppermute(up_own, "tensor", to_worker)
    shares = []
    for half in range(2):
        piece = lax.dynamic_slice_in_dim(
            weight, place * share + half * (share // 2), share // 2, axis=1
        )
        shares.append(lax.ppermute(piece, "tensor", to_worker))
    outer_weights = [lax.all_gather(piece, PLANE, axis=0) for piece in shares]

    chunk_rows = token_rows // CHUNKS
    outer_tokens = []
    previous = shares[1]
    for chunk in range(CHUNKS):
        part = after(tokens[chunk * chunk_rows : (chunk + 1) * chunk_rows], previous)
        previous = lax.ppermute(part, "tensor", to_worker)
        moving = [previous]
        for _ in range(pairs - 1):
            moving.append(lax.ppermute(moving[-1], "tensor", ring))
        outer_tokens.append(moving)

    request_ends = jnp.cumsum(lengths[0])
    request_starts = request_ends - lengths[0]
    at = jnp.arange(token_rows, dtype=jnp.int32)
    member = (at[:, None] >= request_starts[None, :]) & (at[:, None] < request_ends[None, :])
    start = jnp.sum(jnp.where(member, request_starts[None, :], 0), axis=1).astype(jnp.int32)
    position = at - start
    half = head_size // 2
    inv_freq = 10000.0 ** (-2.0 * jnp.arange(half, dtype=jnp.float32) / head_size)
    angles = position.astype(jnp.float32)[:, None] * inv_freq[None, :]
    cosine, sine = jnp.cos(angles), jnp.sin(angles)
    cos = jnp.concatenate([cosine, cosine], axis=1)
    sin = jnp.concatenate([-sine, sine], axis=1)

    down = adapter_down_maps[0].reshape(-1, head_size)
    pack = jnp.concatenate(
        [
            down,
            up_own.reshape(-1, head_size),
            up_outer.reshape(-1, head_size),
            output_up_maps[0].reshape(-1, head_size),
        ],
        axis=0,
    )
    sizes = [down.shape[0], slots * rank, slots * rank]
    order = jnp.array(bit_order(dp_size))
    pack = gather_over(pack, "dp", dp_size)
    down_all, up_all, up_other, out_up_all = jnp.split(
        pack, [sizes[0], sizes[0] + sizes[1], sum(sizes)], axis=1
    )
    down_all = down_all.reshape(dp_size, 3 * rank, depth)
    up_all = jnp.stack([up_all, up_other], axis=1).reshape(
        dp_size, 2, slots, rank, head_size
    )
    out_up_all = out_up_all.reshape(dp_size, rank, columns)
    pool = dp_size
    requests = request_adapter.shape[1]
    chosen_id = jnp.sum(jnp.where(member, request_adapter, 0), axis=1)
    if pool <= requests:
        chosen = chosen_id[:, None] == order[None, :]
    else:
        chosen = member
        spots = jnp.argmax(request_adapter[0][:, None] == order[None, :], axis=1)
        down_all, up_all, out_up_all = (
            jnp.take(maps, spots, axis=0) for maps in (down_all, up_all, out_up_all)
        )
    count = chosen.shape[1]
    partial = jnp.einsum("td,akd->tak", tokens, down_all, preferred_element_type=jnp.float32)
    shrink = jnp.sum(jnp.where(chosen[:, :, None], partial, 0.0), axis=1)
    shrink = shrink + lax.ppermute(shrink, "tensor", to_worker)
    moving = shrink
    for _ in range(pairs - 1):
        moving = lax.ppermute(moving, "tensor", ring)
        shrink = shrink + moving
    shrink = shrink.astype(jnp.bfloat16).reshape(token_rows, 3, 1, rank)
    low = jnp.where(chosen[:, None, :, None], shrink, jnp.zeros((), jnp.bfloat16))
    low = jnp.transpose(low.reshape(token_rows, 3, count * rank), (1, 0, 2))
    ups = jnp.transpose(up_all, (1, 2, 0, 3, 4)).reshape(2, slots, count * rank, head_size)
    out_ups = out_up_all.reshape(count * rank, columns)
    out_mask = jnp.repeat(chosen.astype(jnp.bfloat16), rank, axis=1)

    lines = head_size // plane_size
    piece = lax.dynamic_slice_in_dim(output_weight, place * lines, lines, axis=0)
    piece = jnp.transpose(piece.reshape(lines, queries, planes, columns), (2, 1, 0, 3))
    out_down = output_down_maps[0].reshape(rank, features)
    ready = own_tokens[-1]
    got, got_down = [lax.dynamic_index_in_dim(piece, here, 0, False)], [out_down]
    for turn in range(1, planes):
        send = lax.dynamic_index_in_dim(piece, (here + turn) % planes, 0, False)
        send = jnp.concatenate(
            [send.reshape(-1, columns), out_down.reshape(-1, columns)], axis=0
        )
        got_one = lax.ppermute(
            after(send, ready), "tensor", [(i, (i + turn) % planes) for i in range(planes)]
        )
        lines_got = queries * lines
        got.append(got_one[:lines_got].reshape(queries, lines, columns))
        got_down.append(got_one[lines_got:].reshape(rank, features))
    turned = gather_over(jnp.stack(got), "groups", plane_size // dp_size)
    turned = gather_over(turned, "dp", dp_size)
    turned_down = gather_over(jnp.stack(got_down), "dp", dp_size)
    turned = turned[jnp.argsort(order)]
    out_weight = jnp.transpose(turned, (2, 3, 1, 0, 4, 5)).reshape(planes, features, columns)
    if pool > requests:
        turned_down = jnp.take(turned_down, spots, axis=0)
    out_downs = jnp.transpose(turned_down, (1, 0, 2, 3)).reshape(planes, count * rank, features)

    tables = (start[:, None], cos, sin, low)
    begun = project(worker_ids, [(array,) for array in own_tokens], [weight])
    own_parts, prior = [], ()
    for chunk in range(CHUNKS):
        rows = slice(chunk * chunk_rows, (chunk + 1) * chunk_rows)
        attended, keys, values = attend(
            outer_ids,
            (start[rows, None], cos[rows], sin[rows], low[:, rows]),
            ups[0],
            [(array,) for array in outer_tokens[chunk]],
            [weight],
            [begun[rows]],
            prior,
        )
        prior = (keys, values)
        own_parts.append(attended)
    all_ids = jnp.concatenate([worker_ids, outer_ids])
    outer_part, _, _ = attend(
        all_ids,
        tables,
        ups[1],
        [(array,) for array in own_tokens]
        + [
            tuple(outer_tokens[chunk][step] for chunk in range(CHUNKS)) for step in range(pairs)
        ],
        outer_weights,
        [],
        (),
    )

    def spread(parts):
        result, moving = [], parts
        for step in range(pairs):
            if step:
                moving = [lax.ppermute(part, "tensor", ring) for part in moving]
            result.append(
                [(lax.ppermute(part, "tensor", from_worker), part) for part in moving]
            )
        return result

    def turns(ids):
        return (here - ids + planes) % planes

    begun = project_out(
        turns(worker_ids), is_worker, spread(own_parts), out_weight, out_downs, [], []
    )
    return project_out(
        turns(outer_ids), is_worker, spread([outer_part]), out_weight, out_downs,
        list(begun), [out_mask, out_ups],
    )


def solution(mesh):
    in_specs = (
        P(PLANE, "tensor"),
        P(None, None, "tensor"),
        P("tensor", None, None),
        P(PLANE, None, "tensor"),
        P(PLANE, None, None, "tensor"),
        P(PLANE, None, None, "tensor"),
        P(PLANE, None, "tensor"),
        P(PLANE, None),
        P(PLANE, None),
    )
    function = functools.partial(
        local,
        mesh.shape["dp"],
        mesh.shape["groups"] * mesh.shape["dp"],
        mesh.shape["tensor"],
    )
    return jax.shard_map(
        function, mesh=mesh, in_specs=in_specs, out_specs=P(PLANE, "tensor"), check_vma=False
    )
```

```python
import functools
import math

import jax
import jax.numpy as jnp
from jax import lax
from jax.experimental import pallas as pl
from jax.experimental.pallas import tpu as pltpu
from jax.sharding import PartitionSpec as P

CHUNKS = 2
VMEM_BYTES = 48 * 1024 * 1024
PLANE = ("groups", "dp")


def after(value, *earlier):
    return lax.optimization_barrier((value,) + earlier)[0]


def wide_slots(w_refs, pair):
    if len(w_refs[0].shape) == 3:
        parts = [w_ref[...] for w_ref in w_refs]
    else:
        parts = [
            w_ref[piece] for piece in range(w_refs[0].shape[0]) for w_ref in w_refs
        ]
    wide = [jnp.concatenate([part[2 * pair], part[2 * pair + 1]], axis=1) for part in parts]
    return wide[0] if len(wide) == 1 else jnp.concatenate(wide, axis=0)


def accumulate(acc_ref, token_refs, w_refs, first):
    slots, _, head_size = w_refs[0].shape[-3:]
    for pair in range(slots // 2):
        columns = slice(2 * pair * head_size, (2 * pair + 2) * head_size)
        weight = wide_slots(w_refs, pair)
        row = 0
        for token_ref in token_refs:
            rows = slice(row, row + token_ref.shape[0])
            row = rows.stop
            total = jnp.dot(token_ref[...], weight, preferred_element_type=jnp.float32)
            if first is None:
                acc_ref[rows, columns] = total
            else:
                acc_ref[rows, columns] = first[rows, columns] + total


def split_refs(refs, layout):
    groups, at = [], 0
    for count in layout:
        groups.append(refs[at : at + count])
        at += count
    return groups, refs[at:]


def project_kernel(layout, weights, ids_ref, *refs):
    tokens, rest = split_refs(refs, layout)
    w_refs, acc_ref = rest[:weights], rest[weights]
    step = pl.program_id(0)
    for number, token_refs in enumerate(tokens):
        pl.when(step == number)(
            functools.partial(
                accumulate, acc_ref, token_refs, w_refs, acc_ref if number else None
            )
        )


def attend_kernel(layout, weights, sums, started, which, ids_ref, table_ref, turn_ref, up_ref, *refs):
    sum_refs, refs = refs[:sums], refs[sums:]
    tokens, rest = split_refs(refs, layout)
    w_refs, rest = rest[:weights], rest[weights:]
    begun, prior, rest = rest[:started[0]], rest[started[0] : started[0] + started[1]], rest[sum(started) :]
    attended_ref, keys_ref, values_ref, acc_ref = rest
    first_row = prior[0].shape[0] if prior else 0
    slots, _, head_size = w_refs[0].shape[-3:]
    rank = up_ref.shape[3]
    count = ids_ref.shape[0] - len(layout)
    step = pl.program_id(0)
    rows = acc_ref.shape[0]
    block = min(rows, 256)
    queries = slots - 2

    for number, token_refs in enumerate(tokens):
        first = acc_ref if number else (begun[0] if begun else None)
        pl.when(step == number)(
            functools.partial(accumulate, acc_ref, token_refs, w_refs, first)
        )

    @pl.when(step == len(layout) - 1)
    def _():
        ups = [
            jnp.concatenate(
                [up_ref[ids_ref[len(layout) + j], which, index] for j in range(count)], axis=0
            )
            for index in range(slots)
        ]
        for row in range(0, rows, block):
            at = slice(row, row + block)
            shrink = sum(sum_ref[at, :] for sum_ref in sum_refs).astype(jnp.bfloat16)
            lane = lax.broadcasted_iota(jnp.int32, (block, count * rank), 1)
            kept = (lane >= table_ref[at, 1:2]) & (lane < table_ref[at, 1:2] + rank)
            lows = []
            for part in range(3):
                piece = shrink[:, part * rank : (part + 1) * rank].astype(jnp.float32)
                piece = jnp.concatenate([piece] * count, axis=1)
                lows.append(jnp.where(kept, piece, 0.0).astype(jnp.bfloat16))

            def slot(index):
                low = lows[0 if index < queries else index - queries + 1]
                extra = jnp.dot(low, ups[index], preferred_element_type=jnp.float32)
                return acc_ref[at, index * head_size : (index + 1) * head_size] + extra

            def rotated(index):
                value = slot(index)
                turned = pltpu.roll(value, head_size // 2, 1)
                cos, sin = turn_ref[at, :head_size], turn_ref[at, head_size:]
                return (value * cos + turned * sin).astype(jnp.bfloat16)

            keys_ref[at, :] = rotated(queries)
            values_ref[at, :] = slot(queries + 1).astype(jnp.bfloat16)
            keys, values = keys_ref[: row + block], values_ref[: row + block]
            if prior:
                keys = jnp.concatenate([prior[0][...], keys], axis=0)
                values = jnp.concatenate([prior[1][...], values], axis=0)
            key_rows = keys.shape[0]
            key_at = lax.broadcasted_iota(jnp.int32, (block, key_rows), 1)
            row_at = lax.broadcasted_iota(jnp.int32, (block, key_rows), 0) + (first_row + row)
            allowed = (key_at >= table_ref[at, 0:1]) & (key_at <= row_at)
            for index in range(queries):
                scores = lax.dot_general(
                    rotated(index), keys, (((1,), (1,)), ((), ())),
                    preferred_element_type=jnp.float32,
                )
                scores = jnp.where(allowed, scores * (1.0 / math.sqrt(head_size)), -1e30)
                weights_exp = jnp.exp(scores - jnp.max(scores, axis=1, keepdims=True))
                scale = 1.0 / jnp.sum(weights_exp, axis=1, keepdims=True)
                attended = jnp.dot(
                    (weights_exp * scale).astype(jnp.bfloat16), values,
                    preferred_element_type=jnp.float32,
                )
                attended_ref[at, index * head_size : (index + 1) * head_size] = (
                    attended.astype(jnp.bfloat16)
                )


def weight_specs(weights, depth):
    if len(weights[0].shape) == 3:
        slots, _, head_size = weights[0].shape
        return [pl.BlockSpec((slots, depth, head_size), lambda step, ids: (0, ids[step], 0))]
    pieces = depth // sum(weight.shape[2] for weight in weights)
    return [
        pl.BlockSpec((pieces,) + weight.shape[1:], lambda step, ids: (ids[step], 0, 0, 0))
        for weight in weights
    ]


def fixed(array):
    shape = array.shape
    return pl.BlockSpec(shape, lambda step, ids: (0,) * len(shape))


PARAMS = pltpu.CompilerParams(vmem_limit_bytes=VMEM_BYTES)
COST = pl.CostEstimate(flops=1000, bytes_accessed=1000, transcendentals=0)


def call(kernel, name, ids, grid, specs, arrays, out, scratch=()):
    return pl.pallas_call(
        kernel,
        out_shape=out,
        grid_spec=pltpu.PrefetchScalarGridSpec(
            num_scalar_prefetch=1,
            grid=(grid,),
            in_specs=[fixed(array) if spec is None else spec for spec, array in zip(specs, arrays)],
            out_specs=[fixed(item) for item in out] if isinstance(out, tuple) else fixed(out),
            scratch_shapes=list(scratch),
        ),
        compiler_params=PARAMS,
        cost_estimate=COST,
        name=name,
    )(ids, *arrays)


def project(ids, tokens, weights):
    depth = tokens[0][0].shape[1]
    rows = sum(part.shape[0] for part in tokens[0])
    slots, _, head_size = weights[0].shape[-3:]
    parts = [part for item in tokens for part in item]
    return call(
        functools.partial(project_kernel, [len(item) for item in tokens], len(weights)),
        "project",
        ids,
        len(tokens),
        [None] * len(parts) + weight_specs(weights, depth),
        parts + weights,
        jax.ShapeDtypeStruct((rows, slots * head_size), jnp.float32),
    )


def attend(ids, adapters, row, table, turn, up, which, sums, tokens, weights, begun, prior):
    depth = tokens[0][0].shape[1]
    rows = sum(part.shape[0] for part in tokens[0])
    slots, _, head_size = weights[0].shape[-3:]
    out = (
        jax.ShapeDtypeStruct((rows, (slots - 2) * head_size), jnp.bfloat16),
        jax.ShapeDtypeStruct((rows, head_size), jnp.bfloat16),
        jax.ShapeDtypeStruct((rows, head_size), jnp.bfloat16),
    )
    parts = [part for item in tokens for part in item]

    def rows_of(array):
        return pl.BlockSpec((rows, array.shape[1]), lambda step, ids: (row // rows, 0))

    tables = [table, turn]
    started = (len(begun), len(prior))
    arrays = tables + [up] + sums + parts + weights + begun + list(prior)
    specs = (
        [rows_of(array) for array in tables]
        + [None]
        + [rows_of(array) for array in sums]
        + [None] * len(parts)
        + weight_specs(weights, depth)
        + [rows_of(array) for array in begun]
        + [None] * len(prior)
    )
    return call(
        functools.partial(
            attend_kernel, [len(item) for item in tokens], len(weights), len(sums), started, which
        ),
        "attend",
        jnp.concatenate([ids, adapters]),
        len(tokens),
        specs,
        arrays,
        out,
        [pltpu.VMEM((rows, slots * head_size), jnp.float32)],
    )


def shrink_kernel(ids_ref, table_ref, token_ref, down_ref, out_ref):
    step = pl.program_id(0)
    part = lax.dot_general(
        token_ref[...], down_ref[0], (((1,), (1,)), ((), ())), preferred_element_type=jnp.float32
    )
    rank = part.shape[1] // 3
    part = jnp.where(table_ref[:, 1:2] == step * rank, part, 0.0)

    @pl.when(step == 0)
    def _():
        out_ref[...] = part

    @pl.when(step > 0)
    def _():
        out_ref[...] += part


def shrink_partial(adapters, table, tokens, down):
    _, width, depth = down.shape
    return call(
        shrink_kernel,
        "shrink",
        adapters,
        adapters.shape[0],
        [None, None, pl.BlockSpec((1, width, depth), lambda step, ids: (ids[step], 0, 0))],
        [table, tokens, down],
        jax.ShapeDtypeStruct((tokens.shape[0], width), jnp.float32),
    )


def output_kernel(
    groups, parts, begun, last, dp_size, group_size, planes, count, ids_ref, *refs
):
    attended_refs, rest = refs[: groups * parts * 2], refs[groups * parts * 2 :]
    own_ref, half_refs, rest = rest[0], rest[1:3], rest[3:]
    begun_refs, rest = rest[: 2 * begun], rest[2 * begun :]
    if last:
        table_ref, up_ref, out_ref, acc_ref, low_ref, w_ref, down_ref = rest
    else:
        acc_ref, low_ref, w_ref, down_ref = rest
    step = pl.program_id(0)
    turn = ids_ref[step]
    at_worker, at_group = groups, groups + 1
    at_dp = groups + 2
    at_adapter = at_dp + dp_size
    at_pool = at_adapter + count
    features, columns = own_ref.shape
    share = features // (dp_size * group_size)
    rank = down_ref.shape[0] // count
    lot = (planes - 1) * share
    split = columns // features
    down_share = rank // split
    half_count = dp_size // 2

    def blocks(index, start, size):
        start = pl.multiple_of(start, 16)
        near = half_refs[0][jnp.minimum(index, half_count - 1), pl.ds(start, size), :]
        far = half_refs[1][jnp.maximum(index - half_count, 0), pl.ds(start, size), :]
        return jnp.where(index < half_count, near, far)

    @pl.when(turn == 0)
    def _():
        w_ref[...] = own_ref[...]

    @pl.when(turn > 0)
    def _():
        for group in range(group_size):
            base = (ids_ref[at_group] ^ group) * lot + (turn - 1) * share
            for place in range(dp_size):
                row = (group * dp_size + place) * share
                w_ref[row : row + share, :] = blocks(ids_ref[at_dp + place], base, share)

    for number in range(count):
        block = blocks(
            ids_ref[at_adapter + number], group_size * lot + turn * down_share, down_share
        )
        for piece in range(split):
            row = number * rank + piece * down_share
            down_ref[row : row + down_share, :] = block[
                :, piece * features : (piece + 1) * features
            ]

    def accumulate_group(number, side):
        row = 0
        for part in range(parts):
            attended = attended_refs[(number * parts + part) * 2 + side][...]
            at = slice(row, row + attended.shape[0])
            row = at.stop
            total = jnp.dot(attended, w_ref[...], preferred_element_type=jnp.float32)
            low = lax.dot_general(
                attended, down_ref[...], (((1,), (1,)), ((), ())),
                preferred_element_type=jnp.float32,
            )
            if number:
                total, low = acc_ref[at, :] + total, low_ref[at, :] + low
            elif begun:
                total, low = begun_refs[0][at, :] + total, begun_refs[1][at, :] + low
            acc_ref[at, :] = total
            low_ref[at, :] = low

    for number in range(groups):
        for side in range(2):
            pl.when((step == number) & (ids_ref[at_worker] == side))(
                functools.partial(accumulate_group, number, side)
            )

    if last:
        @pl.when(step == groups - 1)
        def _():
            low = low_ref[...].astype(jnp.bfloat16).astype(jnp.float32)
            lane = lax.broadcasted_iota(jnp.int32, low.shape, 1)
            kept = (lane >= table_ref[:, 1:2]) & (lane < table_ref[:, 1:2] + rank)
            low = jnp.where(kept, low, 0.0).astype(jnp.bfloat16)
            up = jnp.concatenate([up_ref[ids_ref[at_pool + j]] for j in range(count)], axis=0)
            extra = jnp.dot(low, up, preferred_element_type=jnp.float32)
            out_ref[...] = (acc_ref[...] + extra).astype(jnp.bfloat16)


def project_out(ids, attended, weights, sizes, begun, final):
    dp_size, group_size, planes, count, rank = sizes
    groups, parts = len(attended), len(attended[0])
    rows = sum(part[0].shape[0] for part in attended[0])
    features, columns = weights[0].shape
    flat = [array for group in attended for part in group for array in part]
    sums = (
        jax.ShapeDtypeStruct((rows, columns), jnp.float32),
        jax.ShapeDtypeStruct((rows, count * rank), jnp.float32),
    )
    arrays = flat + weights + begun + final
    scratch = [
        pltpu.VMEM((features, columns), jnp.bfloat16),
        pltpu.VMEM((count * rank, features), jnp.bfloat16),
    ]
    if final:
        scratch = [pltpu.VMEM(item.shape, jnp.float32) for item in sums] + scratch
    return call(
        functools.partial(
            output_kernel, groups, parts, len(begun) // 2, bool(final), dp_size, group_size,
            planes, count,
        ),
        "project_out",
        ids,
        groups,
        [None] * len(arrays),
        arrays,
        jax.ShapeDtypeStruct((rows, columns), jnp.bfloat16) if final else sums,
        scratch,
    )


def doubled(value, axis, size):
    distance = size // 2
    moved = lax.ppermute(value, axis, [(i, i ^ distance) for i in range(size)])
    while distance > 1:
        distance //= 2
        value = jnp.concatenate([value, moved], axis=0)
        moved = lax.ppermute(value, axis, [(i, i ^ distance) for i in range(size)])
    return value, moved


def block_of(relative, size):
    block, bit, distance = 0, 1, size // 2
    while distance:
        block = block + jnp.where(relative & distance, bit, 0)
        bit, distance = bit * 2, distance // 2
    return block


def local(
    dp_size,
    group_size,
    planes,
    tokens,
    query_key_value_weight,
    output_weight,
    adapter_down_maps,
    adapter_up_maps,
    output_down_maps,
    output_up_maps,
    request_adapter,
    lengths,
):
    token_rows, depth = tokens.shape
    _, slots, head_size = query_key_value_weight.shape
    queries = slots - 2
    rank = adapter_up_maps.shape[1]
    features = queries * head_size
    columns = output_weight.shape[2] // planes
    pairs = planes // 2
    plane_size = dp_size * group_size

    def worker(pair):
        return 2 * pair + 1 - pair % 2

    def outer(pair):
        return 2 * pair + pair % 2

    to_worker = [(outer(p), worker(p)) for p in range(pairs)]
    from_worker = [(worker(p), outer(p)) for p in range(pairs)]
    ring = [(worker(p), worker((p + 1) % pairs)) for p in range(pairs)]
    here = lax.axis_index("tensor")
    pair = here // 2
    is_worker = here == worker(pair)
    sources = [(pair - step + pairs) % pairs for step in range(pairs)]
    worker_ids = jnp.stack([worker(source) for source in sources]).astype(jnp.int32)
    outer_ids = jnp.stack([outer(source) for source in sources]).astype(jnp.int32)
    dp_here, group_here = lax.axis_index("dp"), lax.axis_index("groups")
    place = group_here * dp_size + dp_here

    own_tokens = [tokens]
    for _ in range(pairs - 1):
        own_tokens.append(lax.ppermute(own_tokens[-1], "tensor", ring))

    weight = jnp.transpose(query_key_value_weight, (1, 0, 2))
    share = weight.shape[1] // plane_size
    piece = lax.dynamic_slice_in_dim(weight, place * share, share, axis=1)
    piece = lax.ppermute(piece, "tensor", to_worker)
    outer_weight = lax.all_gather(piece, PLANE, axis=0)

    chunk_rows = token_rows // CHUNKS
    outer_tokens = []
    previous = piece
    for chunk in range(CHUNKS):
        part = after(tokens[chunk * chunk_rows : (chunk + 1) * chunk_rows], previous)
        previous = lax.ppermute(part, "tensor", to_worker)
        moving = [previous]
        for _ in range(pairs - 1):
            moving.append(lax.ppermute(moving[-1], "tensor", ring))
        outer_tokens.append(moving)

    down_all = lax.all_gather(adapter_down_maps, "dp", axis=0, tiled=True)
    up_own = jnp.transpose(adapter_up_maps[0], (1, 0, 2))
    up_pair = jnp.stack([up_own, lax.ppermute(up_own, "tensor", to_worker)])
    up_all = lax.all_gather(up_pair, "dp", axis=0)
    out_up_all = lax.all_gather(output_up_maps, "dp", axis=0, tiled=True)

    requests = request_adapter.shape[1]
    request_ends = jnp.cumsum(lengths[0])
    request_starts = request_ends - lengths[0]
    at = jnp.arange(token_rows, dtype=jnp.int32)
    member = (at[:, None] >= request_starts[None, :]) & (at[:, None] < request_ends[None, :])
    if dp_size <= requests:
        count, adapters, label = dp_size, jnp.arange(dp_size), request_adapter[0]
    else:
        count, adapters, label = requests, request_adapter[0], jnp.arange(requests)
    adapters = adapters.astype(jnp.int32)
    wanted = jnp.stack([request_starts, label * rank], axis=0)
    table = jnp.sum(jnp.where(member[:, None, :], wanted[None], 0), axis=2).astype(jnp.int32)
    position = at - table[:, 0]
    half = head_size // 2
    inv_freq = 10000.0 ** (-2.0 * jnp.arange(half, dtype=jnp.float32) / head_size)
    angles = position.astype(jnp.float32)[:, None] * inv_freq[None, :]
    cosine, sine = jnp.cos(angles), jnp.sin(angles)
    turn = jnp.concatenate([cosine, cosine, -sine, sine], axis=1)

    shrink = shrink_partial(adapters, table, tokens, down_all)
    shrink = shrink + lax.ppermute(shrink, "tensor", to_worker)
    sums = [shrink]
    for _ in range(pairs - 1):
        sums.append(lax.ppermute(sums[-1], "tensor", ring))

    out_share = features // plane_size
    first = place * out_share
    piece = lax.dynamic_slice(
        output_weight, (first % head_size, first // head_size, 0),
        (out_share, 1, output_weight.shape[2]),
    )[:, 0]
    own_weight = jnp.transpose(
        lax.dynamic_slice_in_dim(output_weight, here * columns, columns, axis=2), (1, 0, 2)
    ).reshape(features, columns)
    out_down = output_down_maps[0].reshape(rank, features)
    split = columns // features
    out_down = jnp.concatenate(jnp.split(out_down, split, axis=0), axis=1)
    received = []
    for turn_by in range(1, planes):
        send = lax.dynamic_slice_in_dim(
            piece, (here + turn_by) % planes * columns, columns, axis=1
        )
        send = jnp.concatenate([send, out_down], axis=0)
        received.append(
            lax.ppermute(
                after(send, own_tokens[-1]), "tensor",
                [(i, (i + turn_by) % planes) for i in range(planes)],
            )
        )
    lot = jnp.concatenate([item[:out_share] for item in received], axis=0)
    lots = jnp.concatenate(doubled(lot, "groups", group_size), axis=0)
    lots = jnp.concatenate(
        [lots, out_down] + [item[out_share:] for item in received], axis=0
    )
    halves = list(doubled(lots[None], "dp", dp_size))

    begun = project(worker_ids, [(array,) for array in own_tokens], [weight])
    own_parts, prior = [], ()
    for chunk in range(CHUNKS):
        attended, keys, values = attend(
            outer_ids, adapters, chunk * chunk_rows, table, turn, up_all, 0, sums,
            [(array,) for array in outer_tokens[chunk]], [weight], [begun], prior,
        )
        prior = (keys, values)
        own_parts.append(attended)
    outer_part, _, _ = attend(
        jnp.concatenate([worker_ids, outer_ids]), adapters, 0, table, turn, up_all, 1, sums,
        [(array,) for array in own_tokens]
        + [
            tuple(outer_tokens[chunk][step] for chunk in range(CHUNKS)) for step in range(pairs)
        ],
        [outer_weight], [], (),
    )

    def spread(parts):
        result, moving = [], parts
        for step in range(pairs):
            if step:
                moving = [lax.ppermute(part, "tensor", ring) for part in moving]
            result.append(
                [(lax.ppermute(part, "tensor", from_worker), part) for part in moving]
            )
        return result

    def lookups(ids):
        return jnp.concatenate(
            [
                (here - ids + planes) % planes,
                jnp.stack([is_worker.astype(jnp.int32), group_here]),
                block_of(dp_here ^ jnp.arange(dp_size), dp_size),
                block_of(dp_here ^ adapters, dp_size),
                adapters,
            ]
        ).astype(jnp.int32)

    weights = [own_weight] + halves
    sizes = (dp_size, group_size, planes, count, rank)
    begun = project_out(lookups(worker_ids), spread(own_parts), weights, sizes, [], [])
    return project_out(
        lookups(outer_ids), spread([outer_part]), weights, sizes, list(begun),
        [table, out_up_all],
    )


def solution(mesh):
    in_specs = (
        P(PLANE, "tensor"),
        P(None, None, "tensor"),
        P("tensor", None, None),
        P(PLANE, None, "tensor"),
        P(PLANE, None, None, "tensor"),
        P(PLANE, None, None, "tensor"),
        P(PLANE, None, "tensor"),
        P(PLANE, None),
        P(PLANE, None),
    )
    function = functools.partial(
        local, mesh.shape["dp"], mesh.shape["groups"], mesh.shape["tensor"]
    )
    return jax.shard_map(
        function, mesh=mesh, in_specs=in_specs, out_specs=P(PLANE, "tensor"), check_vma=False
    )
```

```python
import functools
import math

import jax
import jax.numpy as jnp
from jax import lax
from jax.experimental import pallas as pl
from jax.experimental.pallas import tpu as pltpu
from jax.sharding import PartitionSpec as P

CHUNKS = 2
VMEM_BYTES = 60 * 1024 * 1024
PLANE = ("groups", "dp")


def after(value, *earlier):
    return lax.optimization_barrier((value,) + earlier)[0]


def wide_slots(w_refs, pair):
    if len(w_refs[0].shape) == 3:
        parts = [w_ref[...] for w_ref in w_refs]
    else:
        parts = [
            w_ref[piece] for piece in range(w_refs[0].shape[0]) for w_ref in w_refs
        ]
    wide = [jnp.concatenate([part[2 * pair], part[2 * pair + 1]], axis=1) for part in parts]
    return wide[0] if len(wide) == 1 else jnp.concatenate(wide, axis=0)


def accumulate(acc_ref, token_refs, w_refs, first):
    slots, _, head_size = w_refs[0].shape[-3:]
    for pair in range(slots // 2):
        columns = slice(2 * pair * head_size, (2 * pair + 2) * head_size)
        weight = wide_slots(w_refs, pair)
        row = 0
        for token_ref in token_refs:
            rows = slice(row, row + token_ref.shape[0])
            row = rows.stop
            total = jnp.dot(token_ref[...], weight, preferred_element_type=jnp.float32)
            if first is None:
                acc_ref[rows, columns] = total
            else:
                acc_ref[rows, columns] = first[rows, columns] + total


def split_refs(refs, layout):
    groups, at = [], 0
    for count in layout:
        groups.append(refs[at : at + count])
        at += count
    return groups, refs[at:]


def project_kernel(layout, weights, ids_ref, *refs):
    tokens, rest = split_refs(refs, layout)
    w_refs, acc_ref = rest[:weights], rest[weights]
    step = pl.program_id(0)
    for number, token_refs in enumerate(tokens):
        pl.when(step == number)(
            functools.partial(
                accumulate, acc_ref, token_refs, w_refs, acc_ref if number else None
            )
        )


def attend_kernel(layout, weights, sums, started, which, ids_ref, table_ref, turn_ref, up_ref, *refs):
    sum_refs, refs = refs[:sums], refs[sums:]
    tokens, rest = split_refs(refs, layout)
    w_refs, rest = rest[:weights], rest[weights:]
    begun, prior, rest = rest[:started[0]], rest[started[0] : started[0] + started[1]], rest[sum(started) :]
    attended_ref, keys_ref, values_ref, acc_ref = rest
    first_row = prior[0].shape[0] if prior else 0
    slots, _, head_size = w_refs[0].shape[-3:]
    rank = up_ref.shape[3]
    count = ids_ref.shape[0] - len(layout)
    step = pl.program_id(0)
    rows = acc_ref.shape[0]
    block = min(rows, 256)
    queries = slots - 2

    for number, token_refs in enumerate(tokens):
        first = acc_ref if number else (begun[0] if begun else None)
        pl.when(step == number)(
            functools.partial(accumulate, acc_ref, token_refs, w_refs, first)
        )

    @pl.when(step == len(layout) - 1)
    def _():
        ups = [
            jnp.concatenate(
                [up_ref[ids_ref[len(layout) + j], which, index] for j in range(count)], axis=0
            )
            for index in range(slots)
        ]
        for row in range(0, rows, block):
            at = slice(row, row + block)
            shrink = sum(sum_ref[at, :] for sum_ref in sum_refs).astype(jnp.bfloat16)
            lane = lax.broadcasted_iota(jnp.int32, (block, count * rank), 1)
            kept = (lane >= table_ref[at, 1:2]) & (lane < table_ref[at, 1:2] + rank)
            lows = []
            for part in range(3):
                piece = shrink[:, part * rank : (part + 1) * rank].astype(jnp.float32)
                piece = jnp.concatenate([piece] * count, axis=1)
                lows.append(jnp.where(kept, piece, 0.0).astype(jnp.bfloat16))

            def slot(index):
                low = lows[0 if index < queries else index - queries + 1]
                extra = jnp.dot(low, ups[index], preferred_element_type=jnp.float32)
                return acc_ref[at, index * head_size : (index + 1) * head_size] + extra

            def rotated(index):
                value = slot(index)
                turned = pltpu.roll(value, head_size // 2, 1)
                cos, sin = turn_ref[at, :head_size], turn_ref[at, head_size:]
                return (value * cos + turned * sin).astype(jnp.bfloat16)

            keys_ref[at, :] = rotated(queries)
            values_ref[at, :] = slot(queries + 1).astype(jnp.bfloat16)
            keys, values = keys_ref[: row + block], values_ref[: row + block]
            if prior:
                keys = jnp.concatenate([prior[0][...], keys], axis=0)
                values = jnp.concatenate([prior[1][...], values], axis=0)
            key_rows = keys.shape[0]
            key_at = lax.broadcasted_iota(jnp.int32, (block, key_rows), 1)
            row_at = lax.broadcasted_iota(jnp.int32, (block, key_rows), 0) + (first_row + row)
            allowed = (key_at >= table_ref[at, 0:1]) & (key_at <= row_at)
            for index in range(queries):
                scores = lax.dot_general(
                    rotated(index), keys, (((1,), (1,)), ((), ())),
                    preferred_element_type=jnp.float32,
                )
                scores = jnp.where(allowed, scores * (1.0 / math.sqrt(head_size)), -1e30)
                weights_exp = jnp.exp(scores - jnp.max(scores, axis=1, keepdims=True))
                scale = 1.0 / jnp.sum(weights_exp, axis=1, keepdims=True)
                attended = jnp.dot(
                    (weights_exp * scale).astype(jnp.bfloat16), values,
                    preferred_element_type=jnp.float32,
                )
                attended_ref[at, index * head_size : (index + 1) * head_size] = (
                    attended.astype(jnp.bfloat16)
                )


def weight_specs(weights, depth):
    if len(weights[0].shape) == 3:
        slots, _, head_size = weights[0].shape
        return [pl.BlockSpec((slots, depth, head_size), lambda step, ids: (0, ids[step], 0))]
    pieces = depth // sum(weight.shape[2] for weight in weights)
    return [
        pl.BlockSpec((pieces,) + weight.shape[1:], lambda step, ids: (ids[step], 0, 0, 0))
        for weight in weights
    ]


def fixed(array):
    shape = array.shape
    return pl.BlockSpec(shape, lambda step, ids: (0,) * len(shape))


PARAMS = pltpu.CompilerParams(vmem_limit_bytes=VMEM_BYTES)
COST = pl.CostEstimate(flops=1000, bytes_accessed=1000, transcendentals=0)


def call(kernel, name, ids, grid, specs, arrays, out, scratch=()):
    return pl.pallas_call(
        kernel,
        out_shape=out,
        grid_spec=pltpu.PrefetchScalarGridSpec(
            num_scalar_prefetch=1,
            grid=(grid,),
            in_specs=[fixed(array) if spec is None else spec for spec, array in zip(specs, arrays)],
            out_specs=[fixed(item) for item in out] if isinstance(out, tuple) else fixed(out),
            scratch_shapes=list(scratch),
        ),
        compiler_params=PARAMS,
        cost_estimate=COST,
        name=name,
    )(ids, *arrays)


def project(ids, tokens, weights):
    depth = tokens[0][0].shape[1]
    rows = sum(part.shape[0] for part in tokens[0])
    slots, _, head_size = weights[0].shape[-3:]
    parts = [part for item in tokens for part in item]
    return call(
        functools.partial(project_kernel, [len(item) for item in tokens], len(weights)),
        "project",
        ids,
        len(tokens),
        [None] * len(parts) + weight_specs(weights, depth),
        parts + weights,
        jax.ShapeDtypeStruct((rows, slots * head_size), jnp.float32),
    )


def attend(ids, adapters, row, table, turn, up, which, sums, tokens, weights, begun, prior):
    depth = tokens[0][0].shape[1]
    rows = sum(part.shape[0] for part in tokens[0])
    slots, _, head_size = weights[0].shape[-3:]
    out = (
        jax.ShapeDtypeStruct((rows, (slots - 2) * head_size), jnp.bfloat16),
        jax.ShapeDtypeStruct((rows, head_size), jnp.bfloat16),
        jax.ShapeDtypeStruct((rows, head_size), jnp.bfloat16),
    )
    parts = [part for item in tokens for part in item]

    def rows_of(array):
        return pl.BlockSpec((rows, array.shape[1]), lambda step, ids: (row // rows, 0))

    tables = [table, turn]
    started = (len(begun), len(prior))
    arrays = tables + [up] + sums + parts + weights + begun + list(prior)
    specs = (
        [rows_of(array) for array in tables]
        + [None]
        + [rows_of(array) for array in sums]
        + [None] * len(parts)
        + weight_specs(weights, depth)
        + [rows_of(array) for array in begun]
        + [None] * len(prior)
    )
    return call(
        functools.partial(
            attend_kernel, [len(item) for item in tokens], len(weights), len(sums), started, which
        ),
        "attend",
        jnp.concatenate([ids, adapters]),
        len(tokens),
        specs,
        arrays,
        out,
        [pltpu.VMEM((rows, slots * head_size), jnp.float32)],
    )


def shrink_kernel(ids_ref, table_ref, token_ref, down_ref, out_ref):
    step = pl.program_id(0)
    part = lax.dot_general(
        token_ref[...], down_ref[0], (((1,), (1,)), ((), ())), preferred_element_type=jnp.float32
    )
    rank = part.shape[1] // 3
    part = jnp.where(table_ref[:, 1:2] == step * rank, part, 0.0)

    @pl.when(step == 0)
    def _():
        out_ref[...] = part

    @pl.when(step > 0)
    def _():
        out_ref[...] += part


def shrink_partial(adapters, table, tokens, down):
    _, width, depth = down.shape
    return call(
        shrink_kernel,
        "shrink",
        adapters,
        adapters.shape[0],
        [None, None, pl.BlockSpec((1, width, depth), lambda step, ids: (ids[step], 0, 0))],
        [table, tokens, down],
        jax.ShapeDtypeStruct((tokens.shape[0], width), jnp.float32),
    )


def output_kernel(
    groups, parts, begun, last, dp_size, group_size, planes, count, ids_ref, *refs
):
    attended_refs, rest = refs[: groups * parts * 2], refs[groups * parts * 2 :]
    own_ref, half_refs, rest = rest[0], rest[1:3], rest[3:]
    begun_refs, rest = rest[: 2 * begun], rest[2 * begun :]
    if last:
        table_ref, up_ref, out_ref, acc_ref, low_ref, w_ref, down_ref = rest
    else:
        acc_ref, low_ref, w_ref, down_ref = rest
    step = pl.program_id(0)
    turn = ids_ref[step]
    at_worker, at_group = groups, groups + 1
    at_dp = groups + 2
    at_adapter = at_dp + dp_size
    at_pool = at_adapter + count
    features, columns = own_ref.shape
    share = features // (dp_size * group_size)
    rank = down_ref.shape[0] // count
    lot = (planes - 1) * share
    split = columns // features
    down_share = rank // split
    half_count = dp_size // 2

    def blocks(index, start, size):
        start = pl.multiple_of(start, 16)
        near = half_refs[0][jnp.minimum(index, half_count - 1), pl.ds(start, size), :]
        far = half_refs[1][jnp.maximum(index - half_count, 0), pl.ds(start, size), :]
        return jnp.where(index < half_count, near, far)

    @pl.when(turn == 0)
    def _():
        w_ref[...] = own_ref[...]

    @pl.when(turn > 0)
    def _():
        for group in range(group_size):
            base = (ids_ref[at_group] ^ group) * lot + (turn - 1) * share
            for place in range(dp_size):
                row = (group * dp_size + place) * share
                w_ref[row : row + share, :] = blocks(ids_ref[at_dp + place], base, share)

    for number in range(count):
        block = blocks(
            ids_ref[at_adapter + number], group_size * lot + turn * down_share, down_share
        )
        for piece in range(split):
            row = number * rank + piece * down_share
            down_ref[row : row + down_share, :] = block[
                :, piece * features : (piece + 1) * features
            ]

    def accumulate_group(number, side):
        row = 0
        for part in range(parts):
            attended = attended_refs[(number * parts + part) * 2 + side][...]
            at = slice(row, row + attended.shape[0])
            row = at.stop
            total = jnp.dot(attended, w_ref[...], preferred_element_type=jnp.float32)
            low = lax.dot_general(
                attended, down_ref[...], (((1,), (1,)), ((), ())),
                preferred_element_type=jnp.float32,
            )
            if number:
                total, low = acc_ref[at, :] + total, low_ref[at, :] + low
            elif begun:
                total, low = begun_refs[0][at, :] + total, begun_refs[1][at, :] + low
            acc_ref[at, :] = total
            low_ref[at, :] = low

    for number in range(groups):
        for side in range(2):
            pl.when((step == number) & (ids_ref[at_worker] == side))(
                functools.partial(accumulate_group, number, side)
            )

    if last:
        @pl.when(step == groups - 1)
        def _():
            low = low_ref[...].astype(jnp.bfloat16).astype(jnp.float32)
            lane = lax.broadcasted_iota(jnp.int32, low.shape, 1)
            kept = (lane >= table_ref[:, 1:2]) & (lane < table_ref[:, 1:2] + rank)
            low = jnp.where(kept, low, 0.0).astype(jnp.bfloat16)
            up = jnp.concatenate([up_ref[ids_ref[at_pool + j]] for j in range(count)], axis=0)
            extra = jnp.dot(low, up, preferred_element_type=jnp.float32)
            out_ref[...] = (acc_ref[...] + extra).astype(jnp.bfloat16)


def project_out(ids, attended, weights, sizes, begun, final):
    dp_size, group_size, planes, count, rank = sizes
    groups, parts = len(attended), len(attended[0])
    rows = sum(part[0].shape[0] for part in attended[0])
    features, columns = weights[0].shape
    flat = [array for group in attended for part in group for array in part]
    sums = (
        jax.ShapeDtypeStruct((rows, columns), jnp.float32),
        jax.ShapeDtypeStruct((rows, count * rank), jnp.float32),
    )
    arrays = flat + weights + begun + final
    scratch = [
        pltpu.VMEM((features, columns), jnp.bfloat16),
        pltpu.VMEM((count * rank, features), jnp.bfloat16),
    ]
    if final:
        scratch = [pltpu.VMEM(item.shape, jnp.float32) for item in sums] + scratch
    return call(
        functools.partial(
            output_kernel, groups, parts, len(begun) // 2, bool(final), dp_size, group_size,
            planes, count,
        ),
        "project_out",
        ids,
        groups,
        [None] * len(arrays),
        arrays,
        jax.ShapeDtypeStruct((rows, columns), jnp.bfloat16) if final else sums,
        scratch,
    )


def doubled(value, axis, size):
    distance = size // 2
    moved = lax.ppermute(value, axis, [(i, i ^ distance) for i in range(size)])
    while distance > 1:
        distance //= 2
        value = jnp.concatenate([value, moved], axis=0)
        moved = lax.ppermute(value, axis, [(i, i ^ distance) for i in range(size)])
    return value, moved


def block_of(relative, size):
    block, bit, distance = 0, 1, size // 2
    while distance:
        block = block + jnp.where(relative & distance, bit, 0)
        bit, distance = bit * 2, distance // 2
    return block


def local(
    dp_size,
    group_size,
    planes,
    tokens,
    query_key_value_weight,
    output_weight,
    adapter_down_maps,
    adapter_up_maps,
    output_down_maps,
    output_up_maps,
    request_adapter,
    lengths,
):
    token_rows, depth = tokens.shape
    _, slots, head_size = query_key_value_weight.shape
    queries = slots - 2
    rank = adapter_up_maps.shape[1]
    features = queries * head_size
    columns = output_weight.shape[2] // planes
    pairs = planes // 2
    plane_size = dp_size * group_size

    def worker(pair):
        return 2 * pair + 1 - pair % 2

    def outer(pair):
        return 2 * pair + pair % 2

    to_worker = [(outer(p), worker(p)) for p in range(pairs)]
    from_worker = [(worker(p), outer(p)) for p in range(pairs)]
    ring = [(worker(p), worker((p + 1) % pairs)) for p in range(pairs)]
    here = lax.axis_index("tensor")
    pair = here // 2
    is_worker = here == worker(pair)
    sources = [(pair - step + pairs) % pairs for step in range(pairs)]
    worker_ids = jnp.stack([worker(source) for source in sources]).astype(jnp.int32)
    outer_ids = jnp.stack([outer(source) for source in sources]).astype(jnp.int32)
    dp_here, group_here = lax.axis_index("dp"), lax.axis_index("groups")
    place = group_here * dp_size + dp_here

    own_tokens = [tokens]
    for _ in range(pairs - 1):
        own_tokens.append(lax.ppermute(own_tokens[-1], "tensor", ring))
    weight = jnp.transpose(query_key_value_weight, (1, 0, 2))
    share = weight.shape[1] // plane_size
    piece = lax.dynamic_slice_in_dim(weight, place * share, share, axis=1)
    piece = lax.ppermute(piece, "tensor", to_worker)
    up_own = jnp.transpose(adapter_up_maps[0], (1, 0, 2))
    up_outer = lax.ppermute(up_own, "tensor", to_worker)
    first = (own_tokens[-1], piece)
    outer_weight = lax.all_gather(after(piece, own_tokens[-1]), PLANE, axis=0)
    down_all = lax.all_gather(adapter_down_maps, "dp", axis=0, tiled=True)
    up_all = lax.all_gather(jnp.stack([up_own, up_outer]), "dp", axis=0)
    out_up_all = lax.all_gather(output_up_maps, "dp", axis=0, tiled=True)

    requests = request_adapter.shape[1]
    request_ends = jnp.cumsum(lengths[0])
    request_starts = request_ends - lengths[0]
    at = jnp.arange(token_rows, dtype=jnp.int32)
    member = (at[:, None] >= request_starts[None, :]) & (at[:, None] < request_ends[None, :])
    if dp_size <= requests:
        count, adapters, label = dp_size, jnp.arange(dp_size), request_adapter[0]
    else:
        count, adapters, label = requests, request_adapter[0], jnp.arange(requests)
    adapters = adapters.astype(jnp.int32)
    wanted = jnp.stack([request_starts, label * rank], axis=0)
    table = jnp.sum(jnp.where(member[:, None, :], wanted[None], 0), axis=2).astype(jnp.int32)
    position = at - table[:, 0]
    half = head_size // 2
    inv_freq = 10000.0 ** (-2.0 * jnp.arange(half, dtype=jnp.float32) / head_size)
    angles = position.astype(jnp.float32)[:, None] * inv_freq[None, :]
    cosine, sine = jnp.cos(angles), jnp.sin(angles)
    turn = jnp.concatenate([cosine, cosine, -sine, sine], axis=1)

    chunk_rows = token_rows // CHUNKS
    begun = project(worker_ids, [(array,) for array in own_tokens], [weight])
    outer_first = lax.ppermute(after(tokens[:chunk_rows], *first), "tensor", to_worker)
    shrink = shrink_partial(adapters, table, after(tokens, *first), down_all)
    shrink_outer = lax.ppermute(shrink, "tensor", to_worker)

    out_share = features // plane_size
    line = place * out_share
    piece = lax.dynamic_slice(
        output_weight, (line % head_size, line // head_size, 0),
        (out_share, 1, output_weight.shape[2]),
    )[:, 0]
    own_weight = jnp.transpose(
        lax.dynamic_slice_in_dim(output_weight, here * columns, columns, axis=2), (1, 0, 2)
    ).reshape(features, columns)
    out_down = output_down_maps[0].reshape(rank, features)
    split = columns // features
    out_down = jnp.concatenate(jnp.split(out_down, split, axis=0), axis=1)
    received = []
    for turn_by in range(1, planes):
        send = lax.dynamic_slice_in_dim(
            piece, (here + turn_by) % planes * columns, columns, axis=1
        )
        send = jnp.concatenate([send, out_down], axis=0)
        received.append(
            lax.ppermute(
                after(send, *first), "tensor",
                [(i, (i + turn_by) % planes) for i in range(planes)],
            )
        )
    lot = jnp.concatenate([item[:out_share] for item in received], axis=0)

    second = (outer_first, shrink_outer, lot, begun, up_all, out_up_all)
    outer_tokens = [[outer_first]]
    for _ in range(pairs - 1):
        outer_tokens[0].append(lax.ppermute(outer_tokens[0][-1], "tensor", ring))
    outer_tokens.append([lax.ppermute(after(tokens[chunk_rows:], *second), "tensor", to_worker)])
    sums = [shrink + shrink_outer]
    for _ in range(pairs - 1):
        sums.append(lax.ppermute(sums[-1], "tensor", ring))
    lots = jnp.concatenate(doubled(after(lot, *second), "groups", group_size), axis=0)
    lots = jnp.concatenate(
        [lots, out_down] + [item[out_share:] for item in received], axis=0
    )

    third = (outer_tokens[0][-1], sums[-1], outer_tokens[1][0], lots)
    outer_tokens[1][0] = after(outer_tokens[1][0], *third[:3])
    for _ in range(pairs - 1):
        outer_tokens[1].append(lax.ppermute(outer_tokens[1][-1], "tensor", ring))
    halves = list(doubled(after(lots, *third)[None], "dp", dp_size))

    def own_heads(chunk, prior):
        return attend(
            outer_ids, adapters, chunk * chunk_rows, table, turn, up_all, 0, sums,
            [(array,) for array in outer_tokens[chunk]], [weight], [begun], prior,
        )

    def spread(parts, gates):
        result, moving = [], parts
        for step in range(pairs):
            if step:
                moving = [
                    lax.ppermute(after(part, *gates), "tensor", ring) for part in moving
                ]
            result.append(
                [(lax.ppermute(part, "tensor", from_worker), part) for part in moving]
            )
        return result

    own_first, keys, values = own_heads(0, ())
    spread_first = spread([own_first], ())
    own_second, _, _ = own_heads(1, (keys, values))
    spread_second = spread([own_second], ())
    gates = (own_second, spread_first[-1][0][1], spread_first[0][0][0], halves[0])
    outer_part, _, _ = attend(
        jnp.concatenate([worker_ids, outer_ids]), adapters, 0, table, turn, up_all, 1, sums,
        [(array,) for array in own_tokens]
        + [
            tuple(outer_tokens[chunk][step] for chunk in range(CHUNKS)) for step in range(pairs)
        ],
        [after(outer_weight, *gates)], [], (),
    )
    spread_own = [a + b for a, b in zip(spread_first, spread_second)]
    spread_outer = spread([outer_part], (spread_second[-1][0][1],))

    def lookups(ids):
        return jnp.concatenate(
            [
                (here - ids + planes) % planes,
                jnp.stack([is_worker.astype(jnp.int32), group_here]),
                block_of(dp_here ^ jnp.arange(dp_size), dp_size),
                block_of(dp_here ^ adapters, dp_size),
                adapters,
            ]
        ).astype(jnp.int32)

    weights = [own_weight] + halves
    sizes = (dp_size, group_size, planes, count, rank)
    begun = project_out(lookups(worker_ids), spread_own, weights, sizes, [], [])
    return project_out(
        lookups(outer_ids), spread_outer, weights, sizes, list(begun),
        [table, out_up_all],
    )


def solution(mesh):
    in_specs = (
        P(PLANE, "tensor"),
        P(None, None, "tensor"),
        P("tensor", None, None),
        P(PLANE, None, "tensor"),
        P(PLANE, None, None, "tensor"),
        P(PLANE, None, None, "tensor"),
        P(PLANE, None, "tensor"),
        P(PLANE, None),
        P(PLANE, None),
    )
    function = functools.partial(
        local, mesh.shape["dp"], mesh.shape["groups"], mesh.shape["tensor"]
    )
    return jax.shard_map(
        function, mesh=mesh, in_specs=in_specs, out_specs=P(PLANE, "tensor"), check_vma=False
    )
```

```python
import functools
import math

import jax
import jax.numpy as jnp
from jax import lax
from jax.experimental import pallas as pl
from jax.experimental.pallas import tpu as pltpu
from jax.sharding import PartitionSpec as P

CHUNKS = 2
VMEM_BYTES = 40 * 1024 * 1024
PLANE = ("groups", "dp")


def after(value, *earlier):
    return lax.optimization_barrier((value,) + earlier)[0]


def wide_slots(w_ref, depth, pair):
    if len(w_ref.shape) == 3:
        parts = [w_ref]
    else:
        parts = [w_ref.at[piece, :, : depth // w_ref.shape[0]] for piece in range(w_ref.shape[0])]
    wide = [jnp.concatenate([part[2 * pair], part[2 * pair + 1]], axis=1) for part in parts]
    return wide[0] if len(wide) == 1 else jnp.concatenate(wide, axis=0)


def accumulate(acc_ref, token_refs, w_ref, first):
    slots, _, head_size = w_ref.shape[-3:]
    depth = token_refs[0].shape[1]
    for pair in range(slots // 2):
        columns = slice(2 * pair * head_size, (2 * pair + 2) * head_size)
        weight = wide_slots(w_ref, depth, pair)
        row = 0
        for token_ref in token_refs:
            rows = slice(row, row + token_ref.shape[0])
            row = rows.stop
            total = jnp.dot(token_ref[...], weight, preferred_element_type=jnp.float32)
            if first is None:
                acc_ref[rows, columns] = total
            else:
                acc_ref[rows, columns] = first[rows, columns] + total


def split_refs(refs, layout):
    groups, at = [], 0
    for count in layout:
        groups.append(refs[at : at + count])
        at += count
    return groups, refs[at:]


def project_kernel(layout, ids_ref, *refs):
    tokens, (w_ref, acc_ref) = split_refs(refs, layout)
    step = pl.program_id(0)
    for number, token_refs in enumerate(tokens):
        pl.when(step == number)(
            functools.partial(
                accumulate, acc_ref, token_refs, w_ref, acc_ref if number else None
            )
        )


def attend_kernel(
    layout, sums, started, ids_ref, table_ref, turn_ref, up_ref, *refs
):
    sum_refs, refs = refs[:sums], refs[sums:]
    tokens, rest = split_refs(refs, layout)
    w_ref, rest = rest[0], rest[1:]
    begun, prior, rest = (
        rest[: started[0]], rest[started[0] : sum(started)], rest[sum(started) :]
    )
    attended_ref, keys_ref, values_ref, acc_ref = rest
    first_row = prior[0].shape[0] if prior else 0
    slots, _, head_size = w_ref.shape[-3:]
    rank = up_ref.shape[2]
    at_adapter = len(layout) + 1
    count = ids_ref.shape[0] - at_adapter
    step = pl.program_id(0)
    rows = acc_ref.shape[0]
    block = min(rows, 256)
    queries = slots - 2

    for number, token_refs in enumerate(tokens):
        first = acc_ref if number else (begun[0] if begun else None)
        pl.when(step == number)(
            functools.partial(accumulate, acc_ref, token_refs, w_ref, first)
        )

    @pl.when(step == len(layout) - 1)
    def _():
        ups = [
            jnp.concatenate(
                [up_ref[ids_ref[at_adapter + j], index] for j in range(count)], axis=0
            )
            for index in range(slots)
        ]
        for row in range(0, rows, block):
            at = slice(row, row + block)
            shrink = sum(sum_ref[at, :] for sum_ref in sum_refs).astype(jnp.bfloat16)
            lane = lax.broadcasted_iota(jnp.int32, (block, count * rank), 1)
            kept = (lane >= table_ref[at, 1:2]) & (lane < table_ref[at, 1:2] + rank)
            lows = []
            for part in range(3):
                piece = shrink[:, part * rank : (part + 1) * rank].astype(jnp.float32)
                piece = jnp.concatenate([piece] * count, axis=1)
                lows.append(jnp.where(kept, piece, 0.0).astype(jnp.bfloat16))

            def slot(index):
                low = lows[0 if index < queries else index - queries + 1]
                extra = jnp.dot(low, ups[index], preferred_element_type=jnp.float32)
                return acc_ref[at, index * head_size : (index + 1) * head_size] + extra

            def rotated(index):
                value = slot(index)
                turned = pltpu.roll(value, head_size // 2, 1)
                cos, sin = turn_ref[at, :head_size], turn_ref[at, head_size:]
                return (value * cos + turned * sin).astype(jnp.bfloat16)

            keys_ref[at, :] = rotated(queries)
            values_ref[at, :] = slot(queries + 1).astype(jnp.bfloat16)
            keys, values = keys_ref[: row + block], values_ref[: row + block]
            if prior:
                keys = jnp.concatenate([prior[0][...], keys], axis=0)
                values = jnp.concatenate([prior[1][...], values], axis=0)
            key_rows = keys.shape[0]
            key_at = lax.broadcasted_iota(jnp.int32, (block, key_rows), 1)
            row_at = lax.broadcasted_iota(jnp.int32, (block, key_rows), 0) + (first_row + row)
            allowed = (key_at >= table_ref[at, 0:1]) & (key_at <= row_at)
            for index in range(queries):
                scores = lax.dot_general(
                    rotated(index), keys, (((1,), (1,)), ((), ())),
                    preferred_element_type=jnp.float32,
                )
                scores = jnp.where(allowed, scores * (1.0 / math.sqrt(head_size)), -1e30)
                weights_exp = jnp.exp(scores - jnp.max(scores, axis=1, keepdims=True))
                scale = 1.0 / jnp.sum(weights_exp, axis=1, keepdims=True)
                attended = jnp.dot(
                    (weights_exp * scale).astype(jnp.bfloat16), values,
                    preferred_element_type=jnp.float32,
                )
                attended_ref[at, index * head_size : (index + 1) * head_size] = (
                    attended.astype(jnp.bfloat16)
                )


def weight_spec(weight, tokens):
    depth = tokens[0][0].shape[1]
    if len(weight.shape) == 3:
        slots, _, head_size = weight.shape
        return pl.BlockSpec((slots, depth, head_size), lambda step, ids: (0, ids[step], 0))
    pieces = weight.shape[0] // len(tokens)
    return pl.BlockSpec((pieces,) + weight.shape[1:], lambda step, ids: (ids[step], 0, 0, 0))


def fixed(array):
    shape = array.shape
    return pl.BlockSpec(shape, lambda step, ids: (0,) * len(shape))


PARAMS = pltpu.CompilerParams(vmem_limit_bytes=VMEM_BYTES)


def call(kernel, name, ids, grid, specs, arrays, out, scratch=()):
    total = sum(array.size * array.dtype.itemsize for array in arrays)
    return pl.pallas_call(
        kernel,
        out_shape=out,
        grid_spec=pltpu.PrefetchScalarGridSpec(
            num_scalar_prefetch=1,
            grid=(grid,),
            in_specs=[fixed(array) if spec is None else spec for spec, array in zip(specs, arrays)],
            out_specs=[fixed(item) for item in out] if isinstance(out, tuple) else fixed(out),
            scratch_shapes=list(scratch),
        ),
        compiler_params=PARAMS,
        cost_estimate=pl.CostEstimate(flops=0, bytes_accessed=3 * total, transcendentals=0),
        name=name,
    )(ids, *arrays)


def project(ids, tokens, weight):
    rows = sum(part.shape[0] for part in tokens[0])
    slots, _, head_size = weight.shape[-3:]
    parts = [part for item in tokens for part in item]
    return call(
        functools.partial(project_kernel, [len(item) for item in tokens]),
        "project",
        ids,
        len(tokens),
        [None] * len(parts) + [weight_spec(weight, tokens)],
        parts + [weight],
        jax.ShapeDtypeStruct((rows, slots * head_size), jnp.float32),
    )


def attend(ids, group, adapters, dp_size, row, table, turn, up, rank, sums, tokens, weight, begun, prior):
    rows = sum(part.shape[0] for part in tokens[0])
    slots, _, head_size = weight.shape[-3:]
    out = (
        jax.ShapeDtypeStruct((rows, (slots - 2) * head_size), jnp.bfloat16),
        jax.ShapeDtypeStruct((rows, head_size), jnp.bfloat16),
        jax.ShapeDtypeStruct((rows, head_size), jnp.bfloat16),
    )
    parts = [part for item in tokens for part in item]

    def rows_of(array):
        return pl.BlockSpec((rows, array.shape[1]), lambda step, ids: (row // rows, 0))

    last = up.shape[2] // rank - 1
    group_at = len(tokens)
    up_spec = pl.BlockSpec(
        (dp_size, slots, rank, head_size),
        lambda step, ids: (ids[group_at] if up.shape[0] > dp_size else 0, 0, last, 0),
    )
    tables = [table, turn]
    started = (len(begun), len(prior))
    arrays = tables + [up] + sums + parts + [weight] + begun + list(prior)
    specs = (
        [rows_of(array) for array in tables]
        + [up_spec]
        + [rows_of(array) for array in sums]
        + [None] * len(parts)
        + [weight_spec(weight, tokens)]
        + [rows_of(array) for array in begun]
        + [None] * len(prior)
    )
    return call(
        functools.partial(
            attend_kernel, [len(item) for item in tokens], len(sums), started
        ),
        "attend",
        jnp.concatenate([ids, group.astype(jnp.int32)[None], adapters]),
        len(tokens),
        specs,
        arrays,
        out,
        [pltpu.VMEM((rows, slots * head_size), jnp.float32)],
    )


def shrink_kernel(ids_ref, table_ref, token_ref, down_ref, out_ref):
    step = pl.program_id(0)
    part = lax.dot_general(
        token_ref[...], down_ref[0], (((1,), (1,)), ((), ())), preferred_element_type=jnp.float32
    )
    rank = part.shape[1] // 3
    part = jnp.where(table_ref[:, 1:2] == step * rank, part, 0.0)

    @pl.when(step == 0)
    def _():
        out_ref[...] = part

    @pl.when(step > 0)
    def _():
        out_ref[...] += part


def shrink_partial(adapters, table, tokens, down):
    _, width, depth = down.shape
    return call(
        shrink_kernel,
        "shrink",
        adapters,
        adapters.shape[0],
        [None, None, pl.BlockSpec((1, width, depth), lambda step, ids: (ids[step], 0, 0))],
        [table, tokens, down],
        jax.ShapeDtypeStruct((tokens.shape[0], width), jnp.float32),
    )


def output_kernel(
    groups, parts, begun, last, dp_size, group_size, planes, count, ids_ref, *refs
):
    attended_refs, rest = refs[: groups * parts * 2], refs[groups * parts * 2 :]
    own_ref, half_refs, rest = rest[0], rest[1:3], rest[3:]
    begun_refs, rest = rest[: 2 * begun], rest[2 * begun :]
    if last:
        table_ref, up_ref, out_ref, acc_ref, low_ref, w_ref, down_ref = rest
    else:
        acc_ref, low_ref, w_ref, down_ref = rest
    step = pl.program_id(0)
    turn = ids_ref[step]
    at_worker, at_group = groups, groups + 1
    at_dp = groups + 2
    at_adapter = at_dp + dp_size
    at_pool = at_adapter + count
    features, columns = own_ref.shape
    share = features // (dp_size * group_size)
    rank = down_ref.shape[0] // count
    lot = (planes - 1) * share
    split = columns // features
    down_share = rank // split
    half_count = dp_size // 2

    def blocks(index, start, size):
        start = pl.multiple_of(start, 16)
        near = half_refs[0][jnp.minimum(index, half_count - 1), pl.ds(start, size), :]
        far = half_refs[1][jnp.maximum(index - half_count, 0), pl.ds(start, size), :]
        return jnp.where(index < half_count, near, far)

    @pl.when(turn == 0)
    def _():
        w_ref[...] = own_ref[...]

    @pl.when(turn > 0)
    def _():
        for group in range(group_size):
            base = (ids_ref[at_group] ^ group) * lot + (turn - 1) * share
            for place in range(dp_size):
                row = (group * dp_size + place) * share
                w_ref[row : row + share, :] = blocks(ids_ref[at_dp + place], base, share)

    for number in range(count):
        block = blocks(
            ids_ref[at_adapter + number], group_size * lot + turn * down_share, down_share
        )
        for piece in range(split):
            row = number * rank + piece * down_share
            down_ref[row : row + down_share, :] = block[
                :, piece * features : (piece + 1) * features
            ]

    def accumulate_group(number, side):
        row = 0
        for part in range(parts):
            attended = attended_refs[(number * parts + part) * 2 + side][...]
            at = slice(row, row + attended.shape[0])
            row = at.stop
            total = jnp.dot(attended, w_ref[...], preferred_element_type=jnp.float32)
            low = lax.dot_general(
                attended, down_ref[...], (((1,), (1,)), ((), ())),
                preferred_element_type=jnp.float32,
            )
            if number:
                total, low = acc_ref[at, :] + total, low_ref[at, :] + low
            elif begun:
                total, low = begun_refs[0][at, :] + total, begun_refs[1][at, :] + low
            acc_ref[at, :] = total
            low_ref[at, :] = low

    for number in range(groups):
        for side in range(2):
            pl.when((step == number) & (ids_ref[at_worker] == side))(
                functools.partial(accumulate_group, number, side)
            )

    if last:
        @pl.when(step == groups - 1)
        def _():
            low = low_ref[...].astype(jnp.bfloat16).astype(jnp.float32)
            lane = lax.broadcasted_iota(jnp.int32, low.shape, 1)
            kept = (lane >= table_ref[:, 1:2]) & (lane < table_ref[:, 1:2] + rank)
            low = jnp.where(kept, low, 0.0).astype(jnp.bfloat16)
            up = jnp.concatenate([up_ref[ids_ref[at_pool + j]] for j in range(count)], axis=0)
            extra = jnp.dot(low, up, preferred_element_type=jnp.float32)
            out_ref[...] = (acc_ref[...] + extra).astype(jnp.bfloat16)


def project_out(ids, attended, weights, sizes, begun, final):
    dp_size, group_size, planes, count, rank = sizes
    groups, parts = len(attended), len(attended[0])
    rows = sum(part[0].shape[0] for part in attended[0])
    features, columns = weights[0].shape
    flat = [array for group in attended for part in group for array in part]
    sums = (
        jax.ShapeDtypeStruct((rows, columns), jnp.float32),
        jax.ShapeDtypeStruct((rows, count * rank), jnp.float32),
    )
    arrays = flat + weights + begun + final
    scratch = [
        pltpu.VMEM((features, columns), jnp.bfloat16),
        pltpu.VMEM((count * rank, features), jnp.bfloat16),
    ]
    if final:
        scratch = [pltpu.VMEM(item.shape, jnp.float32) for item in sums] + scratch
    return call(
        functools.partial(
            output_kernel, groups, parts, len(begun) // 2, bool(final), dp_size, group_size,
            planes, count,
        ),
        "project_out",
        ids,
        groups,
        [None] * len(arrays),
        arrays,
        jax.ShapeDtypeStruct((rows, columns), jnp.bfloat16) if final else sums,
        scratch,
    )


def doubled(value, axis, size, moved=None):
    distance = size // 2
    if moved is None:
        moved = lax.ppermute(value, axis, [(i, i ^ distance) for i in range(size)])
    while distance > 1:
        distance //= 2
        value = jnp.concatenate([value, moved], axis=0)
        moved = lax.ppermute(value, axis, [(i, i ^ distance) for i in range(size)])
    return value, moved


def block_of(relative, size):
    block, bit, distance = 0, 1, size // 2
    while distance:
        block = block + jnp.where(relative & distance, bit, 0)
        bit, distance = bit * 2, distance // 2
    return block


def local(
    dp_size,
    group_size,
    planes,
    tokens,
    query_key_value_weight,
    output_weight,
    adapter_down_maps,
    adapter_up_maps,
    output_down_maps,
    output_up_maps,
    request_adapter,
    lengths,
):
    token_rows, depth = tokens.shape
    _, slots, head_size = query_key_value_weight.shape
    queries = slots - 2
    rank = adapter_up_maps.shape[1]
    features = queries * head_size
    columns = output_weight.shape[2] // planes
    pairs = planes // 2
    plane_size = dp_size * group_size

    def worker(pair):
        return 2 * pair + 1 - pair % 2

    def outer(pair):
        return 2 * pair + pair % 2

    to_worker = [(outer(p), worker(p)) for p in range(pairs)]
    from_worker = [(worker(p), outer(p)) for p in range(pairs)]
    ring = [(worker(p), worker((p + 1) % pairs)) for p in range(pairs)]
    here = lax.axis_index("tensor")
    pair = here // 2
    is_worker = here == worker(pair)
    sources = [(pair - step + pairs) % pairs for step in range(pairs)]
    worker_ids = jnp.stack([worker(source) for source in sources]).astype(jnp.int32)
    outer_ids = jnp.stack([outer(source) for source in sources]).astype(jnp.int32)
    dp_here, group_here = lax.axis_index("dp"), lax.axis_index("groups")
    place = group_here * dp_size + dp_here

    own_tokens = [tokens]
    for _ in range(pairs - 1):
        own_tokens.append(lax.ppermute(own_tokens[-1], "tensor", ring))
    weight = jnp.transpose(query_key_value_weight, (1, 0, 2))
    share = weight.shape[1] // plane_size
    up_own = jnp.transpose(adapter_up_maps[0], (1, 0, 2))
    piece = lax.dynamic_slice_in_dim(weight, place * share, share, axis=1)
    piece = lax.ppermute(jnp.concatenate([piece, up_own], axis=1), "tensor", to_worker)
    down_all = lax.all_gather(adapter_down_maps, "dp", axis=0, tiled=True)
    up_all = lax.all_gather(up_own, "dp", axis=0)
    out_up_all = lax.all_gather(output_up_maps, "dp", axis=0, tiled=True)

    requests = request_adapter.shape[1]
    request_ends = jnp.cumsum(lengths[0])
    request_starts = request_ends - lengths[0]
    at = jnp.arange(token_rows, dtype=jnp.int32)
    member = (at[:, None] >= request_starts[None, :]) & (at[:, None] < request_ends[None, :])
    if dp_size <= requests:
        count, adapters, label = dp_size, jnp.arange(dp_size), request_adapter[0]
    else:
        count, adapters, label = requests, request_adapter[0], jnp.arange(requests)
    adapters = adapters.astype(jnp.int32)
    wanted = jnp.stack([request_starts, label * rank], axis=0)
    table = jnp.sum(jnp.where(member[:, None, :], wanted[None], 0), axis=2).astype(jnp.int32)
    position = at - table[:, 0]
    half = head_size // 2
    inv_freq = 10000.0 ** (-2.0 * jnp.arange(half, dtype=jnp.float32) / head_size)
    angles = position.astype(jnp.float32)[:, None] * inv_freq[None, :]
    cosine, sine = jnp.cos(angles), jnp.sin(angles)
    turn = jnp.concatenate([cosine, cosine, -sine, sine], axis=1)

    out_share = features // plane_size
    line = place * out_share
    out_piece = lax.dynamic_slice(
        output_weight, (line % head_size, line // head_size, 0),
        (out_share, 1, output_weight.shape[2]),
    )[:, 0]
    own_weight = jnp.transpose(
        lax.dynamic_slice_in_dim(output_weight, here * columns, columns, axis=2), (1, 0, 2)
    ).reshape(features, columns)
    out_down = output_down_maps[0].reshape(rank, features)
    split = columns // features
    out_down = jnp.concatenate(jnp.split(out_down, split, axis=0), axis=1)
    sends = [
        jnp.concatenate(
            [
                lax.dynamic_slice_in_dim(
                    out_piece, (here + turn_by) % planes * columns, columns, axis=1
                ),
                out_down,
            ],
            axis=0,
        )
        for turn_by in range(1, planes)
    ]

    first = (own_tokens[-1], piece, up_all, table, turn, own_weight) + tuple(sends)
    outer_weight = lax.all_gather(after(piece, *first), PLANE, axis=0)

    chunk_rows = token_rows // CHUNKS
    begun = project(
        worker_ids, [(after(array, *first),) for array in own_tokens], weight
    )
    outer_first = lax.ppermute(after(tokens[:chunk_rows], *first), "tensor", to_worker)
    shrink = shrink_partial(adapters, table, after(tokens, *first), down_all)
    shrink_outer = lax.ppermute(shrink, "tensor", to_worker)

    received = [
        lax.ppermute(
            after(send, shrink), "tensor", [(i, (i + turn_by) % planes) for i in range(planes)]
        )
        for turn_by, send in enumerate(sends, 1)
    ]
    lot = jnp.concatenate([item[:out_share] for item in received], axis=0)

    second = (outer_first, shrink_outer, lot, begun)
    outer_tokens = [[outer_first]]
    for _ in range(pairs - 1):
        outer_tokens[0].append(lax.ppermute(outer_tokens[0][-1], "tensor", ring))
    outer_tokens.append([lax.ppermute(after(tokens[chunk_rows:], *second), "tensor", to_worker)])
    sums = [shrink + shrink_outer]
    for _ in range(pairs - 1):
        sums.append(lax.ppermute(sums[-1], "tensor", ring))
    lots = jnp.concatenate(doubled(after(lot, *second), "groups", group_size), axis=0)
    lots = jnp.concatenate(
        [lots, out_down] + [item[out_share:] for item in received], axis=0
    )

    third = (outer_tokens[0][-1], sums[-1], outer_tokens[1][0], lots)
    outer_tokens[1][0] = after(outer_tokens[1][0], *third[:3])
    for _ in range(pairs - 1):
        outer_tokens[1].append(lax.ppermute(outer_tokens[1][-1], "tensor", ring))

    def own_heads(chunk, prior):
        return attend(
            outer_ids, group_here, adapters, dp_size, chunk * chunk_rows, table, turn, up_all,
            rank, sums,
            [(array,) for array in outer_tokens[chunk]], weight, [begun], prior,
        )

    def spread(parts, gates):
        result, moving = [], parts
        for step in range(pairs):
            if step:
                moving = [
                    lax.ppermute(after(part, *gates), "tensor", ring) for part in moving
                ]
            result.append(
                [(lax.ppermute(part, "tensor", from_worker), part) for part in moving]
            )
        return result

    halves = after(lots, *third)[None]
    moved = lax.ppermute(halves, "dp", [(i, i ^ (dp_size // 2)) for i in range(dp_size)])
    own_first, keys, values = own_heads(0, ())
    spread_first = spread([own_first], ())
    own_second, _, _ = own_heads(1, (keys, values))
    halves = doubled(halves, "dp", dp_size, after(moved, own_second))
    spread_second = spread([own_second], ())
    gates = (own_second, spread_first[-1][0][1], spread_first[0][0][0], halves[0])
    outer_weight = after(outer_weight, *gates)
    outer_part, _, _ = attend(
        jnp.concatenate([worker_ids, outer_ids]), group_here, adapters, dp_size, 0, table, turn,
        outer_weight, rank, sums,
        [(array,) for array in own_tokens]
        + [
            tuple(outer_tokens[chunk][step] for chunk in range(CHUNKS)) for step in range(pairs)
        ],
        outer_weight, [], (),
    )
    spread_own = [a + b for a, b in zip(spread_first, spread_second)]
    spread_outer = spread([outer_part], (spread_second[-1][0][1],))

    def lookups(ids):
        return jnp.concatenate(
            [
                (here - ids + planes) % planes,
                jnp.stack([is_worker.astype(jnp.int32), group_here]),
                block_of(dp_here ^ jnp.arange(dp_size), dp_size),
                block_of(dp_here ^ adapters, dp_size),
                adapters,
            ]
        ).astype(jnp.int32)

    weights = [own_weight] + list(halves)
    sizes = (dp_size, group_size, planes, count, rank)
    begun = project_out(lookups(worker_ids), spread_own, weights, sizes, [], [])
    return project_out(
        lookups(outer_ids), spread_outer, weights, sizes, list(begun),
        [table, out_up_all],
    )


def solution(mesh):
    in_specs = (
        P(PLANE, "tensor"),
        P(None, None, "tensor"),
        P("tensor", None, None),
        P(PLANE, None, "tensor"),
        P(PLANE, None, None, "tensor"),
        P(PLANE, None, None, "tensor"),
        P(PLANE, None, "tensor"),
        P(PLANE, None),
        P(PLANE, None),
    )
    function = functools.partial(
        local, mesh.shape["dp"], mesh.shape["groups"], mesh.shape["tensor"]
    )
    return jax.shard_map(
        function, mesh=mesh, in_specs=in_specs, out_specs=P(PLANE, "tensor"), check_vma=False
    )
```

```python
import functools
import math

import jax
import jax.numpy as jnp
from jax import lax
from jax.experimental import pallas as pl
from jax.experimental.pallas import tpu as pltpu
from jax.sharding import PartitionSpec as P

VMEM_BYTES = 40 * 1024 * 1024
PLANE = ("groups", "dp")


def after(value, *earlier):
    return lax.optimization_barrier((value,) + earlier)[0]


def fixed(array):
    shape = array.shape
    return pl.BlockSpec(shape, lambda step, ids: (0,) * len(shape))


def call(kernel, name, ids, grid, specs, arrays, out, scratch=()):
    total = sum(array.size * array.dtype.itemsize for array in arrays)
    return pl.pallas_call(
        kernel,
        out_shape=out,
        grid_spec=pltpu.PrefetchScalarGridSpec(
            num_scalar_prefetch=1,
            grid=(grid,),
            in_specs=[fixed(array) if spec is None else spec for spec, array in zip(specs, arrays)],
            out_specs=[fixed(item) for item in out] if isinstance(out, tuple) else fixed(out),
            scratch_shapes=list(scratch),
        ),
        compiler_params=pltpu.CompilerParams(vmem_limit_bytes=VMEM_BYTES),
        cost_estimate=pl.CostEstimate(flops=0, bytes_accessed=3 * total, transcendentals=0),
        name=name,
    )(ids.astype(jnp.int32), *arrays)


def accumulate(acc_ref, token_ref, w_ref, first):
    slots, _, head_size = w_ref.shape
    for pair in range(slots // 2):
        columns = slice(2 * pair * head_size, (2 * pair + 2) * head_size)
        weight = jnp.concatenate([w_ref[2 * pair], w_ref[2 * pair + 1]], axis=1)
        total = jnp.dot(token_ref[...], weight, preferred_element_type=jnp.float32)
        acc_ref[:, columns] = total if first is None else first[:, columns] + total


def project_kernel(shards, begun, ids_ref, *refs):
    token_refs, w_ref, rest = refs[:shards], refs[shards], refs[shards + 1 :]
    acc_ref = rest[-1]
    step = pl.program_id(0)
    for number, token_ref in enumerate(token_refs):
        first = acc_ref if number else (rest[0] if begun else None)
        pl.when(step == number)(
            functools.partial(accumulate, acc_ref, token_ref, w_ref, first)
        )


def shard_spec(weight, depth):
    slots, _, head_size = weight.shape
    return pl.BlockSpec((slots, depth, head_size), lambda step, ids: (0, ids[step], 0))


def project(ids, tokens, weight, begun=()):
    rows, depth = tokens[0].shape
    slots, _, head_size = weight.shape
    return call(
        functools.partial(project_kernel, len(tokens), len(begun)),
        "project",
        ids,
        len(tokens),
        [None] * len(tokens) + [shard_spec(weight, depth)] + [None] * len(begun),
        [*tokens, weight, *begun],
        jax.ShapeDtypeStruct((rows, slots * head_size), jnp.float32),
    )


def attend_kernel(
    ids_ref, table_ref, turn_ref, up_ref, shrink_ref, token_ref, w_ref, begun_ref, out_ref,
    acc_ref, keys_ref, values_ref,
):
    accumulate(acc_ref, token_ref, w_ref, begun_ref)
    slots, _, head_size = w_ref.shape
    rank = up_ref.shape[2]
    count = ids_ref.shape[0] - 1
    rows = acc_ref.shape[0]
    block = min(rows, 256)
    queries = slots - 2
    ups = [
        jnp.concatenate([up_ref[ids_ref[1 + j], index] for j in range(count)], axis=0)
        for index in range(slots)
    ]
    for row in range(0, rows, block):
        at = slice(row, row + block)
        lane = lax.broadcasted_iota(jnp.int32, (block, count * rank), 1)
        kept = (lane >= table_ref[at, 1:2]) & (lane < table_ref[at, 1:2] + rank)
        lows = []
        for part in range(3):
            piece = shrink_ref[at, part * rank : (part + 1) * rank].astype(jnp.float32)
            piece = jnp.concatenate([piece] * count, axis=1)
            lows.append(jnp.where(kept, piece, 0.0).astype(jnp.bfloat16))

        def slot(index):
            low = lows[0 if index < queries else index - queries + 1]
            extra = jnp.dot(low, ups[index], preferred_element_type=jnp.float32)
            return acc_ref[at, index * head_size : (index + 1) * head_size] + extra

        def rotated(index):
            value = slot(index)
            turned = pltpu.roll(value, head_size // 2, 1)
            cos, sin = turn_ref[at, :head_size], turn_ref[at, head_size:]
            return (value * cos + turned * sin).astype(jnp.bfloat16)

        keys_ref[at, :] = rotated(queries)
        values_ref[at, :] = slot(queries + 1).astype(jnp.bfloat16)
        key_rows = row + block
        keys, values = keys_ref[:key_rows], values_ref[:key_rows]
        key_at = lax.broadcasted_iota(jnp.int32, (block, key_rows), 1)
        row_at = lax.broadcasted_iota(jnp.int32, (block, key_rows), 0) + row
        allowed = (key_at >= table_ref[at, 0:1]) & (key_at <= row_at)
        for index in range(queries):
            scores = lax.dot_general(
                rotated(index), keys, (((1,), (1,)), ((), ())),
                preferred_element_type=jnp.float32,
            )
            scores = jnp.where(allowed, scores * (1.0 / math.sqrt(head_size)), -1e30)
            weights = jnp.exp(scores - jnp.max(scores, axis=1, keepdims=True))
            scale = 1.0 / jnp.sum(weights, axis=1, keepdims=True)
            attended = jnp.dot(
                (weights * scale).astype(jnp.bfloat16), values, preferred_element_type=jnp.float32
            )
            out_ref[at, index * head_size : (index + 1) * head_size] = attended.astype(
                jnp.bfloat16
            )


def attend(shard, adapters, table, turn, up, shrink, tokens, weight, begun):
    rows, depth = tokens.shape
    slots, _, head_size = weight.shape
    return call(
        attend_kernel,
        "attend",
        jnp.concatenate([shard[None], adapters]),
        1,
        [None] * 5 + [shard_spec(weight, depth), None],
        [table, turn, up, shrink, tokens, weight, begun],
        jax.ShapeDtypeStruct((rows, (slots - 2) * head_size), jnp.bfloat16),
        [
            pltpu.VMEM((rows, slots * head_size), jnp.float32),
            pltpu.VMEM((rows, head_size), jnp.bfloat16),
            pltpu.VMEM((rows, head_size), jnp.bfloat16),
        ],
    )


def shrink_kernel(ids_ref, table_ref, token_ref, down_ref, out_ref):
    step = pl.program_id(0)
    part = lax.dot_general(
        token_ref[...], down_ref[0], (((1,), (1,)), ((), ())), preferred_element_type=jnp.float32
    )
    rank = part.shape[1] // 3
    part = jnp.where(table_ref[:, 1:2] == step * rank, part, 0.0)

    @pl.when(step == 0)
    def _():
        out_ref[...] = part

    @pl.when(step > 0)
    def _():
        out_ref[...] += part


def shrink_partial(adapters, table, tokens, down):
    _, width, depth = down.shape
    return call(
        shrink_kernel,
        "shrink",
        adapters,
        adapters.shape[0],
        [None, None, pl.BlockSpec((1, width, depth), lambda step, ids: (ids[step], 0, 0))],
        [table, tokens, down],
        jax.ShapeDtypeStruct((tokens.shape[0], width), jnp.float32),
    )


def output_kernel(groups, begun, last, ids_ref, *refs):
    attended_refs, w_refs, rest = refs[:groups], refs[groups : 2 * groups], refs[2 * groups :]
    down_ref, rest = rest[0], rest[1:]
    begun_refs, rest = rest[:begun], rest[begun:]
    if last:
        table_ref, up_ref, out_ref = rest
    else:
        acc_ref, low_ref = rest
    count = ids_ref.shape[0] - groups
    step = pl.program_id(0)
    down = jnp.concatenate([down_ref[ids_ref[groups + j], 0] for j in range(count)], axis=0)
    rank = down_ref.shape[2]

    def one(number):
        w_ref = w_refs[number]
        if len(w_ref.shape) == 2:
            weight = w_ref[...]
        else:
            weight = jnp.concatenate([w_ref[i, 0] for i in range(w_ref.shape[0])], axis=0)
        attended = attended_refs[number][...]
        total = jnp.dot(attended, weight, preferred_element_type=jnp.float32)
        low = lax.dot_general(
            attended, down, (((1,), (1,)), ((), ())), preferred_element_type=jnp.float32
        )
        if number:
            total, low = acc_ref[...] + total, low_ref[...] + low
        elif begun:
            total, low = begun_refs[0][...] + total, begun_refs[1][...] + low
        if last:
            low = low.astype(jnp.bfloat16).astype(jnp.float32)
            lane = lax.broadcasted_iota(jnp.int32, low.shape, 1)
            kept = (lane >= table_ref[:, 1:2]) & (lane < table_ref[:, 1:2] + rank)
            low = jnp.where(kept, low, 0.0).astype(jnp.bfloat16)
            up = jnp.concatenate([up_ref[ids_ref[groups + j]] for j in range(count)], axis=0)
            extra = jnp.dot(low, up, preferred_element_type=jnp.float32)
            out_ref[...] = (total + extra).astype(jnp.bfloat16)
        else:
            acc_ref[...] = total
            low_ref[...] = low

    for number in range(groups):
        pl.when(step == number)(functools.partial(one, number))


def project_out(planes_of, adapters, attended, weights, down, begun, final):
    groups = len(attended)
    rows, features = attended[0].shape
    rank = down.shape[2]
    columns = weights[0][0].shape[-1]
    w_arrays, w_specs = [], []
    for array, turn in weights:
        w_arrays.append(array)
        if turn is None:
            w_specs.append(None)
        else:
            w_specs.append(
                pl.BlockSpec(
                    (array.shape[0], 1) + array.shape[2:],
                    lambda step, ids, turn=turn: (0, turn, 0, 0),
                )
            )
    down_spec = pl.BlockSpec(
        (down.shape[0], 1) + down.shape[2:], lambda step, ids: (0, ids[step], 0, 0)
    )
    sums = (
        jax.ShapeDtypeStruct((rows, columns), jnp.float32),
        jax.ShapeDtypeStruct((rows, adapters.shape[0] * rank), jnp.float32),
    )
    return call(
        functools.partial(output_kernel, groups, len(begun), bool(final)),
        "project_out",
        jnp.concatenate([planes_of, adapters]),
        groups,
        [None] * groups + w_specs + [down_spec] + [None] * (len(begun) + len(final)),
        [*attended, *w_arrays, down, *begun, *final],
        jax.ShapeDtypeStruct((rows, columns), jnp.bfloat16) if final else sums,
    )


def local(
    plane_size,
    planes,
    tokens,
    query_key_value_weight,
    output_weight,
    adapter_down_maps,
    adapter_up_maps,
    output_down_maps,
    output_up_maps,
    request_adapter,
    lengths,
):
    token_rows, depth = tokens.shape
    _, slots, head_size = query_key_value_weight.shape
    queries = slots - 2
    pool, rank = plane_size // lax.axis_size("groups"), adapter_up_maps.shape[1]
    features = queries * head_size
    columns = output_weight.shape[2] // planes
    here = lax.axis_index("tensor")
    place = lax.axis_index(PLANE)
    planes_of = (here - jnp.arange(planes) + planes) % planes

    def turned(value, turn=1):
        return lax.ppermute(value, "tensor", [(i, (i + turn) % planes) for i in range(planes)])

    held = [tokens, turned(tokens)]
    weight = jnp.transpose(query_key_value_weight, (1, 0, 2))
    down_all = lax.all_gather(adapter_down_maps, "dp", axis=0, tiled=True)
    up_all = lax.all_gather(jnp.transpose(adapter_up_maps[0], (1, 0, 2)), "dp", axis=0)
    out_down = output_down_maps[0].reshape(rank, features)
    out_downs = lax.all_gather(after(out_down, down_all), ("dp", "tensor"), axis=0)
    out_downs = out_downs.reshape(pool, planes, rank, features)

    requests = request_adapter.shape[1]
    request_ends = jnp.cumsum(lengths[0])
    request_starts = request_ends - lengths[0]
    at = jnp.arange(token_rows, dtype=jnp.int32)
    member = (at[:, None] >= request_starts[None, :]) & (at[:, None] < request_ends[None, :])
    if pool <= requests:
        adapters, label = jnp.arange(pool), request_adapter[0]
    else:
        adapters, label = request_adapter[0], jnp.arange(requests)
    wanted = jnp.stack([request_starts, label * rank], axis=0)
    table = jnp.sum(jnp.where(member[:, None, :], wanted[None], 0), axis=2).astype(jnp.int32)
    position = at - table[:, 0]
    half = head_size // 2
    inv_freq = 10000.0 ** (-2.0 * jnp.arange(half, dtype=jnp.float32) / head_size)
    angles = position.astype(jnp.float32)[:, None] * inv_freq[None, :]
    cosine, sine = jnp.cos(angles), jnp.sin(angles)
    turn = jnp.concatenate([cosine, cosine, -sine, sine], axis=1)

    own_rows = jnp.transpose(
        lax.dynamic_slice_in_dim(output_weight, here * columns, columns, axis=2), (1, 0, 2)
    ).reshape(features, columns)
    share = features // plane_size
    line = place * share
    piece = lax.dynamic_slice(
        output_weight, (line % head_size, line // head_size, 0),
        (share, 1, output_weight.shape[2]),
    )[:, 0]
    sends = [
        lax.dynamic_slice_in_dim(piece, (here + k) % planes * columns, columns, axis=1)
        for k in range(1, planes)
    ]

    begun = project(planes_of[:1], held[:1], weight)
    held[1] = after(held[1], begun, up_all, table, turn, own_rows, *sends)
    lines = [turned(after(send, held[1]), k) for k, send in enumerate(sends, 1)]
    shrink = shrink_partial(adapters, table, after(tokens, held[1]), down_all)
    shrink = lax.psum_scatter(shrink, "tensor", scatter_dimension=0, tiled=True)
    done = (shrink, *lines)
    for step in range(2, planes):
        arrived = held[-1]
        held.append(turned(arrived))
        begun = project(planes_of[step - 1 : step], [arrived], weight, [begun])
        held[-1] = after(held[-1], begun, *done)
        done = ()
    lines = lax.all_gather(jnp.stack(lines), PLANE, axis=0)
    shrink = lax.all_gather(shrink.astype(jnp.bfloat16), "tensor", axis=0, tiled=True)
    out_up_all = lax.all_gather(
        after(output_up_maps, *held[2:3]), "dp", axis=0, tiled=True
    )
    attended = [
        attend(
            planes_of[planes - 1], adapters, table, turn, up_all, after(shrink, out_up_all),
            held[-1], weight, begun,
        )
    ]

    attended.append(turned(attended[0]))
    sums = project_out(
        planes_of[:1], adapters, attended[:1], [(own_rows, None)], out_downs, [], []
    )
    for step in range(2, planes + 1):
        arrived = after(attended[-1], *sums)
        if step < planes:
            attended.append(turned(arrived))
        sums = project_out(
            planes_of[step - 1 : step], adapters, [arrived], [(lines, step - 2)], out_downs,
            list(sums), [] if step < planes else [table, out_up_all],
        )
    return sums


def solution(mesh):
    in_specs = (
        P(PLANE, "tensor"),
        P(None, None, "tensor"),
        P("tensor", None, None),
        P(PLANE, None, "tensor"),
        P(PLANE, None, None, "tensor"),
        P(PLANE, None, None, "tensor"),
        P(PLANE, None, "tensor"),
        P(PLANE, None),
        P(PLANE, None),
    )
    function = functools.partial(
        local, mesh.shape["groups"] * mesh.shape["dp"], mesh.shape["tensor"]
    )
    return jax.shard_map(
        function, mesh=mesh, in_specs=in_specs, out_specs=P(PLANE, "tensor"), check_vma=False
    )
```

```python
import functools
import math

import jax
import jax.numpy as jnp
from jax import lax
from jax.experimental import pallas as pl
from jax.experimental.pallas import tpu as pltpu
from jax.sharding import PartitionSpec as P

VMEM_BYTES = 40 * 1024 * 1024
PLANE = ("groups", "dp")


def after(value, *earlier):
    return lax.optimization_barrier((value,) + earlier)[0]


def fixed(array):
    shape = array.shape
    return pl.BlockSpec(shape, lambda step, ids: (0,) * len(shape))


def call(kernel, name, ids, grid, specs, arrays, out, scratch=()):
    total = sum(array.size * array.dtype.itemsize for array in arrays)
    return pl.pallas_call(
        kernel,
        out_shape=out,
        grid_spec=pltpu.PrefetchScalarGridSpec(
            num_scalar_prefetch=1,
            grid=(grid,),
            in_specs=[fixed(array) if spec is None else spec for spec, array in zip(specs, arrays)],
            out_specs=[fixed(item) for item in out] if isinstance(out, tuple) else fixed(out),
            scratch_shapes=list(scratch),
        ),
        compiler_params=pltpu.CompilerParams(vmem_limit_bytes=VMEM_BYTES),
        cost_estimate=pl.CostEstimate(flops=0, bytes_accessed=3 * total, transcendentals=0),
        name=name,
    )(ids.astype(jnp.int32), *arrays)


def accumulate(acc_ref, token_ref, w_ref, first):
    slots, _, head_size = w_ref.shape
    for pair in range(slots // 2):
        columns = slice(2 * pair * head_size, (2 * pair + 2) * head_size)
        weight = jnp.concatenate([w_ref[2 * pair], w_ref[2 * pair + 1]], axis=1)
        total = jnp.dot(token_ref[...], weight, preferred_element_type=jnp.float32)
        acc_ref[:, columns] = total if first is None else first[:, columns] + total


def project_kernel(shards, begun, ids_ref, *refs):
    token_refs, w_ref, rest = refs[:shards], refs[shards], refs[shards + 1 :]
    acc_ref = rest[-1]
    step = pl.program_id(0)
    for number, token_ref in enumerate(token_refs):
        first = acc_ref if number else (rest[0] if begun else None)
        pl.when(step == number)(
            functools.partial(accumulate, acc_ref, token_ref, w_ref, first)
        )


def shard_spec(weight, depth):
    slots, _, head_size = weight.shape
    return pl.BlockSpec((slots, depth, head_size), lambda step, ids: (0, ids[step], 0))


def project(ids, tokens, weight, begun=()):
    rows, depth = tokens[0].shape
    slots, _, head_size = weight.shape
    return call(
        functools.partial(project_kernel, len(tokens), len(begun)),
        "project",
        ids,
        len(tokens),
        [None] * len(tokens) + [shard_spec(weight, depth)] + [None] * len(begun),
        [*tokens, weight, *begun],
        jax.ShapeDtypeStruct((rows, slots * head_size), jnp.float32),
    )


def attend_kernel(planes, ids_ref, table_ref, turn_ref, up_ref, *refs):
    piece_refs, refs = refs[:planes], refs[planes:]
    token_ref, w_ref, begun_ref, out_ref, acc_ref, keys_ref, values_ref, shrink_ref = refs
    for number, piece_ref in enumerate(piece_refs):
        size = piece_ref.shape[0]
        shrink_ref[pl.ds(pl.multiple_of(ids_ref[number] * size, size), size), :] = piece_ref[...]
    accumulate(acc_ref, token_ref, w_ref, begun_ref)
    slots, _, head_size = w_ref.shape
    rank = up_ref.shape[2]
    count = ids_ref.shape[0] - planes
    rows = acc_ref.shape[0]
    block = min(rows, 256)
    queries = slots - 2
    ups = [
        jnp.concatenate([up_ref[ids_ref[planes + j], index] for j in range(count)], axis=0)
        for index in range(slots)
    ]
    for row in range(0, rows, block):
        at = slice(row, row + block)
        lane = lax.broadcasted_iota(jnp.int32, (block, count * rank), 1)
        kept = (lane >= table_ref[at, 1:2]) & (lane < table_ref[at, 1:2] + rank)
        lows = []
        for part in range(3):
            piece = shrink_ref[at, part * rank : (part + 1) * rank].astype(jnp.float32)
            piece = jnp.concatenate([piece] * count, axis=1)
            lows.append(jnp.where(kept, piece, 0.0).astype(jnp.bfloat16))

        def slot(index):
            low = lows[0 if index < queries else index - queries + 1]
            extra = jnp.dot(low, ups[index], preferred_element_type=jnp.float32)
            return acc_ref[at, index * head_size : (index + 1) * head_size] + extra

        def rotated(index):
            value = slot(index)
            turned = pltpu.roll(value, head_size // 2, 1)
            cos, sin = turn_ref[at, :head_size], turn_ref[at, head_size:]
            return (value * cos + turned * sin).astype(jnp.bfloat16)

        keys_ref[at, :] = rotated(queries)
        values_ref[at, :] = slot(queries + 1).astype(jnp.bfloat16)
        key_rows = row + block
        keys, values = keys_ref[:key_rows], values_ref[:key_rows]
        key_at = lax.broadcasted_iota(jnp.int32, (block, key_rows), 1)
        row_at = lax.broadcasted_iota(jnp.int32, (block, key_rows), 0) + row
        allowed = (key_at >= table_ref[at, 0:1]) & (key_at <= row_at)
        for index in range(queries):
            scores = lax.dot_general(
                rotated(index), keys, (((1,), (1,)), ((), ())),
                preferred_element_type=jnp.float32,
            )
            scores = jnp.where(allowed, scores * (1.0 / math.sqrt(head_size)), -1e30)
            weights = jnp.exp(scores - jnp.max(scores, axis=1, keepdims=True))
            scale = 1.0 / jnp.sum(weights, axis=1, keepdims=True)
            attended = jnp.dot(
                (weights * scale).astype(jnp.bfloat16), values, preferred_element_type=jnp.float32
            )
            out_ref[at, index * head_size : (index + 1) * head_size] = attended.astype(
                jnp.bfloat16
            )


def attend(planes_of, adapters, table, turn, up, shrink, tokens, weight, begun):
    rows, depth = tokens.shape
    slots, _, head_size = weight.shape
    planes = len(shrink)
    return call(
        functools.partial(attend_kernel, planes),
        "attend",
        jnp.concatenate([planes_of, adapters]),
        1,
        [None] * (4 + planes)
        + [
            pl.BlockSpec((slots, depth, head_size), lambda step, ids: (0, ids[planes - 1], 0)),
            None,
        ],
        [table, turn, up, *shrink, tokens, weight, begun],
        jax.ShapeDtypeStruct((rows, (slots - 2) * head_size), jnp.bfloat16),
        [
            pltpu.VMEM((rows, slots * head_size), jnp.float32),
            pltpu.VMEM((rows, head_size), jnp.bfloat16),
            pltpu.VMEM((rows, head_size), jnp.bfloat16),
            pltpu.VMEM((rows, shrink[0].shape[1]), jnp.bfloat16),
        ],
    )


def shrink_kernel(planes, ids_ref, table_ref, token_ref, down_ref, *refs):
    out_refs, acc_ref = refs[:planes], refs[planes]
    step = pl.program_id(0)
    count = ids_ref.shape[0] - 1
    part = lax.dot_general(
        token_ref[...], down_ref[0], (((1,), (1,)), ((), ())), preferred_element_type=jnp.float32
    )
    rank = part.shape[1] // 3
    part = jnp.where(table_ref[:, 1:2] == step * rank, part, 0.0)

    @pl.when(step == 0)
    def _():
        acc_ref[...] = part

    @pl.when(step > 0)
    def _():
        acc_ref[...] += part

    @pl.when(step == count - 1)
    def _():
        for turn, out_ref in enumerate(out_refs):
            rows = out_ref.shape[0]
            plane = lax.rem(ids_ref[count] + turn, planes)
            out_ref[...] = acc_ref[pl.ds(pl.multiple_of(plane * rows, rows), rows), :]


def shrink_partial(adapters, here, planes, table, tokens, down):
    _, width, depth = down.shape
    rows = tokens.shape[0]
    return call(
        functools.partial(shrink_kernel, planes),
        "shrink",
        jnp.concatenate([adapters, here[None]]),
        adapters.shape[0],
        [None, None, pl.BlockSpec((1, width, depth), lambda step, ids: (ids[step], 0, 0))],
        [table, tokens, down],
        (jax.ShapeDtypeStruct((rows // planes, width), jnp.float32),) * planes,
        [pltpu.VMEM((rows, width), jnp.float32)],
    )


def output_kernel(groups, begun, last, ids_ref, *refs):
    attended_refs, w_refs, rest = refs[:groups], refs[groups : 2 * groups], refs[2 * groups :]
    down_ref, rest = rest[0], rest[1:]
    begun_refs, rest = rest[:begun], rest[begun:]
    if last:
        table_ref, up_ref, out_ref = rest
    else:
        acc_ref, low_ref = rest
    count = ids_ref.shape[0] - groups
    step = pl.program_id(0)
    down = jnp.concatenate([down_ref[ids_ref[groups + j], 0] for j in range(count)], axis=0)
    rank = down_ref.shape[2]

    def one(number):
        w_ref = w_refs[number]
        if len(w_ref.shape) == 2:
            weight = w_ref[...]
        else:
            weight = jnp.concatenate([w_ref[i, 0] for i in range(w_ref.shape[0])], axis=0)
        attended = attended_refs[number][...]
        total = jnp.dot(attended, weight, preferred_element_type=jnp.float32)
        low = lax.dot_general(
            attended, down, (((1,), (1,)), ((), ())), preferred_element_type=jnp.float32
        )
        if number:
            total, low = acc_ref[...] + total, low_ref[...] + low
        elif begun:
            total, low = begun_refs[0][...] + total, begun_refs[1][...] + low
        if last:
            low = low.astype(jnp.bfloat16).astype(jnp.float32)
            lane = lax.broadcasted_iota(jnp.int32, low.shape, 1)
            kept = (lane >= table_ref[:, 1:2]) & (lane < table_ref[:, 1:2] + rank)
            low = jnp.where(kept, low, 0.0).astype(jnp.bfloat16)
            up = jnp.concatenate([up_ref[ids_ref[groups + j]] for j in range(count)], axis=0)
            extra = jnp.dot(low, up, preferred_element_type=jnp.float32)
            out_ref[...] = (total + extra).astype(jnp.bfloat16)
        else:
            acc_ref[...] = total
            low_ref[...] = low

    for number in range(groups):
        pl.when(step == number)(functools.partial(one, number))


def project_out(planes_of, adapters, attended, weights, down, begun, final):
    groups = len(attended)
    rows, features = attended[0].shape
    rank = down.shape[2]
    columns = weights[0][0].shape[-1]
    w_arrays, w_specs = [], []
    for array, turn in weights:
        w_arrays.append(array)
        if turn is None:
            w_specs.append(None)
        else:
            w_specs.append(
                pl.BlockSpec(
                    (array.shape[0], 1) + array.shape[2:],
                    lambda step, ids, turn=turn: (0, turn, 0, 0),
                )
            )
    down_spec = pl.BlockSpec(
        (down.shape[0], 1) + down.shape[2:], lambda step, ids: (0, ids[step], 0, 0)
    )
    sums = (
        jax.ShapeDtypeStruct((rows, columns), jnp.float32),
        jax.ShapeDtypeStruct((rows, adapters.shape[0] * rank), jnp.float32),
    )
    return call(
        functools.partial(output_kernel, groups, len(begun), bool(final)),
        "project_out",
        jnp.concatenate([planes_of, adapters]),
        groups,
        [None] * groups + w_specs + [down_spec] + [None] * (len(begun) + len(final)),
        [*attended, *w_arrays, down, *begun, *final],
        jax.ShapeDtypeStruct((rows, columns), jnp.bfloat16) if final else sums,
    )


def local(
    plane_size,
    planes,
    tokens,
    query_key_value_weight,
    output_weight,
    adapter_down_maps,
    adapter_up_maps,
    output_down_maps,
    output_up_maps,
    request_adapter,
    lengths,
):
    token_rows, depth = tokens.shape
    _, slots, head_size = query_key_value_weight.shape
    queries = slots - 2
    pool, rank = plane_size // lax.axis_size("groups"), adapter_up_maps.shape[1]
    features = queries * head_size
    columns = output_weight.shape[2] // planes
    here = lax.axis_index("tensor")
    place = lax.axis_index(PLANE)
    planes_of = (here - jnp.arange(planes) + planes) % planes

    def turned(value, turn=1):
        return lax.ppermute(value, "tensor", [(i, (i + turn) % planes) for i in range(planes)])

    held = [tokens, turned(tokens)]
    weight = jnp.transpose(query_key_value_weight, (1, 0, 2))
    down_all = lax.all_gather(adapter_down_maps, "dp", axis=0, tiled=True)
    up_all = lax.all_gather(jnp.transpose(adapter_up_maps[0], (1, 0, 2)), "dp", axis=0)
    out_down = output_down_maps[0].reshape(rank, features)
    out_downs = lax.all_gather(after(out_down, down_all), ("dp", "tensor"), axis=0)
    out_downs = out_downs.reshape(pool, planes, rank, features)

    requests = request_adapter.shape[1]
    request_ends = jnp.cumsum(lengths[0])
    request_starts = request_ends - lengths[0]
    at = jnp.arange(token_rows, dtype=jnp.int32)
    member = (at[:, None] >= request_starts[None, :]) & (at[:, None] < request_ends[None, :])
    if pool <= requests:
        adapters, label = jnp.arange(pool), request_adapter[0]
    else:
        adapters, label = request_adapter[0], jnp.arange(requests)
    wanted = jnp.stack([request_starts, label * rank], axis=0)
    table = jnp.sum(jnp.where(member[:, None, :], wanted[None], 0), axis=2).astype(jnp.int32)
    position = at - table[:, 0]
    half = head_size // 2
    inv_freq = 10000.0 ** (-2.0 * jnp.arange(half, dtype=jnp.float32) / head_size)
    angles = position.astype(jnp.float32)[:, None] * inv_freq[None, :]
    cosine, sine = jnp.cos(angles), jnp.sin(angles)
    turn = jnp.concatenate([cosine, cosine, -sine, sine], axis=1)

    own_rows = jnp.transpose(
        lax.dynamic_slice_in_dim(output_weight, here * columns, columns, axis=2), (1, 0, 2)
    ).reshape(features, columns)
    share = features // plane_size
    line = place * share
    piece = lax.dynamic_slice(
        output_weight, (line % head_size, line // head_size, 0),
        (share, 1, output_weight.shape[2]),
    )[:, 0]
    sends = [
        lax.dynamic_slice_in_dim(piece, (here + k) % planes * columns, columns, axis=1)
        for k in range(1, planes)
    ]

    begun = project(planes_of[:1], held[:1], weight)
    held[1] = after(held[1], begun, up_all, table, turn, own_rows, *sends)
    lines = [turned(after(send, held[1]), k) for k, send in enumerate(sends, 1)]
    sums = shrink_partial(adapters, here, planes, table, after(tokens, held[1]), down_all)
    sums = [sums[0]] + [turned(sums[k], k) for k in range(1, planes)]
    shrink = sum(sums[1:], sums[0]).astype(jnp.bfloat16)
    for step in range(2, planes):
        arrived = held[-1]
        held.append(turned(arrived))
        begun = project(planes_of[step - 1 : step], [arrived], weight, [begun])
        held[-1] = after(held[-1], begun, *([shrink, *lines] if step == 2 else []))
    lines = lax.all_gather(jnp.stack([after(line, held[2]) for line in lines]), PLANE, axis=0)
    shrink = after(shrink, held[2])
    shrink = [shrink] + [turned(shrink, k) for k in range(1, planes)]
    attended = [
        attend(planes_of, adapters, table, turn, up_all, shrink, held[-1], weight, begun)
    ]

    out_up_all = lax.all_gather(
        after(output_up_maps, attended[0]), "dp", axis=0, tiled=True
    )
    attended.append(turned(attended[0]))
    sums = project_out(
        planes_of[:1], adapters, attended[:1], [(own_rows, None)], out_downs, [], []
    )
    for step in range(2, planes + 1):
        arrived = after(attended[-1], *sums)
        if step < planes:
            attended.append(turned(arrived))
        sums = project_out(
            planes_of[step - 1 : step], adapters, [arrived], [(lines, step - 2)], out_downs,
            list(sums), [] if step < planes else [table, out_up_all],
        )
    return sums


def solution(mesh):
    in_specs = (
        P(PLANE, "tensor"),
        P(None, None, "tensor"),
        P("tensor", None, None),
        P(PLANE, None, "tensor"),
        P(PLANE, None, None, "tensor"),
        P(PLANE, None, None, "tensor"),
        P(PLANE, None, "tensor"),
        P(PLANE, None),
        P(PLANE, None),
    )
    function = functools.partial(
        local, mesh.shape["groups"] * mesh.shape["dp"], mesh.shape["tensor"]
    )
    return jax.shard_map(
        function, mesh=mesh, in_specs=in_specs, out_specs=P(PLANE, "tensor"), check_vma=False
    )
```

```python
import functools
import math

import jax
import jax.numpy as jnp
from jax import lax
from jax.experimental import pallas as pl
from jax.experimental.pallas import tpu as pltpu
from jax.sharding import PartitionSpec as P

VMEM_BYTES = 40 * 1024 * 1024
PLANE = ("groups", "dp")


def after(value, *earlier):
    return lax.optimization_barrier((value,) + earlier)[0]


def fixed(array):
    shape = array.shape
    return pl.BlockSpec(shape, lambda step, ids: (0,) * len(shape))


def call(kernel, name, ids, grid, specs, arrays, out, scratch=()):
    total = sum(array.size * array.dtype.itemsize for array in arrays)
    return pl.pallas_call(
        kernel,
        out_shape=out,
        grid_spec=pltpu.PrefetchScalarGridSpec(
            num_scalar_prefetch=1,
            grid=(grid,),
            in_specs=[fixed(array) if spec is None else spec for spec, array in zip(specs, arrays)],
            out_specs=[fixed(item) for item in out] if isinstance(out, tuple) else fixed(out),
            scratch_shapes=list(scratch),
        ),
        compiler_params=pltpu.CompilerParams(vmem_limit_bytes=VMEM_BYTES),
        cost_estimate=pl.CostEstimate(flops=0, bytes_accessed=3 * total, transcendentals=0),
        name=name,
    )(ids.astype(jnp.int32), *arrays)


def accumulate(acc_ref, token_ref, w_ref, first):
    slots, _, head_size = w_ref.shape
    for pair in range(slots // 2):
        columns = slice(2 * pair * head_size, (2 * pair + 2) * head_size)
        weight = jnp.concatenate([w_ref[2 * pair], w_ref[2 * pair + 1]], axis=1)
        total = jnp.dot(token_ref[...], weight, preferred_element_type=jnp.float32)
        acc_ref[:, columns] = total if first is None else first[:, columns] + total


def project_kernel(shards, begun, ids_ref, *refs):
    token_refs, w_ref, rest = refs[:shards], refs[shards], refs[shards + 1 :]
    acc_ref = rest[-1]
    step = pl.program_id(0)
    for number, token_ref in enumerate(token_refs):
        first = acc_ref if number else (rest[0] if begun else None)
        pl.when(step == number)(
            functools.partial(accumulate, acc_ref, token_ref, w_ref, first)
        )


def shard_spec(weight, depth):
    slots, _, head_size = weight.shape
    return pl.BlockSpec((slots, depth, head_size), lambda step, ids: (0, ids[step], 0))


def project(ids, tokens, weight, begun=()):
    rows, depth = tokens[0].shape
    slots, _, head_size = weight.shape
    return call(
        functools.partial(project_kernel, len(tokens), len(begun)),
        "project",
        ids,
        len(tokens),
        [None] * len(tokens) + [shard_spec(weight, depth)] + [None] * len(begun),
        [*tokens, weight, *begun],
        jax.ShapeDtypeStruct((rows, slots * head_size), jnp.float32),
    )


def attend_kernel(planes, ids_ref, table_ref, turn_ref, up_ref, *refs):
    piece_refs, refs = refs[:planes], refs[planes:]
    token_ref, w_ref, begun_ref, out_ref, acc_ref, keys_ref, values_ref, shrink_ref = refs
    for number, piece_ref in enumerate(piece_refs):
        size = piece_ref.shape[0]
        shrink_ref[pl.ds(pl.multiple_of(ids_ref[number] * size, size), size), :] = piece_ref[...]
    accumulate(acc_ref, token_ref, w_ref, begun_ref)
    slots, _, head_size = w_ref.shape
    rank = up_ref.shape[2]
    count = ids_ref.shape[0] - planes
    rows = acc_ref.shape[0]
    block = min(rows, 256)
    queries = slots - 2
    ups = [
        jnp.concatenate([up_ref[ids_ref[planes + j], index] for j in range(count)], axis=0)
        for index in range(slots)
    ]
    for row in range(0, rows, block):
        at = slice(row, row + block)
        lane = lax.broadcasted_iota(jnp.int32, (block, count * rank), 1)
        kept = (lane >= table_ref[at, 1:2]) & (lane < table_ref[at, 1:2] + rank)
        lows = []
        for part in range(3):
            piece = shrink_ref[at, part * rank : (part + 1) * rank].astype(jnp.float32)
            piece = jnp.concatenate([piece] * count, axis=1)
            lows.append(jnp.where(kept, piece, 0.0).astype(jnp.bfloat16))

        def slot(index):
            low = lows[0 if index < queries else index - queries + 1]
            extra = jnp.dot(low, ups[index], preferred_element_type=jnp.float32)
            return acc_ref[at, index * head_size : (index + 1) * head_size] + extra

        def rotated(index):
            value = slot(index)
            turned = pltpu.roll(value, head_size // 2, 1)
            cos, sin = turn_ref[at, :head_size], turn_ref[at, head_size:]
            return (value * cos + turned * sin).astype(jnp.bfloat16)

        keys_ref[at, :] = rotated(queries)
        values_ref[at, :] = slot(queries + 1).astype(jnp.bfloat16)
        key_rows = row + block
        keys, values = keys_ref[:key_rows], values_ref[:key_rows]
        key_at = lax.broadcasted_iota(jnp.int32, (block, key_rows), 1)
        row_at = lax.broadcasted_iota(jnp.int32, (block, key_rows), 0) + row
        allowed = (key_at >= table_ref[at, 0:1]) & (key_at <= row_at)
        for index in range(queries):
            scores = lax.dot_general(
                rotated(index), keys, (((1,), (1,)), ((), ())),
                preferred_element_type=jnp.float32,
            )
            scores = jnp.where(allowed, scores * (1.0 / math.sqrt(head_size)), -1e30)
            weights = jnp.exp(scores - jnp.max(scores, axis=1, keepdims=True))
            scale = 1.0 / jnp.sum(weights, axis=1, keepdims=True)
            attended = jnp.dot(
                (weights * scale).astype(jnp.bfloat16), values, preferred_element_type=jnp.float32
            )
            out_ref[at, index * head_size : (index + 1) * head_size] = attended.astype(
                jnp.bfloat16
            )


def attend(planes_of, adapters, table, turn, up, shrink, tokens, weight, begun):
    rows, depth = tokens.shape
    slots, _, head_size = weight.shape
    planes = len(shrink)
    return call(
        functools.partial(attend_kernel, planes),
        "attend",
        jnp.concatenate([planes_of, adapters]),
        1,
        [None] * (4 + planes)
        + [
            pl.BlockSpec((slots, depth, head_size), lambda step, ids: (0, ids[planes - 1], 0)),
            None,
        ],
        [table, turn, up, *shrink, tokens, weight, begun],
        jax.ShapeDtypeStruct((rows, (slots - 2) * head_size), jnp.bfloat16),
        [
            pltpu.VMEM((rows, slots * head_size), jnp.float32),
            pltpu.VMEM((rows, head_size), jnp.bfloat16),
            pltpu.VMEM((rows, head_size), jnp.bfloat16),
            pltpu.VMEM((rows, shrink[0].shape[1]), jnp.bfloat16),
        ],
    )


def shrink_kernel(planes, ids_ref, table_ref, token_ref, down_ref, *refs):
    out_refs, acc_ref = refs[:planes], refs[planes]
    step = pl.program_id(0)
    count = ids_ref.shape[0] - 1
    part = lax.dot_general(
        token_ref[...], down_ref[0], (((1,), (1,)), ((), ())), preferred_element_type=jnp.float32
    )
    rank = part.shape[1] // 3
    part = jnp.where(table_ref[:, 1:2] == step * rank, part, 0.0)

    @pl.when(step == 0)
    def _():
        acc_ref[...] = part

    @pl.when(step > 0)
    def _():
        acc_ref[...] += part

    @pl.when(step == count - 1)
    def _():
        for turn, out_ref in enumerate(out_refs):
            rows = out_ref.shape[0]
            plane = lax.rem(ids_ref[count] + turn, planes)
            out_ref[...] = acc_ref[pl.ds(pl.multiple_of(plane * rows, rows), rows), :]


def shrink_partial(adapters, here, planes, table, tokens, down):
    _, width, depth = down.shape
    rows = tokens.shape[0]
    return call(
        functools.partial(shrink_kernel, planes),
        "shrink",
        jnp.concatenate([adapters, here[None]]),
        adapters.shape[0],
        [None, None, pl.BlockSpec((1, width, depth), lambda step, ids: (ids[step], 0, 0))],
        [table, tokens, down],
        (jax.ShapeDtypeStruct((rows // planes, width), jnp.float32),) * planes,
        [pltpu.VMEM((rows, width), jnp.float32)],
    )


def output_kernel(begun, last, lines, ids_ref, attended_ref, w_ref, down_ref, *refs):
    begun_refs, rest = refs[:begun], refs[begun:]
    if last:
        table_ref, up_ref, out_ref = rest
    else:
        acc_ref, low_ref = rest
    count = ids_ref.shape[0] - 1
    attended = attended_ref[...]
    features = attended.shape[1]
    if lines:
        weight = jnp.concatenate([w_ref[i, 0, lines:] for i in range(w_ref.shape[0])], axis=0)
    else:
        weight = w_ref[...]
    downs = []
    for j in range(count):
        down = down_ref[ids_ref[1 + j], 0] if lines else down_ref[ids_ref[1 + j]]
        downs += [down[:, at : at + features] for at in range(0, down.shape[1], features)]
    down = jnp.concatenate(downs, axis=0)
    rank = down.shape[0] // count
    total = jnp.dot(attended, weight, preferred_element_type=jnp.float32)
    low = lax.dot_general(
        attended, down, (((1,), (1,)), ((), ())), preferred_element_type=jnp.float32
    )
    if begun:
        total, low = begun_refs[0][...] + total, begun_refs[1][...] + low
    if last:
        low = low.astype(jnp.bfloat16).astype(jnp.float32)
        lane = lax.broadcasted_iota(jnp.int32, low.shape, 1)
        kept = (lane >= table_ref[:, 1:2]) & (lane < table_ref[:, 1:2] + rank)
        low = jnp.where(kept, low, 0.0).astype(jnp.bfloat16)
        up = jnp.concatenate([up_ref[ids_ref[1 + j]] for j in range(count)], axis=0)
        extra = jnp.dot(low, up, preferred_element_type=jnp.float32)
        out_ref[...] = (total + extra).astype(jnp.bfloat16)
    else:
        acc_ref[...] = total
        low_ref[...] = low


def project_out(ids, rank, attended, weight, down, begun, final, turn=None):
    rows, features = attended.shape
    columns = weight.shape[-1]
    if turn is None:
        specs, down_rows = [None, None, None], 0
    else:
        down_rows = rank * features // columns
        specs = [
            None,
            pl.BlockSpec(
                (weight.shape[0], 1) + weight.shape[2:], lambda step, ids: (0, turn - 1, 0, 0)
            ),
            pl.BlockSpec(
                (down, 1, down_rows, columns),
                lambda step, ids: (ids[0], turn - 1, 0, 0),
            ),
        ]
        down = weight
    sums = (
        jax.ShapeDtypeStruct((rows, columns), jnp.float32),
        jax.ShapeDtypeStruct((rows, (ids.shape[0] - 1) * rank), jnp.float32),
    )
    return call(
        functools.partial(output_kernel, len(begun), bool(final), down_rows),
        "project_out",
        ids,
        1,
        specs + [None] * (len(begun) + len(final)),
        [attended, weight, down, *begun, *final],
        jax.ShapeDtypeStruct((rows, columns), jnp.bfloat16) if final else sums,
    )


def local(
    plane_size,
    planes,
    tokens,
    query_key_value_weight,
    output_weight,
    adapter_down_maps,
    adapter_up_maps,
    output_down_maps,
    output_up_maps,
    request_adapter,
    lengths,
):
    token_rows, depth = tokens.shape
    _, slots, head_size = query_key_value_weight.shape
    queries = slots - 2
    pool, rank = plane_size // lax.axis_size("groups"), adapter_up_maps.shape[1]
    features = queries * head_size
    columns = output_weight.shape[2] // planes
    here = lax.axis_index("tensor")
    place = lax.axis_index(PLANE)
    planes_of = (here - jnp.arange(planes) + planes) % planes

    def turned(value, turn=1):
        return lax.ppermute(value, "tensor", [(i, (i + turn) % planes) for i in range(planes)])

    held = [tokens, turned(tokens)]
    weight = jnp.transpose(query_key_value_weight, (1, 0, 2))
    down_all = lax.all_gather(adapter_down_maps, "dp", axis=0, tiled=True)
    up_all = lax.all_gather(jnp.transpose(adapter_up_maps[0], (1, 0, 2)), "dp", axis=0)

    requests = request_adapter.shape[1]
    request_ends = jnp.cumsum(lengths[0])
    request_starts = request_ends - lengths[0]
    at = jnp.arange(token_rows, dtype=jnp.int32)
    member = (at[:, None] >= request_starts[None, :]) & (at[:, None] < request_ends[None, :])
    if pool <= requests:
        adapters, label = jnp.arange(pool), request_adapter[0]
    else:
        adapters, label = request_adapter[0], jnp.arange(requests)
    wanted = jnp.stack([request_starts, label * rank], axis=0)
    table = jnp.sum(jnp.where(member[:, None, :], wanted[None], 0), axis=2).astype(jnp.int32)
    position = at - table[:, 0]
    half = head_size // 2
    inv_freq = 10000.0 ** (-2.0 * jnp.arange(half, dtype=jnp.float32) / head_size)
    angles = position.astype(jnp.float32)[:, None] * inv_freq[None, :]
    cosine, sine = jnp.cos(angles), jnp.sin(angles)
    turn = jnp.concatenate([cosine, cosine, -sine, sine], axis=1)

    own_rows = jnp.transpose(
        lax.dynamic_slice_in_dim(output_weight, here * columns, columns, axis=2), (1, 0, 2)
    ).reshape(features, columns)
    share = features // plane_size
    line = place * share
    piece = lax.dynamic_slice(
        output_weight, (line % head_size, line // head_size, 0),
        (share, 1, output_weight.shape[2]),
    )[:, 0]
    out_down = output_down_maps[0].reshape(rank, features)
    out_down = jnp.concatenate(jnp.split(out_down, columns // features, axis=0), axis=1)
    sends = [
        jnp.concatenate(
            [
                out_down,
                lax.dynamic_slice_in_dim(piece, (here + k) % planes * columns, columns, axis=1),
            ],
            axis=0,
        )
        for k in range(1, planes)
    ]

    begun = project(planes_of[:1], held[:1], weight)
    lines = [turned(send, k) for k, send in enumerate(sends, 1)]
    held[1] = after(held[1], begun, up_all, table, turn, own_rows, *lines)
    lines = lax.all_gather(jnp.stack(lines), PLANE, axis=0)
    sums = shrink_partial(adapters, here, planes, table, after(tokens, held[1]), down_all)
    sums = [sums[0]] + [turned(sums[k], k) for k in range(1, planes)]
    shrink = sum(sums[1:], sums[0]).astype(jnp.bfloat16)
    for step in range(2, planes):
        arrived = held[-1]
        held.append(turned(arrived))
        begun = project(planes_of[step - 1 : step], [arrived], weight, [begun])
        held[-1] = after(held[-1], begun, *([shrink] if step == 2 else []))
    shrink = after(shrink, held[2])
    shrink = [shrink] + [turned(shrink, k) for k in range(1, planes)]
    out_up_all = lax.all_gather(after(output_up_maps, held[2]), "dp", axis=0, tiled=True)
    own_down = lax.all_gather(after(out_down, held[2]), "dp", axis=0)
    held[-1] = after(held[-1], out_up_all, own_down)
    attended = [
        attend(planes_of, adapters, table, turn, up_all, shrink, held[-1], weight, begun)
    ]

    ids = jnp.concatenate([lax.axis_index("groups")[None], adapters])
    attended.append(turned(attended[0]))
    sums = project_out(ids, rank, attended[0], own_rows, own_down, [], [])
    for step in range(2, planes + 1):
        arrived = after(attended[-1], *sums)
        if step < planes:
            attended.append(turned(arrived))
        sums = project_out(
            ids, rank, arrived, lines, pool, list(sums),
            [] if step < planes else [table, out_up_all], step - 1,
        )
    return sums


def solution(mesh):
    in_specs = (
        P(PLANE, "tensor"),
        P(None, None, "tensor"),
        P("tensor", None, None),
        P(PLANE, None, "tensor"),
        P(PLANE, None, None, "tensor"),
        P(PLANE, None, None, "tensor"),
        P(PLANE, None, "tensor"),
        P(PLANE, None),
        P(PLANE, None),
    )
    function = functools.partial(
        local, mesh.shape["groups"] * mesh.shape["dp"], mesh.shape["tensor"]
    )
    return jax.shard_map(
        function, mesh=mesh, in_specs=in_specs, out_specs=P(PLANE, "tensor"), check_vma=False
    )
```

```python
import functools
import math

import jax
import jax.numpy as jnp
from jax import lax
from jax.experimental import pallas as pl
from jax.experimental.pallas import tpu as pltpu
from jax.sharding import PartitionSpec as P

VMEM_BYTES = 40 * 1024 * 1024
PLANE = ("groups", "dp")


def after(value, *earlier):
    return lax.optimization_barrier((value,) + earlier)[0]


def fixed(array):
    shape = array.shape
    return pl.BlockSpec(shape, lambda step, ids: (0,) * len(shape))


def call(kernel, name, ids, grid, specs, arrays, out, scratch=()):
    total = sum(array.size * array.dtype.itemsize for array in arrays)
    return pl.pallas_call(
        kernel,
        out_shape=out,
        grid_spec=pltpu.PrefetchScalarGridSpec(
            num_scalar_prefetch=1,
            grid=(grid,),
            in_specs=[fixed(array) if spec is None else spec for spec, array in zip(specs, arrays)],
            out_specs=[fixed(item) for item in out] if isinstance(out, tuple) else fixed(out),
            scratch_shapes=list(scratch),
        ),
        compiler_params=pltpu.CompilerParams(vmem_limit_bytes=VMEM_BYTES),
        cost_estimate=pl.CostEstimate(flops=0, bytes_accessed=3 * total, transcendentals=0),
        name=name,
    )(ids.astype(jnp.int32), *arrays)


def accumulate(acc_ref, token_ref, w_ref, first):
    slots, _, head_size = w_ref.shape
    for pair in range(slots // 2):
        columns = slice(2 * pair * head_size, (2 * pair + 2) * head_size)
        weight = jnp.concatenate([w_ref[2 * pair], w_ref[2 * pair + 1]], axis=1)
        total = jnp.dot(token_ref[...], weight, preferred_element_type=jnp.float32)
        acc_ref[:, columns] = total if first is None else first[:, columns] + total


def project_kernel(shards, begun, ids_ref, *refs):
    token_refs, w_ref, rest = refs[:shards], refs[shards], refs[shards + 1 :]
    acc_ref = rest[-1]
    step = pl.program_id(0)
    for number, token_ref in enumerate(token_refs):
        first = acc_ref if number else (rest[0] if begun else None)
        pl.when(step == number)(
            functools.partial(accumulate, acc_ref, token_ref, w_ref, first)
        )


def shard_spec(weight, depth):
    slots, _, head_size = weight.shape
    return pl.BlockSpec((slots, depth, head_size), lambda step, ids: (0, ids[step], 0))


def project(ids, tokens, weight, begun=()):
    rows, depth = tokens[0].shape
    slots, _, head_size = weight.shape
    return call(
        functools.partial(project_kernel, len(tokens), len(begun)),
        "project",
        ids,
        len(tokens),
        [None] * len(tokens) + [shard_spec(weight, depth)] + [None] * len(begun),
        [*tokens, weight, *begun],
        jax.ShapeDtypeStruct((rows, slots * head_size), jnp.float32),
    )


def attend_kernel(planes, ids_ref, table_ref, turn_ref, up_ref, *refs):
    piece_refs, refs = refs[:planes], refs[planes:]
    token_ref, w_ref, begun_ref, out_ref, acc_ref, keys_ref, values_ref, shrink_ref = refs
    for number, piece_ref in enumerate(piece_refs):
        size = piece_ref.shape[0]
        shrink_ref[pl.ds(pl.multiple_of(ids_ref[number] * size, size), size), :] = piece_ref[...]
    accumulate(acc_ref, token_ref, w_ref, begun_ref)
    slots, _, head_size = w_ref.shape
    rank = up_ref.shape[2]
    count = ids_ref.shape[0] - planes
    rows = acc_ref.shape[0]
    block = min(rows, 256)
    queries = slots - 2
    ups = [
        jnp.concatenate([up_ref[ids_ref[planes + j], index] for j in range(count)], axis=0)
        for index in range(slots)
    ]
    for row in range(0, rows, block):
        at = slice(row, row + block)
        lane = lax.broadcasted_iota(jnp.int32, (block, count * rank), 1)
        kept = (lane >= table_ref[at, 1:2]) & (lane < table_ref[at, 1:2] + rank)
        lows = []
        for part in range(3):
            piece = shrink_ref[at, part * rank : (part + 1) * rank].astype(jnp.float32)
            piece = jnp.concatenate([piece] * count, axis=1)
            lows.append(jnp.where(kept, piece, 0.0).astype(jnp.bfloat16))

        def slot(index):
            low = lows[0 if index < queries else index - queries + 1]
            extra = jnp.dot(low, ups[index], preferred_element_type=jnp.float32)
            return acc_ref[at, index * head_size : (index + 1) * head_size] + extra

        def rotated(index):
            value = slot(index)
            turned = pltpu.roll(value, head_size // 2, 1)
            cos, sin = turn_ref[at, :head_size], turn_ref[at, head_size:]
            return (value * cos + turned * sin).astype(jnp.bfloat16)

        keys_ref[at, :] = rotated(queries)
        values_ref[at, :] = slot(queries + 1).astype(jnp.bfloat16)
        key_rows = row + block
        keys, values = keys_ref[:key_rows], values_ref[:key_rows]
        key_at = lax.broadcasted_iota(jnp.int32, (block, key_rows), 1)
        row_at = lax.broadcasted_iota(jnp.int32, (block, key_rows), 0) + row
        allowed = (key_at >= table_ref[at, 0:1]) & (key_at <= row_at)
        for index in range(queries):
            scores = lax.dot_general(
                rotated(index), keys, (((1,), (1,)), ((), ())),
                preferred_element_type=jnp.float32,
            )
            scores = jnp.where(allowed, scores * (1.0 / math.sqrt(head_size)), -1e30)
            weights = jnp.exp(scores - jnp.max(scores, axis=1, keepdims=True))
            scale = 1.0 / jnp.sum(weights, axis=1, keepdims=True)
            attended = jnp.dot(
                (weights * scale).astype(jnp.bfloat16), values, preferred_element_type=jnp.float32
            )
            out_ref[at, index * head_size : (index + 1) * head_size] = attended.astype(
                jnp.bfloat16
            )


def attend(planes_of, adapters, table, turn, up, shrink, tokens, weight, begun):
    rows, depth = tokens.shape
    slots, _, head_size = weight.shape
    planes = len(shrink)
    return call(
        functools.partial(attend_kernel, planes),
        "attend",
        jnp.concatenate([planes_of, adapters]),
        1,
        [None] * (4 + planes)
        + [
            pl.BlockSpec((slots, depth, head_size), lambda step, ids: (0, ids[planes - 1], 0)),
            None,
        ],
        [table, turn, up, *shrink, tokens, weight, begun],
        jax.ShapeDtypeStruct((rows, (slots - 2) * head_size), jnp.bfloat16),
        [
            pltpu.VMEM((rows, slots * head_size), jnp.float32),
            pltpu.VMEM((rows, head_size), jnp.bfloat16),
            pltpu.VMEM((rows, head_size), jnp.bfloat16),
            pltpu.VMEM((rows, shrink[0].shape[1]), jnp.bfloat16),
        ],
    )


def shrink_kernel(planes, ids_ref, table_ref, token_ref, down_ref, *refs):
    out_refs, acc_ref = refs[:planes], refs[planes]
    step = pl.program_id(0)
    count = ids_ref.shape[0] - 1
    part = lax.dot_general(
        token_ref[...], down_ref[0], (((1,), (1,)), ((), ())), preferred_element_type=jnp.float32
    )
    rank = part.shape[1] // 3
    part = jnp.where(table_ref[:, 1:2] == step * rank, part, 0.0)

    @pl.when(step == 0)
    def _():
        acc_ref[...] = part

    @pl.when(step > 0)
    def _():
        acc_ref[...] += part

    @pl.when(step == count - 1)
    def _():
        for turn, out_ref in enumerate(out_refs):
            rows = out_ref.shape[0]
            plane = lax.rem(ids_ref[count] + turn, planes)
            out_ref[...] = acc_ref[pl.ds(pl.multiple_of(plane * rows, rows), rows), :]


def shrink_partial(adapters, here, planes, table, tokens, down):
    _, width, depth = down.shape
    rows = tokens.shape[0]
    return call(
        functools.partial(shrink_kernel, planes),
        "shrink",
        jnp.concatenate([adapters, here[None]]),
        adapters.shape[0],
        [None, None, pl.BlockSpec((1, width, depth), lambda step, ids: (ids[step], 0, 0))],
        [table, tokens, down],
        (jax.ShapeDtypeStruct((rows // planes, width), jnp.float32),) * planes,
        [pltpu.VMEM((rows, width), jnp.float32)],
    )


def output_kernel(begun, last, lines, ids_ref, attended_ref, w_ref, down_ref, *refs):
    begun_refs, rest = refs[:begun], refs[begun:]
    if last:
        table_ref, up_ref, out_ref = rest
    else:
        acc_ref, low_ref = rest
    count = ids_ref.shape[0] - 1
    attended = attended_ref[...]
    features = attended.shape[1]
    if lines:
        weight = jnp.concatenate([w_ref[i, 0, lines:] for i in range(w_ref.shape[0])], axis=0)
    else:
        weight = w_ref[...]
    downs = []
    for j in range(count):
        down = down_ref[ids_ref[1 + j], 0] if lines else down_ref[ids_ref[1 + j]]
        downs += [down[:, at : at + features] for at in range(0, down.shape[1], features)]
    down = jnp.concatenate(downs, axis=0)
    rank = down.shape[0] // count
    total = jnp.dot(attended, weight, preferred_element_type=jnp.float32)
    low = lax.dot_general(
        attended, down, (((1,), (1,)), ((), ())), preferred_element_type=jnp.float32
    )
    if begun:
        total, low = begun_refs[0][...] + total, begun_refs[1][...] + low
    if last:
        low = low.astype(jnp.bfloat16).astype(jnp.float32)
        lane = lax.broadcasted_iota(jnp.int32, low.shape, 1)
        kept = (lane >= table_ref[:, 1:2]) & (lane < table_ref[:, 1:2] + rank)
        low = jnp.where(kept, low, 0.0).astype(jnp.bfloat16)
        up = jnp.concatenate([up_ref[ids_ref[1 + j]] for j in range(count)], axis=0)
        extra = jnp.dot(low, up, preferred_element_type=jnp.float32)
        out_ref[...] = (total + extra).astype(jnp.bfloat16)
    else:
        acc_ref[...] = total
        low_ref[...] = low


def project_out(ids, rank, attended, weight, down, begun, final, turn=None):
    rows, features = attended.shape
    columns = weight.shape[-1]
    if turn is None:
        specs, down_rows = [None, None, None], 0
    else:
        down_rows = rank * features // columns
        specs = [
            None,
            pl.BlockSpec(
                (weight.shape[0], 1) + weight.shape[2:], lambda step, ids: (0, turn - 1, 0, 0)
            ),
            pl.BlockSpec(
                (down, 1, down_rows, columns),
                lambda step, ids: (ids[0], turn - 1, 0, 0),
            ),
        ]
        down = weight
    sums = (
        jax.ShapeDtypeStruct((rows, columns), jnp.float32),
        jax.ShapeDtypeStruct((rows, (ids.shape[0] - 1) * rank), jnp.float32),
    )
    return call(
        functools.partial(output_kernel, len(begun), bool(final), down_rows),
        "project_out",
        ids,
        1,
        specs + [None] * (len(begun) + len(final)),
        [attended, weight, down, *begun, *final],
        jax.ShapeDtypeStruct((rows, columns), jnp.bfloat16) if final else sums,
    )


def local(
    plane_size,
    planes,
    tokens,
    query_key_value_weight,
    output_weight,
    adapter_down_maps,
    adapter_up_maps,
    output_down_maps,
    output_up_maps,
    request_adapter,
    lengths,
):
    token_rows, depth = tokens.shape
    _, slots, head_size = query_key_value_weight.shape
    queries = slots - 2
    pool, rank = plane_size // lax.axis_size("groups"), adapter_up_maps.shape[1]
    features = queries * head_size
    columns = output_weight.shape[2] // planes
    here = lax.axis_index("tensor")
    place = lax.axis_index(PLANE)
    planes_of = (here - jnp.arange(planes) + planes) % planes

    def turned(value, turn=1):
        return lax.ppermute(value, "tensor", [(i, (i + turn) % planes) for i in range(planes)])

    held = [tokens, turned(tokens)]
    weight = jnp.transpose(query_key_value_weight, (1, 0, 2))
    down_all = lax.all_gather(adapter_down_maps, "dp", axis=0, tiled=True)
    up_all = lax.all_gather(jnp.transpose(adapter_up_maps[0], (1, 0, 2)), "dp", axis=0)

    requests = request_adapter.shape[1]
    request_ends = jnp.cumsum(lengths[0])
    request_starts = request_ends - lengths[0]
    at = jnp.arange(token_rows, dtype=jnp.int32)
    member = (at[:, None] >= request_starts[None, :]) & (at[:, None] < request_ends[None, :])
    if pool <= requests:
        adapters, label = jnp.arange(pool), request_adapter[0]
    else:
        adapters, label = request_adapter[0], jnp.arange(requests)
    wanted = jnp.stack([request_starts, label * rank], axis=0)
    table = jnp.sum(jnp.where(member[:, None, :], wanted[None], 0), axis=2).astype(jnp.int32)
    position = at - table[:, 0]
    half = head_size // 2
    inv_freq = 10000.0 ** (-2.0 * jnp.arange(half, dtype=jnp.float32) / head_size)
    angles = position.astype(jnp.float32)[:, None] * inv_freq[None, :]
    cosine, sine = jnp.cos(angles), jnp.sin(angles)
    turn = jnp.concatenate([cosine, cosine, -sine, sine], axis=1)

    own_rows = jnp.transpose(
        lax.dynamic_slice_in_dim(output_weight, here * columns, columns, axis=2), (1, 0, 2)
    ).reshape(features, columns)
    share = features // plane_size
    line = place * share
    piece = lax.dynamic_slice(
        output_weight, (line % head_size, line // head_size, 0),
        (share, 1, output_weight.shape[2]),
    )[:, 0]
    out_down = output_down_maps[0].reshape(rank, features)
    out_down = jnp.concatenate(jnp.split(out_down, columns // features, axis=0), axis=1)
    sends = [
        jnp.concatenate(
            [
                out_down,
                lax.dynamic_slice_in_dim(piece, (here + k) % planes * columns, columns, axis=1),
            ],
            axis=0,
        )
        for k in range(1, planes)
    ]

    begun = project(planes_of[:1], held[:1], weight)
    lines = [turned(send, k) for k, send in enumerate(sends, 1)]
    lines = [after(line, held[1]) for line in lines]
    held[1] = after(held[1], begun, up_all, table, turn, own_rows, *lines)
    lines = lax.all_gather(jnp.stack(lines), PLANE, axis=0)
    sums = shrink_partial(adapters, here, planes, table, after(tokens, held[1]), down_all)
    sums = [sums[0]] + [turned(sums[k], k) for k in range(1, planes)]
    shrink = sum(sums[1:], sums[0]).astype(jnp.bfloat16)
    for step in range(2, planes):
        arrived = held[-1]
        held.append(turned(arrived))
        begun = project(planes_of[step - 1 : step], [arrived], weight, [begun])
        held[-1] = after(held[-1], begun, *([shrink] if step == 2 else []))
    shrink = after(shrink, held[2])
    shrink = [shrink] + [turned(shrink, k) for k in range(1, planes)]
    out_up_all = lax.all_gather(after(output_up_maps, held[2]), "dp", axis=0, tiled=True)
    own_down = lax.all_gather(after(out_down, held[2]), "dp", axis=0)
    held[-1] = after(held[-1], out_up_all, own_down)
    attended = [
        attend(planes_of, adapters, table, turn, up_all, shrink, held[-1], weight, begun)
    ]

    ids = jnp.concatenate([lax.axis_index("groups")[None], adapters])
    attended.append(turned(attended[0]))
    sums = project_out(ids, rank, attended[0], own_rows, own_down, [], [])
    for step in range(2, planes + 1):
        arrived = after(attended[-1], *sums)
        if step < planes:
            attended.append(turned(arrived))
        sums = project_out(
            ids, rank, arrived, lines, pool, list(sums),
            [] if step < planes else [table, out_up_all], step - 1,
        )
    return sums


def solution(mesh):
    in_specs = (
        P(PLANE, "tensor"),
        P(None, None, "tensor"),
        P("tensor", None, None),
        P(PLANE, None, "tensor"),
        P(PLANE, None, None, "tensor"),
        P(PLANE, None, None, "tensor"),
        P(PLANE, None, "tensor"),
        P(PLANE, None),
        P(PLANE, None),
    )
    function = functools.partial(
        local, mesh.shape["groups"] * mesh.shape["dp"], mesh.shape["tensor"]
    )
    return jax.shard_map(
        function, mesh=mesh, in_specs=in_specs, out_specs=P(PLANE, "tensor"), check_vma=False
    )
```

```python
import functools
import math

import jax
import jax.numpy as jnp
from jax import lax
from jax.experimental import pallas as pl
from jax.experimental.pallas import tpu as pltpu
from jax.sharding import PartitionSpec as P

VMEM_BYTES = 40 * 1024 * 1024
PLANE = ("groups", "dp")


def after(value, *earlier):
    return lax.optimization_barrier((value,) + earlier)[0]


def fixed(array):
    shape = array.shape
    return pl.BlockSpec(shape, lambda step, ids: (0,) * len(shape))


def call(kernel, name, ids, grid, specs, arrays, out, scratch=()):
    total = sum(array.size * array.dtype.itemsize for array in arrays)
    return pl.pallas_call(
        kernel,
        out_shape=out,
        grid_spec=pltpu.PrefetchScalarGridSpec(
            num_scalar_prefetch=1,
            grid=(grid,),
            in_specs=[fixed(array) if spec is None else spec for spec, array in zip(specs, arrays)],
            out_specs=[fixed(item) for item in out] if isinstance(out, tuple) else fixed(out),
            scratch_shapes=list(scratch),
        ),
        compiler_params=pltpu.CompilerParams(vmem_limit_bytes=VMEM_BYTES),
        cost_estimate=pl.CostEstimate(flops=0, bytes_accessed=3 * total, transcendentals=0),
        name=name,
    )(ids.astype(jnp.int32), *arrays)


def accumulate(acc_ref, token_ref, w_ref, first):
    slots, _, head_size = w_ref.shape
    for pair in range(slots // 2):
        columns = slice(2 * pair * head_size, (2 * pair + 2) * head_size)
        weight = jnp.concatenate([w_ref[2 * pair], w_ref[2 * pair + 1]], axis=1)
        total = jnp.dot(token_ref[...], weight, preferred_element_type=jnp.float32)
        acc_ref[:, columns] = total if first is None else first[:, columns] + total


def project_kernel(shards, begun, ids_ref, *refs):
    token_refs, w_ref, rest = refs[:shards], refs[shards], refs[shards + 1 :]
    acc_ref = rest[-1]
    step = pl.program_id(0)
    for number, token_ref in enumerate(token_refs):
        first = acc_ref if number else (rest[0] if begun else None)
        pl.when(step == number)(
            functools.partial(accumulate, acc_ref, token_ref, w_ref, first)
        )


def shard_spec(weight, depth, number=0):
    slots, _, head_size = weight.shape
    return pl.BlockSpec((slots, depth, head_size), lambda step, ids: (0, ids[number], 0))


def rows_spec(array, rows, part):
    if array.shape[0] == rows:
        return None
    return pl.BlockSpec((rows, array.shape[1]), lambda step, ids: (part, 0))


def project(ids, tokens, weight, begun=(), part=0):
    rows, depth = tokens.shape
    slots, _, head_size = weight.shape
    return call(
        functools.partial(project_kernel, 1, len(begun)),
        "project",
        ids,
        1,
        [None, shard_spec(weight, depth)] + [rows_spec(array, rows, part) for array in begun],
        [tokens, weight, *begun],
        jax.ShapeDtypeStruct((rows, slots * head_size), jnp.float32),
    )


def attend_kernel(planes, earlier, ids_ref, table_ref, turn_ref, up_ref, *refs):
    piece_refs, refs = refs[:planes], refs[planes:]
    token_ref, w_ref, begun_ref, refs = refs[0], refs[1], refs[2], refs[3:]
    earlier_refs, refs = refs[: 2 * earlier], refs[2 * earlier :]
    out_ref, keys_ref, values_ref, acc_ref, shrink_ref = refs
    for number, piece_ref in enumerate(piece_refs):
        size = piece_ref.shape[0]
        shrink_ref[pl.ds(pl.multiple_of(ids_ref[number] * size, size), size), :] = piece_ref[...]
    accumulate(acc_ref, token_ref, w_ref, begun_ref)
    slots, _, head_size = w_ref.shape
    rank = up_ref.shape[2]
    count = ids_ref.shape[0] - planes
    rows = acc_ref.shape[0]
    first_row = earlier_refs[0].shape[0] if earlier else 0
    queries = slots - 2
    lane = lax.broadcasted_iota(jnp.int32, (rows, count * rank), 1)
    kept = (lane >= table_ref[:, 1:2]) & (lane < table_ref[:, 1:2] + rank)
    lows = []
    for part in range(3):
        piece = shrink_ref[first_row : first_row + rows, part * rank : (part + 1) * rank]
        piece = jnp.concatenate([piece.astype(jnp.float32)] * count, axis=1)
        lows.append(jnp.where(kept, piece, 0.0).astype(jnp.bfloat16))

    def slot(index):
        low = lows[0 if index < queries else index - queries + 1]
        up = jnp.concatenate([up_ref[ids_ref[planes + j], index] for j in range(count)], axis=0)
        extra = jnp.dot(low, up, preferred_element_type=jnp.float32)
        return acc_ref[:, index * head_size : (index + 1) * head_size] + extra

    def rotated(index):
        value = slot(index)
        turned = pltpu.roll(value, head_size // 2, 1)
        return (value * turn_ref[:, :head_size] + turned * turn_ref[:, head_size:]).astype(
            jnp.bfloat16
        )

    keys = rotated(queries)
    values = slot(queries + 1).astype(jnp.bfloat16)
    keys_ref[...] = keys
    values_ref[...] = values
    if earlier:
        keys = jnp.concatenate([earlier_refs[0][...], keys], axis=0)
        values = jnp.concatenate([earlier_refs[1][...], values], axis=0)
    shape = (rows, keys.shape[0])
    key_at = lax.broadcasted_iota(jnp.int32, shape, 1)
    row_at = lax.broadcasted_iota(jnp.int32, shape, 0) + first_row
    allowed = (key_at >= table_ref[:, 0:1]) & (key_at <= row_at)
    for index in range(queries):
        scores = lax.dot_general(
            rotated(index), keys, (((1,), (1,)), ((), ())), preferred_element_type=jnp.float32
        )
        scores = jnp.where(allowed, scores * (1.0 / math.sqrt(head_size)), -1e30)
        weights = jnp.exp(scores - jnp.max(scores, axis=1, keepdims=True))
        scale = 1.0 / jnp.sum(weights, axis=1, keepdims=True)
        attended = jnp.dot(
            (weights * scale).astype(jnp.bfloat16), values, preferred_element_type=jnp.float32
        )
        out_ref[:, index * head_size : (index + 1) * head_size] = attended.astype(jnp.bfloat16)


def attend(planes_of, adapters, part, table, turn, up, shrink, tokens, weight, begun, earlier):
    rows, depth = tokens.shape
    slots, _, head_size = weight.shape
    planes = len(shrink)
    arrays = [table, turn, up, *shrink, tokens, weight, begun, *earlier]
    specs = [None] * len(arrays)
    for index in (0, 1):
        specs[index] = rows_spec(arrays[index], rows, part)
    specs[4 + planes] = shard_spec(weight, depth, planes - 1)
    return call(
        functools.partial(attend_kernel, planes, len(earlier) // 2),
        "attend",
        jnp.concatenate([planes_of, adapters]),
        1,
        specs,
        arrays,
        (
            jax.ShapeDtypeStruct((rows, (slots - 2) * head_size), jnp.bfloat16),
            jax.ShapeDtypeStruct((rows, head_size), jnp.bfloat16),
            jax.ShapeDtypeStruct((rows, head_size), jnp.bfloat16),
        ),
        [
            pltpu.VMEM((rows, slots * head_size), jnp.float32),
            pltpu.VMEM((planes * shrink[0].shape[0], shrink[0].shape[1]), jnp.bfloat16),
        ],
    )


def shrink_kernel(planes, ids_ref, table_ref, token_ref, down_ref, *refs):
    out_refs, acc_ref = refs[:planes], refs[planes]
    step = pl.program_id(0)
    count = ids_ref.shape[0] - 1
    part = lax.dot_general(
        token_ref[...], down_ref[0], (((1,), (1,)), ((), ())), preferred_element_type=jnp.float32
    )
    rank = part.shape[1] // 3
    part = jnp.where(table_ref[:, 1:2] == step * rank, part, 0.0)

    @pl.when(step == 0)
    def _():
        acc_ref[...] = part

    @pl.when(step > 0)
    def _():
        acc_ref[...] += part

    @pl.when(step == count - 1)
    def _():
        for turn, out_ref in enumerate(out_refs):
            rows = out_ref.shape[0]
            plane = lax.rem(ids_ref[count] + turn, planes)
            out_ref[...] = acc_ref[pl.ds(pl.multiple_of(plane * rows, rows), rows), :]


def shrink_partial(adapters, here, planes, table, tokens, down):
    _, width, depth = down.shape
    rows = tokens.shape[0]
    return call(
        functools.partial(shrink_kernel, planes),
        "shrink",
        jnp.concatenate([adapters, here[None]]),
        adapters.shape[0],
        [None, None, pl.BlockSpec((1, width, depth), lambda step, ids: (ids[step], 0, 0))],
        [table, tokens, down],
        (jax.ShapeDtypeStruct((rows // planes, width), jnp.float32),) * planes,
        [pltpu.VMEM((rows, width), jnp.float32)],
    )


def output_kernel(begun, last, lines, ids_ref, attended_ref, w_ref, down_ref, *refs):
    begun_refs, rest = refs[:begun], refs[begun:]
    if last:
        table_ref, up_ref, before_refs, out_ref = rest[0], rest[1], rest[2:-1], rest[-1]
    else:
        acc_ref, low_ref = rest
    count = ids_ref.shape[0] - 1
    attended = attended_ref[...]
    features = attended.shape[1]
    if lines:
        weight = jnp.concatenate([w_ref[i, 0, lines:] for i in range(w_ref.shape[0])], axis=0)
    else:
        weight = w_ref[...]
    downs = []
    for j in range(count):
        down = down_ref[ids_ref[1 + j], 0] if lines else down_ref[ids_ref[1 + j]]
        downs += [down[:, at : at + features] for at in range(0, down.shape[1], features)]
    down = jnp.concatenate(downs, axis=0)
    rank = down.shape[0] // count
    total = jnp.dot(attended, weight, preferred_element_type=jnp.float32)
    low = lax.dot_general(
        attended, down, (((1,), (1,)), ((), ())), preferred_element_type=jnp.float32
    )
    if begun:
        total, low = begun_refs[0][...] + total, begun_refs[1][...] + low
    if last:
        low = low.astype(jnp.bfloat16).astype(jnp.float32)
        lane = lax.broadcasted_iota(jnp.int32, low.shape, 1)
        kept = (lane >= table_ref[:, 1:2]) & (lane < table_ref[:, 1:2] + rank)
        low = jnp.where(kept, low, 0.0).astype(jnp.bfloat16)
        up = jnp.concatenate([up_ref[ids_ref[1 + j]] for j in range(count)], axis=0)
        extra = jnp.dot(low, up, preferred_element_type=jnp.float32)
        first_row = out_ref.shape[0] - total.shape[0]
        for before_ref in before_refs:
            out_ref[:first_row, :] = before_ref[...]
        out_ref[first_row:, :] = (total + extra).astype(jnp.bfloat16)
    else:
        acc_ref[...] = total
        low_ref[...] = low


def project_out(ids, rank, attended, weight, down, begun, final, turn=None, part=0):
    rows, features = attended.shape
    columns = weight.shape[-1]
    if turn is None:
        specs, down_rows = [None, None, None], 0
    else:
        down_rows = rank * features // columns
        specs = [
            None,
            pl.BlockSpec(
                (weight.shape[0], 1) + weight.shape[2:], lambda step, ids: (0, turn - 1, 0, 0)
            ),
            pl.BlockSpec(
                (down, 1, down_rows, columns),
                lambda step, ids: (ids[0], turn - 1, 0, 0),
            ),
        ]
        down = weight
    sums = (
        jax.ShapeDtypeStruct((rows, columns), jnp.float32),
        jax.ShapeDtypeStruct((rows, (ids.shape[0] - 1) * rank), jnp.float32),
    )
    return call(
        functools.partial(output_kernel, len(begun), bool(final), down_rows),
        "project_out",
        ids,
        1,
        specs + [None] * len(begun) + [rows_spec(table, rows, part) for table in final[:1]]
        + [None] * len(final[1:]),
        [attended, weight, down, *begun, *final],
        jax.ShapeDtypeStruct((rows + sum(item.shape[0] for item in final[2:]), columns), jnp.bfloat16)
        if final else sums,
    )


def local(
    plane_size,
    planes,
    tokens,
    query_key_value_weight,
    output_weight,
    adapter_down_maps,
    adapter_up_maps,
    output_down_maps,
    output_up_maps,
    request_adapter,
    lengths,
):
    token_rows, depth = tokens.shape
    _, slots, head_size = query_key_value_weight.shape
    queries = slots - 2
    pool, rank = plane_size // lax.axis_size("groups"), adapter_up_maps.shape[1]
    features = queries * head_size
    columns = output_weight.shape[2] // planes
    here = lax.axis_index("tensor")
    place = lax.axis_index(PLANE)
    planes_of = (here - jnp.arange(planes) + planes) % planes

    def turned(value, turn=1):
        return lax.ppermute(value, "tensor", [(i, (i + turn) % planes) for i in range(planes)])

    half_rows = token_rows // 2
    held = [[tokens[:half_rows]], [tokens[half_rows:]]]
    held[0].append(turned(held[0][0]))
    weight = jnp.transpose(query_key_value_weight, (1, 0, 2))
    down_all = lax.all_gather(adapter_down_maps, "dp", axis=0, tiled=True)
    up_all = lax.all_gather(jnp.transpose(adapter_up_maps[0], (1, 0, 2)), "dp", axis=0)

    requests = request_adapter.shape[1]
    request_ends = jnp.cumsum(lengths[0])
    request_starts = request_ends - lengths[0]
    at = jnp.arange(token_rows, dtype=jnp.int32)
    member = (at[:, None] >= request_starts[None, :]) & (at[:, None] < request_ends[None, :])
    if pool <= requests:
        adapters, label = jnp.arange(pool), request_adapter[0]
    else:
        adapters, label = request_adapter[0], jnp.arange(requests)
    wanted = jnp.stack([request_starts, label * rank], axis=0)
    table = jnp.sum(jnp.where(member[:, None, :], wanted[None], 0), axis=2).astype(jnp.int32)
    position = at - table[:, 0]
    half = head_size // 2
    inv_freq = 10000.0 ** (-2.0 * jnp.arange(half, dtype=jnp.float32) / head_size)
    angles = position.astype(jnp.float32)[:, None] * inv_freq[None, :]
    cosine, sine = jnp.cos(angles), jnp.sin(angles)
    turn = jnp.concatenate([cosine, cosine, -sine, sine], axis=1)

    own_rows = jnp.transpose(
        lax.dynamic_slice_in_dim(output_weight, here * columns, columns, axis=2), (1, 0, 2)
    ).reshape(features, columns)
    share = features // plane_size
    line = place * share
    piece = lax.dynamic_slice(
        output_weight, (line % head_size, line // head_size, 0),
        (share, 1, output_weight.shape[2]),
    )[:, 0]
    out_down = output_down_maps[0].reshape(rank, features)
    out_down = jnp.concatenate(jnp.split(out_down, columns // features, axis=0), axis=1)
    sends = [
        jnp.concatenate(
            [
                out_down,
                lax.dynamic_slice_in_dim(piece, (here + k) % planes * columns, columns, axis=1),
            ],
            axis=0,
        )
        for k in range(1, planes)
    ]

    lines = [turned(send, k) for k, send in enumerate(sends, 1)]
    begun = project(planes_of[:1], tokens, weight)

    done = lax.optimization_barrier(
        (held[0][1], held[1][0], lines, begun, table, turn, up_all, own_rows)
    )
    held[0][1], held[1][0], lines, begun, table, turn, up_all, own_rows = done
    lines = lax.all_gather(jnp.stack(lines), PLANE, axis=0)
    begun = [begun, begun]
    for step in range(2, planes):
        for part in range(2):
            held[part].append(turned(held[part][-1]))
            number = step - 1 - part
            if number > 0:
                begun[part] = project(
                    planes_of[number : number + 1], held[part][number], weight, [begun[part]], part
                )
        if step == 2:
            sums = shrink_partial(adapters, here, planes, table, after(tokens, held[0][1]), down_all)
            side = [sums[0]] + [turned(sums[k], k) for k in range(1, planes)]
        elif step == 3:
            shrink = sum(side[1:], side[0]).astype(jnp.bfloat16)
            out_up = after(output_up_maps, held[0][2])
            own_down = after(out_down, held[0][2])
            side = [shrink] + [turned(shrink, k) for k in range(1, planes)] + [
                lax.all_gather(out_up, "dp", axis=0, tiled=True),
                lax.all_gather(own_down, "dp", axis=0),
            ]
        held[0][-1], held[1][-1], begun, side = lax.optimization_barrier(
            (held[0][-1], held[1][-1], begun, side)
        )
    shrink, out_up_all, own_down = side[:planes], side[-2], side[-1]
    held[1].append(turned(held[1][-1]))
    begun[1] = project(
        planes_of[planes - 2 : planes - 1], held[1][planes - 2], weight, [begun[1]], 1
    )

    ids = jnp.concatenate([lax.axis_index("groups")[None], adapters])
    attended, earlier = [[], []], ()
    for part in range(2):
        made, *earlier = attend(
            planes_of, adapters, part, table, turn, up_all, shrink, held[part][-1], weight,
            begun[part], earlier,
        )
        attended[part] = [made, turned(made)]
        earlier = [after(array, attended[part][1]) for array in earlier]
    sums = [
        project_out(ids, rank, attended[part][0], own_rows, own_down, [], []) for part in range(2)
    ]
    before = []
    for step in range(2, planes + 1):
        for part in range(2):
            arrived = after(attended[part][-1], *sums[part])
            if step < planes:
                attended[part].append(turned(arrived))
            final = [] if step < planes else [table, out_up_all, *before]
            sums[part] = project_out(
                ids, rank, arrived, lines, pool, list(sums[part]), final, step - 1, part
            )
            if final:
                before = [sums[part]]
    return before[0]


def solution(mesh):
    in_specs = (
        P(PLANE, "tensor"),
        P(None, None, "tensor"),
        P("tensor", None, None),
        P(PLANE, None, "tensor"),
        P(PLANE, None, None, "tensor"),
        P(PLANE, None, None, "tensor"),
        P(PLANE, None, "tensor"),
        P(PLANE, None),
        P(PLANE, None),
    )
    function = functools.partial(
        local, mesh.shape["groups"] * mesh.shape["dp"], mesh.shape["tensor"]
    )
    return jax.shard_map(
        function, mesh=mesh, in_specs=in_specs, out_specs=P(PLANE, "tensor"), check_vma=False
    )
```

```python
import functools
import math

import jax
import jax.numpy as jnp
from jax import lax
from jax.experimental import pallas as pl
from jax.experimental.pallas import tpu as pltpu
from jax.sharding import PartitionSpec as P

VMEM_BYTES = 40 * 1024 * 1024
PLANE = ("groups", "dp")


def after(value, *earlier):
    return lax.optimization_barrier((value,) + earlier)[0]


def fixed(array):
    shape = array.shape
    return pl.BlockSpec(shape, lambda step, ids: (0,) * len(shape))


def call(kernel, name, ids, grid, specs, arrays, out, scratch=()):
    total = sum(array.size * array.dtype.itemsize for array in arrays)
    return pl.pallas_call(
        kernel,
        out_shape=out,
        grid_spec=pltpu.PrefetchScalarGridSpec(
            num_scalar_prefetch=1,
            grid=(grid,),
            in_specs=[fixed(array) if spec is None else spec for spec, array in zip(specs, arrays)],
            out_specs=[fixed(item) for item in out] if isinstance(out, tuple) else fixed(out),
            scratch_shapes=list(scratch),
        ),
        compiler_params=pltpu.CompilerParams(vmem_limit_bytes=VMEM_BYTES),
        cost_estimate=pl.CostEstimate(flops=0, bytes_accessed=3 * total, transcendentals=0),
        name=name,
    )(ids.astype(jnp.int32), *arrays)


def accumulate(acc_ref, token_ref, w_ref, first):
    slots, _, head_size = w_ref.shape
    for pair in range(slots // 2):
        columns = slice(2 * pair * head_size, (2 * pair + 2) * head_size)
        weight = jnp.concatenate([w_ref[2 * pair], w_ref[2 * pair + 1]], axis=1)
        total = jnp.dot(token_ref[...], weight, preferred_element_type=jnp.float32)
        acc_ref[:, columns] = total if first is None else first[:, columns] + total


def project_kernel(shards, begun, ids_ref, *refs):
    token_refs, w_ref, rest = refs[:shards], refs[shards], refs[shards + 1 :]
    acc_ref = rest[-1]
    step = pl.program_id(0)
    for number, token_ref in enumerate(token_refs):
        first = acc_ref if number else (rest[0] if begun else None)
        pl.when(step == number)(
            functools.partial(accumulate, acc_ref, token_ref, w_ref, first)
        )


def shard_spec(weight, depth, number=0):
    slots, _, head_size = weight.shape
    return pl.BlockSpec((slots, depth, head_size), lambda step, ids: (0, ids[number], 0))


def rows_spec(array, rows, part):
    if array.shape[0] == rows:
        return None
    return pl.BlockSpec((rows, array.shape[1]), lambda step, ids: (part, 0))


def project(ids, tokens, weight, begun=(), part=0):
    rows, depth = tokens.shape
    slots, _, head_size = weight.shape
    return call(
        functools.partial(project_kernel, 1, len(begun)),
        "project",
        ids,
        1,
        [None, shard_spec(weight, depth)] + [rows_spec(array, rows, part) for array in begun],
        [tokens, weight, *begun],
        jax.ShapeDtypeStruct((rows, slots * head_size), jnp.float32),
    )


def attend_kernel(planes, earlier, ids_ref, table_ref, turn_ref, up_ref, *refs):
    piece_refs, refs = refs[:planes], refs[planes:]
    token_ref, w_ref, begun_ref, refs = refs[0], refs[1], refs[2], refs[3:]
    earlier_refs, refs = refs[: 2 * earlier], refs[2 * earlier :]
    out_ref, keys_ref, values_ref, acc_ref, shrink_ref = refs
    for number, piece_ref in enumerate(piece_refs):
        size = piece_ref.shape[0]
        shrink_ref[pl.ds(pl.multiple_of(ids_ref[number] * size, size), size), :] = piece_ref[...]
    accumulate(acc_ref, token_ref, w_ref, begun_ref)
    slots, _, head_size = w_ref.shape
    rank = up_ref.shape[2]
    count = ids_ref.shape[0] - planes
    rows = acc_ref.shape[0]
    first_row = earlier_refs[0].shape[0] if earlier else 0
    queries = slots - 2
    lane = lax.broadcasted_iota(jnp.int32, (rows, count * rank), 1)
    kept = (lane >= table_ref[:, 1:2]) & (lane < table_ref[:, 1:2] + rank)
    lows = []
    for part in range(3):
        piece = shrink_ref[first_row : first_row + rows, part * rank : (part + 1) * rank]
        piece = jnp.concatenate([piece.astype(jnp.float32)] * count, axis=1)
        lows.append(jnp.where(kept, piece, 0.0).astype(jnp.bfloat16))

    def slot(index):
        low = lows[0 if index < queries else index - queries + 1]
        up = jnp.concatenate([up_ref[ids_ref[planes + j], index] for j in range(count)], axis=0)
        extra = jnp.dot(low, up, preferred_element_type=jnp.float32)
        return acc_ref[:, index * head_size : (index + 1) * head_size] + extra

    def rotated(index):
        value = slot(index)
        turned = pltpu.roll(value, head_size // 2, 1)
        return (value * turn_ref[:, :head_size] + turned * turn_ref[:, head_size:]).astype(
            jnp.bfloat16
        )

    keys = rotated(queries)
    values = slot(queries + 1).astype(jnp.bfloat16)
    keys_ref[...] = keys
    values_ref[...] = values
    if earlier:
        keys = jnp.concatenate([earlier_refs[0][...], keys], axis=0)
        values = jnp.concatenate([earlier_refs[1][...], values], axis=0)
    shape = (rows, keys.shape[0])
    key_at = lax.broadcasted_iota(jnp.int32, shape, 1)
    row_at = lax.broadcasted_iota(jnp.int32, shape, 0) + first_row
    allowed = (key_at >= table_ref[:, 0:1]) & (key_at <= row_at)
    for index in range(queries):
        scores = lax.dot_general(
            rotated(index), keys, (((1,), (1,)), ((), ())), preferred_element_type=jnp.float32
        )
        scores = jnp.where(allowed, scores * (1.0 / math.sqrt(head_size)), -1e30)
        weights = jnp.exp(scores - jnp.max(scores, axis=1, keepdims=True))
        scale = 1.0 / jnp.sum(weights, axis=1, keepdims=True)
        attended = jnp.dot(
            (weights * scale).astype(jnp.bfloat16), values, preferred_element_type=jnp.float32
        )
        out_ref[:, index * head_size : (index + 1) * head_size] = attended.astype(jnp.bfloat16)


def attend(planes_of, adapters, part, table, turn, up, shrink, tokens, weight, begun, earlier):
    rows, depth = tokens.shape
    slots, _, head_size = weight.shape
    planes = len(shrink)
    arrays = [table, turn, up, *shrink, tokens, weight, begun, *earlier]
    specs = [None] * len(arrays)
    for index in (0, 1):
        specs[index] = rows_spec(arrays[index], rows, part)
    specs[4 + planes] = shard_spec(weight, depth, planes - 1)
    return call(
        functools.partial(attend_kernel, planes, len(earlier) // 2),
        "attend",
        jnp.concatenate([planes_of, adapters]),
        1,
        specs,
        arrays,
        (
            jax.ShapeDtypeStruct((rows, (slots - 2) * head_size), jnp.bfloat16),
            jax.ShapeDtypeStruct((rows, head_size), jnp.bfloat16),
            jax.ShapeDtypeStruct((rows, head_size), jnp.bfloat16),
        ),
        [
            pltpu.VMEM((rows, slots * head_size), jnp.float32),
            pltpu.VMEM((planes * shrink[0].shape[0], shrink[0].shape[1]), jnp.bfloat16),
        ],
    )


def shrink_kernel(planes, ids_ref, table_ref, token_ref, down_ref, *refs):
    out_refs, acc_ref = refs[:planes], refs[planes]
    step = pl.program_id(0)
    count = ids_ref.shape[0] - 1
    part = lax.dot_general(
        token_ref[...], down_ref[0], (((1,), (1,)), ((), ())), preferred_element_type=jnp.float32
    )
    rank = part.shape[1] // 3
    part = jnp.where(table_ref[:, 1:2] == step * rank, part, 0.0)

    @pl.when(step == 0)
    def _():
        acc_ref[...] = part

    @pl.when(step > 0)
    def _():
        acc_ref[...] += part

    @pl.when(step == count - 1)
    def _():
        for turn, out_ref in enumerate(out_refs):
            rows = out_ref.shape[0]
            plane = lax.rem(ids_ref[count] + turn, planes)
            out_ref[...] = acc_ref[pl.ds(pl.multiple_of(plane * rows, rows), rows), :]


def shrink_partial(adapters, here, planes, table, tokens, down):
    _, width, depth = down.shape
    rows = tokens.shape[0]
    return call(
        functools.partial(shrink_kernel, planes),
        "shrink",
        jnp.concatenate([adapters, here[None]]),
        adapters.shape[0],
        [None, None, pl.BlockSpec((1, width, depth), lambda step, ids: (ids[step], 0, 0))],
        [table, tokens, down],
        (jax.ShapeDtypeStruct((rows // planes, width), jnp.float32),) * planes,
        [pltpu.VMEM((rows, width), jnp.float32)],
    )


def output_kernel(begun, last, lines, ids_ref, attended_ref, w_ref, down_ref, *refs):
    begun_refs, rest = refs[:begun], refs[begun:]
    if last:
        table_ref, up_ref, before_refs, out_ref = rest[0], rest[1], rest[2:-1], rest[-1]
    else:
        acc_ref, low_ref = rest
    count = ids_ref.shape[0] - 1
    attended = attended_ref[...]
    features = attended.shape[1]
    if lines:
        weight = jnp.concatenate([w_ref[i, 0, lines:] for i in range(w_ref.shape[0])], axis=0)
    else:
        weight = w_ref[...]
    downs = []
    for j in range(count):
        down = down_ref[ids_ref[1 + j], 0] if lines else down_ref[ids_ref[1 + j]]
        downs += [down[:, at : at + features] for at in range(0, down.shape[1], features)]
    down = jnp.concatenate(downs, axis=0)
    rank = down.shape[0] // count
    total = jnp.dot(attended, weight, preferred_element_type=jnp.float32)
    low = lax.dot_general(
        attended, down, (((1,), (1,)), ((), ())), preferred_element_type=jnp.float32
    )
    if begun:
        total, low = begun_refs[0][...] + total, begun_refs[1][...] + low
    if last:
        low = low.astype(jnp.bfloat16).astype(jnp.float32)
        lane = lax.broadcasted_iota(jnp.int32, low.shape, 1)
        kept = (lane >= table_ref[:, 1:2]) & (lane < table_ref[:, 1:2] + rank)
        low = jnp.where(kept, low, 0.0).astype(jnp.bfloat16)
        up = jnp.concatenate([up_ref[ids_ref[1 + j]] for j in range(count)], axis=0)
        extra = jnp.dot(low, up, preferred_element_type=jnp.float32)
        first_row = out_ref.shape[0] - total.shape[0]
        for before_ref in before_refs:
            out_ref[:first_row, :] = before_ref[...]
        out_ref[first_row:, :] = (total + extra).astype(jnp.bfloat16)
    else:
        acc_ref[...] = total
        low_ref[...] = low


def project_out(ids, rank, attended, weight, down, begun, final, turn=None, part=0):
    rows, features = attended.shape
    columns = weight.shape[-1]
    if turn is None:
        specs, down_rows = [None, None, None], 0
    else:
        down_rows = rank * features // columns
        specs = [
            None,
            pl.BlockSpec(
                (weight.shape[0], 1) + weight.shape[2:], lambda step, ids: (0, turn - 1, 0, 0)
            ),
            pl.BlockSpec(
                (down, 1, down_rows, columns),
                lambda step, ids: (ids[0], turn - 1, 0, 0),
            ),
        ]
        down = weight
    sums = (
        jax.ShapeDtypeStruct((rows, columns), jnp.float32),
        jax.ShapeDtypeStruct((rows, (ids.shape[0] - 1) * rank), jnp.float32),
    )
    return call(
        functools.partial(output_kernel, len(begun), bool(final), down_rows),
        "project_out",
        ids,
        1,
        specs + [None] * len(begun) + [rows_spec(table, rows, part) for table in final[:1]]
        + [None] * len(final[1:]),
        [attended, weight, down, *begun, *final],
        jax.ShapeDtypeStruct((rows + sum(item.shape[0] for item in final[2:]), columns), jnp.bfloat16)
        if final else sums,
    )


def local(
    plane_size,
    planes,
    tokens,
    query_key_value_weight,
    output_weight,
    adapter_down_maps,
    adapter_up_maps,
    output_down_maps,
    output_up_maps,
    request_adapter,
    lengths,
):
    token_rows, depth = tokens.shape
    _, slots, head_size = query_key_value_weight.shape
    queries = slots - 2
    pool, rank = plane_size // lax.axis_size("groups"), adapter_up_maps.shape[1]
    features = queries * head_size
    columns = output_weight.shape[2] // planes
    here = lax.axis_index("tensor")
    place = lax.axis_index(PLANE)
    planes_of = (here - jnp.arange(planes) + planes) % planes

    def turned(value, turn=1):
        return lax.ppermute(value, "tensor", [(i, (i + turn) % planes) for i in range(planes)])

    half_rows = token_rows // 2
    held = [[tokens[:half_rows]], [tokens[half_rows:]]]
    held[0].append(turned(held[0][0]))
    weight = jnp.transpose(query_key_value_weight, (1, 0, 2))
    down_all = lax.all_gather(adapter_down_maps, "dp", axis=0, tiled=True)
    up_all = lax.all_gather(jnp.transpose(adapter_up_maps[0], (1, 0, 2)), "dp", axis=0)

    requests = request_adapter.shape[1]
    request_ends = jnp.cumsum(lengths[0])
    request_starts = request_ends - lengths[0]
    at = jnp.arange(token_rows, dtype=jnp.int32)
    member = (at[:, None] >= request_starts[None, :]) & (at[:, None] < request_ends[None, :])
    if pool <= requests:
        adapters, label = jnp.arange(pool), request_adapter[0]
    else:
        adapters, label = request_adapter[0], jnp.arange(requests)
    wanted = jnp.stack([request_starts, label * rank], axis=0)
    table = jnp.sum(jnp.where(member[:, None, :], wanted[None], 0), axis=2).astype(jnp.int32)
    position = at - table[:, 0]
    half = head_size // 2
    inv_freq = 10000.0 ** (-2.0 * jnp.arange(half, dtype=jnp.float32) / head_size)
    angles = position.astype(jnp.float32)[:, None] * inv_freq[None, :]
    cosine, sine = jnp.cos(angles), jnp.sin(angles)
    turn = jnp.concatenate([cosine, cosine, -sine, sine], axis=1)

    own_rows = jnp.transpose(
        lax.dynamic_slice_in_dim(output_weight, here * columns, columns, axis=2), (1, 0, 2)
    ).reshape(features, columns)
    share = features // plane_size
    line = place * share
    piece = lax.dynamic_slice(
        output_weight, (line % head_size, line // head_size, 0),
        (share, 1, output_weight.shape[2]),
    )[:, 0]
    out_down = output_down_maps[0].reshape(rank, features)
    out_down = jnp.concatenate(jnp.split(out_down, columns // features, axis=0), axis=1)
    sends = [
        jnp.concatenate(
            [
                out_down,
                lax.dynamic_slice_in_dim(piece, (here + k) % planes * columns, columns, axis=1),
            ],
            axis=0,
        )
        for k in range(1, planes)
    ]

    held[0][1], held[1][0], sends = lax.optimization_barrier((held[0][1], held[1][0], sends))
    lines = [turned(send, k) for k, send in enumerate(sends, 1)]
    begun = project(planes_of[:1], after(tokens, held[0][1]), weight)
    begun = [begun, begun]
    for step in range(2, planes):
        for part in range(2):
            held[part].append(turned(held[part][-1]))
            number = step - 1 - part
            if number > 0:
                begun[part] = project(
                    planes_of[number : number + 1], held[part][number], weight, [begun[part]], part
                )
        if step == 2:
            sums = shrink_partial(adapters, here, planes, table, after(tokens, held[0][1]), down_all)
            side = [sums[0]] + [turned(sums[k], k) for k in range(1, planes)]
            side = (side, lines, table, turn, up_all, own_rows)
        elif step == 3:
            shrink = sum(side[1:], side[0]).astype(jnp.bfloat16)
            out_up = after(output_up_maps, held[0][2])
            own_down = after(out_down, held[0][2])
            side = [shrink] + [turned(shrink, k) for k in range(1, planes)] + [
                lax.all_gather(out_up, "dp", axis=0, tiled=True),
                lax.all_gather(own_down, "dp", axis=0),
            ]
        held[0][-1], held[1][-1], begun, side = lax.optimization_barrier(
            (held[0][-1], held[1][-1], begun, side)
        )
        if step == 2:
            side, lines, table, turn, up_all, own_rows = side
            lines = lax.all_gather(jnp.stack(lines), PLANE, axis=0)
    shrink, out_up_all, own_down = side[:planes], side[-2], side[-1]
    held[1].append(turned(held[1][-1]))
    begun[1] = project(
        planes_of[planes - 2 : planes - 1], held[1][planes - 2], weight, [begun[1]], 1
    )

    ids = jnp.concatenate([lax.axis_index("groups")[None], adapters])
    attended, earlier = [[], []], ()
    for part in range(2):
        made, *earlier = attend(
            planes_of, adapters, part, table, turn, up_all, shrink, held[part][-1], weight,
            begun[part], earlier,
        )
        attended[part] = [made, turned(after(made, *attended[0][1:]))]
    sums = [
        project_out(ids, rank, attended[part][0], own_rows, own_down, [], []) for part in range(2)
    ]
    before = []
    for step in range(2, planes + 1):
        for part in range(2):
            arrived = after(attended[part][-1], *sums[part])
            if step < planes:
                ahead = attended[0][step:]
                attended[part].append(turned(after(arrived, *ahead)))
            final = [] if step < planes else [table, out_up_all, *before]
            sums[part] = project_out(
                ids, rank, arrived, lines, pool, list(sums[part]), final, step - 1, part
            )
            if final:
                before = [sums[part]]
    return before[0]


def solution(mesh):
    in_specs = (
        P(PLANE, "tensor"),
        P(None, None, "tensor"),
        P("tensor", None, None),
        P(PLANE, None, "tensor"),
        P(PLANE, None, None, "tensor"),
        P(PLANE, None, None, "tensor"),
        P(PLANE, None, "tensor"),
        P(PLANE, None),
        P(PLANE, None),
    )
    function = functools.partial(
        local, mesh.shape["groups"] * mesh.shape["dp"], mesh.shape["tensor"]
    )
    return jax.shard_map(
        function, mesh=mesh, in_specs=in_specs, out_specs=P(PLANE, "tensor"), check_vma=False
    )
```

```python
import functools
import math

import jax
import jax.numpy as jnp
from jax import lax
from jax.experimental import pallas as pl
from jax.experimental.pallas import tpu as pltpu
from jax.sharding import PartitionSpec as P

VMEM_BYTES = 40 * 1024 * 1024
PLANE = ("groups", "dp")


def after(value, *earlier):
    return lax.optimization_barrier((value,) + earlier)[0]


def fixed(array):
    shape = array.shape
    return pl.BlockSpec(shape, lambda step, ids: (0,) * len(shape))


def call(kernel, name, ids, grid, specs, arrays, out, scratch=()):
    total = sum(array.size * array.dtype.itemsize for array in arrays)
    return pl.pallas_call(
        kernel,
        out_shape=out,
        grid_spec=pltpu.PrefetchScalarGridSpec(
            num_scalar_prefetch=1,
            grid=(grid,),
            in_specs=[fixed(array) if spec is None else spec for spec, array in zip(specs, arrays)],
            out_specs=[fixed(item) for item in out] if isinstance(out, tuple) else fixed(out),
            scratch_shapes=list(scratch),
        ),
        compiler_params=pltpu.CompilerParams(vmem_limit_bytes=VMEM_BYTES),
        cost_estimate=pl.CostEstimate(flops=0, bytes_accessed=3 * total, transcendentals=0),
        name=name,
    )(ids.astype(jnp.int32), *arrays)


def accumulate(acc_ref, token_ref, w_ref, first):
    slots, _, head_size = w_ref.shape
    for pair in range(slots // 2):
        columns = slice(2 * pair * head_size, (2 * pair + 2) * head_size)
        weight = jnp.concatenate([w_ref[2 * pair], w_ref[2 * pair + 1]], axis=1)
        total = jnp.dot(token_ref[...], weight, preferred_element_type=jnp.float32)
        acc_ref[:, columns] = total if first is None else first[:, columns] + total


def project_kernel(shards, begun, ids_ref, *refs):
    token_refs, w_ref, rest = refs[:shards], refs[shards], refs[shards + 1 :]
    acc_ref = rest[-1]
    step = pl.program_id(0)
    for number, token_ref in enumerate(token_refs):
        first = acc_ref if number else (rest[0] if begun else None)
        pl.when(step == number)(
            functools.partial(accumulate, acc_ref, token_ref, w_ref, first)
        )


def shard_spec(weight, depth, number=0):
    slots, _, head_size = weight.shape
    return pl.BlockSpec((slots, depth, head_size), lambda step, ids: (0, ids[number], 0))


def rows_spec(array, rows, part):
    if array.shape[0] == rows:
        return None
    return pl.BlockSpec((rows, array.shape[1]), lambda step, ids: (part, 0))


def project(ids, tokens, weight, begun=(), part=0):
    rows, depth = tokens.shape
    slots, _, head_size = weight.shape
    return call(
        functools.partial(project_kernel, 1, len(begun)),
        "project",
        ids,
        1,
        [None, shard_spec(weight, depth)] + [rows_spec(array, rows, part) for array in begun],
        [tokens, weight, *begun],
        jax.ShapeDtypeStruct((rows, slots * head_size), jnp.float32),
    )


def attend_kernel(planes, earlier, ids_ref, table_ref, turn_ref, up_ref, *refs):
    piece_refs, refs = refs[:planes], refs[planes:]
    token_ref, w_ref, begun_ref, refs = refs[0], refs[1], refs[2], refs[3:]
    earlier_refs, refs = refs[: 2 * earlier], refs[2 * earlier :]
    out_ref, keys_ref, values_ref, acc_ref, shrink_ref = refs
    for number, piece_ref in enumerate(piece_refs):
        size = piece_ref.shape[0]
        shrink_ref[pl.ds(pl.multiple_of(ids_ref[number] * size, size), size), :] = piece_ref[...]
    accumulate(acc_ref, token_ref, w_ref, begun_ref)
    slots, _, head_size = w_ref.shape
    rank = up_ref.shape[2]
    count = ids_ref.shape[0] - planes
    rows = acc_ref.shape[0]
    first_row = earlier_refs[0].shape[0] if earlier else 0
    queries = slots - 2
    lane = lax.broadcasted_iota(jnp.int32, (rows, count * rank), 1)
    kept = (lane >= table_ref[:, 1:2]) & (lane < table_ref[:, 1:2] + rank)
    lows = []
    for part in range(3):
        piece = shrink_ref[first_row : first_row + rows, part * rank : (part + 1) * rank]
        piece = jnp.concatenate([piece.astype(jnp.float32)] * count, axis=1)
        lows.append(jnp.where(kept, piece, 0.0).astype(jnp.bfloat16))

    def slot(index):
        low = lows[0 if index < queries else index - queries + 1]
        up = jnp.concatenate([up_ref[ids_ref[planes + j], index] for j in range(count)], axis=0)
        extra = jnp.dot(low, up, preferred_element_type=jnp.float32)
        return acc_ref[:, index * head_size : (index + 1) * head_size] + extra

    def rotated(index):
        value = slot(index)
        turned = pltpu.roll(value, head_size // 2, 1)
        return (value * turn_ref[:, :head_size] + turned * turn_ref[:, head_size:]).astype(
            jnp.bfloat16
        )

    keys = rotated(queries)
    values = slot(queries + 1).astype(jnp.bfloat16)
    keys_ref[...] = keys
    values_ref[...] = values
    if earlier:
        keys = jnp.concatenate([earlier_refs[0][...], keys], axis=0)
        values = jnp.concatenate([earlier_refs[1][...], values], axis=0)
    shape = (rows, keys.shape[0])
    key_at = lax.broadcasted_iota(jnp.int32, shape, 1)
    row_at = lax.broadcasted_iota(jnp.int32, shape, 0) + first_row
    allowed = (key_at >= table_ref[:, 0:1]) & (key_at <= row_at)
    for index in range(queries):
        scores = lax.dot_general(
            rotated(index), keys, (((1,), (1,)), ((), ())), preferred_element_type=jnp.float32
        )
        scores = jnp.where(allowed, scores * (1.0 / math.sqrt(head_size)), -1e30)
        weights = jnp.exp(scores - jnp.max(scores, axis=1, keepdims=True))
        scale = 1.0 / jnp.sum(weights, axis=1, keepdims=True)
        attended = jnp.dot(
            (weights * scale).astype(jnp.bfloat16), values, preferred_element_type=jnp.float32
        )
        out_ref[:, index * head_size : (index + 1) * head_size] = attended.astype(jnp.bfloat16)


def attend(planes_of, adapters, part, table, turn, up, shrink, tokens, weight, begun, earlier):
    rows, depth = tokens.shape
    slots, _, head_size = weight.shape
    planes = len(shrink)
    arrays = [table, turn, up, *shrink, tokens, weight, begun, *earlier]
    specs = [None] * len(arrays)
    for index in (0, 1):
        specs[index] = rows_spec(arrays[index], rows, part)
    specs[4 + planes] = shard_spec(weight, depth, planes - 1)
    return call(
        functools.partial(attend_kernel, planes, len(earlier) // 2),
        "attend",
        jnp.concatenate([planes_of, adapters]),
        1,
        specs,
        arrays,
        (
            jax.ShapeDtypeStruct((rows, (slots - 2) * head_size), jnp.bfloat16),
            jax.ShapeDtypeStruct((rows, head_size), jnp.bfloat16),
            jax.ShapeDtypeStruct((rows, head_size), jnp.bfloat16),
        ),
        [
            pltpu.VMEM((rows, slots * head_size), jnp.float32),
            pltpu.VMEM((planes * shrink[0].shape[0], shrink[0].shape[1]), jnp.bfloat16),
        ],
    )


def shrink_kernel(planes, ids_ref, table_ref, token_ref, down_ref, *refs):
    out_refs, acc_ref = refs[:planes], refs[planes]
    step = pl.program_id(0)
    count = ids_ref.shape[0] - 1
    part = lax.dot_general(
        token_ref[...], down_ref[0], (((1,), (1,)), ((), ())), preferred_element_type=jnp.float32
    )
    rank = part.shape[1] // 3
    part = jnp.where(table_ref[:, 1:2] == step * rank, part, 0.0)

    @pl.when(step == 0)
    def _():
        acc_ref[...] = part

    @pl.when(step > 0)
    def _():
        acc_ref[...] += part

    @pl.when(step == count - 1)
    def _():
        for turn, out_ref in enumerate(out_refs):
            rows = out_ref.shape[0]
            plane = lax.rem(ids_ref[count] + turn, planes)
            out_ref[...] = acc_ref[pl.ds(pl.multiple_of(plane * rows, rows), rows), :]


def shrink_partial(adapters, here, planes, table, tokens, down):
    _, width, depth = down.shape
    rows = tokens.shape[0]
    return call(
        functools.partial(shrink_kernel, planes),
        "shrink",
        jnp.concatenate([adapters, here[None]]),
        adapters.shape[0],
        [None, None, pl.BlockSpec((1, width, depth), lambda step, ids: (ids[step], 0, 0))],
        [table, tokens, down],
        (jax.ShapeDtypeStruct((rows // planes, width), jnp.float32),) * planes,
        [pltpu.VMEM((rows, width), jnp.float32)],
    )


def output_kernel(begun, last, lines, ids_ref, attended_ref, w_ref, down_ref, *refs):
    begun_refs, rest = refs[:begun], refs[begun:]
    if last:
        table_ref, up_ref, before_refs, out_ref = rest[0], rest[1], rest[2:-1], rest[-1]
    else:
        acc_ref, low_ref = rest
    count = ids_ref.shape[0] - 1
    attended = attended_ref[...]
    features = attended.shape[1]
    if lines:
        weight = jnp.concatenate([w_ref[i, 0, lines:] for i in range(w_ref.shape[0])], axis=0)
    else:
        weight = w_ref[...]
    downs = []
    for j in range(count):
        down = down_ref[ids_ref[1 + j], 0] if lines else down_ref[ids_ref[1 + j]]
        downs += [down[:, at : at + features] for at in range(0, down.shape[1], features)]
    down = jnp.concatenate(downs, axis=0)
    rank = down.shape[0] // count
    total = jnp.dot(attended, weight, preferred_element_type=jnp.float32)
    low = lax.dot_general(
        attended, down, (((1,), (1,)), ((), ())), preferred_element_type=jnp.float32
    )
    if begun:
        total, low = begun_refs[0][...] + total, begun_refs[1][...] + low
    if last:
        low = low.astype(jnp.bfloat16).astype(jnp.float32)
        lane = lax.broadcasted_iota(jnp.int32, low.shape, 1)
        kept = (lane >= table_ref[:, 1:2]) & (lane < table_ref[:, 1:2] + rank)
        low = jnp.where(kept, low, 0.0).astype(jnp.bfloat16)
        up = jnp.concatenate([up_ref[ids_ref[1 + j]] for j in range(count)], axis=0)
        extra = jnp.dot(low, up, preferred_element_type=jnp.float32)
        first_row = out_ref.shape[0] - total.shape[0]
        for before_ref in before_refs:
            out_ref[:first_row, :] = before_ref[...]
        out_ref[first_row:, :] = (total + extra).astype(jnp.bfloat16)
    else:
        acc_ref[...] = total
        low_ref[...] = low


def project_out(ids, rank, attended, weight, down, begun, final, turn=None, part=0):
    rows, features = attended.shape
    columns = weight.shape[-1]
    if turn is None:
        specs, down_rows = [None, None, None], 0
    else:
        down_rows = rank * features // columns
        specs = [
            None,
            pl.BlockSpec(
                (weight.shape[0], 1) + weight.shape[2:], lambda step, ids: (0, turn - 1, 0, 0)
            ),
            pl.BlockSpec(
                (down, 1, down_rows, columns),
                lambda step, ids: (ids[0], turn - 1, 0, 0),
            ),
        ]
        down = weight
    sums = (
        jax.ShapeDtypeStruct((rows, columns), jnp.float32),
        jax.ShapeDtypeStruct((rows, (ids.shape[0] - 1) * rank), jnp.float32),
    )
    return call(
        functools.partial(output_kernel, len(begun), bool(final), down_rows),
        "project_out",
        ids,
        1,
        specs + [None] * len(begun) + [rows_spec(table, rows, part) for table in final[:1]]
        + [None] * len(final[1:]),
        [attended, weight, down, *begun, *final],
        jax.ShapeDtypeStruct((rows + sum(item.shape[0] for item in final[2:]), columns), jnp.bfloat16)
        if final else sums,
    )


def local(
    plane_size,
    planes,
    tokens,
    query_key_value_weight,
    output_weight,
    adapter_down_maps,
    adapter_up_maps,
    output_down_maps,
    output_up_maps,
    request_adapter,
    lengths,
):
    token_rows, depth = tokens.shape
    _, slots, head_size = query_key_value_weight.shape
    queries = slots - 2
    pool, rank = plane_size // lax.axis_size("groups"), adapter_up_maps.shape[1]
    features = queries * head_size
    columns = output_weight.shape[2] // planes
    here = lax.axis_index("tensor")
    place = lax.axis_index(PLANE)
    planes_of = (here - jnp.arange(planes) + planes) % planes

    def turned(value, turn=1):
        return lax.ppermute(value, "tensor", [(i, (i + turn) % planes) for i in range(planes)])

    half_rows = token_rows // 2
    held = [[tokens[:half_rows]], [tokens[half_rows:]]]
    held[0].append(turned(held[0][0]))
    weight = jnp.transpose(query_key_value_weight, (1, 0, 2))
    down_all = lax.all_gather(adapter_down_maps, "dp", axis=0, tiled=True)
    up_all = lax.all_gather(jnp.transpose(adapter_up_maps[0], (1, 0, 2)), "dp", axis=0)

    requests = request_adapter.shape[1]
    request_ends = jnp.cumsum(lengths[0])
    request_starts = request_ends - lengths[0]
    at = jnp.arange(token_rows, dtype=jnp.int32)
    member = (at[:, None] >= request_starts[None, :]) & (at[:, None] < request_ends[None, :])
    if pool <= requests:
        adapters, label = jnp.arange(pool), request_adapter[0]
    else:
        adapters, label = request_adapter[0], jnp.arange(requests)
    wanted = jnp.stack([request_starts, label * rank], axis=0)
    table = jnp.sum(jnp.where(member[:, None, :], wanted[None], 0), axis=2).astype(jnp.int32)
    position = at - table[:, 0]
    half = head_size // 2
    inv_freq = 10000.0 ** (-2.0 * jnp.arange(half, dtype=jnp.float32) / head_size)
    angles = position.astype(jnp.float32)[:, None] * inv_freq[None, :]
    cosine, sine = jnp.cos(angles), jnp.sin(angles)
    turn = jnp.concatenate([cosine, cosine, -sine, sine], axis=1)

    own_rows = jnp.transpose(
        lax.dynamic_slice_in_dim(output_weight, here * columns, columns, axis=2), (1, 0, 2)
    ).reshape(features, columns)
    share = features // plane_size
    line = place * share
    piece = lax.dynamic_slice(
        output_weight, (line % head_size, line // head_size, 0),
        (share, 1, output_weight.shape[2]),
    )[:, 0]
    out_down = output_down_maps[0].reshape(rank, features)
    out_down = jnp.concatenate(jnp.split(out_down, columns // features, axis=0), axis=1)
    sends = [
        jnp.concatenate(
            [
                out_down,
                lax.dynamic_slice_in_dim(piece, (here + k) % planes * columns, columns, axis=1),
            ],
            axis=0,
        )
        for k in range(1, planes)
    ]

    lines = [turned(send, k) for k, send in enumerate(sends, 1)]
    begun = project(planes_of[:1], tokens, weight)

    done = lax.optimization_barrier(
        (held[0][1], held[1][0], lines, begun, table, turn, up_all, own_rows)
    )
    held[0][1], held[1][0], lines, begun, table, turn, up_all, own_rows = done
    lines = lax.all_gather(jnp.stack(lines), PLANE, axis=0)
    begun = [begun, begun]
    for step in range(2, planes):
        for part in range(2):
            held[part].append(turned(held[part][-1]))
            number = step - 1 - part
            if number > 0:
                begun[part] = project(
                    planes_of[number : number + 1], held[part][number], weight, [begun[part]], part
                )
        if step == 2:
            sums = shrink_partial(adapters, here, planes, table, after(tokens, held[0][1]), down_all)
            side = [sums[0]] + [turned(sums[k], k) for k in range(1, planes)]
            out_up_all = lax.all_gather(
                after(output_up_maps, held[0][1]), "dp", axis=0, tiled=True
            )
            own_down = lax.all_gather(after(out_down, held[0][1]), "dp", axis=0)
            side = (side, out_up_all, own_down)
        elif step == 3:
            shrink = sum(side[1:], side[0]).astype(jnp.bfloat16)
            side = [shrink] + [turned(shrink, k) for k in range(1, planes)]
        held[0][-1], held[1][-1], begun, side = lax.optimization_barrier(
            (held[0][-1], held[1][-1], begun, side)
        )
        if step == 2:
            side, out_up_all, own_down = side
    shrink = side
    held[1].append(turned(held[1][-1]))
    begun[1] = project(
        planes_of[planes - 2 : planes - 1], held[1][planes - 2], weight, [begun[1]], 1
    )

    ids = jnp.concatenate([lax.axis_index("groups")[None], adapters])
    attended, earlier = [[], []], ()
    for part in range(2):
        made, *earlier = attend(
            planes_of, adapters, part, table, turn, up_all, shrink, held[part][-1], weight,
            begun[part], earlier,
        )
        attended[part] = [made, turned(after(made, *attended[0][1:]))]
    sums = [
        project_out(ids, rank, attended[part][0], own_rows, own_down, [], []) for part in range(2)
    ]
    before = []
    for step in range(2, planes + 1):
        for part in range(2):
            arrived = attended[part][-1]
            if step < planes:
                ahead = attended[0][step:]
                attended[part].append(turned(after(arrived, *ahead)))
            final = [] if step < planes else [table, out_up_all, *before]
            sums[part] = project_out(
                ids, rank, arrived, lines, pool, list(sums[part]), final, step - 1, part
            )
            if final:
                before = [sums[part]]
    return before[0]


def solution(mesh):
    in_specs = (
        P(PLANE, "tensor"),
        P(None, None, "tensor"),
        P("tensor", None, None),
        P(PLANE, None, "tensor"),
        P(PLANE, None, None, "tensor"),
        P(PLANE, None, None, "tensor"),
        P(PLANE, None, "tensor"),
        P(PLANE, None),
        P(PLANE, None),
    )
    function = functools.partial(
        local, mesh.shape["groups"] * mesh.shape["dp"], mesh.shape["tensor"]
    )
    return jax.shard_map(
        function, mesh=mesh, in_specs=in_specs, out_specs=P(PLANE, "tensor"), check_vma=False
    )
```

```python
import functools
import math

import jax
import jax.numpy as jnp
from jax import lax
from jax.experimental import pallas as pl
from jax.experimental.pallas import tpu as pltpu
from jax.sharding import PartitionSpec as P

VMEM_BYTES = 60 * 1024 * 1024
PLANE = ("groups", "dp")


def after(value, *earlier):
    return lax.optimization_barrier((value,) + earlier)[0]


def fixed(array):
    shape = array.shape
    return pl.BlockSpec(shape, lambda step, ids: (0,) * len(shape))


def call(kernel, name, ids, grid, specs, arrays, out, scratch=()):
    total = sum(array.size * array.dtype.itemsize for array in arrays)
    return pl.pallas_call(
        kernel,
        out_shape=out,
        grid_spec=pltpu.PrefetchScalarGridSpec(
            num_scalar_prefetch=1,
            grid=(grid,),
            in_specs=[fixed(array) if spec is None else spec for spec, array in zip(specs, arrays)],
            out_specs=[fixed(item) for item in out] if isinstance(out, tuple) else fixed(out),
            scratch_shapes=list(scratch),
        ),
        compiler_params=pltpu.CompilerParams(vmem_limit_bytes=VMEM_BYTES),
        cost_estimate=pl.CostEstimate(flops=0, bytes_accessed=3 * total, transcendentals=0),
        name=name,
    )(ids.astype(jnp.int32), *arrays)


def accumulate(acc_ref, token_ref, w_ref, first):
    slots, _, head_size = w_ref.shape
    for pair in range(slots // 2):
        columns = slice(2 * pair * head_size, (2 * pair + 2) * head_size)
        weight = jnp.concatenate([w_ref[2 * pair], w_ref[2 * pair + 1]], axis=1)
        total = jnp.dot(token_ref[...], weight, preferred_element_type=jnp.float32)
        acc_ref[:, columns] = total if first is None else first[:, columns] + total


def project_kernel(shards, begun, ids_ref, *refs):
    token_refs, w_ref, rest = refs[:shards], refs[shards], refs[shards + 1 :]
    acc_ref = rest[-1]
    step = pl.program_id(0)
    for number, token_ref in enumerate(token_refs):
        first = acc_ref if number else (rest[0] if begun else None)
        pl.when(step == number)(
            functools.partial(accumulate, acc_ref, token_ref, w_ref, first)
        )


def shard_spec(weight, depth, number=0):
    slots, _, head_size = weight.shape
    return pl.BlockSpec((slots, depth, head_size), lambda step, ids: (0, ids[number], 0))


def rows_spec(array, rows, part):
    if array.shape[0] == rows:
        return None
    return pl.BlockSpec((rows, array.shape[1]), lambda step, ids: (part, 0))


def project(ids, tokens, weight, begun=(), part=0):
    rows, depth = tokens.shape
    slots, _, head_size = weight.shape
    return call(
        functools.partial(project_kernel, 1, len(begun)),
        "project",
        ids,
        1,
        [None, shard_spec(weight, depth)] + [rows_spec(array, rows, part) for array in begun],
        [tokens, weight, *begun],
        jax.ShapeDtypeStruct((rows, slots * head_size), jnp.float32),
    )


def attend_kernel(planes, earlier, ids_ref, table_ref, turn_ref, up_ref, *refs):
    piece_refs, refs = refs[:planes], refs[planes:]
    token_ref, w_ref, begun_ref, refs = refs[0], refs[1], refs[2], refs[3:]
    earlier_refs, refs = refs[: 2 * earlier], refs[2 * earlier :]
    out_ref, keys_ref, values_ref, acc_ref, shrink_ref = refs
    for number, piece_ref in enumerate(piece_refs):
        size = piece_ref.shape[0]
        shrink_ref[pl.ds(pl.multiple_of(ids_ref[number] * size, size), size), :] = piece_ref[...]
    accumulate(acc_ref, token_ref, w_ref, begun_ref)
    slots, _, head_size = w_ref.shape
    rank = up_ref.shape[2]
    count = ids_ref.shape[0] - planes
    rows = acc_ref.shape[0]
    first_row = earlier_refs[0].shape[0] if earlier else 0
    queries = slots - 2
    lane = lax.broadcasted_iota(jnp.int32, (rows, count * rank), 1)
    kept = (lane >= table_ref[:, 1:2]) & (lane < table_ref[:, 1:2] + rank)
    lows = []
    for part in range(3):
        piece = shrink_ref[first_row : first_row + rows, part * rank : (part + 1) * rank]
        piece = jnp.concatenate([piece.astype(jnp.float32)] * count, axis=1)
        lows.append(jnp.where(kept, piece, 0.0).astype(jnp.bfloat16))

    def slot(index):
        low = lows[0 if index < queries else index - queries + 1]
        up = jnp.concatenate([up_ref[ids_ref[planes + j], index] for j in range(count)], axis=0)
        extra = jnp.dot(low, up, preferred_element_type=jnp.float32)
        return acc_ref[:, index * head_size : (index + 1) * head_size] + extra

    def rotated(index):
        value = slot(index)
        turned = pltpu.roll(value, head_size // 2, 1)
        return (value * turn_ref[:, :head_size] + turned * turn_ref[:, head_size:]).astype(
            jnp.bfloat16
        )

    keys = rotated(queries)
    values = slot(queries + 1).astype(jnp.bfloat16)
    keys_ref[...] = keys
    values_ref[...] = values
    if earlier:
        keys = jnp.concatenate([earlier_refs[0][...], keys], axis=0)
        values = jnp.concatenate([earlier_refs[1][...], values], axis=0)
    shape = (rows, keys.shape[0])
    key_at = lax.broadcasted_iota(jnp.int32, shape, 1)
    row_at = lax.broadcasted_iota(jnp.int32, shape, 0) + first_row
    allowed = (key_at >= table_ref[:, 0:1]) & (key_at <= row_at)
    for index in range(queries):
        scores = lax.dot_general(
            rotated(index), keys, (((1,), (1,)), ((), ())), preferred_element_type=jnp.float32
        )
        scores = jnp.where(allowed, scores * (1.0 / math.sqrt(head_size)), -1e30)
        weights = jnp.exp(scores - jnp.max(scores, axis=1, keepdims=True))
        scale = 1.0 / jnp.sum(weights, axis=1, keepdims=True)
        attended = jnp.dot(
            (weights * scale).astype(jnp.bfloat16), values, preferred_element_type=jnp.float32
        )
        out_ref[:, index * head_size : (index + 1) * head_size] = attended.astype(jnp.bfloat16)


def attend(planes_of, adapters, part, table, turn, up, shrink, tokens, weight, begun, earlier):
    rows, depth = tokens.shape
    slots, _, head_size = weight.shape
    planes = len(shrink)
    arrays = [table, turn, up, *shrink, tokens, weight, begun, *earlier]
    specs = [None] * len(arrays)
    for index in (0, 1):
        specs[index] = rows_spec(arrays[index], rows, part)
    specs[4 + planes] = shard_spec(weight, depth, planes - 1)
    return call(
        functools.partial(attend_kernel, planes, len(earlier) // 2),
        "attend",
        jnp.concatenate([planes_of, adapters]),
        1,
        specs,
        arrays,
        (
            jax.ShapeDtypeStruct((rows, (slots - 2) * head_size), jnp.bfloat16),
            jax.ShapeDtypeStruct((rows, head_size), jnp.bfloat16),
            jax.ShapeDtypeStruct((rows, head_size), jnp.bfloat16),
        ),
        [
            pltpu.VMEM((rows, slots * head_size), jnp.float32),
            pltpu.VMEM((planes * shrink[0].shape[0], shrink[0].shape[1]), jnp.bfloat16),
        ],
    )


def shrink_kernel(planes, ids_ref, table_ref, token_ref, down_ref, *refs):
    out_refs, acc_ref = refs[:planes], refs[planes]
    step = pl.program_id(0)
    count = ids_ref.shape[0] - 1
    part = lax.dot_general(
        token_ref[...], down_ref[0], (((1,), (1,)), ((), ())), preferred_element_type=jnp.float32
    )
    rank = part.shape[1] // 3
    part = jnp.where(table_ref[:, 1:2] == step * rank, part, 0.0)

    @pl.when(step == 0)
    def _():
        acc_ref[...] = part

    @pl.when(step > 0)
    def _():
        acc_ref[...] += part

    @pl.when(step == count - 1)
    def _():
        for turn, out_ref in enumerate(out_refs):
            rows = out_ref.shape[0]
            plane = lax.rem(ids_ref[count] + turn, planes)
            out_ref[...] = acc_ref[pl.ds(pl.multiple_of(plane * rows, rows), rows), :]


def shrink_partial(adapters, here, planes, table, tokens, down):
    _, width, depth = down.shape
    rows = tokens.shape[0]
    return call(
        functools.partial(shrink_kernel, planes),
        "shrink",
        jnp.concatenate([adapters, here[None]]),
        adapters.shape[0],
        [None, None, pl.BlockSpec((1, width, depth), lambda step, ids: (ids[step], 0, 0))],
        [table, tokens, down],
        (jax.ShapeDtypeStruct((rows // planes, width), jnp.float32),) * planes,
        [pltpu.VMEM((rows, width), jnp.float32)],
    )


def output_kernel(begun, last, lines, ids_ref, attended_ref, w_ref, down_ref, *refs):
    begun_refs, rest = refs[:begun], refs[begun:]
    if last:
        table_ref, up_ref, before_refs, out_ref = rest[0], rest[1], rest[2:-1], rest[-1]
    else:
        acc_ref, low_ref = rest
    count = ids_ref.shape[0] - 1
    attended = attended_ref[...]
    features = attended.shape[1]
    if lines:
        weight = jnp.concatenate([w_ref[i, 0, lines:] for i in range(w_ref.shape[0])], axis=0)
    else:
        weight = w_ref[...]
    downs = []
    for j in range(count):
        down = down_ref[ids_ref[1 + j], 0] if lines else down_ref[ids_ref[1 + j]]
        downs += [down[:, at : at + features] for at in range(0, down.shape[1], features)]
    down = jnp.concatenate(downs, axis=0)
    rank = down.shape[0] // count
    total = jnp.dot(attended, weight, preferred_element_type=jnp.float32)
    low = lax.dot_general(
        attended, down, (((1,), (1,)), ((), ())), preferred_element_type=jnp.float32
    )
    if begun:
        total, low = begun_refs[0][...] + total, begun_refs[1][...] + low
    if last:
        low = low.astype(jnp.bfloat16).astype(jnp.float32)
        lane = lax.broadcasted_iota(jnp.int32, low.shape, 1)
        kept = (lane >= table_ref[:, 1:2]) & (lane < table_ref[:, 1:2] + rank)
        low = jnp.where(kept, low, 0.0).astype(jnp.bfloat16)
        up = jnp.concatenate([up_ref[ids_ref[1 + j]] for j in range(count)], axis=0)
        extra = jnp.dot(low, up, preferred_element_type=jnp.float32)
        first_row = out_ref.shape[0] - total.shape[0]
        for before_ref in before_refs:
            out_ref[:first_row, :] = before_ref[...]
        out_ref[first_row:, :] = (total + extra).astype(jnp.bfloat16)
    else:
        acc_ref[...] = total
        low_ref[...] = low


def project_out(ids, rank, attended, weight, down, begun, final, turn=None, part=0):
    rows, features = attended.shape
    columns = weight.shape[-1]
    if turn is None:
        specs, down_rows = [None, None, None], 0
    else:
        down_rows = rank * features // columns
        specs = [
            None,
            pl.BlockSpec(
                (weight.shape[0], 1) + weight.shape[2:], lambda step, ids: (0, turn - 1, 0, 0)
            ),
            pl.BlockSpec(
                (down, 1, down_rows, columns),
                lambda step, ids: (ids[0], turn - 1, 0, 0),
            ),
        ]
        down = weight
    sums = (
        jax.ShapeDtypeStruct((rows, columns), jnp.float32),
        jax.ShapeDtypeStruct((rows, (ids.shape[0] - 1) * rank), jnp.float32),
    )
    return call(
        functools.partial(output_kernel, len(begun), bool(final), down_rows),
        "project_out",
        ids,
        1,
        specs + [None] * len(begun) + [rows_spec(table, rows, part) for table in final[:1]]
        + [None] * len(final[1:]),
        [attended, weight, down, *begun, *final],
        jax.ShapeDtypeStruct((rows + sum(item.shape[0] for item in final[2:]), columns), jnp.bfloat16)
        if final else sums,
    )


def local(
    plane_size,
    planes,
    tokens,
    query_key_value_weight,
    output_weight,
    adapter_down_maps,
    adapter_up_maps,
    output_down_maps,
    output_up_maps,
    request_adapter,
    lengths,
):
    token_rows, depth = tokens.shape
    _, slots, head_size = query_key_value_weight.shape
    queries = slots - 2
    pool, rank = plane_size // lax.axis_size("groups"), adapter_up_maps.shape[1]
    features = queries * head_size
    columns = output_weight.shape[2] // planes
    here = lax.axis_index("tensor")
    place = lax.axis_index(PLANE)
    planes_of = (here - jnp.arange(planes) + planes) % planes

    def turned(value, turn=1):
        return lax.ppermute(value, "tensor", [(i, (i + turn) % planes) for i in range(planes)])

    half_rows = token_rows // 2
    held = [[tokens[:half_rows]], [tokens[half_rows:]]]
    held[0].append(turned(held[0][0]))
    weight = jnp.transpose(query_key_value_weight, (1, 0, 2))
    down_all = lax.all_gather(adapter_down_maps, "dp", axis=0, tiled=True)
    up_all = lax.all_gather(jnp.transpose(adapter_up_maps[0], (1, 0, 2)), "dp", axis=0)

    requests = request_adapter.shape[1]
    request_ends = jnp.cumsum(lengths[0])
    request_starts = request_ends - lengths[0]
    at = jnp.arange(token_rows, dtype=jnp.int32)
    member = (at[:, None] >= request_starts[None, :]) & (at[:, None] < request_ends[None, :])
    if pool <= requests:
        adapters, label = jnp.arange(pool), request_adapter[0]
    else:
        adapters, label = request_adapter[0], jnp.arange(requests)
    wanted = jnp.stack([request_starts, label * rank], axis=0)
    table = jnp.sum(jnp.where(member[:, None, :], wanted[None], 0), axis=2).astype(jnp.int32)
    position = at - table[:, 0]
    half = head_size // 2
    inv_freq = 10000.0 ** (-2.0 * jnp.arange(half, dtype=jnp.float32) / head_size)
    angles = position.astype(jnp.float32)[:, None] * inv_freq[None, :]
    cosine, sine = jnp.cos(angles), jnp.sin(angles)
    turn = jnp.concatenate([cosine, cosine, -sine, sine], axis=1)

    own_rows = jnp.transpose(
        lax.dynamic_slice_in_dim(output_weight, here * columns, columns, axis=2), (1, 0, 2)
    ).reshape(features, columns)
    share = features // plane_size
    line = place * share
    piece = lax.dynamic_slice(
        output_weight, (line % head_size, line // head_size, 0),
        (share, 1, output_weight.shape[2]),
    )[:, 0]
    out_down = output_down_maps[0].reshape(rank, features)
    out_down = jnp.concatenate(jnp.split(out_down, columns // features, axis=0), axis=1)
    sends = [
        jnp.concatenate(
            [
                out_down,
                lax.dynamic_slice_in_dim(piece, (here + k) % planes * columns, columns, axis=1),
            ],
            axis=0,
        )
        for k in range(1, planes)
    ]

    lines = [turned(send, k) for k, send in enumerate(sends, 1)]
    begun = project(planes_of[:1], tokens, weight)

    done = lax.optimization_barrier(
        (held[0][1], held[1][0], lines, begun, table, turn, up_all, own_rows)
    )
    held[0][1], held[1][0], lines, begun, table, turn, up_all, own_rows = done
    begun = [begun, begun]
    for step in range(2, planes):
        for part in range(2):
            held[part].append(turned(held[part][-1]))
            number = step - 1 - part
            if number > 0:
                begun[part] = project(
                    planes_of[number : number + 1], held[part][number], weight, [begun[part]], part
                )
        if step == 2:
            sums = shrink_partial(adapters, here, planes, table, after(tokens, held[0][1]), down_all)
            side = [sums[0]] + [turned(sums[k], k) for k in range(1, planes)]
            out_up_all = lax.all_gather(
                after(output_up_maps, sums[0]), "dp", axis=0, tiled=True
            )
            own_down = lax.all_gather(after(out_down, sums[0]), "dp", axis=0)
            lines = jnp.stack([after(line, sums[0]) for line in lines])
            lines = lax.all_gather(lines, PLANE, axis=0)
            side = (side, out_up_all, own_down)
        elif step == 3:
            shrink = sum(side[1:], side[0]).astype(jnp.bfloat16)
            side = [shrink] + [turned(shrink, k) for k in range(1, planes)]
        held[0][-1], held[1][-1], begun, side = lax.optimization_barrier(
            (held[0][-1], held[1][-1], begun, side)
        )
        if step == 2:
            side, out_up_all, own_down = side
    shrink = side
    held[1].append(turned(held[1][-1]))
    begun[1] = project(
        planes_of[planes - 2 : planes - 1], held[1][planes - 2], weight, [begun[1]], 1
    )

    ids = jnp.concatenate([lax.axis_index("groups")[None], adapters])
    attended, earlier = [[], []], ()
    for part in range(2):
        made, *earlier = attend(
            planes_of, adapters, part, table, turn, up_all, shrink, held[part][-1], weight,
            begun[part], earlier,
        )
        attended[part] = [made, turned(after(made, *attended[0][1:]))]
    sums = [
        project_out(ids, rank, attended[part][0], own_rows, own_down, [], []) for part in range(2)
    ]
    before = []
    for step in range(2, planes + 1):
        for part in range(2):
            arrived = attended[part][-1]
            if step < planes:
                ahead = [*attended[0][step:], *sums[part]]
                attended[part].append(turned(after(arrived, *ahead)))
            final = [] if step < planes else [table, out_up_all, *before]
            sums[part] = project_out(
                ids, rank, arrived, lines, pool, list(sums[part]), final, step - 1, part
            )
            if final:
                before = [sums[part]]
    return before[0]


def solution(mesh):
    in_specs = (
        P(PLANE, "tensor"),
        P(None, None, "tensor"),
        P("tensor", None, None),
        P(PLANE, None, "tensor"),
        P(PLANE, None, None, "tensor"),
        P(PLANE, None, None, "tensor"),
        P(PLANE, None, "tensor"),
        P(PLANE, None),
        P(PLANE, None),
    )
    function = functools.partial(
        local, mesh.shape["groups"] * mesh.shape["dp"], mesh.shape["tensor"]
    )
    return jax.shard_map(
        function, mesh=mesh, in_specs=in_specs, out_specs=P(PLANE, "tensor"), check_vma=False
    )
```

```python
import functools
import math

import jax
import jax.numpy as jnp
from jax import lax
from jax.experimental import pallas as pl
from jax.experimental.pallas import tpu as pltpu
from jax.sharding import PartitionSpec as P

VMEM_BYTES = 40 * 1024 * 1024
PLANE = ("groups", "dp")


def after(value, *earlier):
    return lax.optimization_barrier((value,) + earlier)[0]


def fixed(array):
    shape = array.shape
    return pl.BlockSpec(shape, lambda step, ids: (0,) * len(shape))


def call(kernel, name, ids, grid, specs, arrays, out, scratch=()):
    total = sum(array.size * array.dtype.itemsize for array in arrays)
    return pl.pallas_call(
        kernel,
        out_shape=out,
        grid_spec=pltpu.PrefetchScalarGridSpec(
            num_scalar_prefetch=1,
            grid=(grid,),
            in_specs=[fixed(array) if spec is None else spec for spec, array in zip(specs, arrays)],
            out_specs=[fixed(item) for item in out] if isinstance(out, tuple) else fixed(out),
            scratch_shapes=list(scratch),
        ),
        compiler_params=pltpu.CompilerParams(vmem_limit_bytes=VMEM_BYTES),
        cost_estimate=pl.CostEstimate(flops=0, bytes_accessed=3 * total, transcendentals=0),
        name=name,
    )(ids.astype(jnp.int32), *arrays)


def accumulate(acc_ref, token_ref, w_ref, first):
    slots, _, head_size = w_ref.shape
    for pair in range(slots // 2):
        columns = slice(2 * pair * head_size, (2 * pair + 2) * head_size)
        weight = jnp.concatenate([w_ref[2 * pair], w_ref[2 * pair + 1]], axis=1)
        total = jnp.dot(token_ref[...], weight, preferred_element_type=jnp.float32)
        acc_ref[:, columns] = total if first is None else first[:, columns] + total


def project_kernel(begun, ids_ref, token_ref, w_ref, *refs):
    accumulate(refs[-1], token_ref, w_ref, refs[0] if begun else None)


def rows_spec(array, rows, part):
    if array.shape[0] == rows:
        return None
    return pl.BlockSpec((rows, array.shape[1]), lambda step, ids: (part, 0))


def project(ids, tokens, weight, begun=()):
    slots, _, head_size = weight.shape
    return call(
        functools.partial(project_kernel, len(begun)),
        "project",
        ids,
        1,
        [None] * (2 + len(begun)),
        [tokens, weight, *begun],
        jax.ShapeDtypeStruct((tokens.shape[0], slots * head_size), jnp.float32),
    )


def attend_kernel(planes, earlier, ids_ref, table_ref, turn_ref, up_ref, *refs):
    piece_refs, refs = refs[:planes], refs[planes:]
    token_ref, w_ref, begun_ref, refs = refs[0], refs[1], refs[2], refs[3:]
    earlier_refs, refs = refs[: 2 * earlier], refs[2 * earlier :]
    out_ref, keys_ref, values_ref, acc_ref, shrink_ref = refs
    for number, piece_ref in enumerate(piece_refs):
        size = piece_ref.shape[0]
        shrink_ref[pl.ds(pl.multiple_of(ids_ref[number] * size, size), size), :] = piece_ref[...]
    accumulate(acc_ref, token_ref, w_ref, begun_ref)
    slots, _, head_size = w_ref.shape
    rank = up_ref.shape[2]
    count = ids_ref.shape[0] - planes
    rows = acc_ref.shape[0]
    first_row = earlier_refs[0].shape[0] if earlier else 0
    queries = slots - 2
    lane = lax.broadcasted_iota(jnp.int32, (rows, count * rank), 1)
    kept = (lane >= table_ref[:, 1:2]) & (lane < table_ref[:, 1:2] + rank)
    lows = []
    for part in range(3):
        piece = shrink_ref[first_row : first_row + rows, part * rank : (part + 1) * rank]
        piece = jnp.concatenate([piece.astype(jnp.float32)] * count, axis=1)
        lows.append(jnp.where(kept, piece, 0.0).astype(jnp.bfloat16))

    def slot(index):
        low = lows[0 if index < queries else index - queries + 1]
        up = jnp.concatenate([up_ref[ids_ref[planes + j], index] for j in range(count)], axis=0)
        extra = jnp.dot(low, up, preferred_element_type=jnp.float32)
        return acc_ref[:, index * head_size : (index + 1) * head_size] + extra

    def rotated(index):
        value = slot(index)
        turned = pltpu.roll(value, head_size // 2, 1)
        return (value * turn_ref[:, :head_size] + turned * turn_ref[:, head_size:]).astype(
            jnp.bfloat16
        )

    keys = rotated(queries)
    values = slot(queries + 1).astype(jnp.bfloat16)
    keys_ref[...] = keys
    values_ref[...] = values
    if earlier:
        keys = jnp.concatenate([earlier_refs[0][...], keys], axis=0)
        values = jnp.concatenate([earlier_refs[1][...], values], axis=0)
    shape = (rows, keys.shape[0])
    key_at = lax.broadcasted_iota(jnp.int32, shape, 1)
    row_at = lax.broadcasted_iota(jnp.int32, shape, 0) + first_row
    allowed = (key_at >= table_ref[:, 0:1]) & (key_at <= row_at)
    for index in range(queries):
        scores = lax.dot_general(
            rotated(index), keys, (((1,), (1,)), ((), ())), preferred_element_type=jnp.float32
        )
        scores = jnp.where(allowed, scores * (1.0 / math.sqrt(head_size)), -1e30)
        weights = jnp.exp(scores - jnp.max(scores, axis=1, keepdims=True))
        scale = 1.0 / jnp.sum(weights, axis=1, keepdims=True)
        attended = jnp.dot(
            (weights * scale).astype(jnp.bfloat16), values, preferred_element_type=jnp.float32
        )
        out_ref[:, index * head_size : (index + 1) * head_size] = attended.astype(jnp.bfloat16)


def attend(planes_of, adapters, part, table, turn, up, shrink, tokens, weight, begun, earlier):
    rows = tokens.shape[0] // 2
    slots, _, head_size = weight.shape
    planes = len(shrink)
    arrays = [table, turn, up, *shrink, tokens, weight, begun, *earlier]
    specs = [None] * len(arrays)
    for index in (0, 1, 3 + planes, 5 + planes):
        specs[index] = rows_spec(arrays[index], rows, part)
    return call(
        functools.partial(attend_kernel, planes, len(earlier) // 2),
        "attend",
        jnp.concatenate([planes_of, adapters]),
        1,
        specs,
        arrays,
        (
            jax.ShapeDtypeStruct((rows, (slots - 2) * head_size), jnp.bfloat16),
            jax.ShapeDtypeStruct((rows, head_size), jnp.bfloat16),
            jax.ShapeDtypeStruct((rows, head_size), jnp.bfloat16),
        ),
        [
            pltpu.VMEM((rows, slots * head_size), jnp.float32),
            pltpu.VMEM((planes * shrink[0].shape[0], shrink[0].shape[1]), jnp.bfloat16),
        ],
    )


def shrink_kernel(planes, ids_ref, table_ref, token_ref, down_ref, *refs):
    out_refs, acc_ref = refs[:planes], refs[planes]
    step = pl.program_id(0)
    count = ids_ref.shape[0] - 1
    part = lax.dot_general(
        token_ref[...], down_ref[0], (((1,), (1,)), ((), ())), preferred_element_type=jnp.float32
    )
    rank = part.shape[1] // 3
    part = jnp.where(table_ref[:, 1:2] == step * rank, part, 0.0)

    @pl.when(step == 0)
    def _():
        acc_ref[...] = part

    @pl.when(step > 0)
    def _():
        acc_ref[...] += part

    @pl.when(step == count - 1)
    def _():
        for turn, out_ref in enumerate(out_refs):
            rows = out_ref.shape[0]
            plane = lax.rem(ids_ref[count] + turn, planes)
            out_ref[...] = acc_ref[pl.ds(pl.multiple_of(plane * rows, rows), rows), :]


def shrink_partial(adapters, here, planes, table, tokens, down):
    _, width, depth = down.shape
    rows = tokens.shape[0]
    return call(
        functools.partial(shrink_kernel, planes),
        "shrink",
        jnp.concatenate([adapters, here[None]]),
        adapters.shape[0],
        [None, None, pl.BlockSpec((1, width, depth), lambda step, ids: (ids[step], 0, 0))],
        [table, tokens, down],
        (jax.ShapeDtypeStruct((rows // planes, width), jnp.float32),) * planes,
        [pltpu.VMEM((rows, width), jnp.float32)],
    )


def output_kernel(begun, last, lines, ids_ref, attended_ref, w_ref, down_ref, *refs):
    begun_refs, rest = refs[:begun], refs[begun:]
    if last:
        table_ref, up_ref, before_refs, out_ref = rest[0], rest[1], rest[2:-1], rest[-1]
    else:
        acc_ref, low_ref = rest
    count = ids_ref.shape[0] - 1
    attended = attended_ref[...]
    features = attended.shape[1]
    if lines:
        weight = jnp.concatenate([w_ref[i, lines:] for i in range(w_ref.shape[0])], axis=0)
    else:
        weight = w_ref[...]
    downs = []
    for j in range(count):
        down = down_ref[ids_ref[1 + j]]
        downs += [down[:, at : at + features] for at in range(0, down.shape[1], features)]
    down = jnp.concatenate(downs, axis=0)
    rank = down.shape[0] // count
    total = jnp.dot(attended, weight, preferred_element_type=jnp.float32)
    low = lax.dot_general(
        attended, down, (((1,), (1,)), ((), ())), preferred_element_type=jnp.float32
    )
    if begun:
        total, low = begun_refs[0][...] + total, begun_refs[1][...] + low
    if last:
        low = low.astype(jnp.bfloat16).astype(jnp.float32)
        lane = lax.broadcasted_iota(jnp.int32, low.shape, 1)
        kept = (lane >= table_ref[:, 1:2]) & (lane < table_ref[:, 1:2] + rank)
        low = jnp.where(kept, low, 0.0).astype(jnp.bfloat16)
        up = jnp.concatenate([up_ref[ids_ref[1 + j]] for j in range(count)], axis=0)
        extra = jnp.dot(low, up, preferred_element_type=jnp.float32)
        first_row = out_ref.shape[0] - total.shape[0]
        for before_ref in before_refs:
            out_ref[:first_row, :] = before_ref[...]
        out_ref[first_row:, :] = (total + extra).astype(jnp.bfloat16)
    else:
        acc_ref[...] = total
        low_ref[...] = low


def project_out(ids, rank, attended, weight, down, begun, final, part=0):
    rows, features = attended.shape
    columns = weight.shape[-1]
    if len(weight.shape) == 2:
        down_spec, down_rows = None, 0
    else:
        down_rows = rank * features // columns
        down_spec = pl.BlockSpec(
            (down, down_rows, columns), lambda step, ids: (ids[0], 0, 0)
        )
        down = weight
    sums = (
        jax.ShapeDtypeStruct((rows, columns), jnp.float32),
        jax.ShapeDtypeStruct((rows, (ids.shape[0] - 1) * rank), jnp.float32),
    )
    all_rows = rows + sum(item.shape[0] for item in final[2:])
    return call(
        functools.partial(output_kernel, len(begun), bool(final), down_rows),
        "project_out",
        ids,
        1,
        [None, None, down_spec] + [None] * len(begun)
        + [rows_spec(table, rows, part) for table in final[:1]] + [None] * len(final[1:]),
        [attended, weight, down, *begun, *final],
        jax.ShapeDtypeStruct((all_rows, columns), jnp.bfloat16) if final else sums,
    )


def local(
    plane_size,
    planes,
    tokens,
    query_key_value_weight,
    output_weight,
    adapter_down_maps,
    adapter_up_maps,
    output_down_maps,
    output_up_maps,
    request_adapter,
    lengths,
):
    token_rows, depth = tokens.shape
    _, slots, head_size = query_key_value_weight.shape
    queries = slots - 2
    pool, rank = plane_size // lax.axis_size("groups"), adapter_up_maps.shape[1]
    features = queries * head_size
    columns = output_weight.shape[2] // planes
    here = lax.axis_index("tensor")
    place = lax.axis_index(PLANE)
    planes_of = (here - jnp.arange(planes) + planes) % planes

    def turned(value, turn=1):
        return lax.ppermute(value, "tensor", [(i, (i + turn) % planes) for i in range(planes)])

    held = [tokens, turned(tokens)]
    weight = jnp.transpose(query_key_value_weight, (1, 0, 2))
    down_all = lax.all_gather(adapter_down_maps, "dp", axis=0, tiled=True)
    up_all = lax.all_gather(jnp.transpose(adapter_up_maps[0], (1, 0, 2)), "dp", axis=0)

    requests = request_adapter.shape[1]
    request_ends = jnp.cumsum(lengths[0])
    request_starts = request_ends - lengths[0]
    at = jnp.arange(token_rows, dtype=jnp.int32)
    member = (at[:, None] >= request_starts[None, :]) & (at[:, None] < request_ends[None, :])
    if pool <= requests:
        adapters, label = jnp.arange(pool), request_adapter[0]
    else:
        adapters, label = request_adapter[0], jnp.arange(requests)
    wanted = jnp.stack([request_starts, label * rank], axis=0)
    table = jnp.sum(jnp.where(member[:, None, :], wanted[None], 0), axis=2).astype(jnp.int32)
    position = at - table[:, 0]
    half = head_size // 2
    inv_freq = 10000.0 ** (-2.0 * jnp.arange(half, dtype=jnp.float32) / head_size)
    angles = position.astype(jnp.float32)[:, None] * inv_freq[None, :]
    cosine, sine = jnp.cos(angles), jnp.sin(angles)
    turn = jnp.concatenate([cosine, cosine, -sine, sine], axis=1)

    own_rows = jnp.transpose(
        lax.dynamic_slice_in_dim(output_weight, here * columns, columns, axis=2), (1, 0, 2)
    ).reshape(features, columns)
    share = features // plane_size
    line = place * share
    piece = lax.dynamic_slice(
        output_weight, (line % head_size, line // head_size, 0),
        (share, 1, output_weight.shape[2]),
    )[:, 0]
    out_down = output_down_maps[0].reshape(rank, features)
    out_down = jnp.concatenate(jnp.split(out_down, columns // features, axis=0), axis=1)
    sends = [
        jnp.concatenate(
            [
                out_down,
                lax.dynamic_slice_in_dim(piece, (here + k) % planes * columns, columns, axis=1),
            ],
            axis=0,
        )
        for k in range(1, planes)
    ]

    def shard(number):
        start = planes_of[number] * depth
        return lax.dynamic_slice_in_dim(weight, start, depth, axis=1)

    lines = [turned(send, k) for k, send in enumerate(sends, 1)]
    begun = project(planes_of[:1], tokens, shard(0))
    done = (held[1], lines, begun, table, turn, up_all, own_rows, shard(1))
    done = lax.optimization_barrier(done)
    held[1], lines, begun, table, turn, up_all, own_rows, part_weight = done
    lines = lax.all_gather(jnp.stack(lines), PLANE, axis=0)
    for step in range(2, planes):
        arrived = held[-1]
        held.append(turned(arrived))
        begun = project(planes_of[step - 1 : step], arrived, part_weight, [begun])
        side = ()
        if step == 2:
            sums = shrink_partial(adapters, here, planes, table, after(tokens, arrived), down_all)
            sums = [sums[0]] + [turned(sums[k], k) for k in range(1, planes)]
            side = (
                sums,
                lax.all_gather(after(output_up_maps, sums[0]), "dp", axis=0, tiled=True),
                lax.all_gather(after(out_down, sums[0]), "dp", axis=0),
            )
        elif step == 3:
            shrink = sum(sums[1:], sums[0]).astype(jnp.bfloat16)
            shrink = [shrink] + [turned(shrink, k) for k in range(1, planes)]
            side = (shrink, [lines[:, k] for k in range(planes - 1)])
        done = lax.optimization_barrier((held[-1], begun, shard(step), side))
        held[-1], begun, part_weight, side = done
        if step == 2:
            sums, out_up_all, own_down = side
        elif step == 3:
            shrink, lines = side

    ids = jnp.concatenate([lax.axis_index("groups")[None], adapters])
    attended, earlier = [[], []], ()
    for part in range(2):
        made, *earlier = attend(
            planes_of, adapters, part, table, turn, up_all, shrink, held[-1], part_weight,
            begun, earlier,
        )
        attended[part] = [made, turned(after(made, *attended[0][1:]))]
    sums = [
        project_out(ids, rank, attended[part][0], own_rows, own_down, [], []) for part in range(2)
    ]
    before = []
    for step in range(2, planes + 1):
        for part in range(2):
            arrived = attended[part][-1]
            if step < planes:
                ahead = [*attended[0][step:], *sums[part]]
                attended[part].append(turned(after(arrived, *ahead)))
            final = [] if step < planes else [table, out_up_all, *before]
            sums[part] = project_out(
                ids, rank, arrived, lines[step - 2], pool, list(sums[part]), final, part
            )
            if final:
                before = [sums[part]]
    return before[0]


def solution(mesh):
    in_specs = (
        P(PLANE, "tensor"),
        P(None, None, "tensor"),
        P("tensor", None, None),
        P(PLANE, None, "tensor"),
        P(PLANE, None, None, "tensor"),
        P(PLANE, None, None, "tensor"),
        P(PLANE, None, "tensor"),
        P(PLANE, None),
        P(PLANE, None),
    )
    function = functools.partial(
        local, mesh.shape["groups"] * mesh.shape["dp"], mesh.shape["tensor"]
    )
    return jax.shard_map(
        function, mesh=mesh, in_specs=in_specs, out_specs=P(PLANE, "tensor"), check_vma=False
    )
```

```python
import functools
import math

import jax
import jax.numpy as jnp
from jax import lax
from jax.experimental import pallas as pl
from jax.experimental.pallas import tpu as pltpu
from jax.sharding import PartitionSpec as P

VMEM_BYTES = 40 * 1024 * 1024
PLANE = ("groups", "dp")


def after(value, *earlier):
    return lax.optimization_barrier((value,) + earlier)[0]


def fixed(array):
    shape = array.shape
    return pl.BlockSpec(shape, lambda step, ids: (0,) * len(shape))


def call(kernel, name, ids, grid, specs, arrays, out, scratch=()):
    total = sum(array.size * array.dtype.itemsize for array in arrays)
    return pl.pallas_call(
        kernel,
        out_shape=out,
        grid_spec=pltpu.PrefetchScalarGridSpec(
            num_scalar_prefetch=1,
            grid=(grid,),
            in_specs=[fixed(array) if spec is None else spec for spec, array in zip(specs, arrays)],
            out_specs=[fixed(item) for item in out] if isinstance(out, tuple) else fixed(out),
            scratch_shapes=list(scratch),
        ),
        compiler_params=pltpu.CompilerParams(vmem_limit_bytes=VMEM_BYTES),
        cost_estimate=pl.CostEstimate(flops=0, bytes_accessed=3 * total, transcendentals=0),
        name=name,
    )(ids.astype(jnp.int32), *arrays)


def accumulate(acc_ref, token_ref, w_ref, first):
    slots, _, head_size = w_ref.shape
    for pair in range(slots // 2):
        columns = slice(2 * pair * head_size, (2 * pair + 2) * head_size)
        weight = jnp.concatenate([w_ref[2 * pair], w_ref[2 * pair + 1]], axis=1)
        total = jnp.dot(token_ref[...], weight, preferred_element_type=jnp.float32)
        acc_ref[:, columns] = total if first is None else first[:, columns] + total


def project_kernel(begun, ids_ref, token_ref, w_ref, *refs):
    accumulate(refs[-1], token_ref, w_ref, refs[0] if begun else None)


def rows_spec(array, rows, part):
    if array.shape[0] == rows:
        return None
    return pl.BlockSpec((rows, array.shape[1]), lambda step, ids: (part, 0))


def project(tokens, weight, begun=()):
    slots, _, head_size = weight.shape
    return call(
        functools.partial(project_kernel, len(begun)),
        "project",
        jnp.zeros(1),
        1,
        [None] * (2 + len(begun)),
        [tokens, weight, *begun],
        jax.ShapeDtypeStruct((tokens.shape[0], slots * head_size), jnp.float32),
    )


def attend_kernel(planes, earlier, ids_ref, table_ref, turn_ref, up_ref, *refs):
    piece_refs, refs = refs[:planes], refs[planes:]
    token_ref, w_ref, begun_ref, refs = refs[0], refs[1], refs[2], refs[3:]
    earlier_refs, refs = refs[: 2 * earlier], refs[2 * earlier :]
    out_ref, keys_ref, values_ref, acc_ref, shrink_ref = refs
    for number, piece_ref in enumerate(piece_refs):
        size = piece_ref.shape[0]
        shrink_ref[pl.ds(pl.multiple_of(ids_ref[number] * size, size), size), :] = piece_ref[...]
    accumulate(acc_ref, token_ref, w_ref, begun_ref)
    slots, _, head_size = w_ref.shape
    rank = up_ref.shape[2]
    count = ids_ref.shape[0] - planes
    rows = acc_ref.shape[0]
    first_row = earlier_refs[0].shape[0] if earlier else 0
    queries = slots - 2
    lane = lax.broadcasted_iota(jnp.int32, (rows, count * rank), 1)
    kept = (lane >= table_ref[:, 1:2]) & (lane < table_ref[:, 1:2] + rank)
    lows = []
    for part in range(3):
        piece = shrink_ref[first_row : first_row + rows, part * rank : (part + 1) * rank]
        piece = jnp.concatenate([piece.astype(jnp.float32)] * count, axis=1)
        lows.append(jnp.where(kept, piece, 0.0).astype(jnp.bfloat16))

    def slot(index):
        low = lows[0 if index < queries else index - queries + 1]
        up = jnp.concatenate([up_ref[ids_ref[planes + j], index] for j in range(count)], axis=0)
        extra = jnp.dot(low, up, preferred_element_type=jnp.float32)
        return acc_ref[:, index * head_size : (index + 1) * head_size] + extra

    def rotated(index):
        value = slot(index)
        turned = pltpu.roll(value, head_size // 2, 1)
        return (value * turn_ref[:, :head_size] + turned * turn_ref[:, head_size:]).astype(
            jnp.bfloat16
        )

    keys = rotated(queries)
    values = slot(queries + 1).astype(jnp.bfloat16)
    keys_ref[...] = keys
    values_ref[...] = values
    if earlier:
        keys = jnp.concatenate([earlier_refs[0][...], keys], axis=0)
        values = jnp.concatenate([earlier_refs[1][...], values], axis=0)
    shape = (rows, keys.shape[0])
    key_at = lax.broadcasted_iota(jnp.int32, shape, 1)
    row_at = lax.broadcasted_iota(jnp.int32, shape, 0) + first_row
    allowed = (key_at >= table_ref[:, 0:1]) & (key_at <= row_at)
    for index in range(queries):
        scores = lax.dot_general(
            rotated(index), keys, (((1,), (1,)), ((), ())), preferred_element_type=jnp.float32
        )
        scores = jnp.where(allowed, scores * (1.0 / math.sqrt(head_size)), -1e30)
        weights = jnp.exp(scores - jnp.max(scores, axis=1, keepdims=True))
        scale = 1.0 / jnp.sum(weights, axis=1, keepdims=True)
        attended = jnp.dot(
            (weights * scale).astype(jnp.bfloat16), values, preferred_element_type=jnp.float32
        )
        out_ref[:, index * head_size : (index + 1) * head_size] = attended.astype(jnp.bfloat16)


def attend(planes_of, adapters, part, table, turn, up, shrink, tokens, weight, begun, earlier):
    rows = tokens.shape[0]
    slots, _, head_size = weight.shape
    planes = len(shrink)
    arrays = [table, turn, up, *shrink, tokens, weight, begun, *earlier]
    specs = [None] * len(arrays)
    for index in (0, 1, 3 + planes, 5 + planes):
        specs[index] = rows_spec(arrays[index], rows, part)
    return call(
        functools.partial(attend_kernel, planes, len(earlier) // 2),
        "attend",
        jnp.concatenate([planes_of, adapters]),
        1,
        specs,
        arrays,
        (
            jax.ShapeDtypeStruct((rows, (slots - 2) * head_size), jnp.bfloat16),
            jax.ShapeDtypeStruct((rows, head_size), jnp.bfloat16),
            jax.ShapeDtypeStruct((rows, head_size), jnp.bfloat16),
        ),
        [
            pltpu.VMEM((rows, slots * head_size), jnp.float32),
            pltpu.VMEM((planes * shrink[0].shape[0], shrink[0].shape[1]), jnp.bfloat16),
        ],
    )


def shrink_kernel(planes, ids_ref, table_ref, token_ref, down_ref, *refs):
    out_refs, acc_ref = refs[:planes], refs[planes]
    step = pl.program_id(0)
    count = ids_ref.shape[0] - 1
    part = lax.dot_general(
        token_ref[...], down_ref[0], (((1,), (1,)), ((), ())), preferred_element_type=jnp.float32
    )
    rank = part.shape[1] // 3
    part = jnp.where(table_ref[:, 1:2] == step * rank, part, 0.0)

    @pl.when(step == 0)
    def _():
        acc_ref[...] = part

    @pl.when(step > 0)
    def _():
        acc_ref[...] += part

    @pl.when(step == count - 1)
    def _():
        for turn, out_ref in enumerate(out_refs):
            rows = out_ref.shape[0]
            plane = lax.rem(ids_ref[count] + turn, planes)
            out_ref[...] = acc_ref[pl.ds(pl.multiple_of(plane * rows, rows), rows), :]


def shrink_partial(adapters, here, planes, table, tokens, down):
    _, width, depth = down.shape
    rows = tokens.shape[0]
    return call(
        functools.partial(shrink_kernel, planes),
        "shrink",
        jnp.concatenate([adapters, here[None]]),
        adapters.shape[0],
        [None, None, pl.BlockSpec((1, width, depth), lambda step, ids: (ids[step], 0, 0))],
        [table, tokens, down],
        (jax.ShapeDtypeStruct((rows // planes, width), jnp.float32),) * planes,
        [pltpu.VMEM((rows, width), jnp.float32)],
    )


def output_kernel(begun, last, lines, ids_ref, attended_ref, w_ref, down_ref, *refs):
    begun_refs, rest = refs[:begun], refs[begun:]
    if last:
        table_ref, up_ref, before_refs, out_ref = rest[0], rest[1], rest[2:-1], rest[-1]
    else:
        acc_ref, low_ref = rest
    count = ids_ref.shape[0] - 1
    attended = attended_ref[...]
    features = attended.shape[1]
    if lines:
        weight = jnp.concatenate([w_ref[i, lines:] for i in range(w_ref.shape[0])], axis=0)
    else:
        weight = w_ref[...]
    downs = []
    for j in range(count):
        down = down_ref[ids_ref[1 + j]]
        downs += [down[:, at : at + features] for at in range(0, down.shape[1], features)]
    down = jnp.concatenate(downs, axis=0)
    rank = down.shape[0] // count
    total = jnp.dot(attended, weight, preferred_element_type=jnp.float32)
    low = lax.dot_general(
        attended, down, (((1,), (1,)), ((), ())), preferred_element_type=jnp.float32
    )
    if begun:
        total, low = begun_refs[0][...] + total, begun_refs[1][...] + low
    if last:
        low = low.astype(jnp.bfloat16).astype(jnp.float32)
        lane = lax.broadcasted_iota(jnp.int32, low.shape, 1)
        kept = (lane >= table_ref[:, 1:2]) & (lane < table_ref[:, 1:2] + rank)
        low = jnp.where(kept, low, 0.0).astype(jnp.bfloat16)
        up = jnp.concatenate([up_ref[ids_ref[1 + j]] for j in range(count)], axis=0)
        extra = jnp.dot(low, up, preferred_element_type=jnp.float32)
        first_row = out_ref.shape[0] - total.shape[0]
        for before_ref in before_refs:
            out_ref[:first_row, :] = before_ref[...]
        out_ref[first_row:, :] = (total + extra).astype(jnp.bfloat16)
    else:
        acc_ref[...] = total
        low_ref[...] = low


def project_out(ids, rank, attended, weight, down, begun, final, part=0):
    rows, features = attended.shape
    columns = weight.shape[-1]
    if len(weight.shape) == 2:
        down_spec, down_rows = None, 0
    else:
        down_rows = rank * features // columns
        down_spec = pl.BlockSpec(
            (down, down_rows, columns), lambda step, ids: (ids[0], 0, 0)
        )
        down = weight
    sums = (
        jax.ShapeDtypeStruct((rows, columns), jnp.float32),
        jax.ShapeDtypeStruct((rows, (ids.shape[0] - 1) * rank), jnp.float32),
    )
    all_rows = rows + sum(item.shape[0] for item in final[2:])
    return call(
        functools.partial(output_kernel, len(begun), bool(final), down_rows),
        "project_out",
        ids,
        1,
        [None, None, down_spec] + [None] * len(begun)
        + [rows_spec(table, rows, part) for table in final[:1]] + [None] * len(final[1:]),
        [attended, weight, down, *begun, *final],
        jax.ShapeDtypeStruct((all_rows, columns), jnp.bfloat16) if final else sums,
    )


def local(
    plane_size,
    planes,
    tokens,
    query_key_value_weight,
    output_weight,
    adapter_down_maps,
    adapter_up_maps,
    output_down_maps,
    output_up_maps,
    request_adapter,
    lengths,
):
    token_rows, depth = tokens.shape
    _, slots, head_size = query_key_value_weight.shape
    queries = slots - 2
    pool, rank = plane_size // lax.axis_size("groups"), adapter_up_maps.shape[1]
    features = queries * head_size
    columns = output_weight.shape[2] // planes
    here = lax.axis_index("tensor")
    place = lax.axis_index(PLANE)
    planes_of = (here - jnp.arange(planes) + planes) % planes

    def turned(value, turn=1):
        return lax.ppermute(value, "tensor", [(i, (i + turn) % planes) for i in range(planes)])

    weight = jnp.transpose(query_key_value_weight, (1, 0, 2))
    down_all = lax.all_gather(adapter_down_maps, "dp", axis=0, tiled=True)
    up_all = lax.all_gather(jnp.transpose(adapter_up_maps[0], (1, 0, 2)), "dp", axis=0)

    requests = request_adapter.shape[1]
    request_ends = jnp.cumsum(lengths[0])
    request_starts = request_ends - lengths[0]
    at = jnp.arange(token_rows, dtype=jnp.int32)
    member = (at[:, None] >= request_starts[None, :]) & (at[:, None] < request_ends[None, :])
    if pool <= requests:
        adapters, label = jnp.arange(pool), request_adapter[0]
    else:
        adapters, label = request_adapter[0], jnp.arange(requests)
    wanted = jnp.stack([request_starts, label * rank], axis=0)
    table = jnp.sum(jnp.where(member[:, None, :], wanted[None], 0), axis=2).astype(jnp.int32)
    position = at - table[:, 0]
    half = head_size // 2
    inv_freq = 10000.0 ** (-2.0 * jnp.arange(half, dtype=jnp.float32) / head_size)
    angles = position.astype(jnp.float32)[:, None] * inv_freq[None, :]
    cosine, sine = jnp.cos(angles), jnp.sin(angles)
    turn = jnp.concatenate([cosine, cosine, -sine, sine], axis=1)

    own_rows = jnp.transpose(
        lax.dynamic_slice_in_dim(output_weight, here * columns, columns, axis=2), (1, 0, 2)
    ).reshape(features, columns)
    share = features // plane_size
    line = place * share
    piece = lax.dynamic_slice(
        output_weight, (line % head_size, line // head_size, 0),
        (share, 1, output_weight.shape[2]),
    )[:, 0]
    out_down = output_down_maps[0].reshape(rank, features)
    out_down = jnp.concatenate(jnp.split(out_down, columns // features, axis=0), axis=1)
    sends = [
        jnp.concatenate(
            [
                out_down,
                lax.dynamic_slice_in_dim(piece, (here + k) % planes * columns, columns, axis=1),
            ],
            axis=0,
        )
        for k in range(1, planes)
    ]

    def shard(plane):
        start = (plane + planes) % planes * depth
        return lax.dynamic_slice_in_dim(weight, start, depth, axis=1)

    opposite = planes // 2
    half_rows = token_rows // 2
    right, left, begun, weights = [tokens], [tokens], [], [shard(here)]
    for step in range(1, opposite + 1):
        if step < opposite:
            moved = (turned(right[-1]), turned(left[-1], planes - 1))
            ahead = (here - step, here + step)
        else:
            moved = (turned(right[-1][:half_rows]), turned(left[-1][half_rows:], planes - 1))
            ahead = (here - step,)
        for tokens_of, weight_of in zip((right[-1], left[-1]), weights):
            begun = [project(tokens_of, weight_of, begun)]
        side = ()
        if step == 1:
            lines = [turned(send, k) for k, send in enumerate(sends, 1)]
            sums = shrink_partial(adapters, here, planes, table, tokens, down_all)
            sums = [sums[0]] + [turned(sums[k], k) for k in range(1, planes)]
            out_up_all = lax.all_gather(after(output_up_maps, sums[0]), "dp", axis=0, tiled=True)
            own_down = lax.all_gather(after(out_down, sums[0]), "dp", axis=0)
            side = (lines, sums, out_up_all, own_down, table, turn, up_all, own_rows)
        elif step == 2:
            shrink = sum(sums[1:], sums[0]).astype(jnp.bfloat16)
            side = [shrink] + [turned(shrink, k) for k in range(1, planes)]
        weights = [shard(plane) for plane in ahead]
        moved, begun, weights, side = lax.optimization_barrier((moved, begun, weights, side))
        if step == 1:
            lines, sums, out_up_all, own_down, table, turn, up_all, own_rows = side
            lines = lax.all_gather(jnp.stack(lines), PLANE, axis=0)
        elif step == 2:
            shrink = side
        right.append(moved[0])
        left.append(moved[1])

    ids = jnp.concatenate([lax.axis_index("groups")[None], adapters])
    made, earlier = [], ()
    for part in range(2):
        own, *earlier = attend(
            planes_of, adapters, part, table, turn, up_all, shrink, moved[part], weights[0],
            begun[0], earlier,
        )
        made.append([(own,)])
        for step in range(1, opposite):
            source = made[part][-1]
            made[part].append((turned(source[0]), turned(source[-1], planes - 1)))
        source = made[part][-1][part]
        made[part].append((turned(source, (1, planes - 1)[part]),))
    lines = [lines[:, k] for k in range(planes - 1)]
    sums, before = [(), ()], []
    for step in range(opposite + 1):
        for part in range(2):
            arrived = made[part][step]
            for way, array in enumerate(arrived):
                last = step == opposite
                turn_of = (step, planes - step)[way]
                sums[part] = project_out(
                    ids, rank, array, lines[turn_of - 1] if step else own_rows,
                    pool if step else own_down, list(sums[part]),
                    [table, out_up_all, *before] if last else [], part,
                )
                if last:
                    before = [sums[part]]
    return before[0]


def solution(mesh):
    in_specs = (
        P(PLANE, "tensor"),
        P(None, None, "tensor"),
        P("tensor", None, None),
        P(PLANE, None, "tensor"),
        P(PLANE, None, None, "tensor"),
        P(PLANE, None, None, "tensor"),
        P(PLANE, None, "tensor"),
        P(PLANE, None),
        P(PLANE, None),
    )
    function = functools.partial(
        local, mesh.shape["groups"] * mesh.shape["dp"], mesh.shape["tensor"]
    )
    return jax.shard_map(
        function, mesh=mesh, in_specs=in_specs, out_specs=P(PLANE, "tensor"), check_vma=False
    )
```

```python
import functools
import math

import jax
import jax.numpy as jnp
from jax import lax
from jax.experimental import pallas as pl
from jax.experimental.pallas import tpu as pltpu
from jax.sharding import PartitionSpec as P

VMEM_BYTES = 40 * 1024 * 1024
PLANE = ("groups", "dp")


def after(value, *earlier):
    return lax.optimization_barrier((value,) + earlier)[0]


def fixed(array):
    shape = array.shape
    return pl.BlockSpec(shape, lambda step, ids: (0,) * len(shape))


def call(kernel, name, ids, grid, specs, arrays, out, scratch=()):
    total = sum(array.size * array.dtype.itemsize for array in arrays)
    return pl.pallas_call(
        kernel,
        out_shape=out,
        grid_spec=pltpu.PrefetchScalarGridSpec(
            num_scalar_prefetch=1,
            grid=(grid,),
            in_specs=[fixed(array) if spec is None else spec for spec, array in zip(specs, arrays)],
            out_specs=[fixed(item) for item in out] if isinstance(out, tuple) else fixed(out),
            scratch_shapes=list(scratch),
        ),
        compiler_params=pltpu.CompilerParams(vmem_limit_bytes=VMEM_BYTES),
        cost_estimate=pl.CostEstimate(flops=0, bytes_accessed=3 * total, transcendentals=0),
        name=name,
    )(ids.astype(jnp.int32), *arrays)


def accumulate(acc_ref, token_ref, w_ref, first):
    slots, _, head_size = w_ref.shape
    for pair in range(slots // 2):
        columns = slice(2 * pair * head_size, (2 * pair + 2) * head_size)
        weight = jnp.concatenate([w_ref[2 * pair], w_ref[2 * pair + 1]], axis=1)
        total = jnp.dot(token_ref[...], weight, preferred_element_type=jnp.float32)
        acc_ref[:, columns] = total if first is None else first[:, columns] + total


def project_kernel(begun, ids_ref, token_ref, w_ref, *refs):
    accumulate(refs[-1], token_ref, w_ref, refs[0] if begun else None)


def rows_spec(array, rows, part):
    if array.shape[0] == rows:
        return None
    return pl.BlockSpec((rows, array.shape[1]), lambda step, ids: (part, 0))


def project(tokens, weight, begun=()):
    slots, _, head_size = weight.shape
    return call(
        functools.partial(project_kernel, len(begun)),
        "project",
        jnp.zeros(1),
        1,
        [None] * (2 + len(begun)),
        [tokens, weight, *begun],
        jax.ShapeDtypeStruct((tokens.shape[0], slots * head_size), jnp.float32),
    )


def attend_kernel(planes, earlier, ids_ref, table_ref, turn_ref, up_ref, *refs):
    piece_refs, refs = refs[:planes], refs[planes:]
    token_ref, w_ref, begun_ref, refs = refs[0], refs[1], refs[2], refs[3:]
    earlier_refs, refs = refs[: 2 * earlier], refs[2 * earlier :]
    out_ref, keys_ref, values_ref, acc_ref, shrink_ref = refs
    for number, piece_ref in enumerate(piece_refs):
        size = piece_ref.shape[0]
        shrink_ref[pl.ds(pl.multiple_of(ids_ref[number] * size, size), size), :] = piece_ref[...]
    accumulate(acc_ref, token_ref, w_ref, begun_ref)
    slots, _, head_size = w_ref.shape
    rank = up_ref.shape[2]
    count = ids_ref.shape[0] - planes
    rows = acc_ref.shape[0]
    first_row = earlier_refs[0].shape[0] if earlier else 0
    queries = slots - 2
    lane = lax.broadcasted_iota(jnp.int32, (rows, count * rank), 1)
    kept = (lane >= table_ref[:, 1:2]) & (lane < table_ref[:, 1:2] + rank)
    lows = []
    for part in range(3):
        piece = shrink_ref[first_row : first_row + rows, part * rank : (part + 1) * rank]
        piece = jnp.concatenate([piece.astype(jnp.float32)] * count, axis=1)
        lows.append(jnp.where(kept, piece, 0.0).astype(jnp.bfloat16))

    def slot(index):
        low = lows[0 if index < queries else index - queries + 1]
        up = jnp.concatenate([up_ref[ids_ref[planes + j], index] for j in range(count)], axis=0)
        extra = jnp.dot(low, up, preferred_element_type=jnp.float32)
        return acc_ref[:, index * head_size : (index + 1) * head_size] + extra

    def rotated(index):
        value = slot(index)
        turned = pltpu.roll(value, head_size // 2, 1)
        return (value * turn_ref[:, :head_size] + turned * turn_ref[:, head_size:]).astype(
            jnp.bfloat16
        )

    keys = rotated(queries)
    values = slot(queries + 1).astype(jnp.bfloat16)
    keys_ref[...] = keys
    values_ref[...] = values
    if earlier:
        keys = jnp.concatenate([earlier_refs[0][...], keys], axis=0)
        values = jnp.concatenate([earlier_refs[1][...], values], axis=0)
    shape = (rows, keys.shape[0])
    key_at = lax.broadcasted_iota(jnp.int32, shape, 1)
    row_at = lax.broadcasted_iota(jnp.int32, shape, 0) + first_row
    allowed = (key_at >= table_ref[:, 0:1]) & (key_at <= row_at)
    for index in range(queries):
        scores = lax.dot_general(
            rotated(index), keys, (((1,), (1,)), ((), ())), preferred_element_type=jnp.float32
        )
        scores = jnp.where(allowed, scores * (1.0 / math.sqrt(head_size)), -1e30)
        weights = jnp.exp(scores - jnp.max(scores, axis=1, keepdims=True))
        scale = 1.0 / jnp.sum(weights, axis=1, keepdims=True)
        attended = jnp.dot(
            (weights * scale).astype(jnp.bfloat16), values, preferred_element_type=jnp.float32
        )
        out_ref[:, index * head_size : (index + 1) * head_size] = attended.astype(jnp.bfloat16)


def attend(planes_of, adapters, part, table, turn, up, shrink, tokens, weight, begun, earlier):
    rows = tokens.shape[0] // 2
    slots, _, head_size = weight.shape
    planes = len(shrink)
    arrays = [table, turn, up, *shrink, tokens, weight, begun, *earlier]
    specs = [None] * len(arrays)
    for index in (0, 1, 3 + planes, 5 + planes):
        specs[index] = rows_spec(arrays[index], rows, part)
    return call(
        functools.partial(attend_kernel, planes, len(earlier) // 2),
        "attend",
        jnp.concatenate([planes_of, adapters]),
        1,
        specs,
        arrays,
        (
            jax.ShapeDtypeStruct((rows, (slots - 2) * head_size), jnp.bfloat16),
            jax.ShapeDtypeStruct((rows, head_size), jnp.bfloat16),
            jax.ShapeDtypeStruct((rows, head_size), jnp.bfloat16),
        ),
        [
            pltpu.VMEM((rows, slots * head_size), jnp.float32),
            pltpu.VMEM((planes * shrink[0].shape[0], shrink[0].shape[1]), jnp.bfloat16),
        ],
    )


def shrink_kernel(planes, ids_ref, table_ref, token_ref, down_ref, *refs):
    out_refs, acc_ref = refs[:planes], refs[planes]
    step = pl.program_id(0)
    count = ids_ref.shape[0] - 1
    part = lax.dot_general(
        token_ref[...], down_ref[0], (((1,), (1,)), ((), ())), preferred_element_type=jnp.float32
    )
    rank = part.shape[1] // 3
    part = jnp.where(table_ref[:, 1:2] == step * rank, part, 0.0)

    @pl.when(step == 0)
    def _():
        acc_ref[...] = part

    @pl.when(step > 0)
    def _():
        acc_ref[...] += part

    @pl.when(step == count - 1)
    def _():
        for turn, out_ref in enumerate(out_refs):
            rows = out_ref.shape[0]
            plane = lax.rem(ids_ref[count] + turn, planes)
            out_ref[...] = acc_ref[pl.ds(pl.multiple_of(plane * rows, rows), rows), :]


def shrink_partial(adapters, here, planes, table, tokens, down):
    _, width, depth = down.shape
    rows = tokens.shape[0]
    return call(
        functools.partial(shrink_kernel, planes),
        "shrink",
        jnp.concatenate([adapters, here[None]]),
        adapters.shape[0],
        [None, None, pl.BlockSpec((1, width, depth), lambda step, ids: (ids[step], 0, 0))],
        [table, tokens, down],
        (jax.ShapeDtypeStruct((rows // planes, width), jnp.float32),) * planes,
        [pltpu.VMEM((rows, width), jnp.float32)],
    )


def output_kernel(begun, last, lines, ids_ref, attended_ref, w_ref, down_ref, *refs):
    begun_refs, rest = refs[:begun], refs[begun:]
    if last:
        table_ref, up_ref, before_refs, out_ref = rest[0], rest[1], rest[2:-1], rest[-1]
    else:
        acc_ref, low_ref = rest
    count = ids_ref.shape[0] - 1
    attended = attended_ref[...]
    features = attended.shape[1]
    if lines:
        weight = jnp.concatenate([w_ref[i, lines:] for i in range(w_ref.shape[0])], axis=0)
    else:
        weight = w_ref[...]
    downs = []
    for j in range(count):
        down = down_ref[ids_ref[1 + j]]
        downs += [down[:, at : at + features] for at in range(0, down.shape[1], features)]
    down = jnp.concatenate(downs, axis=0)
    rank = down.shape[0] // count
    total = jnp.dot(attended, weight, preferred_element_type=jnp.float32)
    low = lax.dot_general(
        attended, down, (((1,), (1,)), ((), ())), preferred_element_type=jnp.float32
    )
    if begun:
        total, low = begun_refs[0][...] + total, begun_refs[1][...] + low
    if last:
        low = low.astype(jnp.bfloat16).astype(jnp.float32)
        lane = lax.broadcasted_iota(jnp.int32, low.shape, 1)
        kept = (lane >= table_ref[:, 1:2]) & (lane < table_ref[:, 1:2] + rank)
        low = jnp.where(kept, low, 0.0).astype(jnp.bfloat16)
        up = jnp.concatenate([up_ref[ids_ref[1 + j]] for j in range(count)], axis=0)
        extra = jnp.dot(low, up, preferred_element_type=jnp.float32)
        first_row = out_ref.shape[0] - total.shape[0]
        for before_ref in before_refs:
            out_ref[:first_row, :] = before_ref[...]
        out_ref[first_row:, :] = (total + extra).astype(jnp.bfloat16)
    else:
        acc_ref[...] = total
        low_ref[...] = low


def project_out(ids, rank, attended, weight, down, begun, final, part=0):
    rows, features = attended.shape
    columns = weight.shape[-1]
    if len(weight.shape) == 2:
        down_spec, down_rows = None, 0
    else:
        down_rows = rank * features // columns
        down_spec = pl.BlockSpec(
            (down, down_rows, columns), lambda step, ids: (ids[0], 0, 0)
        )
        down = weight
    sums = (
        jax.ShapeDtypeStruct((rows, columns), jnp.float32),
        jax.ShapeDtypeStruct((rows, (ids.shape[0] - 1) * rank), jnp.float32),
    )
    all_rows = rows + sum(item.shape[0] for item in final[2:])
    return call(
        functools.partial(output_kernel, len(begun), bool(final), down_rows),
        "project_out",
        ids,
        1,
        [None, None, down_spec] + [None] * len(begun)
        + [rows_spec(table, rows, part) for table in final[:1]] + [None] * len(final[1:]),
        [attended, weight, down, *begun, *final],
        jax.ShapeDtypeStruct((all_rows, columns), jnp.bfloat16) if final else sums,
    )


def local(
    plane_size,
    planes,
    tokens,
    query_key_value_weight,
    output_weight,
    adapter_down_maps,
    adapter_up_maps,
    output_down_maps,
    output_up_maps,
    request_adapter,
    lengths,
):
    token_rows, depth = tokens.shape
    _, slots, head_size = query_key_value_weight.shape
    queries = slots - 2
    pool, rank = plane_size // lax.axis_size("groups"), adapter_up_maps.shape[1]
    features = queries * head_size
    columns = output_weight.shape[2] // planes
    here = lax.axis_index("tensor")
    place = lax.axis_index(PLANE)
    planes_of = (here - jnp.arange(planes) + planes) % planes

    def turned(value, turn=1):
        return lax.ppermute(value, "tensor", [(i, (i + turn) % planes) for i in range(planes)])

    weight = jnp.transpose(query_key_value_weight, (1, 0, 2))
    down_all = lax.all_gather(adapter_down_maps, "dp", axis=0, tiled=True)
    up_all = lax.all_gather(jnp.transpose(adapter_up_maps[0], (1, 0, 2)), "dp", axis=0)

    requests = request_adapter.shape[1]
    request_ends = jnp.cumsum(lengths[0])
    request_starts = request_ends - lengths[0]
    at = jnp.arange(token_rows, dtype=jnp.int32)
    member = (at[:, None] >= request_starts[None, :]) & (at[:, None] < request_ends[None, :])
    if pool <= requests:
        adapters, label = jnp.arange(pool), request_adapter[0]
    else:
        adapters, label = request_adapter[0], jnp.arange(requests)
    wanted = jnp.stack([request_starts, label * rank], axis=0)
    table = jnp.sum(jnp.where(member[:, None, :], wanted[None], 0), axis=2).astype(jnp.int32)
    position = at - table[:, 0]
    half = head_size // 2
    inv_freq = 10000.0 ** (-2.0 * jnp.arange(half, dtype=jnp.float32) / head_size)
    angles = position.astype(jnp.float32)[:, None] * inv_freq[None, :]
    cosine, sine = jnp.cos(angles), jnp.sin(angles)
    turn = jnp.concatenate([cosine, cosine, -sine, sine], axis=1)

    own_rows = jnp.transpose(
        lax.dynamic_slice_in_dim(output_weight, here * columns, columns, axis=2), (1, 0, 2)
    ).reshape(features, columns)
    share = features // plane_size
    line = place * share
    piece = lax.dynamic_slice(
        output_weight, (line % head_size, line // head_size, 0),
        (share, 1, output_weight.shape[2]),
    )[:, 0]
    out_down = output_down_maps[0].reshape(rank, features)
    out_down = jnp.concatenate(jnp.split(out_down, columns // features, axis=0), axis=1)
    sends = [
        jnp.concatenate(
            [
                out_down,
                lax.dynamic_slice_in_dim(piece, (here + k) % planes * columns, columns, axis=1),
            ],
            axis=0,
        )
        for k in range(1, planes)
    ]

    def shard(plane):
        start = (plane + planes) % planes * depth
        return lax.dynamic_slice_in_dim(weight, start, depth, axis=1)

    opposite = planes // 2
    right, left, begun, weights = [tokens], [tokens], [], [shard(here)]
    for step in range(1, opposite + 1):
        if step < opposite:
            moved = (turned(right[-1]), turned(left[-1], planes - 1))
            ahead = (here - step, here + step)
        else:
            moved = (turned(right[-1]),)
            ahead = (here - step,)
        for tokens_of, weight_of in zip((right[-1], left[-1]), weights):
            begun = [project(tokens_of, weight_of, begun)]
        side = ()
        if step == 1:
            lines = [turned(send, k) for k, send in enumerate(sends, 1)]
            sums = shrink_partial(adapters, here, planes, table, tokens, down_all)
            sums = [sums[0]] + [turned(sums[k], k) for k in range(1, planes)]
            out_up_all = lax.all_gather(after(output_up_maps, sums[0]), "dp", axis=0, tiled=True)
            own_down = lax.all_gather(after(out_down, sums[0]), "dp", axis=0)
            side = (jnp.stack(lines), sums, out_up_all, own_down, table, turn, up_all, own_rows)
        elif step == 2:
            shrink = sum(sums[1:], sums[0]).astype(jnp.bfloat16)
            side = [shrink] + [turned(shrink, k) for k in range(1, planes)]
        weights = [shard(plane) for plane in ahead]
        moved, begun, weights, side = lax.optimization_barrier((moved, begun, weights, side))
        if step == 1:
            lines, sums, out_up_all, own_down, table, turn, up_all, own_rows = side
            lines = lax.all_gather(lines, PLANE, axis=0)
        elif step == 2:
            shrink = side
        right.append(moved[0])
        left.append(moved[-1])

    ids = jnp.concatenate([lax.axis_index("groups")[None], adapters])
    lines = [lines[:, k] for k in range(planes - 1)]
    made, earlier = [], ()
    for part in range(2):
        own, *earlier = attend(
            planes_of, adapters, part, table, turn, up_all, shrink, right[-1], weights[0],
            begun[0], earlier,
        )
        first = [*made[0][1], *lines] if part else []
        made.append([(own,)])
        for step in range(1, opposite):
            source = made[part][-1]
            made[part].append(
                (turned(source[0]), turned(after(source[-1], *first), planes - 1))
            )
            first = []
        made[part].append((turned(made[part][-1][part], (1, planes - 1)[part]),))
    sums, before = [(), ()], []
    for step in range(opposite + 1):
        for part in range(2):
            arrived = made[part][step]
            for way, array in enumerate(arrived):
                last = step == opposite
                turn_of = (step, planes - step)[way]
                sums[part] = project_out(
                    ids, rank, array, lines[turn_of - 1] if step else own_rows,
                    pool if step else own_down, list(sums[part]),
                    [table, out_up_all, *before] if last else [], part,
                )
                if last:
                    before = [sums[part]]
    return before[0]


def solution(mesh):
    in_specs = (
        P(PLANE, "tensor"),
        P(None, None, "tensor"),
        P("tensor", None, None),
        P(PLANE, None, "tensor"),
        P(PLANE, None, None, "tensor"),
        P(PLANE, None, None, "tensor"),
        P(PLANE, None, "tensor"),
        P(PLANE, None),
        P(PLANE, None),
    )
    function = functools.partial(
        local, mesh.shape["groups"] * mesh.shape["dp"], mesh.shape["tensor"]
    )
    return jax.shard_map(
        function, mesh=mesh, in_specs=in_specs, out_specs=P(PLANE, "tensor"), check_vma=False
    )
```

```python
import functools
import math

import jax
import jax.numpy as jnp
from jax import lax
from jax.experimental import pallas as pl
from jax.experimental.pallas import tpu as pltpu
from jax.sharding import PartitionSpec as P

VMEM_BYTES = 40 * 1024 * 1024
PLANE = ("groups", "dp")


def after(value, *earlier):
    return lax.optimization_barrier((value,) + earlier)[0]


def fixed(array):
    shape = array.shape
    return pl.BlockSpec(shape, lambda step, ids: (0,) * len(shape))


def call(kernel, name, ids, grid, specs, arrays, out, scratch=()):
    total = sum(array.size * array.dtype.itemsize for array in arrays)
    return pl.pallas_call(
        kernel,
        out_shape=out,
        grid_spec=pltpu.PrefetchScalarGridSpec(
            num_scalar_prefetch=1,
            grid=(grid,),
            in_specs=[fixed(array) if spec is None else spec for spec, array in zip(specs, arrays)],
            out_specs=[fixed(item) for item in out] if isinstance(out, tuple) else fixed(out),
            scratch_shapes=list(scratch),
        ),
        compiler_params=pltpu.CompilerParams(vmem_limit_bytes=VMEM_BYTES),
        cost_estimate=pl.CostEstimate(flops=0, bytes_accessed=3 * total, transcendentals=0),
        name=name,
    )(ids.astype(jnp.int32), *arrays)


def accumulate(acc_ref, token_ref, w_ref, first):
    slots, _, head_size = w_ref.shape
    for pair in range(slots // 2):
        columns = slice(2 * pair * head_size, (2 * pair + 2) * head_size)
        weight = jnp.concatenate([w_ref[2 * pair], w_ref[2 * pair + 1]], axis=1)
        total = jnp.dot(token_ref[...], weight, preferred_element_type=jnp.float32)
        acc_ref[:, columns] = total if first is None else first[:, columns] + total


def project_kernel(begun, ids_ref, token_ref, w_ref, *refs):
    accumulate(refs[-1], token_ref, w_ref, refs[0] if begun else None)


def rows_spec(array, rows, part):
    if array.shape[0] == rows:
        return None
    return pl.BlockSpec((rows, array.shape[1]), lambda step, ids: (part, 0))


def project(ids, tokens, weight, begun=()):
    slots, _, head_size = weight.shape
    return call(
        functools.partial(project_kernel, len(begun)),
        "project",
        ids,
        1,
        [None] * (2 + len(begun)),
        [tokens, weight, *begun],
        jax.ShapeDtypeStruct((tokens.shape[0], slots * head_size), jnp.float32),
    )


def attend_kernel(planes, earlier, ids_ref, table_ref, turn_ref, up_ref, *refs):
    piece_refs, refs = refs[:planes], refs[planes:]
    token_ref, w_ref, begun_ref, refs = refs[0], refs[1], refs[2], refs[3:]
    earlier_refs, refs = refs[: 2 * earlier], refs[2 * earlier :]
    out_ref, keys_ref, values_ref, acc_ref, shrink_ref = refs
    for number, piece_ref in enumerate(piece_refs):
        width = piece_ref.shape[1]
        size = piece_ref.shape[0] * 2 // 3
        start = pl.multiple_of(ids_ref[number] * size, size)
        shrink_ref[pl.ds(start, size), :width] = piece_ref[:size, :]
        shrink_ref[pl.ds(start, size // 2), width:] = piece_ref[size:, : width // 2]
        shrink_ref[pl.ds(start + size // 2, size // 2), width:] = piece_ref[size:, width // 2 :]
    accumulate(acc_ref, token_ref, w_ref, begun_ref)
    slots, _, head_size = w_ref.shape
    rank = up_ref.shape[2]
    count = ids_ref.shape[0] - planes
    rows = acc_ref.shape[0]
    first_row = earlier_refs[0].shape[0] if earlier else 0
    queries = slots - 2
    lane = lax.broadcasted_iota(jnp.int32, (rows, count * rank), 1)
    kept = (lane >= table_ref[:, 1:2]) & (lane < table_ref[:, 1:2] + rank)
    lows = []
    for part in range(3):
        piece = shrink_ref[first_row : first_row + rows, part * rank : (part + 1) * rank]
        piece = jnp.concatenate([piece.astype(jnp.float32)] * count, axis=1)
        lows.append(jnp.where(kept, piece, 0.0).astype(jnp.bfloat16))

    def slot(index):
        low = lows[0 if index < queries else index - queries + 1]
        up = jnp.concatenate([up_ref[ids_ref[planes + j], index] for j in range(count)], axis=0)
        extra = jnp.dot(low, up, preferred_element_type=jnp.float32)
        return acc_ref[:, index * head_size : (index + 1) * head_size] + extra

    def rotated(index):
        value = slot(index)
        turned = pltpu.roll(value, head_size // 2, 1)
        return (value * turn_ref[:, :head_size] + turned * turn_ref[:, head_size:]).astype(
            jnp.bfloat16
        )

    keys = rotated(queries)
    values = slot(queries + 1).astype(jnp.bfloat16)
    keys_ref[...] = keys
    values_ref[...] = values
    if earlier:
        keys = jnp.concatenate([earlier_refs[0][...], keys], axis=0)
        values = jnp.concatenate([earlier_refs[1][...], values], axis=0)
    shape = (rows, keys.shape[0])
    key_at = lax.broadcasted_iota(jnp.int32, shape, 1)
    row_at = lax.broadcasted_iota(jnp.int32, shape, 0) + first_row
    allowed = (key_at >= table_ref[:, 0:1]) & (key_at <= row_at)
    for index in range(queries):
        scores = lax.dot_general(
            rotated(index), keys, (((1,), (1,)), ((), ())), preferred_element_type=jnp.float32
        )
        scores = jnp.where(allowed, scores * (1.0 / math.sqrt(head_size)), -1e30)
        weights = jnp.exp(scores - jnp.max(scores, axis=1, keepdims=True))
        scale = 1.0 / jnp.sum(weights, axis=1, keepdims=True)
        attended = jnp.dot(
            (weights * scale).astype(jnp.bfloat16), values, preferred_element_type=jnp.float32
        )
        out_ref[:, index * head_size : (index + 1) * head_size] = attended.astype(jnp.bfloat16)


def attend(planes_of, adapters, part, table, turn, up, shrink, tokens, weight, begun, earlier):
    rows = tokens.shape[0] // 2
    slots, _, head_size = weight.shape
    planes = len(shrink)
    arrays = [table, turn, up, *shrink, tokens, weight, begun, *earlier]
    specs = [None] * len(arrays)
    for index in (0, 1, 3 + planes, 5 + planes):
        specs[index] = rows_spec(arrays[index], rows, part)
    return call(
        functools.partial(attend_kernel, planes, len(earlier) // 2),
        "attend",
        jnp.concatenate([planes_of, adapters]),
        1,
        specs,
        arrays,
        (
            jax.ShapeDtypeStruct((rows, (slots - 2) * head_size), jnp.bfloat16),
            jax.ShapeDtypeStruct((rows, head_size), jnp.bfloat16),
            jax.ShapeDtypeStruct((rows, head_size), jnp.bfloat16),
        ),
        [
            pltpu.VMEM((rows, slots * head_size), jnp.float32),
            pltpu.VMEM(
                (planes * shrink[0].shape[0] * 2 // 3, shrink[0].shape[1] * 3 // 2), jnp.bfloat16
            ),
        ],
    )


def shrink_kernel(planes, ids_ref, table_ref, token_ref, down_ref, *refs):
    out_refs, acc_ref = refs[:planes], refs[planes]
    step = pl.program_id(0)
    count = ids_ref.shape[0] - 1
    part = lax.dot_general(
        token_ref[...], down_ref[0], (((1,), (1,)), ((), ())), preferred_element_type=jnp.float32
    )
    rank = part.shape[1] // 3
    part = jnp.where(table_ref[:, 1:2] == step * rank, part, 0.0)

    @pl.when(step == 0)
    def _():
        acc_ref[...] = part

    @pl.when(step > 0)
    def _():
        acc_ref[...] += part

    @pl.when(step == count - 1)
    def _():
        for turn, out_ref in enumerate(out_refs):
            rows = out_ref.shape[0] * 2 // 3
            plane = lax.rem(ids_ref[count] + turn, planes)
            piece = acc_ref[pl.ds(pl.multiple_of(plane * rows, rows), rows), :]
            out_ref[:rows, :] = piece[:, : 2 * rank]
            out_ref[rows:, :] = jnp.concatenate(
                [piece[: rows // 2, 2 * rank :], piece[rows // 2 :, 2 * rank :]], axis=1
            )


def shrink_partial(adapters, here, planes, table, tokens, down):
    _, width, depth = down.shape
    rows = tokens.shape[0]
    return call(
        functools.partial(shrink_kernel, planes),
        "shrink",
        jnp.concatenate([adapters, here[None]]),
        adapters.shape[0],
        [None, None, pl.BlockSpec((1, width, depth), lambda step, ids: (ids[step], 0, 0))],
        [table, tokens, down],
        (jax.ShapeDtypeStruct((rows // planes * 3 // 2, width * 2 // 3), jnp.float32),) * planes,
        [pltpu.VMEM((rows, width), jnp.float32)],
    )


def output_kernel(begun, last, lines, ids_ref, attended_ref, w_ref, down_ref, *refs):
    begun_refs, rest = refs[:begun], refs[begun:]
    if last:
        table_ref, up_ref, before_refs, out_ref = rest[0], rest[1], rest[2:-1], rest[-1]
    else:
        acc_ref, low_ref = rest
    count = ids_ref.shape[0] - 1
    attended = attended_ref[...]
    features = attended.shape[1]
    if lines:
        weight = jnp.concatenate([w_ref[i, lines:] for i in range(w_ref.shape[0])], axis=0)
    else:
        weight = w_ref[...]
    downs = []
    for j in range(count):
        down = down_ref[ids_ref[1 + j]]
        downs += [down[:, at : at + features] for at in range(0, down.shape[1], features)]
    down = jnp.concatenate(downs, axis=0)
    rank = down.shape[0] // count
    total = jnp.dot(attended, weight, preferred_element_type=jnp.float32)
    low = lax.dot_general(
        attended, down, (((1,), (1,)), ((), ())), preferred_element_type=jnp.float32
    )
    if begun:
        total, low = begun_refs[0][...] + total, begun_refs[1][...] + low
    if last:
        low = low.astype(jnp.bfloat16).astype(jnp.float32)
        lane = lax.broadcasted_iota(jnp.int32, low.shape, 1)
        kept = (lane >= table_ref[:, 1:2]) & (lane < table_ref[:, 1:2] + rank)
        low = jnp.where(kept, low, 0.0).astype(jnp.bfloat16)
        up = jnp.concatenate([up_ref[ids_ref[1 + j]] for j in range(count)], axis=0)
        extra = jnp.dot(low, up, preferred_element_type=jnp.float32)
        first_row = out_ref.shape[0] - total.shape[0]
        for before_ref in before_refs:
            out_ref[:first_row, :] = before_ref[...]
        out_ref[first_row:, :] = (total + extra).astype(jnp.bfloat16)
    else:
        acc_ref[...] = total
        low_ref[...] = low


def project_out(ids, rank, attended, weight, down, begun, final, part=0):
    rows, features = attended.shape
    columns = weight.shape[-1]
    if len(weight.shape) == 2:
        down_spec, down_rows = None, 0
    else:
        down_rows = rank * features // columns
        down_spec = pl.BlockSpec(
            (down, down_rows, columns), lambda step, ids: (ids[0], 0, 0)
        )
        down = weight
    sums = (
        jax.ShapeDtypeStruct((rows, columns), jnp.float32),
        jax.ShapeDtypeStruct((rows, (ids.shape[0] - 1) * rank), jnp.float32),
    )
    all_rows = rows + sum(item.shape[0] for item in final[2:])
    return call(
        functools.partial(output_kernel, len(begun), bool(final), down_rows),
        "project_out",
        ids,
        1,
        [None, None, down_spec] + [None] * len(begun)
        + [rows_spec(table, rows, part) for table in final[:1]] + [None] * len(final[1:]),
        [attended, weight, down, *begun, *final],
        jax.ShapeDtypeStruct((all_rows, columns), jnp.bfloat16) if final else sums,
    )


def local(
    plane_size,
    planes,
    tokens,
    query_key_value_weight,
    output_weight,
    adapter_down_maps,
    adapter_up_maps,
    output_down_maps,
    output_up_maps,
    request_adapter,
    lengths,
):
    token_rows, depth = tokens.shape
    _, slots, head_size = query_key_value_weight.shape
    queries = slots - 2
    pool, rank = plane_size // lax.axis_size("groups"), adapter_up_maps.shape[1]
    features = queries * head_size
    columns = output_weight.shape[2] // planes
    here = lax.axis_index("tensor")
    place = lax.axis_index(PLANE)
    planes_of = (here - jnp.arange(planes) + planes) % planes

    def turned(value, turn=1):
        return lax.ppermute(value, "tensor", [(i, (i + turn) % planes) for i in range(planes)])

    held = [tokens, turned(tokens)]
    weight = jnp.transpose(query_key_value_weight, (1, 0, 2))
    down_all = lax.all_gather(adapter_down_maps, "dp", axis=0, tiled=True)
    up_all = lax.all_gather(jnp.transpose(adapter_up_maps[0], (1, 0, 2)), "dp", axis=0)

    requests = request_adapter.shape[1]
    request_ends = jnp.cumsum(lengths[0])
    request_starts = request_ends - lengths[0]
    at = jnp.arange(token_rows, dtype=jnp.int32)
    member = (at[:, None] >= request_starts[None, :]) & (at[:, None] < request_ends[None, :])
    if pool <= requests:
        adapters, label = jnp.arange(pool), request_adapter[0]
    else:
        adapters, label = request_adapter[0], jnp.arange(requests)
    wanted = jnp.stack([request_starts, label * rank], axis=0)
    table = jnp.sum(jnp.where(member[:, None, :], wanted[None], 0), axis=2).astype(jnp.int32)
    position = at - table[:, 0]
    half = head_size // 2
    inv_freq = 10000.0 ** (-2.0 * jnp.arange(half, dtype=jnp.float32) / head_size)
    angles = position.astype(jnp.float32)[:, None] * inv_freq[None, :]
    cosine, sine = jnp.cos(angles), jnp.sin(angles)
    turn = jnp.concatenate([cosine, cosine, -sine, sine], axis=1)

    own_rows = jnp.transpose(
        lax.dynamic_slice_in_dim(output_weight, here * columns, columns, axis=2), (1, 0, 2)
    ).reshape(features, columns)
    share = features // plane_size
    line = place * share
    piece = lax.dynamic_slice(
        output_weight, (line % head_size, line // head_size, 0),
        (share, 1, output_weight.shape[2]),
    )[:, 0]
    out_down = output_down_maps[0].reshape(rank, features)
    out_down = jnp.concatenate(jnp.split(out_down, columns // features, axis=0), axis=1)
    sends = [
        jnp.concatenate(
            [
                out_down,
                lax.dynamic_slice_in_dim(piece, (here + k) % planes * columns, columns, axis=1),
            ],
            axis=0,
        )
        for k in range(1, planes)
    ]

    def shard(number):
        start = planes_of[number] * depth
        return lax.dynamic_slice_in_dim(weight, start, depth, axis=1)

    lines = [turned(send, k) for k, send in enumerate(sends, 1)]
    begun = project(planes_of[:1], tokens, shard(0))
    sums = shrink_partial(adapters, here, planes, table, tokens, down_all)
    done = (held[1], lines, begun, table, turn, up_all, own_rows, shard(1), sums)
    done = lax.optimization_barrier(done)
    held[1], lines, begun, table, turn, up_all, own_rows, part_weight, sums = done
    lines = lax.all_gather(jnp.stack(lines), PLANE, axis=0)
    for step in range(2, planes):
        arrived = held[-1]
        held.append(turned(arrived))
        begun = project(planes_of[step - 1 : step], arrived, part_weight, [begun])
        side = ()
        if step == 2:
            sums = [sums[0]] + [turned(sums[k], k) for k in range(1, planes)]
            side = (
                sums,
                lax.all_gather(after(output_up_maps, sums[0]), "dp", axis=0, tiled=True),
                lax.all_gather(after(out_down, sums[0]), "dp", axis=0),
            )
        elif step == 3:
            shrink = sum(sums[1:], sums[0]).astype(jnp.bfloat16)
            shrink = [shrink] + [turned(shrink, k) for k in range(1, planes)]
            side = (shrink, [lines[:, k] for k in range(planes - 1)])
        done = lax.optimization_barrier((held[-1], begun, shard(step), side))
        held[-1], begun, part_weight, side = done
        if step == 2:
            sums, out_up_all, own_down = side
        elif step == 3:
            shrink, lines = side

    ids = jnp.concatenate([lax.axis_index("groups")[None], adapters])
    attended, earlier = [[], []], ()
    for part in range(2):
        made, *earlier = attend(
            planes_of, adapters, part, table, turn, up_all, shrink, held[-1], part_weight,
            begun, earlier,
        )
        attended[part] = [made, turned(after(made, *attended[0][1:]))]
    sums = [
        project_out(ids, rank, attended[part][0], own_rows, own_down, [], []) for part in range(2)
    ]
    before = []
    for step in range(2, planes + 1):
        for part in range(2):
            arrived = attended[part][-1]
            if step < planes:
                ahead = [*attended[0][step:], *sums[part]]
                attended[part].append(turned(after(arrived, *ahead)))
            final = [] if step < planes else [table, out_up_all, *before]
            sums[part] = project_out(
                ids, rank, arrived, lines[step - 2], pool, list(sums[part]), final, part
            )
            if final:
                before = [sums[part]]
    return before[0]


def solution(mesh):
    in_specs = (
        P(PLANE, "tensor"),
        P(None, None, "tensor"),
        P("tensor", None, None),
        P(PLANE, None, "tensor"),
        P(PLANE, None, None, "tensor"),
        P(PLANE, None, None, "tensor"),
        P(PLANE, None, "tensor"),
        P(PLANE, None),
        P(PLANE, None),
    )
    function = functools.partial(
        local, mesh.shape["groups"] * mesh.shape["dp"], mesh.shape["tensor"]
    )
    return jax.shard_map(
        function, mesh=mesh, in_specs=in_specs, out_specs=P(PLANE, "tensor"), check_vma=False
    )
```

```python
import functools
import math

import jax
import jax.numpy as jnp
from jax import lax
from jax.experimental import pallas as pl
from jax.experimental.pallas import tpu as pltpu
from jax.sharding import PartitionSpec as P

VMEM_BYTES = 40 * 1024 * 1024
PLANE = ("groups", "dp")


def after(value, *earlier):
    return lax.optimization_barrier((value,) + earlier)[0]


def fixed(array):
    shape = array.shape
    return pl.BlockSpec(shape, lambda step, ids: (0,) * len(shape))


def call(kernel, name, ids, grid, specs, arrays, out, scratch=()):
    total = sum(array.size * array.dtype.itemsize for array in arrays)
    return pl.pallas_call(
        kernel,
        out_shape=out,
        grid_spec=pltpu.PrefetchScalarGridSpec(
            num_scalar_prefetch=1,
            grid=(grid,),
            in_specs=[fixed(array) if spec is None else spec for spec, array in zip(specs, arrays)],
            out_specs=[fixed(item) for item in out] if isinstance(out, tuple) else fixed(out),
            scratch_shapes=list(scratch),
        ),
        compiler_params=pltpu.CompilerParams(vmem_limit_bytes=VMEM_BYTES),
        cost_estimate=pl.CostEstimate(flops=0, bytes_accessed=3 * total, transcendentals=0),
        name=name,
    )(ids.astype(jnp.int32), *arrays)


def accumulate(acc_ref, token_ref, w_ref, first):
    slots, _, head_size = w_ref.shape
    for pair in range(slots // 2):
        columns = slice(2 * pair * head_size, (2 * pair + 2) * head_size)
        weight = jnp.concatenate([w_ref[2 * pair], w_ref[2 * pair + 1]], axis=1)
        total = jnp.dot(token_ref[...], weight, preferred_element_type=jnp.float32)
        acc_ref[:, columns] = total if first is None else first[:, columns] + total


def project_kernel(parts, begun, ids_ref, *refs):
    w_ref, acc_ref = refs[parts], refs[-1]
    row = 0
    for token_ref in refs[:parts]:
        rows = pl.ds(row, token_ref.shape[0])
        first = refs[parts + 1].at[rows] if begun else None
        accumulate(acc_ref.at[rows], token_ref, w_ref, first)
        row += token_ref.shape[0]


def rows_spec(array, rows, part):
    if array.shape[0] == rows:
        return None
    return pl.BlockSpec((rows, array.shape[1]), lambda step, ids: (part, 0))


def project(tokens, weight, begun=()):
    slots, _, head_size = weight.shape
    rows = sum(part.shape[0] for part in tokens)
    return call(
        functools.partial(project_kernel, len(tokens), len(begun)),
        "project",
        jnp.zeros(1),
        1,
        [None] * (len(tokens) + 1 + len(begun)),
        [*tokens, weight, *begun],
        jax.ShapeDtypeStruct((rows, slots * head_size), jnp.float32),
    )


def attend_kernel(planes, earlier, ids_ref, table_ref, turn_ref, up_ref, *refs):
    piece_refs, refs = refs[:planes], refs[planes:]
    token_ref, w_ref, begun_ref, refs = refs[0], refs[1], refs[2], refs[3:]
    earlier_refs, refs = refs[: 2 * earlier], refs[2 * earlier :]
    out_ref, keys_ref, values_ref, acc_ref, shrink_ref = refs
    for number, piece_ref in enumerate(piece_refs):
        width = piece_ref.shape[1]
        size = piece_ref.shape[0] * 2 // 3
        start = pl.multiple_of(ids_ref[number] * size, size)
        shrink_ref[pl.ds(start, size), :width] = piece_ref[:size, :]
        shrink_ref[pl.ds(start, size // 2), width:] = piece_ref[size:, : width // 2]
        shrink_ref[pl.ds(start + size // 2, size // 2), width:] = piece_ref[size:, width // 2 :]
    accumulate(acc_ref, token_ref, w_ref, begun_ref)
    slots, _, head_size = w_ref.shape
    rank = up_ref.shape[2]
    count = ids_ref.shape[0] - planes
    rows = acc_ref.shape[0]
    first_row = earlier_refs[0].shape[0] if earlier else 0
    queries = slots - 2
    lane = lax.broadcasted_iota(jnp.int32, (rows, count * rank), 1)
    kept = (lane >= table_ref[:, 1:2]) & (lane < table_ref[:, 1:2] + rank)
    lows = []
    for part in range(3):
        piece = shrink_ref[first_row : first_row + rows, part * rank : (part + 1) * rank]
        piece = jnp.concatenate([piece.astype(jnp.float32)] * count, axis=1)
        lows.append(jnp.where(kept, piece, 0.0).astype(jnp.bfloat16))

    def slot(index):
        low = lows[0 if index < queries else index - queries + 1]
        up = jnp.concatenate([up_ref[ids_ref[planes + j], index] for j in range(count)], axis=0)
        extra = jnp.dot(low, up, preferred_element_type=jnp.float32)
        return acc_ref[:, index * head_size : (index + 1) * head_size] + extra

    def rotated(index):
        value = slot(index)
        turned = pltpu.roll(value, head_size // 2, 1)
        return (value * turn_ref[:, :head_size] + turned * turn_ref[:, head_size:]).astype(
            jnp.bfloat16
        )

    keys = rotated(queries)
    values = slot(queries + 1).astype(jnp.bfloat16)
    keys_ref[...] = keys
    values_ref[...] = values
    if earlier:
        keys = jnp.concatenate([earlier_refs[0][...], keys], axis=0)
        values = jnp.concatenate([earlier_refs[1][...], values], axis=0)
    shape = (rows, keys.shape[0])
    key_at = lax.broadcasted_iota(jnp.int32, shape, 1)
    row_at = lax.broadcasted_iota(jnp.int32, shape, 0) + first_row
    allowed = (key_at >= table_ref[:, 0:1]) & (key_at <= row_at)
    for index in range(queries):
        scores = lax.dot_general(
            rotated(index), keys, (((1,), (1,)), ((), ())), preferred_element_type=jnp.float32
        )
        scores = jnp.where(allowed, scores * (1.0 / math.sqrt(head_size)), -1e30)
        weights = jnp.exp(scores - jnp.max(scores, axis=1, keepdims=True))
        scale = 1.0 / jnp.sum(weights, axis=1, keepdims=True)
        attended = jnp.dot(
            (weights * scale).astype(jnp.bfloat16), values, preferred_element_type=jnp.float32
        )
        out_ref[:, index * head_size : (index + 1) * head_size] = attended.astype(jnp.bfloat16)


def attend(planes_of, adapters, part, table, turn, up, shrink, tokens, weight, begun, earlier):
    rows = tokens.shape[0]
    slots, _, head_size = weight.shape
    planes = len(shrink)
    arrays = [table, turn, up, *shrink, tokens, weight, begun, *earlier]
    specs = [None] * len(arrays)
    for index in (0, 1, 3 + planes, 5 + planes):
        specs[index] = rows_spec(arrays[index], rows, part)
    return call(
        functools.partial(attend_kernel, planes, len(earlier) // 2),
        "attend",
        jnp.concatenate([planes_of, adapters]),
        1,
        specs,
        arrays,
        (
            jax.ShapeDtypeStruct((rows, (slots - 2) * head_size), jnp.bfloat16),
            jax.ShapeDtypeStruct((rows, head_size), jnp.bfloat16),
            jax.ShapeDtypeStruct((rows, head_size), jnp.bfloat16),
        ),
        [
            pltpu.VMEM((rows, slots * head_size), jnp.float32),
            pltpu.VMEM(
                (planes * shrink[0].shape[0] * 2 // 3, shrink[0].shape[1] * 3 // 2), jnp.bfloat16
            ),
        ],
    )


def shrink_kernel(planes, ids_ref, table_ref, token_ref, down_ref, *refs):
    out_refs, acc_ref = refs[:planes], refs[planes]
    step = pl.program_id(0)
    count = ids_ref.shape[0] - 1
    part = lax.dot_general(
        token_ref[...], down_ref[0], (((1,), (1,)), ((), ())), preferred_element_type=jnp.float32
    )
    rank = part.shape[1] // 3
    part = jnp.where(table_ref[:, 1:2] == step * rank, part, 0.0)

    @pl.when(step == 0)
    def _():
        acc_ref[...] = part

    @pl.when(step > 0)
    def _():
        acc_ref[...] += part

    @pl.when(step == count - 1)
    def _():
        for turn, out_ref in enumerate(out_refs):
            rows = out_ref.shape[0] * 2 // 3
            plane = lax.rem(ids_ref[count] + turn, planes)
            piece = acc_ref[pl.ds(pl.multiple_of(plane * rows, rows), rows), :]
            out_ref[:rows, :] = piece[:, : 2 * rank]
            out_ref[rows:, :] = jnp.concatenate(
                [piece[: rows // 2, 2 * rank :], piece[rows // 2 :, 2 * rank :]], axis=1
            )


def shrink_partial(adapters, here, planes, table, tokens, down):
    _, width, depth = down.shape
    rows = tokens.shape[0]
    return call(
        functools.partial(shrink_kernel, planes),
        "shrink",
        jnp.concatenate([adapters, here[None]]),
        adapters.shape[0],
        [None, None, pl.BlockSpec((1, width, depth), lambda step, ids: (ids[step], 0, 0))],
        [table, tokens, down],
        (jax.ShapeDtypeStruct((rows // planes * 3 // 2, width * 2 // 3), jnp.float32),) * planes,
        [pltpu.VMEM((rows, width), jnp.float32)],
    )


def output_kernel(begun, last, lines, ids_ref, attended_ref, w_ref, down_ref, *refs):
    begun_refs, rest = refs[:begun], refs[begun:]
    if last:
        table_ref, up_ref, before_refs, out_ref = rest[0], rest[1], rest[2:-1], rest[-1]
    else:
        acc_ref, low_ref = rest
    count = ids_ref.shape[0] - 1
    attended = attended_ref[...]
    features = attended.shape[1]
    if lines:
        weight = jnp.concatenate([w_ref[i, lines:] for i in range(w_ref.shape[0])], axis=0)
    else:
        weight = w_ref[...]
    downs = []
    for j in range(count):
        down = down_ref[ids_ref[1 + j]]
        downs += [down[:, at : at + features] for at in range(0, down.shape[1], features)]
    down = jnp.concatenate(downs, axis=0)
    rank = down.shape[0] // count
    total = jnp.dot(attended, weight, preferred_element_type=jnp.float32)
    low = lax.dot_general(
        attended, down, (((1,), (1,)), ((), ())), preferred_element_type=jnp.float32
    )
    if begun:
        total, low = begun_refs[0][...] + total, begun_refs[1][...] + low
    if last:
        low = low.astype(jnp.bfloat16).astype(jnp.float32)
        lane = lax.broadcasted_iota(jnp.int32, low.shape, 1)
        kept = (lane >= table_ref[:, 1:2]) & (lane < table_ref[:, 1:2] + rank)
        low = jnp.where(kept, low, 0.0).astype(jnp.bfloat16)
        up = jnp.concatenate([up_ref[ids_ref[1 + j]] for j in range(count)], axis=0)
        extra = jnp.dot(low, up, preferred_element_type=jnp.float32)
        first_row = out_ref.shape[0] - total.shape[0]
        for before_ref in before_refs:
            out_ref[:first_row, :] = before_ref[...]
        out_ref[first_row:, :] = (total + extra).astype(jnp.bfloat16)
    else:
        acc_ref[...] = total
        low_ref[...] = low


def project_out(ids, rank, attended, weight, down, begun, final, part=0):
    rows, features = attended.shape
    columns = weight.shape[-1]
    if len(weight.shape) == 2:
        down_spec, down_rows = None, 0
    else:
        down_rows = rank * features // columns
        down_spec = pl.BlockSpec(
            (down, down_rows, columns), lambda step, ids: (ids[0], 0, 0)
        )
        down = weight
    sums = (
        jax.ShapeDtypeStruct((rows, columns), jnp.float32),
        jax.ShapeDtypeStruct((rows, (ids.shape[0] - 1) * rank), jnp.float32),
    )
    all_rows = rows + sum(item.shape[0] for item in final[2:])
    return call(
        functools.partial(output_kernel, len(begun), bool(final), down_rows),
        "project_out",
        ids,
        1,
        [None, None, down_spec] + [None] * len(begun)
        + [rows_spec(table, rows, part) for table in final[:1]] + [None] * len(final[1:]),
        [attended, weight, down, *begun, *final],
        jax.ShapeDtypeStruct((all_rows, columns), jnp.bfloat16) if final else sums,
    )


def local(
    plane_size,
    planes,
    tokens,
    query_key_value_weight,
    output_weight,
    adapter_down_maps,
    adapter_up_maps,
    output_down_maps,
    output_up_maps,
    request_adapter,
    lengths,
):
    token_rows, depth = tokens.shape
    _, slots, head_size = query_key_value_weight.shape
    queries = slots - 2
    pool, rank = plane_size // lax.axis_size("groups"), adapter_up_maps.shape[1]
    features = queries * head_size
    columns = output_weight.shape[2] // planes
    here = lax.axis_index("tensor")
    place = lax.axis_index(PLANE)
    planes_of = (here - jnp.arange(planes) + planes) % planes

    def turned(value, turn=1):
        return lax.ppermute(value, "tensor", [(i, (i + turn) % planes) for i in range(planes)])

    weight = jnp.transpose(query_key_value_weight, (1, 0, 2))
    down_all = lax.all_gather(adapter_down_maps, "dp", axis=0, tiled=True)
    up_all = lax.all_gather(jnp.transpose(adapter_up_maps[0], (1, 0, 2)), "dp", axis=0)

    requests = request_adapter.shape[1]
    request_ends = jnp.cumsum(lengths[0])
    request_starts = request_ends - lengths[0]
    at = jnp.arange(token_rows, dtype=jnp.int32)
    member = (at[:, None] >= request_starts[None, :]) & (at[:, None] < request_ends[None, :])
    if pool <= requests:
        adapters, label = jnp.arange(pool), request_adapter[0]
    else:
        adapters, label = request_adapter[0], jnp.arange(requests)
    wanted = jnp.stack([request_starts, label * rank], axis=0)
    table = jnp.sum(jnp.where(member[:, None, :], wanted[None], 0), axis=2).astype(jnp.int32)
    position = at - table[:, 0]
    half = head_size // 2
    inv_freq = 10000.0 ** (-2.0 * jnp.arange(half, dtype=jnp.float32) / head_size)
    angles = position.astype(jnp.float32)[:, None] * inv_freq[None, :]
    cosine, sine = jnp.cos(angles), jnp.sin(angles)
    turn = jnp.concatenate([cosine, cosine, -sine, sine], axis=1)

    own_rows = jnp.transpose(
        lax.dynamic_slice_in_dim(output_weight, here * columns, columns, axis=2), (1, 0, 2)
    ).reshape(features, columns)
    share = features // plane_size
    line = place * share
    piece = lax.dynamic_slice(
        output_weight, (line % head_size, line // head_size, 0),
        (share, 1, output_weight.shape[2]),
    )[:, 0]
    out_down = output_down_maps[0].reshape(rank, features)
    out_down = jnp.concatenate(jnp.split(out_down, columns // features, axis=0), axis=1)
    sends = [
        jnp.concatenate(
            [
                out_down,
                lax.dynamic_slice_in_dim(piece, (here + k) % planes * columns, columns, axis=1),
            ],
            axis=0,
        )
        for k in range(1, planes)
    ]

    def shard(number):
        start = planes_of[number] * depth
        return lax.dynamic_slice_in_dim(weight, start, depth, axis=1)

    half_rows = token_rows // 2
    arrived = [tokens[:half_rows], tokens[half_rows:]]
    moved = [turned(half) for half in arrived]
    lines = [turned(send, k) for k, send in enumerate(sends, 1)]
    begun = project(arrived, shard(0))
    sums = shrink_partial(adapters, here, planes, table, tokens, down_all)
    done = (moved, lines, begun, table, turn, up_all, own_rows, shard(1), sums)
    done = lax.optimization_barrier(done)
    moved, lines, begun, table, turn, up_all, own_rows, part_weight, sums = done
    for step in range(2, planes):
        arrived = moved
        last = step == planes - 1
        moved = [turned(arrived[0]), arrived[1] if last else turned(arrived[1])]
        begun = project(arrived, part_weight, [begun])
        side = ()
        if step == 2:
            sums = [sums[0]] + [turned(sums[k], k) for k in range(1, planes)]
            lines = lax.all_gather(jnp.stack(lines), PLANE, axis=0)
            side = (
                sums,
                lax.all_gather(after(output_up_maps, sums[0]), "dp", axis=0, tiled=True),
                lax.all_gather(after(out_down, sums[0]), "dp", axis=0),
            )
        elif step == 3:
            shrink = sum(sums[1:], sums[0]).astype(jnp.bfloat16)
            shrink = [shrink] + [turned(shrink, k) for k in range(1, planes)]
            side = (shrink, [lines[:, k] for k in range(planes - 1)])
        done = lax.optimization_barrier((moved, begun, shard(step), side))
        moved, begun, part_weight, side = done
        if step == 2:
            sums, out_up_all, own_down = side
        elif step == 3:
            shrink, lines = side
    moved[1] = turned(moved[1])

    ids = jnp.concatenate([lax.axis_index("groups")[None], adapters])
    attended, earlier = [[], []], ()
    for part in range(2):
        made, *earlier = attend(
            planes_of, adapters, part, table, turn, up_all, shrink, moved[part], part_weight,
            begun, earlier,
        )
        attended[part] = [made, turned(after(made, *attended[0][1:]))]
    sums = [
        project_out(ids, rank, attended[part][0], own_rows, own_down, [], []) for part in range(2)
    ]
    before = []
    for step in range(2, planes + 1):
        for part in range(2):
            arrived = attended[part][-1]
            if step < planes:
                ahead = [*attended[0][step:], *sums[part]]
                attended[part].append(turned(after(arrived, *ahead)))
            final = [] if step < planes else [table, out_up_all, *before]
            sums[part] = project_out(
                ids, rank, arrived, lines[step - 2], pool, list(sums[part]), final, part
            )
            if final:
                before = [sums[part]]
    return before[0]


def solution(mesh):
    in_specs = (
        P(PLANE, "tensor"),
        P(None, None, "tensor"),
        P("tensor", None, None),
        P(PLANE, None, "tensor"),
        P(PLANE, None, None, "tensor"),
        P(PLANE, None, None, "tensor"),
        P(PLANE, None, "tensor"),
        P(PLANE, None),
        P(PLANE, None),
    )
    function = functools.partial(
        local, mesh.shape["groups"] * mesh.shape["dp"], mesh.shape["tensor"]
    )
    return jax.shard_map(
        function, mesh=mesh, in_specs=in_specs, out_specs=P(PLANE, "tensor"), check_vma=False
    )
```

```python
import functools
import math

import jax
import jax.numpy as jnp
from jax import lax
from jax.experimental import pallas as pl
from jax.experimental.pallas import tpu as pltpu
from jax.sharding import PartitionSpec as P

VMEM_BYTES = 40 * 1024 * 1024
PLANE = ("groups", "dp")


def after(value, *earlier):
    return lax.optimization_barrier((value,) + earlier)[0]


def fixed(array):
    shape = array.shape
    return pl.BlockSpec(shape, lambda step, ids: (0,) * len(shape))


def call(kernel, name, ids, grid, specs, arrays, out, scratch=()):
    total = sum(array.size * array.dtype.itemsize for array in arrays)
    return pl.pallas_call(
        kernel,
        out_shape=out,
        grid_spec=pltpu.PrefetchScalarGridSpec(
            num_scalar_prefetch=1,
            grid=(grid,),
            in_specs=[fixed(array) if spec is None else spec for spec, array in zip(specs, arrays)],
            out_specs=[fixed(item) for item in out] if isinstance(out, tuple) else fixed(out),
            scratch_shapes=list(scratch),
        ),
        compiler_params=pltpu.CompilerParams(vmem_limit_bytes=VMEM_BYTES),
        cost_estimate=pl.CostEstimate(flops=0, bytes_accessed=3 * total, transcendentals=0),
        name=name,
    )(ids.astype(jnp.int32), *arrays)


def accumulate(acc_ref, token_ref, w_ref, first):
    slots, _, head_size = w_ref.shape
    for pair in range(slots // 2):
        columns = slice(2 * pair * head_size, (2 * pair + 2) * head_size)
        weight = jnp.concatenate([w_ref[2 * pair], w_ref[2 * pair + 1]], axis=1)
        total = jnp.dot(token_ref[...], weight, preferred_element_type=jnp.float32)
        acc_ref[:, columns] = total if first is None else first[:, columns] + total


def project_kernel(parts, begun, ids_ref, *refs):
    w_ref, acc_ref = refs[parts], refs[-1]
    row = 0
    for token_ref in refs[:parts]:
        rows = pl.ds(row, token_ref.shape[0])
        first = refs[parts + 1].at[rows] if begun else None
        accumulate(acc_ref.at[rows], token_ref, w_ref, first)
        row += token_ref.shape[0]


def rows_spec(array, rows, part):
    if array.shape[0] == rows:
        return None
    return pl.BlockSpec((rows, array.shape[1]), lambda step, ids: (part, 0))


def project(tokens, weight, begun=()):
    slots, _, head_size = weight.shape
    rows = sum(part.shape[0] for part in tokens)
    return call(
        functools.partial(project_kernel, len(tokens), len(begun)),
        "project",
        jnp.zeros(1),
        1,
        [None] * (len(tokens) + 1 + len(begun)),
        [*tokens, weight, *begun],
        jax.ShapeDtypeStruct((rows, slots * head_size), jnp.float32),
    )


def attend_kernel(planes, earlier, ids_ref, table_ref, turn_ref, up_ref, *refs):
    piece_refs, refs = refs[:planes], refs[planes:]
    token_ref, w_ref, begun_ref, refs = refs[0], refs[1], refs[2], refs[3:]
    earlier_refs, refs = refs[: 2 * earlier], refs[2 * earlier :]
    out_ref, keys_ref, values_ref, acc_ref, shrink_ref = refs
    for number, piece_ref in enumerate(piece_refs):
        width = piece_ref.shape[1]
        size = piece_ref.shape[0] * 2 // 3
        start = pl.multiple_of(ids_ref[number] * size, size)
        shrink_ref[pl.ds(start, size), :width] = piece_ref[:size, :]
        shrink_ref[pl.ds(start, size // 2), width:] = piece_ref[size:, : width // 2]
        shrink_ref[pl.ds(start + size // 2, size // 2), width:] = piece_ref[size:, width // 2 :]
    accumulate(acc_ref, token_ref, w_ref, begun_ref)
    slots, _, head_size = w_ref.shape
    rank = up_ref.shape[2]
    count = ids_ref.shape[0] - planes
    rows = acc_ref.shape[0]
    first_row = earlier_refs[0].shape[0] if earlier else 0
    queries = slots - 2
    lane = lax.broadcasted_iota(jnp.int32, (rows, count * rank), 1)
    kept = (lane >= table_ref[:, 1:2]) & (lane < table_ref[:, 1:2] + rank)
    lows = []
    for part in range(3):
        piece = shrink_ref[first_row : first_row + rows, part * rank : (part + 1) * rank]
        piece = jnp.concatenate([piece.astype(jnp.float32)] * count, axis=1)
        lows.append(jnp.where(kept, piece, 0.0).astype(jnp.bfloat16))

    def slot(index):
        low = lows[0 if index < queries else index - queries + 1]
        up = jnp.concatenate([up_ref[ids_ref[planes + j], index] for j in range(count)], axis=0)
        extra = jnp.dot(low, up, preferred_element_type=jnp.float32)
        return acc_ref[:, index * head_size : (index + 1) * head_size] + extra

    def rotated(index):
        value = slot(index)
        turned = pltpu.roll(value, head_size // 2, 1)
        return (value * turn_ref[:, :head_size] + turned * turn_ref[:, head_size:]).astype(
            jnp.bfloat16
        )

    keys = rotated(queries)
    values = slot(queries + 1).astype(jnp.bfloat16)
    keys_ref[...] = keys
    values_ref[...] = values
    if earlier:
        keys = jnp.concatenate([earlier_refs[0][...], keys], axis=0)
        values = jnp.concatenate([earlier_refs[1][...], values], axis=0)
    shape = (rows, keys.shape[0])
    key_at = lax.broadcasted_iota(jnp.int32, shape, 1)
    row_at = lax.broadcasted_iota(jnp.int32, shape, 0) + first_row
    allowed = (key_at >= table_ref[:, 0:1]) & (key_at <= row_at)
    for index in range(queries):
        scores = lax.dot_general(
            rotated(index), keys, (((1,), (1,)), ((), ())), preferred_element_type=jnp.float32
        )
        scores = jnp.where(allowed, scores * (1.0 / math.sqrt(head_size)), -1e30)
        weights = jnp.exp(scores - jnp.max(scores, axis=1, keepdims=True))
        scale = 1.0 / jnp.sum(weights, axis=1, keepdims=True)
        attended = jnp.dot(
            (weights * scale).astype(jnp.bfloat16), values, preferred_element_type=jnp.float32
        )
        out_ref[:, index * head_size : (index + 1) * head_size] = attended.astype(jnp.bfloat16)


def attend(planes_of, adapters, part, table, turn, up, shrink, tokens, weight, begun, earlier):
    rows = tokens.shape[0]
    slots, _, head_size = weight.shape
    planes = len(shrink)
    arrays = [table, turn, up, *shrink, tokens, weight, begun, *earlier]
    specs = [None] * len(arrays)
    for index in (0, 1, 3 + planes, 5 + planes):
        specs[index] = rows_spec(arrays[index], rows, part)
    return call(
        functools.partial(attend_kernel, planes, len(earlier) // 2),
        "attend",
        jnp.concatenate([planes_of, adapters]),
        1,
        specs,
        arrays,
        (
            jax.ShapeDtypeStruct((rows, (slots - 2) * head_size), jnp.bfloat16),
            jax.ShapeDtypeStruct((rows, head_size), jnp.bfloat16),
            jax.ShapeDtypeStruct((rows, head_size), jnp.bfloat16),
        ),
        [
            pltpu.VMEM((rows, slots * head_size), jnp.float32),
            pltpu.VMEM(
                (planes * shrink[0].shape[0] * 2 // 3, shrink[0].shape[1] * 3 // 2), jnp.bfloat16
            ),
        ],
    )


def shrink_kernel(planes, ids_ref, table_ref, token_ref, down_ref, *refs):
    out_refs, acc_ref = refs[:planes], refs[planes]
    step = pl.program_id(0)
    count = ids_ref.shape[0] - 1
    part = lax.dot_general(
        token_ref[...], down_ref[0], (((1,), (1,)), ((), ())), preferred_element_type=jnp.float32
    )
    rank = part.shape[1] // 3
    part = jnp.where(table_ref[:, 1:2] == step * rank, part, 0.0)

    @pl.when(step == 0)
    def _():
        acc_ref[...] = part

    @pl.when(step > 0)
    def _():
        acc_ref[...] += part

    @pl.when(step == count - 1)
    def _():
        for turn, out_ref in enumerate(out_refs):
            rows = out_ref.shape[0] * 2 // 3
            plane = lax.rem(ids_ref[count] + turn, planes)
            piece = acc_ref[pl.ds(pl.multiple_of(plane * rows, rows), rows), :]
            out_ref[:rows, :] = piece[:, : 2 * rank]
            out_ref[rows:, :] = jnp.concatenate(
                [piece[: rows // 2, 2 * rank :], piece[rows // 2 :, 2 * rank :]], axis=1
            )


def shrink_partial(adapters, here, planes, table, tokens, down):
    _, width, depth = down.shape
    rows = tokens.shape[0]
    return call(
        functools.partial(shrink_kernel, planes),
        "shrink",
        jnp.concatenate([adapters, here[None]]),
        adapters.shape[0],
        [None, None, pl.BlockSpec((1, width, depth), lambda step, ids: (ids[step], 0, 0))],
        [table, tokens, down],
        (jax.ShapeDtypeStruct((rows // planes * 3 // 2, width * 2 // 3), jnp.float32),) * planes,
        [pltpu.VMEM((rows, width), jnp.float32)],
    )


def output_kernel(begun, last, lines, ids_ref, attended_ref, w_ref, down_ref, *refs):
    begun_refs, rest = refs[:begun], refs[begun:]
    if last:
        table_ref, up_ref, before_refs, out_ref = rest[0], rest[1], rest[2:-1], rest[-1]
    else:
        acc_ref, low_ref = rest
    count = ids_ref.shape[0] - 1
    attended = attended_ref[...]
    features = attended.shape[1]
    if lines:
        weight = jnp.concatenate([w_ref[i, lines:] for i in range(w_ref.shape[0])], axis=0)
    else:
        weight = w_ref[...]
    downs = []
    for j in range(count):
        down = down_ref[ids_ref[1 + j]]
        downs += [down[:, at : at + features] for at in range(0, down.shape[1], features)]
    down = jnp.concatenate(downs, axis=0)
    rank = down.shape[0] // count
    total = jnp.dot(attended, weight, preferred_element_type=jnp.float32)
    low = lax.dot_general(
        attended, down, (((1,), (1,)), ((), ())), preferred_element_type=jnp.float32
    )
    if begun:
        total, low = begun_refs[0][...] + total, begun_refs[1][...] + low
    if last:
        low = low.astype(jnp.bfloat16).astype(jnp.float32)
        lane = lax.broadcasted_iota(jnp.int32, low.shape, 1)
        kept = (lane >= table_ref[:, 1:2]) & (lane < table_ref[:, 1:2] + rank)
        low = jnp.where(kept, low, 0.0).astype(jnp.bfloat16)
        up = jnp.concatenate([up_ref[ids_ref[1 + j]] for j in range(count)], axis=0)
        extra = jnp.dot(low, up, preferred_element_type=jnp.float32)
        first_row = out_ref.shape[0] - total.shape[0]
        for before_ref in before_refs:
            out_ref[:first_row, :] = before_ref[...]
        out_ref[first_row:, :] = (total + extra).astype(jnp.bfloat16)
    else:
        acc_ref[...] = total
        low_ref[...] = low


def project_out(ids, rank, attended, weight, down, begun, final, part=0):
    rows, features = attended.shape
    columns = weight.shape[-1]
    if len(weight.shape) == 2:
        down_spec, down_rows = None, 0
    else:
        down_rows = rank * features // columns
        down_spec = pl.BlockSpec(
            (down, down_rows, columns), lambda step, ids: (ids[0], 0, 0)
        )
        down = weight
    sums = (
        jax.ShapeDtypeStruct((rows, columns), jnp.float32),
        jax.ShapeDtypeStruct((rows, (ids.shape[0] - 1) * rank), jnp.float32),
    )
    all_rows = rows + sum(item.shape[0] for item in final[2:])
    return call(
        functools.partial(output_kernel, len(begun), bool(final), down_rows),
        "project_out",
        ids,
        1,
        [None, None, down_spec] + [None] * len(begun)
        + [rows_spec(table, rows, part) for table in final[:1]] + [None] * len(final[1:]),
        [attended, weight, down, *begun, *final],
        jax.ShapeDtypeStruct((all_rows, columns), jnp.bfloat16) if final else sums,
    )


def local(
    plane_size,
    planes,
    tokens,
    query_key_value_weight,
    output_weight,
    adapter_down_maps,
    adapter_up_maps,
    output_down_maps,
    output_up_maps,
    request_adapter,
    lengths,
):
    token_rows, depth = tokens.shape
    _, slots, head_size = query_key_value_weight.shape
    queries = slots - 2
    pool, rank = plane_size // lax.axis_size("groups"), adapter_up_maps.shape[1]
    features = queries * head_size
    columns = output_weight.shape[2] // planes
    here = lax.axis_index("tensor")
    place = lax.axis_index(PLANE)
    planes_of = (here - jnp.arange(planes) + planes) % planes

    def turned(value, turn=1):
        return lax.ppermute(value, "tensor", [(i, (i + turn) % planes) for i in range(planes)])

    weight = jnp.transpose(query_key_value_weight, (1, 0, 2))
    down_all = lax.all_gather(adapter_down_maps, "dp", axis=0, tiled=True)
    up_all = lax.all_gather(jnp.transpose(adapter_up_maps[0], (1, 0, 2)), "dp", axis=0)

    requests = request_adapter.shape[1]
    request_ends = jnp.cumsum(lengths[0])
    request_starts = request_ends - lengths[0]
    at = jnp.arange(token_rows, dtype=jnp.int32)
    member = (at[:, None] >= request_starts[None, :]) & (at[:, None] < request_ends[None, :])
    if pool <= requests:
        adapters, label = jnp.arange(pool), request_adapter[0]
    else:
        adapters, label = request_adapter[0], jnp.arange(requests)
    wanted = jnp.stack([request_starts, label * rank], axis=0)
    table = jnp.sum(jnp.where(member[:, None, :], wanted[None], 0), axis=2).astype(jnp.int32)
    position = at - table[:, 0]
    half = head_size // 2
    inv_freq = 10000.0 ** (-2.0 * jnp.arange(half, dtype=jnp.float32) / head_size)
    angles = position.astype(jnp.float32)[:, None] * inv_freq[None, :]
    cosine, sine = jnp.cos(angles), jnp.sin(angles)
    turn = jnp.concatenate([cosine, cosine, -sine, sine], axis=1)

    own_rows = jnp.transpose(
        lax.dynamic_slice_in_dim(output_weight, here * columns, columns, axis=2), (1, 0, 2)
    ).reshape(features, columns)
    share = features // plane_size
    line = place * share
    piece = lax.dynamic_slice(
        output_weight, (line % head_size, line // head_size, 0),
        (share, 1, output_weight.shape[2]),
    )[:, 0]
    out_down = output_down_maps[0].reshape(rank, features)
    out_down = jnp.concatenate(jnp.split(out_down, columns // features, axis=0), axis=1)
    sends = [
        jnp.concatenate(
            [
                out_down,
                lax.dynamic_slice_in_dim(piece, (here + k) % planes * columns, columns, axis=1),
            ],
            axis=0,
        )
        for k in range(1, planes)
    ]

    def shard(number):
        start = planes_of[number] * depth
        return lax.dynamic_slice_in_dim(weight, start, depth, axis=1)

    half_rows = token_rows // 2
    arrived = [tokens[:half_rows], tokens[half_rows:]]
    moved = [turned(half) for half in arrived]
    lines = [turned(send, k) for k, send in enumerate(sends, 1)]
    begun = project(arrived, shard(0))
    sums = shrink_partial(adapters, here, planes, table, tokens, down_all)
    done = (moved, lines, begun, table, turn, up_all, own_rows, shard(1), sums)
    done = lax.optimization_barrier(done)
    moved, lines, begun, table, turn, up_all, own_rows, part_weight, sums = done
    for step in range(2, planes):
        arrived = moved
        last = step == planes - 1
        moved = [turned(arrived[0]), arrived[1] if last else turned(arrived[1])]
        begun = project(arrived, part_weight, [begun])
        side = ()
        if step == 2:
            sums = [sums[0]] + [turned(sums[k], k) for k in range(1, planes)]
            lines = lax.all_gather(jnp.stack(lines), PLANE, axis=0)
            side = (
                sums,
                lax.all_gather(after(output_up_maps, sums[0]), "dp", axis=0, tiled=True),
                lax.all_gather(after(out_down, sums[0]), "dp", axis=0),
            )
        elif step == 3:
            shrink = sum(sums[1:], sums[0]).astype(jnp.bfloat16)
            shrink = [shrink] + [turned(shrink, k) for k in range(1, planes)]
            side = (shrink, [lines[:, k] for k in range(planes - 1)])
        if step == 3:
            shrink, lines = side
        if last:
            part_weight = shard(step)
            moved[1] = turned(after(moved[1], moved[0], *lines))
            break
        done = lax.optimization_barrier((moved, begun, shard(step), side))
        moved, begun, part_weight, side = done
        if step == 2:
            sums, out_up_all, own_down = side

    ids = jnp.concatenate([lax.axis_index("groups")[None], adapters])
    attended, earlier = [[], []], ()
    for part in range(2):
        made, *earlier = attend(
            planes_of, adapters, part, table, turn, up_all, shrink, moved[part], part_weight,
            begun, earlier,
        )
        attended[part] = [made, turned(after(made, *attended[0][1:]))]
    sums = [
        project_out(ids, rank, attended[part][0], own_rows, own_down, [], []) for part in range(2)
    ]
    before = []
    for step in range(2, planes + 1):
        for part in range(2):
            arrived = attended[part][-1]
            if step < planes:
                ahead = [*attended[0][step:], *sums[part]]
                attended[part].append(turned(after(arrived, *ahead)))
            final = [] if step < planes else [table, out_up_all, *before]
            sums[part] = project_out(
                ids, rank, arrived, lines[step - 2], pool, list(sums[part]), final, part
            )
            if final:
                before = [sums[part]]
    return before[0]


def solution(mesh):
    in_specs = (
        P(PLANE, "tensor"),
        P(None, None, "tensor"),
        P("tensor", None, None),
        P(PLANE, None, "tensor"),
        P(PLANE, None, None, "tensor"),
        P(PLANE, None, None, "tensor"),
        P(PLANE, None, "tensor"),
        P(PLANE, None),
        P(PLANE, None),
    )
    function = functools.partial(
        local, mesh.shape["groups"] * mesh.shape["dp"], mesh.shape["tensor"]
    )
    return jax.shard_map(
        function, mesh=mesh, in_specs=in_specs, out_specs=P(PLANE, "tensor"), check_vma=False
    )
```

```python
import functools
import math

import jax
import jax.numpy as jnp
from jax import lax
from jax.experimental import pallas as pl
from jax.experimental.pallas import tpu as pltpu
from jax.sharding import PartitionSpec as P

VMEM_BYTES = 40 * 1024 * 1024
PLANE = ("groups", "dp")


def after(value, *earlier):
    return lax.optimization_barrier((value,) + earlier)[0]


def fixed(array):
    shape = array.shape
    return pl.BlockSpec(shape, lambda step, ids: (0,) * len(shape))


def call(kernel, name, ids, grid, specs, arrays, out, scratch=()):
    total = sum(array.size * array.dtype.itemsize for array in arrays)
    return pl.pallas_call(
        kernel,
        out_shape=out,
        grid_spec=pltpu.PrefetchScalarGridSpec(
            num_scalar_prefetch=1,
            grid=(grid,),
            in_specs=[fixed(array) if spec is None else spec for spec, array in zip(specs, arrays)],
            out_specs=[fixed(item) for item in out] if isinstance(out, tuple) else fixed(out),
            scratch_shapes=list(scratch),
        ),
        compiler_params=pltpu.CompilerParams(vmem_limit_bytes=VMEM_BYTES),
        cost_estimate=pl.CostEstimate(flops=0, bytes_accessed=3 * total, transcendentals=0),
        name=name,
    )(ids.astype(jnp.int32), *arrays)


def accumulate(acc_ref, token_ref, w_ref, first):
    slots, _, head_size = w_ref.shape
    for pair in range(slots // 2):
        columns = slice(2 * pair * head_size, (2 * pair + 2) * head_size)
        weight = jnp.concatenate([w_ref[2 * pair], w_ref[2 * pair + 1]], axis=1)
        total = jnp.dot(token_ref[...], weight, preferred_element_type=jnp.float32)
        acc_ref[:, columns] = total if first is None else first[:, columns] + total


def project_kernel(parts, begun, ids_ref, *refs):
    w_ref, acc_ref = refs[parts], refs[-1]
    row = 0
    for token_ref in refs[:parts]:
        rows = pl.ds(row, token_ref.shape[0])
        first = refs[parts + 1].at[rows] if begun else None
        accumulate(acc_ref.at[rows], token_ref, w_ref, first)
        row += token_ref.shape[0]


def rows_spec(array, rows, part):
    if array.shape[0] == rows:
        return None
    return pl.BlockSpec((rows, array.shape[1]), lambda step, ids: (part, 0))


def project(tokens, weight, begun=()):
    slots, _, head_size = weight.shape
    rows = sum(part.shape[0] for part in tokens)
    return call(
        functools.partial(project_kernel, len(tokens), len(begun)),
        "project",
        jnp.zeros(1),
        1,
        [None] * (len(tokens) + 1 + len(begun)),
        [*tokens, weight, *begun],
        jax.ShapeDtypeStruct((rows, slots * head_size), jnp.float32),
    )


def attend_kernel(planes, earlier, ids_ref, table_ref, turn_ref, up_ref, *refs):
    piece_refs, refs = refs[:planes], refs[planes:]
    token_ref, w_ref, begun_ref, refs = refs[0], refs[1], refs[2], refs[3:]
    earlier_refs, refs = refs[: 2 * earlier], refs[2 * earlier :]
    out_ref, keys_ref, values_ref, acc_ref, shrink_ref = refs
    for number, piece_ref in enumerate(piece_refs):
        width = piece_ref.shape[1]
        size = piece_ref.shape[0] * 2 // 3
        start = pl.multiple_of(ids_ref[number] * size, size)
        shrink_ref[pl.ds(start, size), :width] = piece_ref[:size, :]
        shrink_ref[pl.ds(start, size // 2), width:] = piece_ref[size:, : width // 2]
        shrink_ref[pl.ds(start + size // 2, size // 2), width:] = piece_ref[size:, width // 2 :]
    accumulate(acc_ref, token_ref, w_ref, begun_ref)
    slots, _, head_size = w_ref.shape
    rank = up_ref.shape[2]
    count = ids_ref.shape[0] - planes
    rows = acc_ref.shape[0]
    first_row = earlier_refs[0].shape[0] if earlier else 0
    queries = slots - 2
    lane = lax.broadcasted_iota(jnp.int32, (rows, count * rank), 1)
    kept = (lane >= table_ref[:, 1:2]) & (lane < table_ref[:, 1:2] + rank)
    lows = []
    for part in range(3):
        piece = shrink_ref[first_row : first_row + rows, part * rank : (part + 1) * rank]
        piece = jnp.concatenate([piece.astype(jnp.float32)] * count, axis=1)
        lows.append(jnp.where(kept, piece, 0.0).astype(jnp.bfloat16))

    def slot(index):
        low = lows[0 if index < queries else index - queries + 1]
        up = jnp.concatenate([up_ref[ids_ref[planes + j], index] for j in range(count)], axis=0)
        extra = jnp.dot(low, up, preferred_element_type=jnp.float32)
        return acc_ref[:, index * head_size : (index + 1) * head_size] + extra

    def rotated(index):
        value = slot(index)
        turned = pltpu.roll(value, head_size // 2, 1)
        return (value * turn_ref[:, :head_size] + turned * turn_ref[:, head_size:]).astype(
            jnp.bfloat16
        )

    keys = rotated(queries)
    values = slot(queries + 1).astype(jnp.bfloat16)
    keys_ref[...] = keys
    values_ref[...] = values
    if earlier:
        keys = jnp.concatenate([earlier_refs[0][...], keys], axis=0)
        values = jnp.concatenate([earlier_refs[1][...], values], axis=0)
    shape = (rows, keys.shape[0])
    key_at = lax.broadcasted_iota(jnp.int32, shape, 1)
    row_at = lax.broadcasted_iota(jnp.int32, shape, 0) + first_row
    allowed = (key_at >= table_ref[:, 0:1]) & (key_at <= row_at)
    for index in range(queries):
        scores = lax.dot_general(
            rotated(index), keys, (((1,), (1,)), ((), ())), preferred_element_type=jnp.float32
        )
        scores = jnp.where(allowed, scores * (1.0 / math.sqrt(head_size)), -1e30)
        weights = jnp.exp(scores - jnp.max(scores, axis=1, keepdims=True))
        scale = 1.0 / jnp.sum(weights, axis=1, keepdims=True)
        attended = jnp.dot(
            (weights * scale).astype(jnp.bfloat16), values, preferred_element_type=jnp.float32
        )
        out_ref[:, index * head_size : (index + 1) * head_size] = attended.astype(jnp.bfloat16)


def attend(planes_of, adapters, part, table, turn, up, shrink, tokens, weight, begun, earlier):
    rows = tokens.shape[0]
    slots, _, head_size = weight.shape
    planes = len(shrink)
    arrays = [table, turn, up, *shrink, tokens, weight, begun, *earlier]
    specs = [None] * len(arrays)
    for index in (0, 1, 3 + planes, 5 + planes):
        specs[index] = rows_spec(arrays[index], rows, part)
    return call(
        functools.partial(attend_kernel, planes, len(earlier) // 2),
        "attend",
        jnp.concatenate([planes_of, adapters]),
        1,
        specs,
        arrays,
        (
            jax.ShapeDtypeStruct((rows, (slots - 2) * head_size), jnp.bfloat16),
            jax.ShapeDtypeStruct((rows, head_size), jnp.bfloat16),
            jax.ShapeDtypeStruct((rows, head_size), jnp.bfloat16),
        ),
        [
            pltpu.VMEM((rows, slots * head_size), jnp.float32),
            pltpu.VMEM(
                (planes * shrink[0].shape[0] * 2 // 3, shrink[0].shape[1] * 3 // 2), jnp.bfloat16
            ),
        ],
    )


def shrink_kernel(planes, ids_ref, table_ref, token_ref, down_ref, *refs):
    out_refs, acc_ref = refs[:planes], refs[planes]
    step = pl.program_id(0)
    count = ids_ref.shape[0] - 1
    part = lax.dot_general(
        token_ref[...], down_ref[0], (((1,), (1,)), ((), ())), preferred_element_type=jnp.float32
    )
    rank = part.shape[1] // 3
    part = jnp.where(table_ref[:, 1:2] == step * rank, part, 0.0)

    @pl.when(step == 0)
    def _():
        acc_ref[...] = part

    @pl.when(step > 0)
    def _():
        acc_ref[...] += part

    @pl.when(step == count - 1)
    def _():
        for turn, out_ref in enumerate(out_refs):
            rows = out_ref.shape[0] * 2 // 3
            plane = lax.rem(ids_ref[count] + turn, planes)
            piece = acc_ref[pl.ds(pl.multiple_of(plane * rows, rows), rows), :]
            out_ref[:rows, :] = piece[:, : 2 * rank]
            out_ref[rows:, :] = jnp.concatenate(
                [piece[: rows // 2, 2 * rank :], piece[rows // 2 :, 2 * rank :]], axis=1
            )


def shrink_partial(adapters, here, planes, table, tokens, down):
    _, width, depth = down.shape
    rows = tokens.shape[0]
    return call(
        functools.partial(shrink_kernel, planes),
        "shrink",
        jnp.concatenate([adapters, here[None]]),
        adapters.shape[0],
        [None, None, pl.BlockSpec((1, width, depth), lambda step, ids: (ids[step], 0, 0))],
        [table, tokens, down],
        (jax.ShapeDtypeStruct((rows // planes * 3 // 2, width * 2 // 3), jnp.float32),) * planes,
        [pltpu.VMEM((rows, width), jnp.float32)],
    )


def output_kernel(begun, last, lines, ids_ref, attended_ref, w_ref, down_ref, *refs):
    begun_refs, rest = refs[:begun], refs[begun:]
    if last:
        table_ref, up_ref, before_refs, out_ref = rest[0], rest[1], rest[2:-1], rest[-1]
    else:
        acc_ref, low_ref = rest
    count = ids_ref.shape[0] - 1
    attended = attended_ref[...]
    features = attended.shape[1]
    if lines:
        weight = jnp.concatenate([w_ref[i, lines:] for i in range(w_ref.shape[0])], axis=0)
    else:
        weight = w_ref[...]
    downs = []
    for j in range(count):
        down = down_ref[ids_ref[1 + j]]
        downs += [down[:, at : at + features] for at in range(0, down.shape[1], features)]
    down = jnp.concatenate(downs, axis=0)
    rank = down.shape[0] // count
    total = jnp.dot(attended, weight, preferred_element_type=jnp.float32)
    low = lax.dot_general(
        attended, down, (((1,), (1,)), ((), ())), preferred_element_type=jnp.float32
    )
    if begun:
        total, low = begun_refs[0][...] + total, begun_refs[1][...] + low
    if last:
        low = low.astype(jnp.bfloat16).astype(jnp.float32)
        lane = lax.broadcasted_iota(jnp.int32, low.shape, 1)
        kept = (lane >= table_ref[:, 1:2]) & (lane < table_ref[:, 1:2] + rank)
        low = jnp.where(kept, low, 0.0).astype(jnp.bfloat16)
        up = jnp.concatenate([up_ref[ids_ref[1 + j]] for j in range(count)], axis=0)
        extra = jnp.dot(low, up, preferred_element_type=jnp.float32)
        first_row = out_ref.shape[0] - total.shape[0]
        for before_ref in before_refs:
            out_ref[:first_row, :] = before_ref[...]
        out_ref[first_row:, :] = (total + extra).astype(jnp.bfloat16)
    else:
        acc_ref[...] = total
        low_ref[...] = low


def project_out(ids, rank, attended, weight, down, begun, final, part=0):
    rows, features = attended.shape
    columns = weight.shape[-1]
    if len(weight.shape) == 2:
        down_spec, down_rows = None, 0
    else:
        down_rows = rank * features // columns
        down_spec = pl.BlockSpec(
            (down, down_rows, columns), lambda step, ids: (ids[0], 0, 0)
        )
        down = weight
    sums = (
        jax.ShapeDtypeStruct((rows, columns), jnp.float32),
        jax.ShapeDtypeStruct((rows, (ids.shape[0] - 1) * rank), jnp.float32),
    )
    all_rows = rows + sum(item.shape[0] for item in final[2:])
    return call(
        functools.partial(output_kernel, len(begun), bool(final), down_rows),
        "project_out",
        ids,
        1,
        [None, None, down_spec] + [None] * len(begun)
        + [rows_spec(table, rows, part) for table in final[:1]] + [None] * len(final[1:]),
        [attended, weight, down, *begun, *final],
        jax.ShapeDtypeStruct((all_rows, columns), jnp.bfloat16) if final else sums,
    )


def local(
    plane_size,
    planes,
    tokens,
    query_key_value_weight,
    output_weight,
    adapter_down_maps,
    adapter_up_maps,
    output_down_maps,
    output_up_maps,
    request_adapter,
    lengths,
):
    token_rows, depth = tokens.shape
    _, slots, head_size = query_key_value_weight.shape
    queries = slots - 2
    pool, rank = plane_size // lax.axis_size("groups"), adapter_up_maps.shape[1]
    features = queries * head_size
    columns = output_weight.shape[2] // planes
    here = lax.axis_index("tensor")
    place = lax.axis_index(PLANE)
    planes_of = (here - jnp.arange(planes) + planes) % planes

    def turned(value, turn=1):
        return lax.ppermute(value, "tensor", [(i, (i + turn) % planes) for i in range(planes)])

    weight = jnp.transpose(query_key_value_weight, (1, 0, 2))
    down_all = lax.all_gather(adapter_down_maps, "dp", axis=0, tiled=True)
    up_all = lax.all_gather(jnp.transpose(adapter_up_maps[0], (1, 0, 2)), "dp", axis=0)

    requests = request_adapter.shape[1]
    request_ends = jnp.cumsum(lengths[0])
    request_starts = request_ends - lengths[0]
    at = jnp.arange(token_rows, dtype=jnp.int32)
    member = (at[:, None] >= request_starts[None, :]) & (at[:, None] < request_ends[None, :])
    if pool <= requests:
        adapters, label = jnp.arange(pool), request_adapter[0]
    else:
        adapters, label = request_adapter[0], jnp.arange(requests)
    wanted = jnp.stack([request_starts, label * rank], axis=0)
    table = jnp.sum(jnp.where(member[:, None, :], wanted[None], 0), axis=2).astype(jnp.int32)
    position = at - table[:, 0]
    half = head_size // 2
    inv_freq = 10000.0 ** (-2.0 * jnp.arange(half, dtype=jnp.float32) / head_size)
    angles = position.astype(jnp.float32)[:, None] * inv_freq[None, :]
    cosine, sine = jnp.cos(angles), jnp.sin(angles)
    turn = jnp.concatenate([cosine, cosine, -sine, sine], axis=1)

    own_rows = jnp.transpose(
        lax.dynamic_slice_in_dim(output_weight, here * columns, columns, axis=2), (1, 0, 2)
    ).reshape(features, columns)
    share = features // plane_size
    line = place * share
    piece = lax.dynamic_slice(
        output_weight, (line % head_size, line // head_size, 0),
        (share, 1, output_weight.shape[2]),
    )[:, 0]
    out_down = output_down_maps[0].reshape(rank, features)
    out_down = jnp.concatenate(jnp.split(out_down, columns // features, axis=0), axis=1)
    sends = [
        jnp.concatenate(
            [
                out_down,
                lax.dynamic_slice_in_dim(piece, (here + k) % planes * columns, columns, axis=1),
            ],
            axis=0,
        )
        for k in range(1, planes)
    ]

    def shard(number):
        start = planes_of[number] * depth
        return lax.dynamic_slice_in_dim(weight, start, depth, axis=1)

    half_rows = token_rows // 2
    arrived = [tokens[:half_rows], tokens[half_rows:]]
    moved = [turned(half) for half in arrived]
    lines = [turned(send, k) for k, send in enumerate(sends, 1)]
    begun = project(arrived, shard(0))
    sums = shrink_partial(adapters, here, planes, table, tokens, down_all)
    done = (moved, lines, begun, table, turn, up_all, own_rows, shard(1), sums)
    done = lax.optimization_barrier(done)
    moved, lines, begun, table, turn, up_all, own_rows, part_weight, sums = done
    for step in range(2, planes):
        arrived = moved
        last = step == planes - 1
        moved = [turned(arrived[0]), arrived[1] if last else turned(arrived[1])]
        begun = project(arrived, part_weight, [begun])
        side = ()
        if step == 2:
            sums = [sums[0]] + [turned(sums[k], k) for k in range(1, planes)]
            lines = lax.all_gather(jnp.stack(lines), PLANE, axis=0)
            side = (
                sums,
                lax.all_gather(after(output_up_maps, sums[0]), "dp", axis=0, tiled=True),
                lax.all_gather(after(out_down, sums[0]), "dp", axis=0),
            )
        elif step == 3:
            shrink = sum(sums[1:], sums[0]).astype(jnp.bfloat16)
            shrink = [shrink] + [turned(shrink, k) for k in range(1, planes)]
            side = (shrink, [lines[:, k] for k in range(planes - 1)])
        if step == 3:
            shrink, lines = side
        if last:
            part_weight = shard(step)
            moved[1] = turned(after(moved[1], moved[0], *shrink))
            break
        done = lax.optimization_barrier((moved, begun, shard(step), side))
        moved, begun, part_weight, side = done
        if step == 2:
            sums, out_up_all, own_down = side

    ids = jnp.concatenate([lax.axis_index("groups")[None], adapters])
    attended, earlier = [[], []], ()
    for part in range(2):
        made, *earlier = attend(
            planes_of, adapters, part, table, turn, up_all, shrink, moved[part], part_weight,
            begun, earlier,
        )
        ahead = [attended[0][1], *lines] if part else []
        attended[part] = [made, turned(after(made, *ahead))]
    sums = [
        project_out(ids, rank, attended[part][0], own_rows, own_down, [], []) for part in range(2)
    ]
    before = []
    for step in range(2, planes + 1):
        for part in range(2):
            arrived = attended[part][-1]
            if step < planes:
                ahead = [*attended[0][step:], *sums[part]]
                attended[part].append(turned(after(arrived, *ahead)))
            final = [] if step < planes else [table, out_up_all, *before]
            sums[part] = project_out(
                ids, rank, arrived, lines[step - 2], pool, list(sums[part]), final, part
            )
            if final:
                before = [sums[part]]
    return before[0]


def solution(mesh):
    in_specs = (
        P(PLANE, "tensor"),
        P(None, None, "tensor"),
        P("tensor", None, None),
        P(PLANE, None, "tensor"),
        P(PLANE, None, None, "tensor"),
        P(PLANE, None, None, "tensor"),
        P(PLANE, None, "tensor"),
        P(PLANE, None),
        P(PLANE, None),
    )
    function = functools.partial(
        local, mesh.shape["groups"] * mesh.shape["dp"], mesh.shape["tensor"]
    )
    return jax.shard_map(
        function, mesh=mesh, in_specs=in_specs, out_specs=P(PLANE, "tensor"), check_vma=False
    )
```

```python
import functools
import math

import jax
import jax.numpy as jnp
from jax import lax
from jax.experimental import pallas as pl
from jax.experimental.pallas import tpu as pltpu
from jax.sharding import PartitionSpec as P

VMEM_BYTES = 40 * 1024 * 1024
PLANE = ("groups", "dp")


def after(value, *earlier):
    return lax.optimization_barrier((value,) + earlier)[0]


def fixed(array):
    shape = array.shape
    return pl.BlockSpec(shape, lambda step, ids: (0,) * len(shape))


def call(kernel, name, ids, grid, specs, arrays, out, scratch=()):
    total = sum(array.size * array.dtype.itemsize for array in arrays)
    return pl.pallas_call(
        kernel,
        out_shape=out,
        grid_spec=pltpu.PrefetchScalarGridSpec(
            num_scalar_prefetch=1,
            grid=(grid,),
            in_specs=[fixed(array) if spec is None else spec for spec, array in zip(specs, arrays)],
            out_specs=[fixed(item) for item in out] if isinstance(out, tuple) else fixed(out),
            scratch_shapes=list(scratch),
        ),
        compiler_params=pltpu.CompilerParams(vmem_limit_bytes=VMEM_BYTES),
        cost_estimate=pl.CostEstimate(flops=0, bytes_accessed=3 * total, transcendentals=0),
        name=name,
    )(ids.astype(jnp.int32), *arrays)


def accumulate(acc_ref, token_ref, w_ref, first):
    slots, _, head_size = w_ref.shape
    for pair in range(slots // 2):
        columns = slice(2 * pair * head_size, (2 * pair + 2) * head_size)
        weight = jnp.concatenate([w_ref[2 * pair], w_ref[2 * pair + 1]], axis=1)
        total = jnp.dot(token_ref[...], weight, preferred_element_type=jnp.float32)
        acc_ref[:, columns] = total if first is None else first[:, columns] + total


def project_kernel(parts, begun, ids_ref, *refs):
    w_ref, acc_ref = refs[parts], refs[-1]
    row = 0
    for token_ref in refs[:parts]:
        rows = pl.ds(row, token_ref.shape[0])
        first = refs[parts + 1].at[rows] if begun else None
        accumulate(acc_ref.at[rows], token_ref, w_ref, first)
        row += token_ref.shape[0]


def rows_spec(array, rows, part):
    if array.shape[0] == rows:
        return None
    return pl.BlockSpec((rows, array.shape[1]), lambda step, ids: (part, 0))


def project(tokens, weight, begun=()):
    slots, _, head_size = weight.shape
    rows = sum(part.shape[0] for part in tokens)
    return call(
        functools.partial(project_kernel, len(tokens), len(begun)),
        "project",
        jnp.zeros(1),
        1,
        [None] * (len(tokens) + 1 + len(begun)),
        [*tokens, weight, *begun],
        jax.ShapeDtypeStruct((rows, slots * head_size), jnp.float32),
    )


def attend_kernel(planes, earlier, ids_ref, table_ref, turn_ref, up_ref, *refs):
    piece_refs, refs = refs[:planes], refs[planes:]
    token_ref, w_ref, begun_ref, refs = refs[0], refs[1], refs[2], refs[3:]
    earlier_refs, refs = refs[: 2 * earlier], refs[2 * earlier :]
    out_ref, keys_ref, values_ref, acc_ref, shrink_ref = refs
    for number, piece_ref in enumerate(piece_refs):
        width = piece_ref.shape[1]
        size = piece_ref.shape[0] * 2 // 3
        start = pl.multiple_of(ids_ref[number] * size, size)
        shrink_ref[pl.ds(start, size), :width] = piece_ref[:size, :]
        shrink_ref[pl.ds(start, size // 2), width:] = piece_ref[size:, : width // 2]
        shrink_ref[pl.ds(start + size // 2, size // 2), width:] = piece_ref[size:, width // 2 :]
    accumulate(acc_ref, token_ref, w_ref, begun_ref)
    slots, _, head_size = w_ref.shape
    rank = up_ref.shape[2]
    count = ids_ref.shape[0] - planes
    rows = acc_ref.shape[0]
    first_row = earlier_refs[0].shape[0] if earlier else 0
    queries = slots - 2
    lane = lax.broadcasted_iota(jnp.int32, (rows, count * rank), 1)
    kept = (lane >= table_ref[:, 1:2]) & (lane < table_ref[:, 1:2] + rank)
    lows = []
    for part in range(3):
        piece = shrink_ref[first_row : first_row + rows, part * rank : (part + 1) * rank]
        piece = jnp.concatenate([piece.astype(jnp.float32)] * count, axis=1)
        lows.append(jnp.where(kept, piece, 0.0).astype(jnp.bfloat16))

    def slot(index):
        low = lows[0 if index < queries else index - queries + 1]
        up = jnp.concatenate([up_ref[ids_ref[planes + j], index] for j in range(count)], axis=0)
        extra = jnp.dot(low, up, preferred_element_type=jnp.float32)
        return acc_ref[:, index * head_size : (index + 1) * head_size] + extra

    def rotated(index):
        value = slot(index)
        turned = pltpu.roll(value, head_size // 2, 1)
        return (value * turn_ref[:, :head_size] + turned * turn_ref[:, head_size:]).astype(
            jnp.bfloat16
        )

    keys = rotated(queries)
    values = slot(queries + 1).astype(jnp.bfloat16)
    keys_ref[...] = keys
    values_ref[...] = values
    if earlier:
        keys = jnp.concatenate([earlier_refs[0][...], keys], axis=0)
        values = jnp.concatenate([earlier_refs[1][...], values], axis=0)
    shape = (rows, keys.shape[0])
    key_at = lax.broadcasted_iota(jnp.int32, shape, 1)
    row_at = lax.broadcasted_iota(jnp.int32, shape, 0) + first_row
    allowed = (key_at >= table_ref[:, 0:1]) & (key_at <= row_at)
    for index in range(queries):
        scores = lax.dot_general(
            rotated(index), keys, (((1,), (1,)), ((), ())), preferred_element_type=jnp.float32
        )
        scores = jnp.where(allowed, scores * (1.0 / math.sqrt(head_size)), -1e30)
        weights = jnp.exp(scores - jnp.max(scores, axis=1, keepdims=True))
        scale = 1.0 / jnp.sum(weights, axis=1, keepdims=True)
        attended = jnp.dot(
            (weights * scale).astype(jnp.bfloat16), values, preferred_element_type=jnp.float32
        )
        out_ref[:, index * head_size : (index + 1) * head_size] = attended.astype(jnp.bfloat16)


def attend(planes_of, adapters, part, table, turn, up, shrink, tokens, weight, begun, earlier):
    rows = tokens.shape[0]
    slots, _, head_size = weight.shape
    planes = len(shrink)
    arrays = [table, turn, up, *shrink, tokens, weight, begun, *earlier]
    specs = [None] * len(arrays)
    for index in (0, 1, 3 + planes, 5 + planes):
        specs[index] = rows_spec(arrays[index], rows, part)
    return call(
        functools.partial(attend_kernel, planes, len(earlier) // 2),
        "attend",
        jnp.concatenate([planes_of, adapters]),
        1,
        specs,
        arrays,
        (
            jax.ShapeDtypeStruct((rows, (slots - 2) * head_size), jnp.bfloat16),
            jax.ShapeDtypeStruct((rows, head_size), jnp.bfloat16),
            jax.ShapeDtypeStruct((rows, head_size), jnp.bfloat16),
        ),
        [
            pltpu.VMEM((rows, slots * head_size), jnp.float32),
            pltpu.VMEM(
                (planes * shrink[0].shape[0] * 2 // 3, shrink[0].shape[1] * 3 // 2), jnp.bfloat16
            ),
        ],
    )


def shrink_kernel(planes, ids_ref, table_ref, token_ref, down_ref, *refs):
    out_refs, acc_ref = refs[:planes], refs[planes]
    step = pl.program_id(0)
    count = ids_ref.shape[0] - 1
    part = lax.dot_general(
        token_ref[...], down_ref[0], (((1,), (1,)), ((), ())), preferred_element_type=jnp.float32
    )
    rank = part.shape[1] // 3
    part = jnp.where(table_ref[:, 1:2] == step * rank, part, 0.0)

    @pl.when(step == 0)
    def _():
        acc_ref[...] = part

    @pl.when(step > 0)
    def _():
        acc_ref[...] += part

    @pl.when(step == count - 1)
    def _():
        for turn, out_ref in enumerate(out_refs):
            rows = out_ref.shape[0] * 2 // 3
            plane = lax.rem(ids_ref[count] + turn, planes)
            piece = acc_ref[pl.ds(pl.multiple_of(plane * rows, rows), rows), :]
            out_ref[:rows, :] = piece[:, : 2 * rank]
            out_ref[rows:, :] = jnp.concatenate(
                [piece[: rows // 2, 2 * rank :], piece[rows // 2 :, 2 * rank :]], axis=1
            )


def shrink_partial(adapters, here, planes, table, tokens, down):
    _, width, depth = down.shape
    rows = tokens.shape[0]
    return call(
        functools.partial(shrink_kernel, planes),
        "shrink",
        jnp.concatenate([adapters, here[None]]),
        adapters.shape[0],
        [None, None, pl.BlockSpec((1, width, depth), lambda step, ids: (ids[step], 0, 0))],
        [table, tokens, down],
        (jax.ShapeDtypeStruct((rows // planes * 3 // 2, width * 2 // 3), jnp.float32),) * planes,
        [pltpu.VMEM((rows, width), jnp.float32)],
    )


def output_kernel(begun, last, lines, ids_ref, attended_ref, w_ref, down_ref, *refs):
    begun_refs, rest = refs[:begun], refs[begun:]
    if last:
        table_ref, up_ref, before_refs, out_ref = rest[0], rest[1], rest[2:-1], rest[-1]
    else:
        acc_ref, low_ref = rest
    count = ids_ref.shape[0] - 1
    attended = attended_ref[...]
    features = attended.shape[1]
    if lines:
        weight = jnp.concatenate([w_ref[i, lines:] for i in range(w_ref.shape[0])], axis=0)
    else:
        weight = w_ref[...]
    downs = []
    for j in range(count):
        down = down_ref[ids_ref[1 + j]]
        downs += [down[:, at : at + features] for at in range(0, down.shape[1], features)]
    down = jnp.concatenate(downs, axis=0)
    rank = down.shape[0] // count
    total = jnp.dot(attended, weight, preferred_element_type=jnp.float32)
    low = lax.dot_general(
        attended, down, (((1,), (1,)), ((), ())), preferred_element_type=jnp.float32
    )
    if begun:
        total, low = begun_refs[0][...] + total, begun_refs[1][...] + low
    if last:
        low = low.astype(jnp.bfloat16).astype(jnp.float32)
        lane = lax.broadcasted_iota(jnp.int32, low.shape, 1)
        kept = (lane >= table_ref[:, 1:2]) & (lane < table_ref[:, 1:2] + rank)
        low = jnp.where(kept, low, 0.0).astype(jnp.bfloat16)
        up = jnp.concatenate([up_ref[ids_ref[1 + j]] for j in range(count)], axis=0)
        extra = jnp.dot(low, up, preferred_element_type=jnp.float32)
        first_row = out_ref.shape[0] - total.shape[0]
        for before_ref in before_refs:
            out_ref[:first_row, :] = before_ref[...]
        out_ref[first_row:, :] = (total + extra).astype(jnp.bfloat16)
    else:
        acc_ref[...] = total
        low_ref[...] = low


def project_out(ids, rank, attended, weight, down, begun, final, part=0):
    rows, features = attended.shape
    columns = weight.shape[-1]
    if len(weight.shape) == 2:
        down_spec, down_rows = None, 0
    else:
        down_rows = rank * features // columns
        down_spec = pl.BlockSpec(
            (down, down_rows, columns), lambda step, ids: (ids[0], 0, 0)
        )
        down = weight
    sums = (
        jax.ShapeDtypeStruct((rows, columns), jnp.float32),
        jax.ShapeDtypeStruct((rows, (ids.shape[0] - 1) * rank), jnp.float32),
    )
    all_rows = rows + sum(item.shape[0] for item in final[2:])
    return call(
        functools.partial(output_kernel, len(begun), bool(final), down_rows),
        "project_out",
        ids,
        1,
        [None, None, down_spec] + [None] * len(begun)
        + [rows_spec(table, rows, part) for table in final[:1]] + [None] * len(final[1:]),
        [attended, weight, down, *begun, *final],
        jax.ShapeDtypeStruct((all_rows, columns), jnp.bfloat16) if final else sums,
    )


def local(
    plane_size,
    planes,
    tokens,
    query_key_value_weight,
    output_weight,
    adapter_down_maps,
    adapter_up_maps,
    output_down_maps,
    output_up_maps,
    request_adapter,
    lengths,
):
    token_rows, depth = tokens.shape
    _, slots, head_size = query_key_value_weight.shape
    queries = slots - 2
    pool, rank = plane_size // lax.axis_size("groups"), adapter_up_maps.shape[1]
    features = queries * head_size
    columns = output_weight.shape[2] // planes
    here = lax.axis_index("tensor")
    place = lax.axis_index(PLANE)
    planes_of = (here - jnp.arange(planes) + planes) % planes

    def turned(value, turn=1):
        return lax.ppermute(value, "tensor", [(i, (i + turn) % planes) for i in range(planes)])

    weight = jnp.transpose(query_key_value_weight, (1, 0, 2))
    down_all = lax.all_gather(adapter_down_maps, "dp", axis=0, tiled=True)
    up_all = lax.all_gather(jnp.transpose(adapter_up_maps[0], (1, 0, 2)), "dp", axis=0)

    requests = request_adapter.shape[1]
    request_ends = jnp.cumsum(lengths[0])
    request_starts = request_ends - lengths[0]
    at = jnp.arange(token_rows, dtype=jnp.int32)
    member = (at[:, None] >= request_starts[None, :]) & (at[:, None] < request_ends[None, :])
    if pool <= requests:
        adapters, label = jnp.arange(pool), request_adapter[0]
    else:
        adapters, label = request_adapter[0], jnp.arange(requests)
    wanted = jnp.stack([request_starts, label * rank], axis=0)
    table = jnp.sum(jnp.where(member[:, None, :], wanted[None], 0), axis=2).astype(jnp.int32)
    position = at - table[:, 0]
    half = head_size // 2
    inv_freq = 10000.0 ** (-2.0 * jnp.arange(half, dtype=jnp.float32) / head_size)
    angles = position.astype(jnp.float32)[:, None] * inv_freq[None, :]
    cosine, sine = jnp.cos(angles), jnp.sin(angles)
    turn = jnp.concatenate([cosine, cosine, -sine, sine], axis=1)

    own_rows = jnp.transpose(
        lax.dynamic_slice_in_dim(output_weight, here * columns, columns, axis=2), (1, 0, 2)
    ).reshape(features, columns)
    share = features // plane_size
    line = place * share
    piece = lax.dynamic_slice(
        output_weight, (line % head_size, line // head_size, 0),
        (share, 1, output_weight.shape[2]),
    )[:, 0]
    out_down = output_down_maps[0].reshape(rank, features)
    out_down = jnp.concatenate(jnp.split(out_down, columns // features, axis=0), axis=1)
    sends = [
        jnp.concatenate(
            [
                out_down,
                lax.dynamic_slice_in_dim(piece, (here + k) % planes * columns, columns, axis=1),
            ],
            axis=0,
        )
        for k in range(1, planes)
    ]

    def shard(number):
        start = planes_of[number] * depth
        return lax.dynamic_slice_in_dim(weight, start, depth, axis=1)

    half_rows = token_rows // 2
    arrived = [tokens[:half_rows], tokens[half_rows:]]
    moved = [turned(half) for half in arrived]
    lines = [turned(send, k) for k, send in enumerate(sends, 1)]
    begun = project(arrived, shard(0))
    sums = shrink_partial(adapters, here, planes, table, tokens, down_all)
    done = (moved, lines, begun, table, turn, up_all, own_rows, shard(1), sums)
    done = lax.optimization_barrier(done)
    moved, lines, begun, table, turn, up_all, own_rows, part_weight, sums = done
    for step in range(2, planes):
        arrived = moved
        last = step == planes - 1
        moved = [turned(arrived[0]), arrived[1] if last else turned(arrived[1])]
        begun = project(arrived, part_weight, [begun])
        side = ()
        if step == 2:
            sums = [sums[0]] + [turned(sums[k], k) for k in range(1, planes)]
            lines = lax.all_gather(jnp.stack(lines), PLANE, axis=0)
            side = (
                sums,
                lax.all_gather(after(output_up_maps, sums[0]), "dp", axis=0, tiled=True),
                lax.all_gather(after(out_down, sums[0]), "dp", axis=0),
            )
        elif step == 3:
            shrink = sum(sums[1:], sums[0]).astype(jnp.bfloat16)
            shrink = [shrink] + [turned(shrink, k) for k in range(1, planes)]
            side = (shrink, [lines[:, k] for k in range(planes - 1)])
        if step == 3:
            shrink, lines = side
        if last:
            part_weight = shard(step)
            moved[1] = turned(after(moved[1], moved[0], begun, *shrink, *lines))
            break
        done = lax.optimization_barrier((moved, begun, shard(step), side))
        moved, begun, part_weight, side = done
        if step == 2:
            sums, out_up_all, own_down = side

    ids = jnp.concatenate([lax.axis_index("groups")[None], adapters])
    attended, earlier = [[], []], ()
    for part in range(2):
        made, *earlier = attend(
            planes_of, adapters, part, table, turn, up_all, shrink, moved[part], part_weight,
            begun, earlier,
        )
        attended[part] = [made, turned(after(made, *attended[0][1:]))]
    sums = [
        project_out(ids, rank, attended[part][0], own_rows, own_down, [], []) for part in range(2)
    ]
    before = []
    for step in range(2, planes + 1):
        for part in range(2):
            arrived = attended[part][-1]
            if step < planes:
                ahead = [*attended[0][step:], *sums[part]]
                attended[part].append(turned(after(arrived, *ahead)))
            final = [] if step < planes else [table, out_up_all, *before]
            sums[part] = project_out(
                ids, rank, arrived, lines[step - 2], pool, list(sums[part]), final, part
            )
            if final:
                before = [sums[part]]
    return before[0]


def solution(mesh):
    in_specs = (
        P(PLANE, "tensor"),
        P(None, None, "tensor"),
        P("tensor", None, None),
        P(PLANE, None, "tensor"),
        P(PLANE, None, None, "tensor"),
        P(PLANE, None, None, "tensor"),
        P(PLANE, None, "tensor"),
        P(PLANE, None),
        P(PLANE, None),
    )
    function = functools.partial(
        local, mesh.shape["groups"] * mesh.shape["dp"], mesh.shape["tensor"]
    )
    return jax.shard_map(
        function, mesh=mesh, in_specs=in_specs, out_specs=P(PLANE, "tensor"), check_vma=False
    )
```

```python
import functools
import math

import jax
import jax.numpy as jnp
from jax import lax
from jax.experimental import pallas as pl
from jax.experimental.pallas import tpu as pltpu
from jax.sharding import PartitionSpec as P

VMEM_BYTES = 40 * 1024 * 1024
PLANE = ("groups", "dp")


def after(value, *earlier):
    return lax.optimization_barrier((value,) + earlier)[0]


def fixed(array):
    shape = array.shape
    return pl.BlockSpec(shape, lambda step, ids: (0,) * len(shape))


def call(kernel, name, ids, grid, specs, arrays, out, scratch=(), grant=VMEM_BYTES):
    total = sum(array.size * array.dtype.itemsize for array in arrays)
    return pl.pallas_call(
        kernel,
        out_shape=out,
        grid_spec=pltpu.PrefetchScalarGridSpec(
            num_scalar_prefetch=1,
            grid=(grid,),
            in_specs=[fixed(array) if spec is None else spec for spec, array in zip(specs, arrays)],
            out_specs=[fixed(item) for item in out] if isinstance(out, tuple) else fixed(out),
            scratch_shapes=list(scratch),
        ),
        compiler_params=pltpu.CompilerParams(vmem_limit_bytes=grant),
        cost_estimate=pl.CostEstimate(flops=0, bytes_accessed=3 * total, transcendentals=0),
        name=name,
    )(ids.astype(jnp.int32), *arrays)


def accumulate(acc_ref, token_ref, w_ref, first):
    slots, _, head_size = w_ref.shape
    for pair in range(slots // 2):
        columns = slice(2 * pair * head_size, (2 * pair + 2) * head_size)
        weight = jnp.concatenate([w_ref[2 * pair], w_ref[2 * pair + 1]], axis=1)
        total = jnp.dot(token_ref[...], weight, preferred_element_type=jnp.float32)
        acc_ref[:, columns] = total if first is None else first[:, columns] + total


def project_kernel(parts, begun, ids_ref, *refs):
    w_ref, acc_ref = refs[parts], refs[-1]
    row = 0
    for token_ref in refs[:parts]:
        rows = pl.ds(row, token_ref.shape[0])
        first = refs[parts + 1].at[rows] if begun else None
        accumulate(acc_ref.at[rows], token_ref, w_ref, first)
        row += token_ref.shape[0]


def rows_spec(array, rows, part):
    if array.shape[0] == rows:
        return None
    return pl.BlockSpec((rows, array.shape[1]), lambda step, ids: (part, 0))


def project(tokens, weight, begun=()):
    slots, _, head_size = weight.shape
    rows = sum(part.shape[0] for part in tokens)
    return call(
        functools.partial(project_kernel, len(tokens), len(begun)),
        "project",
        jnp.zeros(1),
        1,
        [None] * (len(tokens) + 1 + len(begun)),
        [*tokens, weight, *begun],
        jax.ShapeDtypeStruct((rows, slots * head_size), jnp.float32),
    )


def attend_kernel(planes, earlier, ids_ref, table_ref, turn_ref, up_ref, *refs):
    piece_refs, refs = refs[:planes], refs[planes:]
    token_ref, w_ref, begun_ref, refs = refs[0], refs[1], refs[2], refs[3:]
    earlier_refs, refs = refs[: 2 * earlier], refs[2 * earlier :]
    out_ref, keys_ref, values_ref, acc_ref, shrink_ref = refs
    for number, piece_ref in enumerate(piece_refs):
        width = piece_ref.shape[1]
        size = piece_ref.shape[0] * 2 // 3
        start = pl.multiple_of(ids_ref[number] * size, size)
        shrink_ref[pl.ds(start, size), :width] = piece_ref[:size, :]
        shrink_ref[pl.ds(start, size // 2), width:] = piece_ref[size:, : width // 2]
        shrink_ref[pl.ds(start + size // 2, size // 2), width:] = piece_ref[size:, width // 2 :]
    accumulate(acc_ref, token_ref, w_ref, begun_ref)
    slots, _, head_size = w_ref.shape
    rank = up_ref.shape[2]
    count = ids_ref.shape[0] - planes
    rows = acc_ref.shape[0]
    first_row = earlier_refs[0].shape[0] if earlier else 0
    queries = slots - 2
    lane = lax.broadcasted_iota(jnp.int32, (rows, count * rank), 1)
    kept = (lane >= table_ref[:, 1:2]) & (lane < table_ref[:, 1:2] + rank)
    lows = []
    for part in range(3):
        piece = shrink_ref[first_row : first_row + rows, part * rank : (part + 1) * rank]
        piece = jnp.concatenate([piece.astype(jnp.float32)] * count, axis=1)
        lows.append(jnp.where(kept, piece, 0.0).astype(jnp.bfloat16))

    def slot(index):
        low = lows[0 if index < queries else index - queries + 1]
        up = jnp.concatenate([up_ref[ids_ref[planes + j], index] for j in range(count)], axis=0)
        extra = jnp.dot(low, up, preferred_element_type=jnp.float32)
        return acc_ref[:, index * head_size : (index + 1) * head_size] + extra

    def rotated(index):
        value = slot(index)
        turned = pltpu.roll(value, head_size // 2, 1)
        return (value * turn_ref[:, :head_size] + turned * turn_ref[:, head_size:]).astype(
            jnp.bfloat16
        )

    keys = rotated(queries)
    values = slot(queries + 1).astype(jnp.bfloat16)
    keys_ref[...] = keys
    values_ref[...] = values
    if earlier:
        keys = jnp.concatenate([earlier_refs[0][...], keys], axis=0)
        values = jnp.concatenate([earlier_refs[1][...], values], axis=0)
    shape = (rows, keys.shape[0])
    key_at = lax.broadcasted_iota(jnp.int32, shape, 1)
    row_at = lax.broadcasted_iota(jnp.int32, shape, 0) + first_row
    allowed = (key_at >= table_ref[:, 0:1]) & (key_at <= row_at)
    for index in range(queries):
        scores = lax.dot_general(
            rotated(index), keys, (((1,), (1,)), ((), ())), preferred_element_type=jnp.float32
        )
        scores = jnp.where(allowed, scores * (1.0 / math.sqrt(head_size)), -1e30)
        weights = jnp.exp(scores - jnp.max(scores, axis=1, keepdims=True))
        scale = 1.0 / jnp.sum(weights, axis=1, keepdims=True)
        attended = jnp.dot(
            (weights * scale).astype(jnp.bfloat16), values, preferred_element_type=jnp.float32
        )
        out_ref[:, index * head_size : (index + 1) * head_size] = attended.astype(jnp.bfloat16)


def attend(planes_of, adapters, part, table, turn, up, shrink, tokens, weight, begun, earlier):
    rows = tokens.shape[0]
    slots, _, head_size = weight.shape
    planes = len(shrink)
    arrays = [table, turn, up, *shrink, tokens, weight, begun, *earlier]
    specs = [None] * len(arrays)
    for index in (0, 1, 3 + planes, 5 + planes):
        specs[index] = rows_spec(arrays[index], rows, part)
    return call(
        functools.partial(attend_kernel, planes, len(earlier) // 2),
        "attend",
        jnp.concatenate([planes_of, adapters]),
        1,
        specs,
        arrays,
        (
            jax.ShapeDtypeStruct((rows, (slots - 2) * head_size), jnp.bfloat16),
            jax.ShapeDtypeStruct((rows, head_size), jnp.bfloat16),
            jax.ShapeDtypeStruct((rows, head_size), jnp.bfloat16),
        ),
        [
            pltpu.VMEM((rows, slots * head_size), jnp.float32),
            pltpu.VMEM(
                (planes * shrink[0].shape[0] * 2 // 3, shrink[0].shape[1] * 3 // 2), jnp.bfloat16
            ),
        ],
        VMEM_BYTES if earlier else 60 * 1024 * 1024,
    )


def shrink_kernel(planes, ids_ref, table_ref, token_ref, down_ref, *refs):
    out_refs, acc_ref = refs[:planes], refs[planes]
    step = pl.program_id(0)
    count = ids_ref.shape[0] - 1
    part = lax.dot_general(
        token_ref[...], down_ref[0], (((1,), (1,)), ((), ())), preferred_element_type=jnp.float32
    )
    rank = part.shape[1] // 3
    part = jnp.where(table_ref[:, 1:2] == step * rank, part, 0.0)

    @pl.when(step == 0)
    def _():
        acc_ref[...] = part

    @pl.when(step > 0)
    def _():
        acc_ref[...] += part

    @pl.when(step == count - 1)
    def _():
        for turn, out_ref in enumerate(out_refs):
            rows = out_ref.shape[0] * 2 // 3
            plane = lax.rem(ids_ref[count] + turn, planes)
            piece = acc_ref[pl.ds(pl.multiple_of(plane * rows, rows), rows), :]
            out_ref[:rows, :] = piece[:, : 2 * rank]
            out_ref[rows:, :] = jnp.concatenate(
                [piece[: rows // 2, 2 * rank :], piece[rows // 2 :, 2 * rank :]], axis=1
            )


def shrink_partial(adapters, here, planes, table, tokens, down):
    _, width, depth = down.shape
    rows = tokens.shape[0]
    return call(
        functools.partial(shrink_kernel, planes),
        "shrink",
        jnp.concatenate([adapters, here[None]]),
        adapters.shape[0],
        [None, None, pl.BlockSpec((1, width, depth), lambda step, ids: (ids[step], 0, 0))],
        [table, tokens, down],
        (jax.ShapeDtypeStruct((rows // planes * 3 // 2, width * 2 // 3), jnp.float32),) * planes,
        [pltpu.VMEM((rows, width), jnp.float32)],
    )


def output_kernel(begun, last, lines, ids_ref, attended_ref, w_ref, down_ref, *refs):
    begun_refs, rest = refs[:begun], refs[begun:]
    if last:
        table_ref, up_ref, before_refs, out_ref = rest[0], rest[1], rest[2:-1], rest[-1]
    else:
        acc_ref, low_ref = rest
    count = ids_ref.shape[0] - 1
    attended = attended_ref[...]
    features = attended.shape[1]
    if lines:
        weight = jnp.concatenate([w_ref[i, lines:] for i in range(w_ref.shape[0])], axis=0)
    else:
        weight = w_ref[...]
    downs = []
    for j in range(count):
        down = down_ref[ids_ref[1 + j]]
        downs += [down[:, at : at + features] for at in range(0, down.shape[1], features)]
    down = jnp.concatenate(downs, axis=0)
    rank = down.shape[0] // count
    total = jnp.dot(attended, weight, preferred_element_type=jnp.float32)
    low = lax.dot_general(
        attended, down, (((1,), (1,)), ((), ())), preferred_element_type=jnp.float32
    )
    if begun:
        total, low = begun_refs[0][...] + total, begun_refs[1][...] + low
    if last:
        low = low.astype(jnp.bfloat16).astype(jnp.float32)
        lane = lax.broadcasted_iota(jnp.int32, low.shape, 1)
        kept = (lane >= table_ref[:, 1:2]) & (lane < table_ref[:, 1:2] + rank)
        low = jnp.where(kept, low, 0.0).astype(jnp.bfloat16)
        up = jnp.concatenate([up_ref[ids_ref[1 + j]] for j in range(count)], axis=0)
        extra = jnp.dot(low, up, preferred_element_type=jnp.float32)
        first_row = out_ref.shape[0] - total.shape[0]
        for before_ref in before_refs:
            out_ref[:first_row, :] = before_ref[...]
        out_ref[first_row:, :] = (total + extra).astype(jnp.bfloat16)
    else:
        acc_ref[...] = total
        low_ref[...] = low


def project_out(ids, rank, attended, weight, down, begun, final, part=0):
    rows, features = attended.shape
    columns = weight.shape[-1]
    if len(weight.shape) == 2:
        down_spec, down_rows = None, 0
    else:
        down_rows = rank * features // columns
        down_spec = pl.BlockSpec(
            (down, down_rows, columns), lambda step, ids: (ids[0], 0, 0)
        )
        down = weight
    sums = (
        jax.ShapeDtypeStruct((rows, columns), jnp.float32),
        jax.ShapeDtypeStruct((rows, (ids.shape[0] - 1) * rank), jnp.float32),
    )
    all_rows = rows + sum(item.shape[0] for item in final[2:])
    return call(
        functools.partial(output_kernel, len(begun), bool(final), down_rows),
        "project_out",
        ids,
        1,
        [None, None, down_spec] + [None] * len(begun)
        + [rows_spec(table, rows, part) for table in final[:1]] + [None] * len(final[1:]),
        [attended, weight, down, *begun, *final],
        jax.ShapeDtypeStruct((all_rows, columns), jnp.bfloat16) if final else sums,
    )


def local(
    plane_size,
    planes,
    tokens,
    query_key_value_weight,
    output_weight,
    adapter_down_maps,
    adapter_up_maps,
    output_down_maps,
    output_up_maps,
    request_adapter,
    lengths,
):
    token_rows, depth = tokens.shape
    _, slots, head_size = query_key_value_weight.shape
    queries = slots - 2
    pool, rank = plane_size // lax.axis_size("groups"), adapter_up_maps.shape[1]
    features = queries * head_size
    columns = output_weight.shape[2] // planes
    here = lax.axis_index("tensor")
    place = lax.axis_index(PLANE)
    planes_of = (here - jnp.arange(planes) + planes) % planes

    def turned(value, turn=1):
        return lax.ppermute(value, "tensor", [(i, (i + turn) % planes) for i in range(planes)])

    weight = jnp.transpose(query_key_value_weight, (1, 0, 2))
    down_all = lax.all_gather(adapter_down_maps, "dp", axis=0, tiled=True)
    up_all = lax.all_gather(jnp.transpose(adapter_up_maps[0], (1, 0, 2)), "dp", axis=0)

    requests = request_adapter.shape[1]
    request_ends = jnp.cumsum(lengths[0])
    request_starts = request_ends - lengths[0]
    at = jnp.arange(token_rows, dtype=jnp.int32)
    member = (at[:, None] >= request_starts[None, :]) & (at[:, None] < request_ends[None, :])
    if pool <= requests:
        adapters, label = jnp.arange(pool), request_adapter[0]
    else:
        adapters, label = request_adapter[0], jnp.arange(requests)
    wanted = jnp.stack([request_starts, label * rank], axis=0)
    table = jnp.sum(jnp.where(member[:, None, :], wanted[None], 0), axis=2).astype(jnp.int32)
    position = at - table[:, 0]
    half = head_size // 2
    inv_freq = 10000.0 ** (-2.0 * jnp.arange(half, dtype=jnp.float32) / head_size)
    angles = position.astype(jnp.float32)[:, None] * inv_freq[None, :]
    cosine, sine = jnp.cos(angles), jnp.sin(angles)
    turn = jnp.concatenate([cosine, cosine, -sine, sine], axis=1)

    own_rows = jnp.transpose(
        lax.dynamic_slice_in_dim(output_weight, here * columns, columns, axis=2), (1, 0, 2)
    ).reshape(features, columns)
    share = features // plane_size
    line = place * share
    piece = lax.dynamic_slice(
        output_weight, (line % head_size, line // head_size, 0),
        (share, 1, output_weight.shape[2]),
    )[:, 0]
    out_down = output_down_maps[0].reshape(rank, features)
    out_down = jnp.concatenate(jnp.split(out_down, columns // features, axis=0), axis=1)
    sends = [
        jnp.concatenate(
            [
                out_down,
                lax.dynamic_slice_in_dim(piece, (here + k) % planes * columns, columns, axis=1),
            ],
            axis=0,
        )
        for k in range(1, planes)
    ]

    def shard(number):
        start = planes_of[number] * depth
        return lax.dynamic_slice_in_dim(weight, start, depth, axis=1)

    half_rows = token_rows // 2
    arrived = [tokens[:half_rows], tokens[half_rows:]]
    moved = [turned(half) for half in arrived]
    lines = [turned(send, k) for k, send in enumerate(sends, 1)]
    begun = project(arrived, shard(0))
    sums = shrink_partial(adapters, here, planes, table, tokens, down_all)
    done = (moved, lines, begun, table, turn, up_all, own_rows, shard(1), sums)
    done = lax.optimization_barrier(done)
    moved, lines, begun, table, turn, up_all, own_rows, part_weight, sums = done
    for step in range(2, planes):
        arrived = moved
        last = step == planes - 1
        moved = [turned(arrived[0]), arrived[1] if last else turned(arrived[1])]
        begun = project(arrived, part_weight, [begun])
        side = ()
        if step == 2:
            sums = [sums[0]] + [turned(sums[k], k) for k in range(1, planes)]
            lines = lax.all_gather(jnp.stack(lines), PLANE, axis=0)
            side = (
                sums,
                lax.all_gather(after(output_up_maps, sums[0]), "dp", axis=0, tiled=True),
                lax.all_gather(after(out_down, sums[0]), "dp", axis=0),
            )
        elif step == 3:
            shrink = sum(sums[1:], sums[0]).astype(jnp.bfloat16)
            shrink = [shrink] + [turned(shrink, k) for k in range(1, planes)]
            side = (shrink, [lines[:, k] for k in range(planes - 1)])
        done = lax.optimization_barrier((moved, begun, shard(step), side))
        moved, begun, part_weight, side = done
        if step == 2:
            sums, out_up_all, own_down = side
        elif step == 3:
            shrink, lines = side
    moved[1] = turned(moved[1])

    ids = jnp.concatenate([lax.axis_index("groups")[None], adapters])
    attended, earlier = [[], []], ()
    for part in range(2):
        made, *earlier = attend(
            planes_of, adapters, part, table, turn, up_all, shrink, moved[part], part_weight,
            begun, earlier,
        )
        attended[part] = [made, turned(after(made, *attended[0][1:]))]
    sums = [
        project_out(ids, rank, attended[part][0], own_rows, own_down, [], []) for part in range(2)
    ]
    before = []
    for step in range(2, planes + 1):
        for part in range(2):
            arrived = attended[part][-1]
            if step < planes:
                ahead = [*attended[0][step:], *sums[part]]
                attended[part].append(turned(after(arrived, *ahead)))
            final = [] if step < planes else [table, out_up_all, *before]
            sums[part] = project_out(
                ids, rank, arrived, lines[step - 2], pool, list(sums[part]), final, part
            )
            if final:
                before = [sums[part]]
    return before[0]


def solution(mesh):
    in_specs = (
        P(PLANE, "tensor"),
        P(None, None, "tensor"),
        P("tensor", None, None),
        P(PLANE, None, "tensor"),
        P(PLANE, None, None, "tensor"),
        P(PLANE, None, None, "tensor"),
        P(PLANE, None, "tensor"),
        P(PLANE, None),
        P(PLANE, None),
    )
    function = functools.partial(
        local, mesh.shape["groups"] * mesh.shape["dp"], mesh.shape["tensor"]
    )
    return jax.shard_map(
        function, mesh=mesh, in_specs=in_specs, out_specs=P(PLANE, "tensor"), check_vma=False
    )
```
